32 devices in a mesh: dp: 8 (over z, y), win: 4 (over x, core).
Axes of the slice: x: 2, y: 2, z: 4, core: 2. Of those that a mesh axis runs over, the one named last changes fastest.
Arguments:
- patches: bfloat16 [96, 4, 49, 768], P('dp', 'win'), may hold values from -6 to 6
- cotangent: bfloat16 [96, 4, 49, 768], P('dp', 'win'), may hold values from -6 to 6
- grid_sizes: int32 [96], P('dp'), may hold values from 7 to 12, as said below
- conv_weight: bfloat16 [3, 9, 768], P(None, None, 'dp'), may hold values from -2 to 2
- conv_bias: bfloat16 [3, 768], P(None, 'dp'), may hold values from -1.796875 to 1.796875
- norm_gain: bfloat16 [4, 768], P(None, 'dp'), may hold values from 0.25 to 1.75
- norm_bias: bfloat16 [4, 768], P(None, 'dp'), may hold values from -1.796875 to 1.796875
- qkv_weight: bfloat16 [2, 768, 2304], P(None, 'dp'), may hold values from -0.21875 to 0.21875
- spatial_bias: bfloat16 [1536], P('dp'), may hold values from -1.796875 to 1.796875
- channel_bias: bfloat16 [2304], P('dp'), may hold values from -1.796875 to 1.796875
- proj_weight: bfloat16 [2, 768, 768], P(None, 'dp'), may hold values from -0.625 to 0.625
- proj_bias: bfloat16 [2, 768], P(None, 'dp'), may hold values from -1.796875 to 1.796875
- hidden_weight: bfloat16 [2, 768, 3072], P(None, 'dp'), may hold values from -0.21875 to 0.21875
- hidden_bias: bfloat16 [2, 3072], P(None, 'dp'), may hold values from -1.796875 to 1.796875
- output_weight: bfloat16 [2, 3072, 768], P(None, 'dp'), may hold values from -0.109375 to 0.109375
- output_bias: bfloat16 [2, 768], P(None, 'dp'), may hold values from -1.796875 to 1.796875
Outputs:
- activations: bfloat16 [96, 4, 49, 768], P('dp', 'win')
- patches_grad: bfloat16 [96, 4, 49, 768], P('dp', 'win')
- conv_weight_grad: float32 [3, 9, 768], P(None, None, 'dp')
- conv_bias_grad: float32 [3, 768], P(None, 'dp')
- norm_gain_grad: float32 [4, 768], P(None, 'dp')
- norm_bias_grad: float32 [4, 768], P(None, 'dp')
- qkv_weight_grad: float32 [2, 768, 2304], P(None, 'dp')
- spatial_bias_grad: float32 [1536], P('dp')
- channel_bias_grad: float32 [2304], P('dp')
- proj_weight_grad: float32 [2, 768, 768], P(None, 'dp')
- proj_bias_grad: float32 [2, 768], P(None, 'dp')
- hidden_weight_grad: float32 [2, 768, 3072], P(None, 'dp')
- hidden_bias_grad: float32 [2, 3072], P(None, 'dp')
- output_weight_grad: float32 [2, 3072, 768], P(None, 'dp')
- output_bias_grad: float32 [2, 768], P(None, 'dp')
The draws below stay inside these ranges and needn't reach their ends.
Inputs may be any that keep to these rules, and one draw needn't show every extreme that they name: `grid_sizes`: each image's grid side is 7, 9 or 12; among the 12 images of each index of dp at least one has side 12.
All inputs are finite; a program needn't handle non-finite values.
Results may differ from the reference program's by a relative error of at most 0.035.
Values may be sent and summed in bfloat16 or wider, within the bound.
A program may use at most 384 MiB of HBM per device.

```python
import jax
import jax.numpy as jnp
from jax import lax

D = 768
HEADS = 24
HEAD = 32
FF = 3072
IMG_DEV = 12
IMAGES = 96


def draw_grid_sizes(key, part):
    key = jax.random.fold_in(key, 11)
    coin_key, pick_key = jax.random.split(key)
    coins = jax.random.randint(coin_key, (IMAGES,), 0, 4)
    chosen = jax.random.randint(pick_key, (IMAGES // IMG_DEV,), 0, IMG_DEV)
    positions = jnp.arange(IMAGES, dtype=jnp.int32)
    forced = positions % IMG_DEV == jnp.repeat(chosen, IMG_DEV)
    drawn = jnp.where(coins == 3, 12, jnp.where(coins == 2, 9, 7))
    return jnp.where(forced, 12, drawn).astype(jnp.int32)


def spiked(result, stream_key, source, target, parts, factor):
    owner, partner = [(jnp.arange(result.shape[position]) // (result.shape[position] // parts)).reshape([-1 if axis == position else 1 for axis in range(result.ndim)]) for position in (source, target)]
    chosen = jax.random.permutation(stream_key, parts)[partner]
    strong = (owner == chosen) | (owner == (partner + parts // 2) % parts)
    return jnp.where(strong, factor * result, result)


def level_of(stream_key, shape, shards, smallest, top_value):
    def one(position, parts):
        draws = jax.random.uniform(jax.random.fold_in(jax.random.fold_in(stream_key, 6), position), (parts,), jnp.float32, smallest / len(shards), top_value / len(shards))
        return jnp.repeat(jnp.exp(draws), shape[position] // parts).reshape((-1,) + (1,) * (len(shape) - position - 1))

    level = one(*shards[0])
    for cut in shards[1:]:
        level = level * one(*cut)
    return level


def centred(own_key, extent, deviation, reach, cuts=(), kind=jnp.bfloat16):
    values = jax.random.normal(own_key, extent, jnp.float32) * deviation
    if len(cuts) > 0:
        values = level_of(own_key, extent, cuts, -0.22, 0.18) * values
    return jnp.clip(values, min=-reach, max=reach).astype(kind)


def gaussian_with(own_key, dims, width, most, pieces, heavy, held_as=jnp.bfloat16):
    entries = width * jax.random.normal(own_key, dims, jnp.float32)
    if pieces:
        entries = entries * level_of(own_key, dims, pieces, -0.22, 0.18)
    return jnp.clip(spiked(entries, jax.random.fold_in(own_key, 3), *heavy), -most, most).astype(held_as)


def setup_inputs(seed: int = 0) -> dict:
    seeds = jax.random.split(jax.random.key(seed), 17)
    return {
        "patches": centred(seeds[0], (IMAGES, 4, 49, D), 1.0, 6.0, ((0, 8), (1, 4))),
        "cotangent": gaussian_with(seeds[1], (IMAGES, 4, 49, D), 1.0, 6.0, ((0, 8), (1, 4)), (0, 3, 8, 2.0)),
        "grid_sizes": draw_grid_sizes(jax.random.fold_in(seeds[16], 71), 0),
        "conv_weight": centred(seeds[3], (3, 9, D), 9 ** -0.5, 2.0, ((2, 8),)),
        "conv_bias": centred(seeds[4], (3, D), 0.3, 1.796875, ((1, 8),)),
        "norm_gain": jnp.clip(1.0 + 0.15 * jax.random.normal(seeds[5], (4, D), jnp.float32), 0.25, 1.75).astype(jnp.bfloat16),
        "norm_bias": centred(seeds[6], (4, D), 0.3, 1.796875, ((1, 8),)),
        "qkv_weight": centred(seeds[7], (2, D, 3 * D), D ** -0.5, 0.21875, ((1, 8),)),
        "spatial_bias": centred(seeds[8], (2 * D,), 0.3, 1.796875, ((0, 8),)),
        "channel_bias": centred(seeds[9], (3 * D,), 0.3, 1.796875, ((0, 8),)),
        "proj_weight": centred(seeds[10], (2, D, D), (D // 8) ** -0.5, 0.625, ((1, 8),)),
        "proj_bias": centred(seeds[11], (2, D), 0.3, 1.796875, ((1, 8),)),
        "hidden_weight": centred(seeds[12], (2, D, FF), D ** -0.5, 0.21875, ((1, 8),)),
        "hidden_bias": centred(seeds[13], (2, FF), 0.3, 1.796875, ((1, 8),)),
        "output_weight": centred(seeds[14], (2, FF, D), FF ** -0.5, 0.109375, ((1, 8),)),
        "output_bias": centred(seeds[15], (2, D), 0.3, 1.796875, ((1, 8),)),
    }


EPS = 1e-05
HIGHEST = lax.Precision.HIGHEST

@jax.custom_vjp
def low(v):
    return lax.optimization_barrier(v.astype(jnp.bfloat16)).astype(jnp.float32)

@jax.custom_vjp
def low_back(v):
    return v

def low_keep(v):
    return (low(v), None)

def low_pass(kept, grad):
    return (grad,)

def back_keep(v):
    return (v, None)

def back_low(kept, grad):
    return (low(grad),)
low.defvjp(low_keep, low_pass)
low_back.defvjp(back_keep, back_low)

def image_valid(grid_sizes):
    rows = jnp.arange(7, dtype=jnp.int32)
    windows = jnp.arange(4, dtype=jnp.int32)
    top_rows = (windows // 2)[:, None] * 7 + rows[None, :]
    left_cols = (windows % 2)[:, None] * 7 + rows[None, :]
    sizes = grid_sizes.astype(jnp.int32)[:, None, None, None]
    inside = (top_rows[None, :, :, None] < sizes) & (left_cols[None, :, None, :] < sizes)
    return inside.astype(jnp.float32).reshape(grid_sizes.shape[0], 4, 49, 1)

def layer_norm(stream, gain_row, shift_row):
    centre = lax.optimization_barrier(jnp.mean(stream, -1, keepdims=True))
    centered = stream - centre
    variance = lax.optimization_barrier(jnp.mean(centered * centered, -1, keepdims=True))
    return centered * lax.rsqrt(variance + EPS) * gain_row + shift_row

def project(rows_in, weight):
    return jnp.einsum('...c,cd->...d', rows_in, weight, precision=HIGHEST)

def to_grid(stream):
    images = stream.shape[0]
    channels = stream.shape[-1]
    return stream.reshape(images, 2, 2, 7, 7, channels).transpose(0, 1, 3, 2, 4, 5).reshape(images, 14, 14, channels)

def from_grid(image_grid):
    images = image_grid.shape[0]
    channels = image_grid.shape[-1]
    return image_grid.reshape(images, 2, 7, 2, 7, channels).transpose(0, 1, 3, 2, 4, 5).reshape(images, 4, 49, channels)

def position_conv(stream, weight9, shift_row, valid):
    image_grid = to_grid(stream)
    padded = jnp.pad(image_grid, ((0, 0), (1, 1), (1, 1), (0, 0)))
    summed = jnp.zeros_like(image_grid)
    for tap_index in range(9):
        row_shift, col_shift = divmod(tap_index, 3)
        summed = summed + weight9[tap_index] * padded[:, row_shift:row_shift + 14, col_shift:col_shift + 14]
    return stream + valid * from_grid(summed + shift_row)

def mlp_branch(normed, weight_in, bias_in, weight_out, bias_out):
    hidden_pre = low_back(project(normed, weight_in) + bias_in)
    activated = low(jax.nn.gelu(hidden_pre, approximate=False))
    return low_back(project(activated, weight_out) + bias_out)

def layer_pair(params, patch_rows, valid):
    conv_w, conv_b, gains, shifts, qkv_w, sp_bias, ch_bias, proj_w, proj_b, hid_w, hid_b, out_w, out_b = params
    images = patch_rows.shape[0]
    model_width = patch_rows.shape[-1]
    scaling = HEAD ** (-0.5)
    stream = patch_rows * valid
    stream = position_conv(stream, conv_w[0], conv_b[0], valid)
    normed = low(layer_norm(stream, gains[0], shifts[0]))
    packed_bias = jnp.concatenate([sp_bias[:model_width], jnp.zeros((model_width,), sp_bias.dtype), sp_bias[model_width:]])
    packed = low(low_back(project(normed, qkv_w[0]) + packed_bias)).reshape(images, 4, 49, 3, HEADS, HEAD)
    key_ok = valid.reshape(images, 4, 1, 1, 49) > 0.5
    raw_scores = jnp.einsum('bwphe,bwqhe->bwhpq', packed[:, :, :, 0], packed[:, :, :, 1], precision=HIGHEST) * scaling
    scores = low_back(jnp.where(key_ok, raw_scores, -1000000000.0))
    attention = low(jax.nn.softmax(scores, axis=-1))
    context = jnp.einsum('bwhpq,bwqhe->bwphe', attention, packed[:, :, :, 2], precision=HIGHEST).reshape(images, 4, 49, model_width)
    context = low(low_back(context))
    stream = stream + valid * low_back(project(context, proj_w[0]) + proj_b[0])
    stream = position_conv(stream, conv_w[1], conv_b[1], valid)
    stream = stream + valid * mlp_branch(low(layer_norm(stream, gains[1], shifts[1])), hid_w[0], hid_b[0], out_w[0], out_b[0])
    stream = position_conv(stream, conv_w[2], conv_b[2], valid)
    normed = low(layer_norm(stream, gains[2], shifts[2]))
    packed = low(low_back(project(normed, qkv_w[1]) + ch_bias)).reshape(images, 196, 3, HEADS, HEAD)
    flat_valid = valid.reshape(images, 196, 1, 1)
    key_masked = packed[:, :, 1] * flat_valid
    value_masked = packed[:, :, 2] * flat_valid
    gram = low_back(jnp.einsum('bpgc,bpgd->bgcd', key_masked, value_masked, precision=HIGHEST) * scaling)
    mixing = low(jax.nn.softmax(gram, axis=-1))
    context = jnp.einsum('bgcd,bpgd->bpgc', mixing, packed[:, :, 0], precision=HIGHEST).reshape(images, 4, 49, model_width)
    context = low(low_back(context))
    stream = stream + valid * low_back(project(context, proj_w[1]) + proj_b[1])
    stream = stream + valid * mlp_branch(low(layer_norm(stream, gains[3], shifts[3])), hid_w[1], hid_b[1], out_w[1], out_b[1])
    return stream

def reference(patches, cotangent, grid_sizes, conv_weight, conv_bias, norm_gain, norm_bias, qkv_weight, spatial_bias, channel_bias, proj_weight, proj_bias, hidden_weight, hidden_bias, output_weight, output_bias):
    params = tuple((weight_arg.astype(jnp.float32) for weight_arg in (conv_weight, conv_bias, norm_gain, norm_bias, qkv_weight, spatial_bias, channel_bias, proj_weight, proj_bias, hidden_weight, hidden_bias, output_weight, output_bias)))
    groups = IMAGES // IMG_DEV
    patch_blocks = patches.astype(jnp.float32).reshape(groups, IMG_DEV, 4, 49, D)
    cot_blocks = cotangent.astype(jnp.float32).reshape(groups, IMG_DEV, 4, 49, D)
    valid_blocks = image_valid(grid_sizes).reshape(groups, IMG_DEV, 4, 49, 1)

    def one_block(totals, block_data):
        patch_block, cot_block, valid_block = block_data

        def forward(weights, inputs):
            return layer_pair(weights, inputs, valid_block)
        output, pullback = jax.vjp(forward, params, patch_block)
        weight_grads, input_grad = pullback(cot_block)
        totals = jax.tree.map(jnp.add, totals, weight_grads)
        return (totals, (output.astype(jnp.bfloat16), input_grad.astype(jnp.bfloat16)))
    zeros = jax.tree.map(jnp.zeros_like, params)
    totals, (outputs, input_grads) = lax.scan(one_block, zeros, (patch_blocks, cot_blocks, valid_blocks))
    return (outputs.reshape(IMAGES, 4, 49, D), input_grads.reshape(IMAGES, 4, 49, D), totals[0], totals[1], totals[2], totals[3], totals[4], totals[5], totals[6], totals[7], totals[8], totals[9], totals[10], totals[11], totals[12])
```

```python
import functools

import jax
import jax.numpy as jnp
from jax import lax
from jax.experimental import pallas as pl
from jax.experimental.pallas import tpu as pltpu
from jax.sharding import PartitionSpec as P

HEADS = 24
HEAD = 32
EPS = 1e-05
MESH = pl.DeviceIdType.MESH
F32 = jnp.float32
BF16 = jnp.bfloat16
SCALE = HEAD ** (-0.5)
CELLS = 56
PAIR = 112


def dot(left, right):
    return jnp.dot(left, right, preferred_element_type=F32)


def dot_t(left, right):
    return lax.dot_general(left, right, (((1,), (1,)), ((), ())), preferred_element_type=F32)


def t_dot(left, right):
    return lax.dot_general(left, right, (((0,), (0,)), ((), ())), preferred_element_type=F32)


def iota(shape, dim):
    return lax.broadcasted_iota(jnp.int32, shape, dim)


def rows_at(index, count):
    return pl.ds(pl.multiple_of(index * count, count), count)


def lanes_at(index, count, base=0):
    return pl.ds(pl.multiple_of(base + index * count, 128), count)


def each(count, body):
    def step(i, carry):
        body(i)
        return carry

    lax.fori_loop(0, count, step, 0)


def gelu_pair(pre):
    t = 1.0 / (1.0 + 0.23164190 * jnp.abs(pre))
    e = jnp.exp(-0.5 * pre * pre)
    poly = (((1.061405429 * t - 1.453152027) * t + 1.421413741) * t - 0.284496736) * t + 0.254829592
    tail = 0.5 * poly * t * e
    cdf = jnp.where(pre >= 0.0, 1.0 - tail, tail)
    return pre * cdf, cdf + pre * (e * 0.3989422804014327)


def place():
    d = lax.axis_index("dp")
    w = lax.axis_index("win")
    return d, w, w // 2, w % 2


def greet(peers):
    barrier = pltpu.get_barrier_semaphore()
    for peer in peers:
        pl.semaphore_signal(barrier, inc=1, device_id=peer, device_id_type=MESH)
    pl.semaphore_wait(barrier, len(peers))


def remote(src, dst, sems, peer):
    return pltpu.make_async_remote_copy(
        src_ref=src, dst_ref=dst, send_sem=sems.at[0], recv_sem=sems.at[1], device_id=peer, device_id_type=MESH
    )


def fill_valid(valid, sizes, images, wr, wc):
    def one(i):
        cell = iota((CELLS, 128), 0)
        r, c = cell >> 3, cell & 7
        inside = (r + 7 * wr < sizes[i]) & (c + 7 * wc < sizes[i]) & (c < 7)
        valid[rows_at(i, CELLS), :] = jnp.where(inside, 1.0, 0.0).astype(F32)

    each(images, one)


def spread(valid_rows, width):
    return jnp.concatenate([valid_rows] * (width // 128), axis=1)


def halo(pad, images, wr, wc, row_out, row_in, col_out, col_in, sems, vertical, horizontal):
    edge = 7 - 6 * wr

    def pack(p):
        one = pad[pl.ds(pl.multiple_of((18 * p + edge) * 8, 8), 8), :]
        two = pad[pl.ds(pl.multiple_of((18 * p + 9 + edge) * 8, 8), 8), :]
        row_out[rows_at(p, 16), :] = jnp.concatenate([one, two], axis=0).astype(BF16)

    each(images // 2, pack)
    copy = remote(row_out, row_in, sems.at[0], vertical)
    copy.start()
    copy.wait()
    border = 8 - 8 * wr

    def unpack(p):
        both = row_in[rows_at(p, 16), :].astype(F32)
        pad[pl.ds(pl.multiple_of((18 * p + border) * 8, 8), 8), :] = both[:8]
        pad[pl.ds(pl.multiple_of((18 * p + 9 + border) * 8, 8), 8), :] = both[8:]

    each(images // 2, unpack)
    turn = 2 - 2 * wc
    sub = iota((8, 128), 0)

    def row_of(i, s):
        at_row = border if s == 7 else s + 1
        return pl.ds(pl.multiple_of((9 * i + at_row) * 8, 8), 8)

    def pack_col(p):
        for part in range(pad.shape[1] // 128):
            at = pl.ds(part * 128, 128)
            both = []
            for i in (2 * p, 2 * p + 1):
                line = jnp.zeros((8, 128), F32)
                for s in range(8):
                    line = jnp.where(sub == s, pltpu.roll(pad[row_of(i, s), at], s + turn, 0), line)
                both.append(line)
            col_out[rows_at(p, 16), at] = jnp.concatenate(both, axis=0).astype(BF16)

    each(images // 2, pack_col)
    copy = remote(col_out, col_in, sems.at[1], horizontal)
    copy.start()
    copy.wait()

    def unpack_col(p):
        for part in range(pad.shape[1] // 128):
            at = pl.ds(part * 128, 128)
            both = col_in[rows_at(p, 16), at].astype(F32)
            for one in range(2):
                line = both[8 * one : 8 * one + 8]
                for s in range(8):
                    to = row_of(2 * p + one, s)
                    pad[to, at] = jnp.where(sub == 7, pltpu.roll(line, 7 - s, 0), pad[to, at])

    each(images // 2, unpack_col)


def side_masks(wr, wc):
    c = iota((8, 128), 0)
    left = jnp.where((c == 0) & (wc == 0), 0.0, 1.0).astype(F32)
    right = jnp.where((c == 6) & (wc == 1), 0.0, 1.0).astype(F32)
    return left, right


def three(pad, i, at, left, right):
    rows = [pad[pl.ds(pl.multiple_of((9 * i + r) * 8, 8), 8), at] for r in range(9)]
    return [(pltpu.roll(v, 1, 0) * left, v, pltpu.roll(v, 7, 0) * right) for v in rows]


def conv_forward(pad, images, vec, k, valid, out, left, right):
    def one(i):
        for part in range(pad.shape[1] // 128):
            at = pl.ds(part * 128, 128)
            moved = three(pad, i, at, left, right)
            bias = vec[27 + k : 28 + k, at]
            taps = [vec[9 * k + t : 9 * k + t + 1, at] for t in range(9)]
            for r in range(7):
                total = jnp.broadcast_to(bias, (8, 128))
                for t in range(9):
                    total = total + taps[t] * moved[r + t // 3][t % 3]
                to = pl.ds(pl.multiple_of((7 * i + r) * 8, 8), 8)
                out[to, at] = moved[r + 1][1] + valid[to, :] * total

    each(images, one)


def norm_rows(src, images, vec, k, dst):
    gain = vec[30 + k : 31 + k, :]
    shift = vec[34 + k : 35 + k, :]

    def one(p):
        x = src[rows_at(p, PAIR), :]
        centered = x - jnp.mean(x, -1, keepdims=True)
        variance = jnp.mean(centered * centered, -1, keepdims=True)
        dst[rows_at(p, PAIR), :] = (centered * lax.rsqrt(variance + EPS) * gain + shift).astype(BF16)

    each(images // 2, one)


def to_pad(pad, p, rows):
    pad[pl.ds(pl.multiple_of((18 * p + 1) * 8, 8), CELLS), :] = rows[:CELLS]
    pad[pl.ds(pl.multiple_of((18 * p + 10) * 8, 8), CELLS), :] = rows[CELLS:]


def of_pad(pad, p):
    return jnp.concatenate(
        [
            pad[pl.ds(pl.multiple_of((18 * p + 1) * 8, 8), CELLS), :],
            pad[pl.ds(pl.multiple_of((18 * p + 10) * 8, 8), CELLS), :],
        ],
        axis=0,
    )


def clear_borders(pad, images):
    zero = jnp.zeros((8, pad.shape[1]), F32)

    def one(i):
        pad[pl.ds(pl.multiple_of(72 * i, 8), 8), :] = zero
        pad[pl.ds(pl.multiple_of(72 * i + 64, 8), 8), :] = zero

    each(images, one)


def head_masks(kind):
    lane = iota((PAIR, 128), 1) >> 5
    return [jnp.where(lane == h, 1.0, 0.0).astype(F32).astype(kind) for h in range(4)]


def pair_mask(sizes, p, wr, wc):
    row = iota((PAIR, PAIR), 0)
    lane = iota((PAIR, PAIR), 1)
    second = lane >= CELLS
    cell = jnp.where(second, lane - CELLS, lane)
    side = jnp.where(second, sizes[2 * p + 1], sizes[2 * p])
    r, c = cell >> 3, cell & 7
    inside = (r + 7 * wr < side) & (c + 7 * wc < side) & (c < 7)
    return inside & (second == (row >= CELLS))


def stacked(value, masks):
    return jnp.concatenate([value * m for m in masks], axis=0)


def folded(value, masks):
    total = value[:PAIR] * masks[0]
    for h in range(1, 4):
        total = total + value[h * PAIR : (h + 1) * PAIR] * masks[h]
    return total


def pair_probs(query_bd, key, allowed):
    scores = dot_t(query_bd, key) * SCALE
    scores = jnp.where(allowed, scores, -1000000000.0)
    e = jnp.exp(scores - jnp.max(scores, -1, keepdims=True))
    return e * (1.0 / jnp.sum(e, -1, keepdims=True))


def window_attention(packed, images, sizes, wr, wc, context):
    width = context.shape[1]

    def pair(p):
        rows = rows_at(p, PAIR)
        allowed = jnp.concatenate([pair_mask(sizes, p, wr, wc).astype(F32)] * 4, axis=0) > 0.5
        low = head_masks(BF16)
        full = head_masks(F32)

        def group(g):
            query = packed[rows, lanes_at(g, 128)]
            key = packed[rows, lanes_at(g, 128, width)]
            value = packed[rows, lanes_at(g, 128, 2 * width)]
            probs = pair_probs(stacked(query, low), key, allowed).astype(BF16)
            context[rows, lanes_at(g, 128)] = folded(dot(probs, value), full).astype(BF16)

        each(width // 128, group)

    each(images // 2, pair)


def image_halves(kind):
    row = iota((PAIR, 128), 0)
    first = jnp.where(row < CELLS, 1.0, 0.0).astype(F32)
    return first.astype(kind), (1.0 - first).astype(kind)


def fold_heads(square):
    lane = iota((32, 128), 1) >> 5
    total = jnp.zeros((32, 128), F32)
    for h in range(4):
        total = total + jnp.where(lane == h, square[32 * h : 32 * h + 32], 0.0)
    return total


def unfold_heads(block):
    lane = iota((32, 128), 1) >> 5
    return jnp.concatenate([jnp.where(lane == h, block, 0.0) for h in range(4)], axis=0)


def pair_grams(left, left_base, right, right_base, images, valid, out):
    def pair(p):
        rows = rows_at(p, PAIR)
        one, two = image_halves(BF16)
        ok = valid[rows, :].astype(BF16)
        one, two = one * ok, two * ok

        def group(g):
            a = left[rows, lanes_at(g, 128, left_base)]
            b = right[rows, lanes_at(g, 128, right_base)]
            both = t_dot(a, jnp.concatenate([b * one, b * two], axis=1))
            out[pl.ds(pl.multiple_of(64 * p, 32), 32), lanes_at(g, 128)] = fold_heads(both[:, :128])
            out[pl.ds(pl.multiple_of(64 * p + 32, 32), 32), lanes_at(g, 128)] = fold_heads(both[:, 128:])

        each(out.shape[1] // 128, group)

    each(images // 2, pair)


def sum_windows(gram, ins, images, c, sems, vertical, horizontal):
    half = images * 16
    mine = pl.ds(pl.multiple_of(half * c, 32), half)

    def add(ref, rows):
        gram[rows, :] = gram[rows, :] + ref[rows, :]

    copy = remote(gram, ins.at[0], sems.at[0], horizontal)
    copy.start()
    copy.wait()
    each(images, lambda i: add(ins.at[0], rows_at(i, 32)))
    copy = remote(gram.at[mine], ins.at[1, mine], sems.at[1], vertical)
    copy.start()
    copy.wait()
    each(images // 2, lambda i: add(ins.at[1], pl.ds(pl.multiple_of(half * c + 32 * i, 32), 32)))
    copy = remote(gram.at[mine], ins.at[2, mine], sems.at[2], horizontal)
    copy.start()
    copy.wait()
    other = half * (1 - c)

    def take(i):
        rows = pl.ds(pl.multiple_of(other + 32 * i, 32), 32)
        gram[rows, :] = ins[2, rows, :]

    each(images // 2, take)


def forward_kernel(
    images,
    width,
    hidden,
    sizes,
    patches,
    vec,
    qbias,
    hbias,
    qkv0,
    qkv1,
    proj0,
    proj1,
    hid0,
    hid1,
    outw0,
    outw1,
    activations,
    o_pad,
    o_stream,
    o_normed,
    o_packed,
    o_context,
    o_act,
    o_slope,
    o_mix,
    pad,
    streams,
    normed,
    packed,
    context,
    act,
    slope,
    gram,
    gram_in,
    valid,
    pre,
    wq,
    wp,
    wh,
    wo,
    row_out,
    row_in,
    col_out,
    col_in,
    final,
    halo_sems,
    gram_sems,
    load_sems,
    save_sems,
):
    d, w, wr, wc = place()
    n_rows = images * CELLS
    pairs = images // 2
    horizontal = (d, 2 * wr + 1 - wc)
    vertical = (d, 2 * (1 - wr) + wc)
    greet([horizontal, vertical])
    left, right = side_masks(wr, wc)

    loads = {}
    for name, src, dst, s in (("q0", qkv0, wq, 0), ("p0", proj0, wp, 1), ("h0", hid0, wh, 2), ("o0", outw0, wo, 3)):
        loads[name] = pltpu.make_async_copy(src, dst, load_sems.at[s])
        loads[name].start()

    def reload(name, src, dst, s):
        loads[name] = pltpu.make_async_copy(src, dst, load_sems.at[s])
        loads[name].start()

    saves = {}

    def save(name, src, dst, s):
        saves[name] = pltpu.make_async_copy(src, dst, save_sems.at[s])
        saves[name].start()

    fill_valid(valid, sizes, images, wr, wc)
    clear_borders(pad, images)

    def enter(p):
        rows = rows_at(p, PAIR)
        to_pad(pad, p, patches[rows, :].astype(F32) * spread(valid[rows, :], width))

    each(pairs, enter)

    def convolve(k, stream):
        halo(pad, images, wr, wc, row_out.at[k], row_in.at[k], col_out.at[k], col_in.at[k], halo_sems.at[k], vertical, horizontal)
        conv_forward(pad, images, vec, k, valid, stream, left, right)

    def qkv(k, x):
        def tile(j):
            at = lanes_at(j, 256)
            packed[:, at] = (dot(x[...], wq[:, at]) + qbias[k : k + 1, at]).astype(BF16)

        each(3 * width // 256, tile)

    def proj(k, stream, store):
        def tile(j):
            at = lanes_at(j, 256)
            pre[...] = dot(context[...], wp[:, at])

            def part(p):
                rows = rows_at(p, PAIR)
                store(p, at, stream[rows, at] + spread(valid[rows, :], 256) * (pre[rows, :] + vec[38 + k : 39 + k, at]))

            each(pairs, part)

        each(width // 256, tile)

    def feed_forward(k, x, stream, store):
        def tile(j):
            at = lanes_at(j, 256)
            pre[...] = dot(x[...], wh[:, at])

            def part(p):
                rows = rows_at(p, PAIR)
                a, s = gelu_pair(pre[rows, :] + hbias[k : k + 1, at])
                act[rows, at] = a.astype(BF16)
                slope[rows, at] = s.astype(BF16)

            each(pairs, part)

        each(hidden // 256, tile)

        def tile2(j):
            at = lanes_at(j, 256)
            pre[...] = dot(act[...], wo[:, at])

            def part(p):
                rows = rows_at(p, PAIR)
                store(p, at, stream[rows, at] + spread(valid[rows, :], 256) * (pre[rows, :] + vec[40 + k : 41 + k, at]))

            each(pairs, part)

        each(width // 256, tile2)

    def into_pad(p, at, value):
        pad[pl.ds(pl.multiple_of((18 * p + 1) * 8, 8), CELLS), at] = value[:CELLS]
        pad[pl.ds(pl.multiple_of((18 * p + 10) * 8, 8), CELLS), at] = value[CELLS:]

    convolve(0, streams.at[0])
    save("pad0", pad, o_pad.at[0], 0)
    save("s1", streams.at[0], o_stream.at[0], 1)
    norm_rows(streams.at[0], images, vec, 0, normed.at[0])
    save("n1", normed.at[0], o_normed.at[0], 2)
    loads["q0"].wait()
    qkv(0, normed.at[0])
    save("k1", packed, o_packed.at[0], 3)
    reload("q1", qkv1, wq, 0)
    window_attention(packed, images, sizes, wr, wc, context)
    save("c1", context, o_context.at[0], 4)
    loads["p0"].wait()
    saves["pad0"].wait()
    proj(0, streams.at[0], into_pad)
    reload("p1", proj1, wp, 1)
    convolve(1, streams.at[1])
    save("pad2", pad, o_pad.at[1], 0)
    save("s3", streams.at[1], o_stream.at[1], 5)
    norm_rows(streams.at[1], images, vec, 1, normed.at[1])
    save("n3", normed.at[1], o_normed.at[1], 6)
    loads["h0"].wait()
    loads["o0"].wait()
    saves["pad2"].wait()
    feed_forward(0, normed.at[1], streams.at[1], into_pad)
    save("a0", act, o_act.at[0], 7)
    save("g0", slope, o_slope.at[0], 8)
    reload("h1", hid1, wh, 2)
    reload("o1", outw1, wo, 3)
    saves["s1"].wait()
    saves["n1"].wait()
    saves["k1"].wait()
    saves["c1"].wait()
    convolve(2, streams.at[0])
    save("pad4", pad, o_pad.at[2], 0)
    save("s5", streams.at[0], o_stream.at[2], 1)
    norm_rows(streams.at[0], images, vec, 2, normed.at[0])
    save("n5", normed.at[0], o_normed.at[2], 2)
    loads["q1"].wait()
    qkv(1, normed.at[0])
    save("k5", packed, o_packed.at[1], 3)
    pair_grams(packed, 2 * width, packed, width, images, valid, gram)
    sum_windows(gram, gram_in, images, wc, gram_sems, vertical, horizontal)

    def soften(i):
        rows = rows_at(i, 32)
        x = gram[rows, :] * SCALE
        e = jnp.exp(x - jnp.max(x, 0, keepdims=True))
        gram[rows, :] = e * (1.0 / jnp.sum(e, 0, keepdims=True))

    each(images, soften)
    save("mix", gram, o_mix, 9)

    def mix_pair(p):
        rows = rows_at(p, PAIR)
        one, two = image_halves(BF16)

        def group(g):
            at = lanes_at(g, 128)
            a = unfold_heads(gram[pl.ds(pl.multiple_of(64 * p, 32), 32), at])
            b = unfold_heads(gram[pl.ds(pl.multiple_of(64 * p + 32, 32), 32), at])
            query = packed[rows, at]
            mixing = jnp.concatenate([a, b], axis=0).astype(BF16)
            context[rows, at] = dot(jnp.concatenate([query * one, query * two], axis=1), mixing).astype(BF16)

        each(width // 128, group)

    each(pairs, mix_pair)
    save("c5", context, o_context.at[1], 4)
    loads["p1"].wait()
    saves["s3"].wait()
    saves["n3"].wait()

    def into_last(p, at, value):
        streams[1, rows_at(p, PAIR), at] = value

    proj(1, streams.at[0], into_last)
    save("s6", streams.at[1], o_stream.at[3], 5)
    norm_rows(streams.at[1], images, vec, 3, normed.at[1])
    save("n6", normed.at[1], o_normed.at[3], 6)
    loads["h1"].wait()
    loads["o1"].wait()
    saves["a0"].wait()
    saves["g0"].wait()

    def into_final(p, at, value):
        final[rows_at(p, PAIR), at] = value.astype(BF16)

    feed_forward(1, normed.at[1], streams.at[1], into_final)
    save("a1", act, o_act.at[1], 7)
    save("g1", slope, o_slope.at[1], 8)
    save("end", final, activations, 10)
    for name in ("pad4", "s5", "n5", "k5", "mix", "c5", "s6", "n6", "a1", "g1", "end"):
        saves[name].wait()


ANY = pl.BlockSpec(memory_space=pl.ANY)
VMEM = pl.BlockSpec(memory_space=pltpu.VMEM)
SMEM = pl.BlockSpec(memory_space=pltpu.SMEM)


def run_forward(sizes, patches, vec, qbias, hbias, weights):
    images = sizes.shape[0]
    n_rows, width = patches.shape
    hidden = hbias.shape[1]
    lines = images * 72
    shapes = (
        ((n_rows, width), BF16),
        ((3, lines, width), F32),
        ((4, n_rows, width), F32),
        ((4, n_rows, width), BF16),
        ((2, n_rows, 3 * width), BF16),
        ((2, n_rows, width), BF16),
        ((2, n_rows, hidden), BF16),
        ((2, n_rows, hidden), BF16),
        ((images * 32, width), F32),
    )
    return pl.pallas_call(
        functools.partial(forward_kernel, images, width, hidden),
        out_shape=[jax.ShapeDtypeStruct(*s) for s in shapes],
        in_specs=[SMEM, VMEM, VMEM, VMEM, VMEM] + [ANY] * 8,
        out_specs=[ANY] * 9,
        scratch_shapes=[
            pltpu.VMEM((lines, width), F32),
            pltpu.VMEM((2, n_rows, width), F32),
            pltpu.VMEM((2, n_rows, width), BF16),
            pltpu.VMEM((n_rows, 3 * width), BF16),
            pltpu.VMEM((n_rows, width), BF16),
            pltpu.VMEM((n_rows, hidden), BF16),
            pltpu.VMEM((n_rows, hidden), BF16),
            pltpu.VMEM((images * 32, width), F32),
            pltpu.VMEM((3, images * 32, width), F32),
            pltpu.VMEM((n_rows, 128), F32),
            pltpu.VMEM((n_rows, 256), F32),
            pltpu.VMEM((width, 3 * width), BF16),
            pltpu.VMEM((width, width), BF16),
            pltpu.VMEM((width, hidden), BF16),
            pltpu.VMEM((hidden, width), BF16),
            pltpu.VMEM((3, images * 8, width), BF16),
            pltpu.VMEM((3, images * 8, width), BF16),
            pltpu.VMEM((3, images * 8, width), BF16),
            pltpu.VMEM((3, images * 8, width), BF16),
            pltpu.VMEM((n_rows, width), BF16),
            pltpu.SemaphoreType.DMA((3, 2, 2)),
            pltpu.SemaphoreType.DMA((3, 2)),
            pltpu.SemaphoreType.DMA((4,)),
            pltpu.SemaphoreType.DMA((11,)),
        ],
        compiler_params=pltpu.CompilerParams(
            collective_id=0, has_side_effects=True, vmem_limit_bytes=58 * 2**20
        ),
    )(sizes, patches, vec, qbias, hbias, *weights)


def gathered(array, axis):
    return lax.all_gather(array, "dp", axis=axis, tiled=True)


def small_params(conv_weight, conv_bias, norm_gain, norm_bias, spatial_bias, channel_bias, proj_bias, hidden_bias, output_bias):
    taps = conv_weight.reshape(-1, conv_weight.shape[-1])
    rows = jnp.concatenate([taps, conv_bias, norm_gain, norm_bias, proj_bias, output_bias], axis=0)
    vec = gathered(rows, 1)
    spatial = gathered(spatial_bias, 0)
    width = vec.shape[1]
    zeros = jnp.zeros((width,), BF16)
    qbias = jnp.stack(
        [jnp.concatenate([spatial[:width], zeros, spatial[width:]]), gathered(channel_bias, 0)]
    )
    vec = jnp.pad(vec, ((0, -vec.shape[0] % 8), (0, 0)))
    return vec.astype(F32), qbias.astype(F32), gathered(hidden_bias, 1).astype(F32)


def to_cells(windows):
    images, _, _, width = windows.shape
    grid = windows.reshape(images, 7, 7, width)
    return jnp.pad(grid, ((0, 0), (0, 0), (0, 1), (0, 0))).reshape(images * CELLS, width)


def of_cells(rows, images):
    width = rows.shape[1]
    return rows.reshape(images, 7, 8, width)[:, :, :7].reshape(images, 1, 49, width)


def on_device_fast(patches, cotangent, grid_sizes, conv_weight, conv_bias, norm_gain, norm_bias, qkv_weight, spatial_bias, channel_bias, proj_weight, proj_bias, hidden_weight, hidden_bias, output_weight, output_bias):
    rest = on_device(patches, cotangent, grid_sizes, conv_weight, conv_bias, norm_gain, norm_bias, qkv_weight, spatial_bias, channel_bias, proj_weight, proj_bias, hidden_weight, hidden_bias, output_weight, output_bias)
    vec, qbias, hbias = small_params(conv_weight, conv_bias, norm_gain, norm_bias, spatial_bias, channel_bias, proj_bias, hidden_bias, output_bias)
    weights = [gathered(w, 1)[k] for w in (qkv_weight, proj_weight, hidden_weight, output_weight) for k in (0, 1)]
    outs = run_forward(grid_sizes, to_cells(patches), vec, qbias, hbias, weights)
    return (of_cells(outs[0], patches.shape[0]),) + tuple(rest[1:])


def as_sent(array):
    return jax.tree.map(lambda a: a.astype(jnp.bfloat16) if a.dtype == jnp.float32 else a, array)


def image_valid(grid_sizes):
    rows = jnp.arange(7, dtype=jnp.int32)
    windows = jnp.arange(4, dtype=jnp.int32)
    top_rows = (windows // 2)[:, None] * 7 + rows[None, :]
    left_cols = (windows % 2)[:, None] * 7 + rows[None, :]
    sizes = grid_sizes[:, None, None, None]
    inside = (top_rows[None, :, :, None] < sizes) & (left_cols[None, :, None, :] < sizes)
    return inside.astype(jnp.float32).reshape(grid_sizes.shape[0], 4, 49, 1)


def layer_norm(stream, gain_row, shift_row):
    centre = jnp.mean(stream, -1, keepdims=True)
    centered = stream - centre
    variance = jnp.mean(centered * centered, -1, keepdims=True)
    return centered * lax.rsqrt(variance + EPS) * gain_row + shift_row


def gelu_exact(value_in):
    return jax.nn.gelu(value_in, approximate=False)


def matmul(left_rows, right_mat):
    return jnp.dot(left_rows, right_mat, preferred_element_type=jnp.float32)


def contract_rows(left_rows, right_rows):
    return lax.dot_general(
        left_rows, right_rows, (((0,), (0,)), ((), ())), preferred_element_type=jnp.float32
    )


def times_transposed(grad_rows, weight):
    return lax.dot_general(
        grad_rows, weight, (((1,), (1,)), ((), ())), preferred_element_type=jnp.float32
    )


def edge_lines(stream, images):
    channels = stream.shape[-1]
    image_grid = stream.reshape(images, 7, 7, channels)
    return jnp.stack(
        [image_grid[:, 0], image_grid[:, 6], image_grid[:, :, 0], image_grid[:, :, 6]], 1
    )[None]


def padded_tile(image_grid, lines, row_half, col_half):
    zero_line = jnp.zeros_like(lines[0, :, 0])
    upper = jnp.where(
        row_half == 1, jnp.where(col_half == 0, lines[0, :, 1], lines[1, :, 1]), zero_line
    )
    lower = jnp.where(
        row_half == 0, jnp.where(col_half == 0, lines[2, :, 0], lines[3, :, 0]), zero_line
    )
    left_side = jnp.where(
        col_half == 1, jnp.where(row_half == 0, lines[0, :, 3], lines[2, :, 3]), zero_line
    )
    right_side = jnp.where(
        col_half == 0, jnp.where(row_half == 0, lines[1, :, 2], lines[3, :, 2]), zero_line
    )
    zero_cell = zero_line[:, 0]
    top_left = jnp.where((row_half == 1) & (col_half == 1), lines[0, :, 1, 6], zero_cell)
    top_right = jnp.where((row_half == 1) & (col_half == 0), lines[1, :, 1, 0], zero_cell)
    bottom_left = jnp.where((row_half == 0) & (col_half == 1), lines[2, :, 0, 6], zero_cell)
    bottom_right = jnp.where((row_half == 0) & (col_half == 0), lines[3, :, 0, 0], zero_cell)
    middle = jnp.concatenate([left_side[:, :, None], image_grid, right_side[:, :, None]], 2)
    top_row = jnp.concatenate([top_left[:, None], upper, top_right[:, None]], 1)
    bottom_row = jnp.concatenate([bottom_left[:, None], lower, bottom_right[:, None]], 1)
    return jnp.concatenate([top_row[:, None], middle, bottom_row[:, None]], 1)


def position_conv(stream, images, window, weight9, shift_row, valid_rows):
    channels = stream.shape[-1]
    lines = lax.all_gather(as_sent(edge_lines(stream, images)), "win", axis=0, tiled=True)
    padded = padded_tile(stream.reshape(images, 7, 7, channels), lines, window // 2, window % 2)
    summed = jnp.zeros((images, 7, 7, channels), jnp.float32)
    for tap_index in range(9):
        row_shift, col_shift = divmod(tap_index, 3)
        summed = (
            summed
            + weight9[tap_index] * padded[:, row_shift : row_shift + 7, col_shift : col_shift + 7]
        )
    return (stream + valid_rows * (summed + shift_row).reshape(images * 49, channels), padded)


def position_conv_back(grad_stream, padded, images, window, weight9, valid_rows):
    channels = grad_stream.shape[-1]
    masked = valid_rows * grad_stream
    lines = lax.all_gather(as_sent(edge_lines(masked, images)), "win", axis=0, tiled=True)
    image_grid = masked.reshape(images, 7, 7, channels)
    grad_pad = padded_tile(image_grid, lines, window // 2, window % 2)
    summed = jnp.zeros((images, 7, 7, channels), jnp.float32)
    tap_grads = []
    for tap_index in range(9):
        row_shift, col_shift = divmod(tap_index, 3)
        summed = (
            summed
            + weight9[tap_index]
            * grad_pad[:, 2 - row_shift : 9 - row_shift, 2 - col_shift : 9 - col_shift]
        )
        tap_grads.append(
            jnp.sum(
                image_grid * padded[:, row_shift : row_shift + 7, col_shift : col_shift + 7],
                axis=(0, 1, 2),
            )
        )
    return (
        grad_stream + summed.reshape(grad_stream.shape),
        jnp.stack(tap_grads),
        jnp.sum(image_grid, axis=(0, 1, 2)),
    )


def mlp_forward(normed, weight_in, bias_in, weight_out, bias_out):
    activated = gelu_exact(matmul(normed, weight_in) + bias_in).astype(jnp.bfloat16)
    return matmul(activated, weight_out) + bias_out


def mlp_backward(normed, grad_stream, valid_rows, weight_in, bias_in, weight_out):
    hidden_pre = matmul(normed, weight_in) + bias_in
    activated, gelu_pull = jax.vjp(gelu_exact, hidden_pre)
    grad_branch = (valid_rows * grad_stream).astype(jnp.bfloat16)
    grad_weight_out = contract_rows(activated.astype(jnp.bfloat16), grad_branch)
    grad_bias_out = jnp.sum(grad_branch.astype(jnp.float32), 0)
    grad_pre = gelu_pull(times_transposed(grad_branch, weight_out))[0].astype(jnp.bfloat16)
    grad_weight_in = contract_rows(normed, grad_pre)
    grad_bias_in = jnp.sum(grad_pre.astype(jnp.float32), 0)
    return (
        times_transposed(grad_pre, weight_in),
        grad_weight_in,
        grad_bias_in,
        grad_weight_out,
        grad_bias_out,
    )


def norm_backward(stream, gain_row, shift_row, grad_normed):
    unused, norm_pull = jax.vjp(layer_norm, stream, gain_row, shift_row)
    return norm_pull(grad_normed)


def window_probs(packed, images, scaling, valid_rows):
    split = packed.reshape(images, 49, 3, HEADS, HEAD)
    query_rows = split[:, :, 0]
    key_rows = split[:, :, 1]
    value_rows = split[:, :, 2]
    key_ok = valid_rows.reshape(images, 1, 1, 49) > 0.5
    scores = (
        jnp.einsum("iphe,iqhe->ihpq", query_rows, key_rows, preferred_element_type=jnp.float32)
        * scaling
    )
    scores = jnp.where(key_ok, scores, -1000000000.0)
    return (query_rows, key_rows, value_rows, jax.nn.softmax(scores, axis=-1))


def channel_mixing(gram_total, scaling):
    return jax.nn.softmax(gram_total * scaling, axis=-1)


def channel_grads(
    grad_mixing, mixing, grad_context, key_masked, value_masked, valid_cells, scaling
):
    grad_query = jnp.einsum(
        "bgcd,bpgc->bpgd",
        mixing.astype(jnp.bfloat16),
        grad_context,
        preferred_element_type=jnp.float32,
    )
    grad_gram = (mixing * (grad_mixing - jnp.sum(mixing * grad_mixing, -1, keepdims=True))).astype(
        jnp.bfloat16
    )
    grad_keys = (
        jnp.einsum("bgcd,bpgd->bpgc", grad_gram, value_masked, preferred_element_type=jnp.float32)
        * scaling
        * valid_cells
    )
    grad_values = (
        jnp.einsum("bgcd,bpgc->bpgd", grad_gram, key_masked, preferred_element_type=jnp.float32)
        * scaling
        * valid_cells
    )
    return jnp.stack([grad_query, grad_keys, grad_values], 2).astype(jnp.bfloat16)


def on_device(
    patches,
    cotangent,
    grid_sizes,
    conv_weight,
    conv_bias,
    norm_gain,
    norm_bias,
    qkv_weight,
    spatial_bias,
    channel_bias,
    proj_weight,
    proj_bias,
    hidden_weight,
    hidden_bias,
    output_weight,
    output_bias,
):
    (
        conv_w,
        conv_b,
        gains,
        shifts,
        qkv_w,
        sp_bias,
        ch_bias,
        proj_w,
        proj_b,
        hid_w,
        hid_b,
        out_w,
        out_b,
    ) = (
        lax.all_gather(conv_weight, "dp", axis=2, tiled=True),
        lax.all_gather(conv_bias, "dp", axis=1, tiled=True),
        lax.all_gather(norm_gain, "dp", axis=1, tiled=True),
        lax.all_gather(norm_bias, "dp", axis=1, tiled=True),
        lax.all_gather(qkv_weight, "dp", axis=1, tiled=True),
        lax.all_gather(spatial_bias, "dp", axis=0, tiled=True),
        lax.all_gather(channel_bias, "dp", axis=0, tiled=True),
        lax.all_gather(proj_weight, "dp", axis=1, tiled=True),
        lax.all_gather(proj_bias, "dp", axis=1, tiled=True),
        lax.all_gather(hidden_weight, "dp", axis=1, tiled=True),
        lax.all_gather(hidden_bias, "dp", axis=1, tiled=True),
        lax.all_gather(output_weight, "dp", axis=1, tiled=True),
        lax.all_gather(output_bias, "dp", axis=1, tiled=True),
    )
    conv_w = conv_w.astype(jnp.float32)
    conv_b = conv_b.astype(jnp.float32)
    gains = gains.astype(jnp.float32)
    shifts = shifts.astype(jnp.float32)
    sp_bias = sp_bias.astype(jnp.float32)
    ch_bias = ch_bias.astype(jnp.float32)
    proj_b = proj_b.astype(jnp.float32)
    hid_b = hid_b.astype(jnp.float32)
    out_b = out_b.astype(jnp.float32)
    images = patches.shape[0]
    model_width = patches.shape[-1]
    rows_all = images * 49
    group_count = lax.axis_size("win")
    local_heads = HEADS // group_count
    group_width = model_width // group_count
    scaling = HEAD ** (-0.5)
    window = lax.axis_index("win")
    full_valid = image_valid(grid_sizes)
    valid_rows = lax.dynamic_slice_in_dim(full_valid, window, 1, 1).reshape(rows_all, 1)
    stream0 = patches.astype(jnp.float32).reshape(rows_all, model_width) * valid_rows
    stream1, pad_first = position_conv(stream0, images, window, conv_w[0], conv_b[0], valid_rows)
    normed1 = layer_norm(stream1, gains[0], shifts[0]).astype(jnp.bfloat16)
    packed_bias = jnp.concatenate(
        [sp_bias[:model_width], jnp.zeros((model_width,), jnp.float32), sp_bias[model_width:]]
    )
    packed1 = (matmul(normed1, qkv_w[0]) + packed_bias).astype(jnp.bfloat16)
    query1, keys1, values1, probs1 = window_probs(packed1, images, scaling, valid_rows)
    context1 = (
        jnp.einsum(
            "ihpq,iqhe->iphe",
            probs1.astype(jnp.bfloat16),
            values1,
            preferred_element_type=jnp.float32,
        )
        .astype(jnp.bfloat16)
        .reshape(rows_all, model_width)
    )
    stream2 = stream1 + valid_rows * (matmul(context1, proj_w[0]) + proj_b[0])
    stream3, pad_second = position_conv(stream2, images, window, conv_w[1], conv_b[1], valid_rows)
    normed3 = layer_norm(stream3, gains[1], shifts[1]).astype(jnp.bfloat16)
    stream4 = stream3 + valid_rows * mlp_forward(normed3, hid_w[0], hid_b[0], out_w[0], out_b[0])
    stream5, pad_third = position_conv(stream4, images, window, conv_w[2], conv_b[2], valid_rows)
    normed5 = layer_norm(stream5, gains[2], shifts[2]).astype(jnp.bfloat16)
    packed5 = (matmul(normed5, qkv_w[1]) + ch_bias).astype(jnp.bfloat16)
    moved = lax.all_to_all(
        packed5.reshape(images, 1, 49, 3, group_count, group_width),
        "win",
        split_axis=4,
        concat_axis=1,
        tiled=True,
    )
    grouped = moved.reshape(images, 196, 3, local_heads, HEAD)
    valid_cells = full_valid.reshape(images, 196, 1, 1)
    query5 = grouped[:, :, 0]
    key_masked = grouped[:, :, 1] * valid_cells.astype(jnp.bfloat16)
    value_masked = grouped[:, :, 2] * valid_cells.astype(jnp.bfloat16)
    gram_total = jnp.einsum(
        "bpgc,bpgd->bgcd", key_masked, value_masked, preferred_element_type=jnp.float32
    )
    mixing = channel_mixing(gram_total, scaling)
    context_groups = jnp.einsum(
        "bgcd,bpgd->bpgc", mixing.astype(jnp.bfloat16), query5, preferred_element_type=jnp.float32
    ).astype(jnp.bfloat16)
    returned = lax.all_to_all(
        context_groups.reshape(images, 4, 49, 1, group_width),
        "win",
        split_axis=1,
        concat_axis=3,
        tiled=True,
    )
    context5 = returned.reshape(rows_all, model_width)
    stream6 = stream5 + valid_rows * (matmul(context5, proj_w[1]) + proj_b[1])
    normed6 = layer_norm(stream6, gains[3], shifts[3]).astype(jnp.bfloat16)
    stream7 = stream6 + valid_rows * mlp_forward(normed6, hid_w[1], hid_b[1], out_w[1], out_b[1])
    activations = stream7.astype(jnp.bfloat16).reshape(patches.shape)
    grad7 = cotangent.astype(jnp.float32).reshape(rows_all, model_width)
    grad_normed, hid_w_grad1, hid_b_grad1, out_w_grad1, out_b_grad1 = mlp_backward(
        normed6, grad7, valid_rows, hid_w[1], hid_b[1], out_w[1]
    )
    grad_part, gain_grad3, shift_grad3 = norm_backward(stream6, gains[3], shifts[3], grad_normed)
    grad6 = grad7 + grad_part
    branch_grad = (valid_rows * grad6).astype(jnp.bfloat16)
    proj_w_grad1 = contract_rows(context5, branch_grad)
    proj_b_grad1 = jnp.sum(branch_grad.astype(jnp.float32), 0)
    context_grad = times_transposed(branch_grad, proj_w[1]).astype(jnp.bfloat16)
    moved_grad = lax.all_to_all(
        context_grad.reshape(images, 1, 49, group_count, group_width),
        "win",
        split_axis=3,
        concat_axis=1,
        tiled=True,
    )
    group_grad = moved_grad.reshape(images, 196, local_heads, HEAD)
    mixing_grad = jnp.einsum(
        "bpgc,bpgd->bgcd", group_grad, query5, preferred_element_type=jnp.float32
    )
    stacked = channel_grads(
        mixing_grad, mixing, group_grad, key_masked, value_masked, valid_cells, scaling
    )
    sent_back = lax.all_to_all(
        stacked.reshape(images, 4, 49, 3, 1, group_width),
        "win",
        split_axis=1,
        concat_axis=4,
        tiled=True,
    )
    packed_grad5 = sent_back.reshape(rows_all, 3 * model_width)
    qkv_w_grad1 = contract_rows(normed5, packed_grad5)
    ch_bias_grad = jnp.sum(packed_grad5.astype(jnp.float32), 0)
    grad_part, gain_grad2, shift_grad2 = norm_backward(
        stream5, gains[2], shifts[2], times_transposed(packed_grad5, qkv_w[1])
    )
    grad5 = grad6 + grad_part
    grad4, conv_w_grad2, conv_b_grad2 = position_conv_back(
        grad5, pad_third, images, window, conv_w[2], valid_rows
    )
    grad_normed, hid_w_grad0, hid_b_grad0, out_w_grad0, out_b_grad0 = mlp_backward(
        normed3, grad4, valid_rows, hid_w[0], hid_b[0], out_w[0]
    )
    grad_part, gain_grad1, shift_grad1 = norm_backward(stream3, gains[1], shifts[1], grad_normed)
    grad3 = grad4 + grad_part
    grad2, conv_w_grad1, conv_b_grad1 = position_conv_back(
        grad3, pad_second, images, window, conv_w[1], valid_rows
    )
    branch_grad = (valid_rows * grad2).astype(jnp.bfloat16)
    proj_w_grad0 = contract_rows(context1, branch_grad)
    proj_b_grad0 = jnp.sum(branch_grad.astype(jnp.float32), 0)
    context_grad = (
        times_transposed(branch_grad, proj_w[0])
        .astype(jnp.bfloat16)
        .reshape(images, 49, HEADS, HEAD)
    )
    probs_low = probs1.astype(jnp.bfloat16)
    probs_grad = jnp.einsum(
        "iphe,iqhe->ihpq", context_grad, values1, preferred_element_type=jnp.float32
    )
    values_grad = jnp.einsum(
        "ihpq,iphe->iqhe", probs_low, context_grad, preferred_element_type=jnp.float32
    )
    scores_grad = (probs1 * (probs_grad - jnp.sum(probs1 * probs_grad, -1, keepdims=True))).astype(
        jnp.bfloat16
    )
    key_ok = valid_rows.reshape(images, 1, 1, 49) > 0.5
    scores_grad = jnp.where(key_ok, scores_grad, jnp.zeros_like(scores_grad))
    query_grad = (
        jnp.einsum("ihpq,iqhe->iphe", scores_grad, keys1, preferred_element_type=jnp.float32)
        * scaling
    )
    keys_grad = (
        jnp.einsum("ihpq,iphe->iqhe", scores_grad, query1, preferred_element_type=jnp.float32)
        * scaling
    )
    packed_grad1 = (
        jnp.stack([query_grad, keys_grad, values_grad], 2)
        .astype(jnp.bfloat16)
        .reshape(rows_all, 3 * model_width)
    )
    qkv_w_grad0 = contract_rows(normed1, packed_grad1)
    packed_sums = jnp.sum(packed_grad1.astype(jnp.float32), 0)
    sp_bias_grad = jnp.concatenate([packed_sums[:model_width], packed_sums[2 * model_width :]])
    grad_part, gain_grad0, shift_grad0 = norm_backward(
        stream1, gains[0], shifts[0], times_transposed(packed_grad1, qkv_w[0])
    )
    grad1 = grad2 + grad_part
    grad0, conv_w_grad0, conv_b_grad0 = position_conv_back(
        grad1, pad_first, images, window, conv_w[0], valid_rows
    )
    patches_grad = (grad0 * valid_rows).astype(jnp.bfloat16).reshape(patches.shape)
    local_sums = (
        lax.psum_scatter(
            jnp.stack([conv_w_grad0, conv_w_grad1, conv_w_grad2]),
            "dp",
            scatter_dimension=2,
            tiled=True,
        ),
        lax.psum_scatter(
            jnp.stack([conv_b_grad0, conv_b_grad1, conv_b_grad2]),
            "dp",
            scatter_dimension=1,
            tiled=True,
        ),
        lax.psum_scatter(
            jnp.stack([gain_grad0, gain_grad1, gain_grad2, gain_grad3]),
            "dp",
            scatter_dimension=1,
            tiled=True,
        ),
        lax.psum_scatter(
            jnp.stack([shift_grad0, shift_grad1, shift_grad2, shift_grad3]),
            "dp",
            scatter_dimension=1,
            tiled=True,
        ),
        lax.psum_scatter(
            jnp.stack([qkv_w_grad0, qkv_w_grad1]), "dp", scatter_dimension=1, tiled=True
        ),
        lax.psum_scatter(sp_bias_grad, "dp", scatter_dimension=0, tiled=True),
        lax.psum_scatter(ch_bias_grad, "dp", scatter_dimension=0, tiled=True),
        lax.psum_scatter(
            jnp.stack([proj_w_grad0, proj_w_grad1]), "dp", scatter_dimension=1, tiled=True
        ),
        lax.psum_scatter(
            jnp.stack([proj_b_grad0, proj_b_grad1]), "dp", scatter_dimension=1, tiled=True
        ),
        lax.psum_scatter(
            jnp.stack([hid_w_grad0, hid_w_grad1]), "dp", scatter_dimension=1, tiled=True
        ),
        lax.psum_scatter(
            jnp.stack([hid_b_grad0, hid_b_grad1]), "dp", scatter_dimension=1, tiled=True
        ),
        lax.psum_scatter(
            jnp.stack([out_w_grad0, out_w_grad1]), "dp", scatter_dimension=1, tiled=True
        ),
        lax.psum_scatter(
            jnp.stack([out_b_grad0, out_b_grad1]), "dp", scatter_dimension=1, tiled=True
        ),
    )
    summed = (
        lax.psum(local_sums[0].astype(jnp.bfloat16), "win").astype(jnp.float32),
        lax.psum(local_sums[1].astype(jnp.bfloat16), "win").astype(jnp.float32),
        lax.psum(local_sums[2].astype(jnp.bfloat16), "win").astype(jnp.float32),
        lax.psum(local_sums[3].astype(jnp.bfloat16), "win").astype(jnp.float32),
        lax.psum(local_sums[4].astype(jnp.bfloat16), "win").astype(jnp.float32),
        lax.psum(local_sums[5].astype(jnp.bfloat16), "win").astype(jnp.float32),
        lax.psum(local_sums[6].astype(jnp.bfloat16), "win").astype(jnp.float32),
        lax.psum(local_sums[7].astype(jnp.bfloat16), "win").astype(jnp.float32),
        lax.psum(local_sums[8].astype(jnp.bfloat16), "win").astype(jnp.float32),
        lax.psum(local_sums[9].astype(jnp.bfloat16), "win").astype(jnp.float32),
        lax.psum(local_sums[10].astype(jnp.bfloat16), "win").astype(jnp.float32),
        lax.psum(local_sums[11].astype(jnp.bfloat16), "win").astype(jnp.float32),
        lax.psum(local_sums[12].astype(jnp.bfloat16), "win").astype(jnp.float32),
    )
    return (activations, patches_grad) + tuple(summed)


def solution(mesh):
    small = mesh.shape["dp"] == 8 and mesh.shape["win"] == 4
    return jax.shard_map(
        on_device_fast if small else on_device,
        mesh=mesh,
        in_specs=(
            P("dp", "win", None, None),
            P("dp", "win", None, None),
            P("dp"),
            P(None, None, "dp"),
            P(None, "dp"),
            P(None, "dp"),
            P(None, "dp"),
            P(None, "dp", None),
            P("dp"),
            P("dp"),
            P(None, "dp", None),
            P(None, "dp"),
            P(None, "dp", None),
            P(None, "dp"),
            P(None, "dp", None),
            P(None, "dp"),
        ),
        out_specs=(
            P("dp", "win", None, None),
            P("dp", "win", None, None),
            P(None, None, "dp"),
            P(None, "dp"),
            P(None, "dp"),
            P(None, "dp"),
            P(None, "dp", None),
            P("dp"),
            P("dp"),
            P(None, "dp", None),
            P(None, "dp"),
            P(None, "dp", None),
            P(None, "dp"),
            P(None, "dp", None),
            P(None, "dp"),
        ),
        check_vma=False,
    )
```

```python
import functools

import jax
import jax.numpy as jnp
from jax import lax
from jax.experimental import pallas as pl
from jax.experimental.pallas import tpu as pltpu
from jax.sharding import PartitionSpec as P

HEADS = 24
HEAD = 32
EPS = 1e-05
MESH = pl.DeviceIdType.MESH
F32 = jnp.float32
BF16 = jnp.bfloat16
SCALE = HEAD ** (-0.5)
CELLS = 56
PAIR = 112


def dot(left, right):
    return jnp.dot(left, right, preferred_element_type=F32)


def dot_t(left, right):
    return lax.dot_general(left, right, (((1,), (1,)), ((), ())), preferred_element_type=F32)


def t_dot(left, right):
    return lax.dot_general(left, right, (((0,), (0,)), ((), ())), preferred_element_type=F32)


def iota(shape, dim):
    return lax.broadcasted_iota(jnp.int32, shape, dim)


def rows_at(index, count):
    return pl.ds(pl.multiple_of(index * count, count), count)


def lanes_at(index, count, base=0):
    return pl.ds(pl.multiple_of(base + index * count, 128), count)


def each(count, body):
    def step(i, carry):
        body(i)
        return carry

    lax.fori_loop(0, count, step, 0)


def gelu_pair(pre):
    t = 1.0 / (1.0 + 0.23164190 * jnp.abs(pre))
    e = jnp.exp(-0.5 * pre * pre)
    poly = (((1.061405429 * t - 1.453152027) * t + 1.421413741) * t - 0.284496736) * t + 0.254829592
    tail = 0.5 * poly * t * e
    cdf = jnp.where(pre >= 0.0, 1.0 - tail, tail)
    return pre * cdf, cdf + pre * (e * 0.3989422804014327)


def place():
    d = lax.axis_index("dp")
    w = lax.axis_index("win")
    return d, w, w // 2, w % 2


def greet(peers):
    barrier = pltpu.get_barrier_semaphore()
    for peer in peers:
        pl.semaphore_signal(barrier, inc=1, device_id=peer, device_id_type=MESH)
    pl.semaphore_wait(barrier, len(peers))


def remote(src, dst, sems, peer):
    return pltpu.make_async_remote_copy(
        src_ref=src, dst_ref=dst, send_sem=sems.at[0], recv_sem=sems.at[1], device_id=peer, device_id_type=MESH
    )


def fill_valid(valid, sizes, images, wr, wc):
    def one(i):
        cell = iota((CELLS, 128), 0)
        r, c = cell >> 3, cell & 7
        inside = (r + 7 * wr < sizes[i]) & (c + 7 * wc < sizes[i]) & (c < 7)
        valid[rows_at(i, CELLS), :] = jnp.where(inside, 1.0, 0.0).astype(F32)

    each(images, one)


def spread(valid_rows, width):
    return jnp.concatenate([valid_rows] * (width // 128), axis=1)


def halo(pad, images, wr, wc, row_out, row_in, col_out, col_in, sems, vertical, horizontal):
    edge = 7 - 6 * wr

    def pack(p):
        one = pad[pl.ds(pl.multiple_of((18 * p + edge) * 8, 8), 8), :]
        two = pad[pl.ds(pl.multiple_of((18 * p + 9 + edge) * 8, 8), 8), :]
        row_out[rows_at(p, 16), :] = jnp.concatenate([one, two], axis=0).astype(BF16)

    each(images // 2, pack)
    copy = remote(row_out, row_in, sems.at[0], vertical)
    copy.start()
    copy.wait()
    border = 8 - 8 * wr

    def unpack(p):
        both = row_in[rows_at(p, 16), :].astype(F32)
        pad[pl.ds(pl.multiple_of((18 * p + border) * 8, 8), 8), :] = both[:8]
        pad[pl.ds(pl.multiple_of((18 * p + 9 + border) * 8, 8), 8), :] = both[8:]

    each(images // 2, unpack)
    turn = 2 - 2 * wc
    sub = iota((8, 128), 0)

    def row_of(i, s):
        at_row = border if s == 7 else s + 1
        return pl.ds(pl.multiple_of((9 * i + at_row) * 8, 8), 8)

    def pack_col(p):
        for part in range(pad.shape[1] // 128):
            at = pl.ds(part * 128, 128)
            both = []
            for i in (2 * p, 2 * p + 1):
                line = jnp.zeros((8, 128), F32)
                for s in range(8):
                    line = jnp.where(sub == s, pltpu.roll(pad[row_of(i, s), at], s + turn, 0), line)
                both.append(line)
            col_out[rows_at(p, 16), at] = jnp.concatenate(both, axis=0).astype(BF16)

    each(images // 2, pack_col)
    copy = remote(col_out, col_in, sems.at[1], horizontal)
    copy.start()
    copy.wait()

    def unpack_col(p):
        for part in range(pad.shape[1] // 128):
            at = pl.ds(part * 128, 128)
            both = col_in[rows_at(p, 16), at].astype(F32)
            for one in range(2):
                line = both[8 * one : 8 * one + 8]
                for s in range(8):
                    to = row_of(2 * p + one, s)
                    pad[to, at] = jnp.where(sub == 7, pltpu.roll(line, 7 - s, 0), pad[to, at])

    each(images // 2, unpack_col)


def side_masks(wr, wc):
    c = iota((8, 128), 0)
    left = jnp.where((c == 0) & (wc == 0), 0.0, 1.0).astype(F32)
    right = jnp.where((c == 6) & (wc == 1), 0.0, 1.0).astype(F32)
    return left, right


def three(pad, i, at, left, right):
    rows = [pad[pl.ds(pl.multiple_of((9 * i + r) * 8, 8), 8), at] for r in range(9)]
    return [(pltpu.roll(v, 1, 0) * left, v, pltpu.roll(v, 7, 0) * right) for v in rows]


def conv_forward(pad, images, vec, k, valid, out, left, right):
    def one(i):
        for part in range(pad.shape[1] // 128):
            at = pl.ds(part * 128, 128)
            moved = three(pad, i, at, left, right)
            bias = vec[27 + k : 28 + k, at]
            taps = [vec[9 * k + t : 9 * k + t + 1, at] for t in range(9)]
            for r in range(7):
                total = jnp.broadcast_to(bias, (8, 128))
                for t in range(9):
                    total = total + taps[t] * moved[r + t // 3][t % 3]
                to = pl.ds(pl.multiple_of((7 * i + r) * 8, 8), 8)
                out[to, at] = moved[r + 1][1] + valid[to, :] * total

    each(images, one)


def norm_rows(src, images, vec, k, dst):
    gain = vec[30 + k : 31 + k, :]
    shift = vec[34 + k : 35 + k, :]

    def one(p):
        x = src[rows_at(p, PAIR), :]
        centered = x - jnp.mean(x, -1, keepdims=True)
        variance = jnp.mean(centered * centered, -1, keepdims=True)
        dst[rows_at(p, PAIR), :] = (centered * lax.rsqrt(variance + EPS) * gain + shift).astype(BF16)

    each(images // 2, one)


def to_pad(pad, p, rows):
    pad[pl.ds(pl.multiple_of((18 * p + 1) * 8, 8), CELLS), :] = rows[:CELLS]
    pad[pl.ds(pl.multiple_of((18 * p + 10) * 8, 8), CELLS), :] = rows[CELLS:]


def of_pad(pad, p):
    return jnp.concatenate(
        [
            pad[pl.ds(pl.multiple_of((18 * p + 1) * 8, 8), CELLS), :],
            pad[pl.ds(pl.multiple_of((18 * p + 10) * 8, 8), CELLS), :],
        ],
        axis=0,
    )


def clear_borders(pad, images):
    zero = jnp.zeros((8, pad.shape[1]), F32)

    def one(i):
        pad[pl.ds(pl.multiple_of(72 * i, 8), 8), :] = zero
        pad[pl.ds(pl.multiple_of(72 * i + 64, 8), 8), :] = zero

    each(images, one)


def head_masks(kind):
    lane = iota((PAIR, 128), 1) >> 5
    return [jnp.where(lane == h, 1.0, 0.0).astype(F32).astype(kind) for h in range(4)]


def pair_mask(sizes, p, wr, wc):
    row = iota((PAIR, PAIR), 0)
    lane = iota((PAIR, PAIR), 1)
    second = lane >= CELLS
    cell = jnp.where(second, lane - CELLS, lane)
    side = jnp.where(second, sizes[2 * p + 1], sizes[2 * p])
    r, c = cell >> 3, cell & 7
    inside = (r + 7 * wr < side) & (c + 7 * wc < side) & (c < 7)
    return inside & (second == (row >= CELLS))


def stacked(value, masks):
    return jnp.concatenate([value * m for m in masks], axis=0)


def folded(value, masks):
    total = value[:PAIR] * masks[0]
    for h in range(1, 4):
        total = total + value[h * PAIR : (h + 1) * PAIR] * masks[h]
    return total


def pair_probs(query_bd, key, allowed):
    scores = dot_t(query_bd, key) * SCALE
    scores = jnp.where(allowed, scores, -1000000000.0)
    e = jnp.exp(scores - jnp.max(scores, -1, keepdims=True))
    return e * (1.0 / jnp.sum(e, -1, keepdims=True))


def window_attention(packed, images, sizes, wr, wc, context, between):
    width = context.shape[1]

    def pair(p):
        rows = rows_at(p, PAIR)
        allowed = jnp.concatenate([pair_mask(sizes, p, wr, wc).astype(F32)] * 4, axis=0) > 0.5
        low = head_masks(BF16)
        full = head_masks(F32)

        def group(g):
            query = packed[rows, lanes_at(g, 128)]
            key = packed[rows, lanes_at(g, 128, width)]
            value = packed[rows, lanes_at(g, 128, 2 * width)]
            probs = pair_probs(stacked(query, low), key, allowed).astype(BF16)
            context[rows, lanes_at(g, 128)] = folded(dot(probs, value), full).astype(BF16)

        each(width // 128, group)

    for p in range(images // 2):
        pair(p)
        between(1)


def image_halves(kind):
    row = iota((PAIR, 128), 0)
    first = jnp.where(row < CELLS, 1.0, 0.0).astype(F32)
    return first.astype(kind), (1.0 - first).astype(kind)


def fold_heads(square):
    lane = iota((32, 128), 1) >> 5
    total = jnp.zeros((32, 128), F32)
    for h in range(4):
        total = total + jnp.where(lane == h, square[32 * h : 32 * h + 32], 0.0)
    return total


def unfold_heads(block):
    lane = iota((32, 128), 1) >> 5
    return jnp.concatenate([jnp.where(lane == h, block, 0.0) for h in range(4)], axis=0)


def pair_grams(left, left_base, right, right_base, images, valid, out):
    def pair(p):
        rows = rows_at(p, PAIR)
        one, two = image_halves(BF16)
        ok = valid[rows, :].astype(BF16)
        one, two = one * ok, two * ok

        def group(g):
            a = left[rows, lanes_at(g, 128, left_base)]
            b = right[rows, lanes_at(g, 128, right_base)]
            both = t_dot(a, jnp.concatenate([b * one, b * two], axis=1))
            out[pl.ds(pl.multiple_of(64 * p, 32), 32), lanes_at(g, 128)] = fold_heads(both[:, :128])
            out[pl.ds(pl.multiple_of(64 * p + 32, 32), 32), lanes_at(g, 128)] = fold_heads(both[:, 128:])

        each(out.shape[1] // 128, group)

    each(images // 2, pair)


def sum_windows(gram, ins, images, c, sems, vertical, horizontal):
    half = images * 16
    mine = pl.ds(pl.multiple_of(half * c, 32), half)
    other = pl.ds(pl.multiple_of(half * (1 - c), 32), half)

    def add(k):
        def one(i):
            rows = pl.ds(pl.multiple_of(half * c + 32 * i, 32), 32)
            gram[rows, :] = gram[rows, :] + ins[k, rows_at(i, 32), :]

        each(images // 2, one)

    copy = remote(gram.at[other], ins.at[0], sems.at[0], horizontal)
    copy.start()
    copy.wait()
    add(0)
    copy = remote(gram.at[mine], ins.at[1], sems.at[1], vertical)
    copy.start()
    copy.wait()
    add(1)
    copy = remote(gram.at[mine], ins.at[2], sems.at[2], horizontal)
    copy.start()
    copy.wait()

    def take(i):
        gram[pl.ds(pl.multiple_of(half * (1 - c) + 32 * i, 32), 32), :] = ins[2, rows_at(i, 32), :]

    each(images // 2, take)


ROWS_WIDE = 42
ROWS_SMALL = 64
SHORT = 96


def join(pieces):
    tiles = [None] * (SHORT * len(pieces) // 128)
    lane = iota(pieces[0].shape, 1)
    for i, piece in enumerate(pieces):
        t, shift = divmod(SHORT * i, 128)
        moved = pltpu.roll(piece, shift, 1) if shift else piece
        head = jnp.where(lane >= shift, moved, 0.0)
        tiles[t] = head if tiles[t] is None else tiles[t] + head
        if shift > 128 - SHORT:
            tiles[t + 1] = jnp.where(lane < shift - (128 - SHORT), moved, 0.0)
    return tiles


def cut(tiles):
    lane = iota(tiles[0].shape, 1)
    pieces = []
    for i in range(128 * len(tiles) // SHORT):
        t, shift = divmod(SHORT * i, 128)
        piece = pltpu.roll(tiles[t], 128 - shift, 1) if shift else tiles[t]
        if shift > 128 - SHORT:
            piece = jnp.where(lane < 128 - shift, piece, pltpu.roll(tiles[t + 1], 128 - shift, 1))
        pieces.append(piece)
    return pieces


def small_rows():
    return ((42, 2, 0), (44, 3, 1), (47, 4, 2), (51, 4, 3))


def unpack_small(gathered_small, vec, qbias, hbias):
    blocks = [gathered_small[d].astype(F32) for d in range(gathered_small.shape[0])]
    for t, tile in enumerate(join(blocks)):
        vec[:, 128 * t : 128 * t + 128] = tile
    width = vec.shape[1]
    qbias[...] = jnp.zeros(qbias.shape, F32)
    for first, count, row in small_rows():
        lines = [
            jnp.broadcast_to(block[first + r : first + r + 1], (8, 128)) for block in blocks for r in range(count)
        ]
        for t, tile in enumerate(join(lines)):
            line = tile[0:1]
            if row == 0:
                at = 128 * t if 128 * t < width else 128 * t + width
                qbias[0:1, at : at + 128] = line
            elif row == 1:
                qbias[1:2, 128 * t : 128 * t + 128] = line
            else:
                hbias[row - 2 : row - 1, 128 * t : 128 * t + 128] = line


def pack_small(vecg, qbg, hbg, out):
    width = vecg.shape[1]
    for d, piece in enumerate(cut([vecg[:, 128 * t : 128 * t + 128] for t in range(width // 128)])):
        out[d, 0 : vecg.shape[0]] = piece
    for first, count, row in small_rows():
        if row == 0:
            at = [128 * t if 128 * t < width else 128 * t + width for t in range(2 * width // 128)]
            lines = [qbg[0:1, a : a + 128] for a in at]
        elif row == 1:
            lines = [qbg[1:2, 128 * t : 128 * t + 128] for t in range(3 * width // 128)]
        else:
            lines = [hbg[row - 2 : row - 1, 128 * t : 128 * t + 128] for t in range(4 * width // 128)]
        for i, piece in enumerate(cut([jnp.broadcast_to(line, (8, 128)) for line in lines])):
            d, r = divmod(i, count)
            out[d, first + r : first + r + 1] = piece[0:1]


LINE = 4
AHEAD = 4
LAG = 1


def forward_kernel(
    images,
    width,
    hidden,
    sizes,
    patches,
    small,
    qkv_s,
    proj_s,
    hid_s,
    out_s,
    activations,
    o_w,
    vec,
    o_pad,
    o_stream,
    o_normed,
    o_packed,
    o_context,
    o_act,
    o_slope,
    o_mix,
    pad,
    streams,
    normed,
    packed,
    context,
    act,
    slope,
    gram,
    gram_in,
    valid,
    pre,
    wq,
    wp,
    wh,
    wo,
    row_out,
    row_in,
    col_out,
    col_in,
    final,
    halo_sems,
    gram_sems,
    load_sems,
    save_sems,
    z_sems,
    y_sems,
    xa_sems,
    xb_sems,
    c_sems,
    own_sems,
    small_in,
    qbias,
    hbias,
    small_sems,
):
    d, w, wr, wc = place()
    pairs = images // 2
    horizontal = (d, 2 * wr + 1 - wc)
    vertical = (d, 2 * (1 - wr) + wc)
    z, y = d // 2, d % 2
    depth = qkv_s.shape[1]
    others = [lax.rem(z + k, LINE) for k in range(1, LINE)]
    in_line = [(2 * other + y, w) for other in others]
    across = (2 * z + 1 - y, w)
    alike = [(lax.rem(d + k, 2 * LINE), w) for k in range(1, 2 * LINE)]
    greet([horizontal, vertical] + alike)
    for peer in alike:
        remote(small, small_in.at[d], small_sems, peer).start()
    left, right = side_masks(wr, wc)

    columns = pl.ds(pl.multiple_of(wc * (width // 2), 128), width // 2)

    def split(t):
        return t % 4 != 3

    def rows_of(t):
        return pl.ds(pl.multiple_of(wr * (depth // 2), 16), depth // 2) if split(t) else pl.ds(0, depth)

    def shard(t, rows):
        layer, j = t // 12, t % 12
        base = (0, 0, 0, 0, 4, 4, 4, 4, 8, 8, 8, 8)[j]
        if j >= 8:
            start = (j - base) * depth
            return out_s.at[layer, pl.ds(pl.multiple_of(start + rows.start, 16), rows.size), columns]
        source = qkv_s if j < 3 else proj_s if j < 4 else hid_s
        shift = 0 if j == 3 else (j - base) * width
        return source.at[layer, rows, pl.ds(pl.multiple_of(shift + wc * (width // 2), 128), width // 2)]

    def piece(t, z_at, y_at):
        return o_w.at[t, z_at, y_at, rows_of(t), columns]

    def send(src, dst, sems, peer):
        remote(src, dst, sems, peer).start()

    def arrived(ref, sems):
        pltpu.make_async_copy(ref, ref, sems.at[1]).wait()

    def left_here(ref, sems):
        pltpu.make_async_copy(ref, ref, sems.at[0]).wait()

    def all_left(t):
        left_here(o_w.at[t, pl.ds(0, LINE - 1), y, rows_of(t), columns], z_sems.at[t])
        left_here(piece(t, pl.ds(0, LINE), y), y_sems.at[t])
        if split(t):
            left_here(o_w.at[t, pl.ds(0, LINE - 1), y, rows_of(t), columns], xa_sems.at[t])
            left_here(piece(t, pl.ds(0, LINE), 1 - y), xb_sems.at[t])
        left_here(o_w.at[t, pl.ds(0, LINE), pl.ds(0, 2), pl.ds(0, depth), columns], c_sems.at[t])

    def own_copy(t):
        return pltpu.make_async_copy(
            shard(t, pl.ds(0, depth)), o_w.at[t, z, y, pl.ds(0, depth), columns], own_sems.at[t]
        )

    def open_chunk(t):
        own_copy(t).start()
        for peer in in_line:
            send(shard(t, rows_of(t)), piece(t, z, y), z_sems.at[t], peer)
        send(shard(t, rows_of(t)), piece(t, z, y), y_sems.at[t], across)

    def stage_a(t):
        arrived(o_w.at[t, pl.ds(0, LINE - 1), y, rows_of(t), columns], z_sems.at[t])
        for other in others:
            send(piece(t, other, y), piece(t, other, y), y_sems.at[t], across)
        if split(t):
            for other in others:
                send(piece(t, other, y), piece(t, other, y), xa_sems.at[t], vertical)

    def stage_b(t):
        beside = piece(t, pl.ds(0, LINE), 1 - y)
        arrived(beside, y_sems.at[t])
        if split(t):
            send(beside, beside, xb_sems.at[t], vertical)

    def stage_c(t):
        own_copy(t).wait()
        if split(t):
            rows = pl.ds(pl.multiple_of((1 - wr) * (depth // 2), 16), depth // 2)
            arrived(o_w.at[t, pl.ds(0, LINE - 1), y, rows, columns], xa_sems.at[t])
            arrived(o_w.at[t, pl.ds(0, LINE), 1 - y, rows, columns], xb_sems.at[t])
        half = o_w.at[t, pl.ds(0, LINE), pl.ds(0, 2), pl.ds(0, depth), columns]
        send(half, half, c_sems.at[t], horizontal)

    chunks = 24
    kinds = ("q", "q", "q", "p", "h", "h", "h", "h", "o", "o", "o", "o")
    busy = {"q": True, "p": True, "h": True, "o": True}
    landed, waiting = set(), []
    clock = [0]

    def load_of(t):
        j = t % 12
        if j < 3:
            dst = wq.at[:, :, :, pl.ds(j * width, width)]
        elif j < 4:
            dst = wp
        elif j < 8:
            dst = wh.at[:, :, :, pl.ds((j - 4) * width, width)]
        else:
            dst = wo.at[:, :, j - 8]
        return pltpu.make_async_copy(o_w.at[t], dst, load_sems.at[t])

    def stage_d(t):
        other = pl.ds(pl.multiple_of((1 - wc) * (width // 2), 128), width // 2)
        arrived(o_w.at[t, pl.ds(0, LINE), pl.ds(0, 2), pl.ds(0, depth), other], c_sems.at[t])
        if t < 12 or not busy[kinds[t % 12]]:
            load_of(t).start()
            landed.add(t)
        else:
            waiting.append(t)

    def advance(count):
        for _ in range(count):
            t = clock[0]
            if t >= chunks + 3 * LAG:
                return
            if t < chunks:
                stage_a(t)
                if t + AHEAD < chunks:
                    open_chunk(t + AHEAD)
            if 0 <= t - LAG < chunks:
                stage_b(t - LAG)
            if 0 <= t - 2 * LAG < chunks:
                stage_c(t - 2 * LAG)
            if 0 <= t - 3 * LAG < chunks:
                stage_d(t - 3 * LAG)
            clock[0] += 1

    def need(t):
        while clock[0] <= t + 3 * LAG and clock[0] < chunks + 3 * LAG:
            advance(1)
        load_of(t).wait()

    def release(kind):
        busy[kind] = False
        for t in [t for t in waiting if kinds[t % 12] == kind]:
            load_of(t).start()
            landed.add(t)
            waiting.remove(t)

    for t in range(AHEAD):
        open_chunk(t)

    saves = {}

    def save(name, src, dst, s):
        saves[name] = pltpu.make_async_copy(src, dst, save_sems.at[s])
        saves[name].start()

    small_in[d] = small[...]
    fill_valid(valid, sizes, images, wr, wc)
    clear_borders(pad, images)

    def enter(p):
        rows = rows_at(p, PAIR)
        to_pad(pad, p, patches[rows, :].astype(F32) * spread(valid[rows, :], width))

    each(pairs, enter)
    arrived(small_in.at[pl.ds(0, 2 * LINE - 1)], small_sems)
    unpack_small(small_in, vec, qbias, hbias)

    def convolve(k, stream):
        halo(pad, images, wr, wc, row_out.at[k], row_in.at[k], col_out.at[k], col_in.at[k], halo_sems.at[k], vertical, horizontal)
        conv_forward(pad, images, vec, k, valid, stream, left, right)

    def columns_of(weights, at):
        block = weights[:, :, :, at]
        return block.reshape(width, block.shape[-1])

    def qkv(k, x):
        for part in range(3):
            need(12 * k + part)

            def tile(j):
                at = lanes_at(j, 256, part * width)
                packed[:, at] = (dot(x[...], columns_of(wq, at)) + qbias[k : k + 1, at]).astype(BF16)

            each(width // 256, tile)
        release("q")

    def proj(k, stream, store):
        need(12 * k + 3)

        def tile(j):
            at = lanes_at(j, 256)
            pre[...] = dot(context[...], columns_of(wp, at))

            def part(p):
                rows = rows_at(p, PAIR)
                store(p, at, stream[rows, at] + spread(valid[rows, :], 256) * (pre[rows, :] + vec[38 + k : 39 + k, at]))

            each(pairs, part)

        each(width // 256, tile)
        release("p")

    def feed_forward(k, x, stream, store):
        for block in range(4):
            need(12 * k + 4 + block)

            def tile(j):
                at = lanes_at(j, 256, block * width)
                pre[...] = dot(x[...], columns_of(wh, at))

                def part(p):
                    rows = rows_at(p, PAIR)
                    a, s = gelu_pair(pre[rows, :] + hbias[k : k + 1, at])
                    act[rows, at] = a.astype(BF16)
                    slope[rows, at] = s.astype(BF16)

                each(pairs, part)

            each(width // 256, tile)
            advance(1)
        release("h")
        for block in range(4):
            need(12 * k + 8 + block)

        def tile2(j):
            at = lanes_at(j, 256)
            block = wo[:, :, :, :, at]
            pre[...] = dot(act[...], block.reshape(hidden, 256))

            def part(p):
                rows = rows_at(p, PAIR)
                store(p, at, stream[rows, at] + spread(valid[rows, :], 256) * (pre[rows, :] + vec[40 + k : 41 + k, at]))

            each(pairs, part)

        each(width // 256, tile2)
        release("o")

    def into_pad(p, at, value):
        pad[pl.ds(pl.multiple_of((18 * p + 1) * 8, 8), CELLS), at] = value[:CELLS]
        pad[pl.ds(pl.multiple_of((18 * p + 10) * 8, 8), CELLS), at] = value[CELLS:]

    convolve(0, streams.at[0])
    save("pad0", pad, o_pad.at[0], 0)
    save("s1", streams.at[0], o_stream.at[0], 1)
    norm_rows(streams.at[0], images, vec, 0, normed.at[0])
    save("n1", normed.at[0], o_normed.at[0], 2)
    qkv(0, normed.at[0])
    save("k1", packed, o_packed.at[0], 3)
    window_attention(packed, images, sizes, wr, wc, context, advance)
    save("c1", context, o_context.at[0], 4)
    saves["pad0"].wait()
    proj(0, streams.at[0], into_pad)
    convolve(1, streams.at[1])
    save("pad2", pad, o_pad.at[1], 0)
    save("s3", streams.at[1], o_stream.at[1], 5)
    norm_rows(streams.at[1], images, vec, 1, normed.at[1])
    save("n3", normed.at[1], o_normed.at[1], 6)
    saves["pad2"].wait()
    feed_forward(0, normed.at[1], streams.at[1], into_pad)
    save("a0", act, o_act.at[0], 7)
    save("g0", slope, o_slope.at[0], 8)
    saves["s1"].wait()
    saves["n1"].wait()
    saves["k1"].wait()
    saves["c1"].wait()
    convolve(2, streams.at[0])
    save("pad4", pad, o_pad.at[2], 0)
    save("s5", streams.at[0], o_stream.at[2], 1)
    norm_rows(streams.at[0], images, vec, 2, normed.at[0])
    save("n5", normed.at[0], o_normed.at[2], 2)
    qkv(1, normed.at[0])
    save("k5", packed, o_packed.at[1], 3)
    pair_grams(packed, 2 * width, packed, width, images, valid, gram)
    sum_windows(gram, gram_in, images, wc, gram_sems, vertical, horizontal)

    def soften(i):
        rows = rows_at(i, 32)
        x = gram[rows, :] * SCALE
        e = jnp.exp(x - jnp.max(x, 0, keepdims=True))
        gram[rows, :] = e * (1.0 / jnp.sum(e, 0, keepdims=True))

    each(images, soften)
    save("mix", gram, o_mix, 9)

    def mix_pair(p):
        rows = rows_at(p, PAIR)
        one, two = image_halves(BF16)

        def group(g):
            at = lanes_at(g, 128)
            a = unfold_heads(gram[pl.ds(pl.multiple_of(64 * p, 32), 32), at])
            b = unfold_heads(gram[pl.ds(pl.multiple_of(64 * p + 32, 32), 32), at])
            query = packed[rows, at]
            mixing = jnp.concatenate([a, b], axis=0).astype(BF16)
            context[rows, at] = dot(jnp.concatenate([query * one, query * two], axis=1), mixing).astype(BF16)

        each(width // 128, group)

    each(pairs, mix_pair)
    save("c5", context, o_context.at[1], 4)
    saves["s3"].wait()
    saves["n3"].wait()

    def into_last(p, at, value):
        streams[1, rows_at(p, PAIR), at] = value

    proj(1, streams.at[0], into_last)
    save("s6", streams.at[1], o_stream.at[3], 5)
    norm_rows(streams.at[1], images, vec, 3, normed.at[1])
    save("n6", normed.at[1], o_normed.at[3], 6)
    saves["a0"].wait()
    saves["g0"].wait()

    def into_final(p, at, value):
        final[rows_at(p, PAIR), at] = value.astype(BF16)

    feed_forward(1, normed.at[1], streams.at[1], into_final)
    save("a1", act, o_act.at[1], 7)
    save("g1", slope, o_slope.at[1], 8)
    save("end", final, activations, 10)
    advance(chunks + 3 * LAG)
    for t in range(chunks):
        all_left(t)
    left_here(small_in.at[pl.ds(0, 2 * LINE - 1)], small_sems)
    for name in ("pad4", "s5", "n5", "k5", "mix", "c5", "s6", "n6", "a1", "g1", "end"):
        saves[name].wait()


ANY = pl.BlockSpec(memory_space=pl.ANY)
VMEM = pl.BlockSpec(memory_space=pltpu.VMEM)
SMEM = pl.BlockSpec(memory_space=pltpu.SMEM)


def run_forward(sizes, patches, small, shards):
    images = sizes.shape[0]
    n_rows, width = patches.shape
    hidden = shards[2].shape[2]
    lines = images * 72
    depth = shards[0].shape[1]
    shapes = (
        ((n_rows, width), BF16),
        ((24, LINE, 2, depth, width), BF16),
        ((ROWS_SMALL, width), F32),
        ((3, lines, width), F32),
        ((4, n_rows, width), F32),
        ((4, n_rows, width), BF16),
        ((2, n_rows, 3 * width), BF16),
        ((2, n_rows, width), BF16),
        ((2, n_rows, hidden), BF16),
        ((2, n_rows, hidden), BF16),
        ((images * 32, width), F32),
    )
    return pl.pallas_call(
        functools.partial(forward_kernel, images, width, hidden),
        out_shape=[jax.ShapeDtypeStruct(*s) for s in shapes],
        in_specs=[SMEM, VMEM, VMEM] + [ANY] * 4,
        out_specs=[ANY] * 2 + [VMEM] + [ANY] * 8,
        scratch_shapes=[
            pltpu.VMEM((lines, width), F32),
            pltpu.VMEM((2, n_rows, width), F32),
            pltpu.VMEM((2, n_rows, width), BF16),
            pltpu.VMEM((n_rows, 3 * width), BF16),
            pltpu.VMEM((n_rows, width), BF16),
            pltpu.VMEM((n_rows, hidden), BF16),
            pltpu.VMEM((n_rows, hidden), BF16),
            pltpu.VMEM((images * 32, width), F32),
            pltpu.VMEM((3, images * 16, width), F32),
            pltpu.VMEM((n_rows, 128), F32),
            pltpu.VMEM((n_rows, 256), F32),
            pltpu.VMEM((LINE, 2, depth, 3 * width), BF16),
            pltpu.VMEM((LINE, 2, depth, width), BF16),
            pltpu.VMEM((LINE, 2, depth, hidden), BF16),
            pltpu.VMEM((LINE, 2, 4, depth, width), BF16),
            pltpu.VMEM((3, images * 8, width), BF16),
            pltpu.VMEM((3, images * 8, width), BF16),
            pltpu.VMEM((3, images * 8, width), BF16),
            pltpu.VMEM((3, images * 8, width), BF16),
            pltpu.VMEM((n_rows, width), BF16),
            pltpu.SemaphoreType.DMA((3, 2, 2)),
            pltpu.SemaphoreType.DMA((3, 2)),
            pltpu.SemaphoreType.DMA((24,)),
            pltpu.SemaphoreType.DMA((11,)),
            pltpu.SemaphoreType.DMA((24, 2)),
            pltpu.SemaphoreType.DMA((24, 2)),
            pltpu.SemaphoreType.DMA((24, 2)),
            pltpu.SemaphoreType.DMA((24, 2)),
            pltpu.SemaphoreType.DMA((24, 2)),
            pltpu.SemaphoreType.DMA((24,)),
            pltpu.VMEM((2 * LINE, ROWS_SMALL, 128), BF16),
            pltpu.VMEM((8, 3 * width), F32),
            pltpu.VMEM((8, hidden), F32),
            pltpu.SemaphoreType.DMA((2,)),
        ],
        compiler_params=pltpu.CompilerParams(
            collective_id=0, has_side_effects=True, vmem_limit_bytes=58 * 2**20
        ),
    )(sizes, patches, small, *shards)


def column_sums(src, images, width, store):
    for part in range(src.shape[1] // width):
        at = pl.ds(part * width, width)

        def one(p, total):
            x = src[rows_at(p, PAIR), at].astype(F32)
            return total + jnp.sum(x.reshape(PAIR // 8, 8, width), axis=0)

        total = lax.fori_loop(0, images // 2, one, jnp.zeros((8, width), F32))
        store(at, jnp.sum(total, axis=0, keepdims=True))


def norm_back(stream, images, vec, k, grad_normed, grad, vecg):
    gain = vec[30 + k : 31 + k, :]
    width = stream.shape[1]

    def one(p, carry):
        rows = rows_at(p, PAIR)
        x = stream[rows, :]
        dn = grad_normed[rows, :]
        centered = x - jnp.mean(x, -1, keepdims=True)
        rstd = lax.rsqrt(jnp.mean(centered * centered, -1, keepdims=True) + EPS)
        xhat = centered * rstd
        scaled = dn * gain
        inner = jnp.mean(scaled * xhat, -1, keepdims=True)
        grad[rows, :] = grad[rows, :] + rstd * (scaled - jnp.mean(scaled, -1, keepdims=True) - xhat * inner)
        gains = jnp.sum((dn * xhat).reshape(PAIR // 8, 8, width), axis=0)
        shifts = jnp.sum(dn.reshape(PAIR // 8, 8, width), axis=0)
        return carry[0] + gains, carry[1] + shifts

    zero = jnp.zeros((8, width), F32)
    gains, shifts = lax.fori_loop(0, images // 2, one, (zero, zero))
    vecg[30 + k : 31 + k, :] = jnp.sum(gains, axis=0, keepdims=True)
    vecg[34 + k : 35 + k, :] = jnp.sum(shifts, axis=0, keepdims=True)


def conv_back(grad_pad, pad, images, vec, k, valid, grad, vecg, left, right):
    keep = jnp.where(iota((8, 128), 0) < 7, 1.0, 0.0).astype(F32)
    for part in range(pad.shape[1] // 128):
        at = pl.ds(part * 128, 128)
        taps = [vec[9 * k + t : 9 * k + t + 1, at] for t in range(9)]

        def one(i, sums):
            back = three(grad_pad, i, at, left, right)
            ahead = three(pad, i, at, left, right)
            sums = list(sums)
            for r in range(7):
                own = back[r + 1][1] * keep
                total = own
                for t in range(9):
                    total = total + taps[t] * back[r + 2 - t // 3][2 - t % 3]
                    sums[t] = sums[t] + own * ahead[r + t // 3][t % 3]
                sums[9] = sums[9] + own
                to = pl.ds(pl.multiple_of((7 * i + r) * 8, 8), 8)
                grad[to, at] = valid[to, :] * total
            return tuple(sums)

        sums = lax.fori_loop(0, images, one, tuple(jnp.zeros((8, 128), F32) for _ in range(10)))
        for t in range(9):
            vecg[9 * k + t : 9 * k + t + 1, at] = jnp.sum(sums[t], axis=0, keepdims=True)
        vecg[27 + k : 28 + k, at] = jnp.sum(sums[9], axis=0, keepdims=True)


def window_back(packed, images, sizes, wr, wc, grad_context, between):
    width = grad_context.shape[1]

    def pair(p):
        rows = rows_at(p, PAIR)
        allowed = jnp.concatenate([pair_mask(sizes, p, wr, wc).astype(F32)] * 4, axis=0) > 0.5
        low = head_masks(BF16)
        full = head_masks(F32)

        def group(g):
            at_q, at_k, at_v = (lanes_at(g, 128, n * width) for n in range(3))
            key = packed[rows, at_k]
            query_bd = stacked(packed[rows, at_q], low)
            grad_bd = stacked(grad_context[rows, lanes_at(g, 128)], low)
            probs = pair_probs(query_bd, key, allowed)
            grad_probs = dot_t(grad_bd, packed[rows, at_v])
            packed[rows, at_v] = t_dot(probs.astype(BF16), grad_bd).astype(BF16)
            inner = jnp.sum(probs * grad_probs, -1, keepdims=True)
            grad_scores = jnp.where(allowed, probs * (grad_probs - inner), 0.0).astype(BF16)
            packed[rows, at_q] = (folded(dot(grad_scores, key), full) * SCALE).astype(BF16)
            packed[rows, at_k] = (t_dot(grad_scores, query_bd) * SCALE).astype(BF16)

        each(width // 128, group)

    for p in range(images // 2):
        pair(p)
        between(1)


def channel_back(packed, images, mix, grad_gram, valid, grad_context):
    width = grad_context.shape[1]

    def pair(p):
        rows = rows_at(p, PAIR)
        one, two = image_halves(BF16)
        ok = valid[rows, :] * SCALE
        first = pl.ds(pl.multiple_of(64 * p, 32), 32)
        second = pl.ds(pl.multiple_of(64 * p + 32, 32), 32)

        def both(ref, at, axis):
            return jnp.concatenate(
                [unfold_heads(ref[first, at]), unfold_heads(ref[second, at])], axis=axis
            ).astype(BF16)

        def split(value):
            return jnp.concatenate([value * one, value * two], axis=1)

        def group(g):
            at = lanes_at(g, 128)
            at_k, at_v = lanes_at(g, 128, width), lanes_at(g, 128, 2 * width)
            key, value = packed[rows, at_k], packed[rows, at_v]
            packed[rows, at] = dot_t(split(grad_context[rows, at]), both(mix, at, 1)).astype(BF16)
            packed[rows, at_k] = (dot(split(value), both(grad_gram, at, 0)) * ok).astype(BF16)
            packed[rows, at_v] = (dot_t(split(key), both(grad_gram, at, 1)) * ok).astype(BF16)

        each(width // 128, group)

    each(images // 2, pair)


ORDER = (20, 21, 22, 23, 16, 17, 18, 19, 15, 12, 13, 14, 8, 9, 10, 11, 4, 5, 6, 7, 3, 0, 1, 2)
RING = 4
AHEAD_SUMS = 1
HELD = 12
WAIT = 1


def backward_kernel(
    images,
    width,
    hidden,
    sizes,
    cotangent,
    vec,
    i_pad,
    i_stream,
    i_normed,
    i_packed,
    i_context,
    i_act,
    i_slope,
    i_mix,
    i_w,
    patches_grad,
    tiny,
    g_qkv,
    g_proj,
    g_hid,
    g_out,
    grad,
    grad_pad,
    pad,
    stream,
    normed,
    packed,
    context,
    act,
    slope,
    dn,
    branch,
    gram,
    mix,
    gram_in,
    valid,
    w_wide,
    w_tall,
    row_out,
    row_in,
    col_out,
    col_in,
    go_out,
    go_in,
    held,
    x_in,
    y_in,
    z_in,
    part,
    part_in,
    whole,
    whole_in,
    stage,
    halo_sems,
    gram_sems,
    load_sems,
    stage_sems,
    weight_sems,
    sums_sems,
    credits,
    vecg,
    qbg,
    hbg,
    small_out,
    small_in,
    small_sum,
    small_sems,
):
    d, w, wr, wc = place()
    depth = i_w.shape[3]
    pairs = images // 2
    horizontal = (d, 2 * wr + 1 - wc)
    vertical = (d, 2 * (1 - wr) + wc)
    z, y = d // 2, d % 2
    others = [lax.rem(z + k, LINE) for k in range(1, LINE)]
    in_line = [(2 * other + y, w) for other in others]
    across = (2 * z + 1 - y, w)
    alike = [(lax.rem(d + k, 2 * LINE), w) for k in range(1, 2 * LINE)]
    windows = [(d, lax.rem(w + k, 4)) for k in range(1, 4)]
    greet(alike + windows)
    vecg[...] = jnp.zeros(vecg.shape, F32)
    left, right = side_masks(wr, wc)
    loads = {}
    half = width // 2
    rows_mine = pl.ds(pl.multiple_of(wr * (depth // 2), 16), depth // 2)
    rows_other = pl.ds(pl.multiple_of((1 - wr) * (depth // 2), 16), depth // 2)
    cols_mine = pl.ds(pl.multiple_of(wc * half, 128), half)
    cols_other = pl.ds(pl.multiple_of((1 - wc) * half, 128), half)
    chunks = len(ORDER)
    halves = [n for n in range(chunks) if n % 2 == 0]

    def post(n, kind, src, dst, peer):
        copy = remote(src, dst, sums_sems.at[n, kind], peer)
        copy.start()

    def settle(n, kind, ref):
        pltpu.make_async_copy(ref, ref, sums_sems.at[n, kind, 1]).wait()
        pltpu.make_async_copy(ref, ref, sums_sems.at[n, kind, 0]).wait()

    def credit(n, kind, peer):
        if n + RING < chunks:
            pl.semaphore_signal(credits.at[kind], inc=1, device_id=peer, device_id_type=MESH)

    def take_credit(n, kind):
        if n >= RING:
            pl.semaphore_wait(credits.at[kind], 1)

    def open_sum(n):
        take_credit(n, 0)
        post(n, 0, go_out.at[n % RING], go_in.at[n % RING], horizontal)

    def sum_cores(n):
        s, h = n % RING, n % HELD
        settle(n, 0, go_in.at[s])

        def add(i):
            held[h, i // 2, i % 2] = held[h, i // 2, i % 2] + go_in[s, i // 2, i % 2]

        each(2 * LINE, add)
        credit(n, 0, horizontal)
        if n in halves:
            if n >= RING:
                pl.semaphore_wait(credits.at[1], 1)
            post(n, 1, held.at[h, :, :, rows_other], x_in.at[s], vertical)
        else:
            take_credit(n, 2)
            post(n, 2, held.at[h, :, 1 - y], y_in.at[s], across)

    def sum_x(n):
        if n not in halves:
            return
        s, h = n % RING, n % HELD
        settle(n, 1, x_in.at[s])

        def add(i):
            held[h, i // 2, i % 2, rows_mine] = held[h, i // 2, i % 2, rows_mine] + x_in[s, i // 2, i % 2]

        each(2 * LINE, add)
        credit(n, 1, vertical)
        take_credit(n, 2)
        post(n, 2, held.at[h, :, 1 - y, rows_mine], y_in.at[s, :, 0 : depth // 2], across)

    def share(n):
        return (rows_mine, depth // 2) if n in halves else (pl.ds(0, depth), depth)

    def sum_y(n):
        s, h = n % RING, n % HELD
        rows, count = share(n)
        settle(n, 2, y_in.at[s, :, 0:count])

        def add(i):
            held[h, i, y, rows] = held[h, i, y, rows] + y_in[s, i, 0:count]

        each(LINE, add)
        credit(n, 2, across)
        for k in range(LINE - 1):
            take_credit(n, 3 + k)
        for k, (other, peer) in enumerate(zip(others, in_line)):
            post(n, 3, held.at[h, other, y, rows], z_in.at[s, LINE - 2 - k, 0:count], peer)

    def sum_z(n):
        s, h = n % RING, n % HELD
        rows, count = share(n)
        settle(n, 3, z_in.at[s, :, 0:count])
        total = held[h, z, y, rows].astype(F32)
        for k in range(LINE - 1):
            total = total + z_in[s, k, 0:count].astype(F32)
        part[s, rows] = total.astype(BF16)
        for k, peer in enumerate(in_line):
            credit(n, 3 + LINE - 2 - k, peer)
        take_credit(n, 6)
        post(n, 4, part.at[s, rows], part_in.at[s, rows], vertical)

    def sum_windows_x(n):
        s = n % RING
        if n in halves:
            settle(n, 4, part_in.at[s, rows_other])
            whole[s, rows_mine] = part[s, rows_mine]
            whole[s, rows_other] = part_in[s, rows_other]
        else:
            settle(n, 4, part_in.at[s])
            whole[s] = part[s] + part_in[s]
        credit(n, 6, vertical)
        take_credit(n, 7)
        post(n, 5, whole.at[s], whole_in.at[s], horizontal)

    def result_of(n):
        layer, j = ORDER[n] // 12, ORDER[n] % 12
        if j < 3:
            return g_qkv.at[layer, :, pl.ds(j * width, width)]
        if j < 4:
            return g_proj.at[layer]
        if j < 8:
            return g_hid.at[layer, :, pl.ds((j - 4) * width, width)]
        return g_out.at[layer, pl.ds((j - 8) * depth, depth)]

    def write_out(n):
        return pltpu.make_async_copy(stage.at[n % RING], result_of(n), stage_sems.at[n % RING])

    def finish(n):
        s = n % RING
        settle(n, 5, whole_in.at[s])
        if n >= RING:
            write_out(n - RING).wait()
        stage[s, :, cols_mine] = whole[s].astype(F32)
        stage[s, :, cols_other] = whole_in[s].astype(F32)
        credit(n, 7, horizontal)
        write_out(n).start()

    stages = (sum_cores, sum_x, sum_y, sum_z, sum_windows_x, finish)
    made, clock = [0], [0]

    def turn():
        for lag in reversed(range(len(stages))):
            n = clock[0] - lag * WAIT
            if 0 <= n < chunks:
                stages[lag](n)
        clock[0] += 1

    def pump(count):
        for _ in range(count):
            if clock[0] < made[0] - AHEAD_SUMS or (made[0] == chunks and clock[0] < chunks + len(stages) * WAIT):
                turn()

    def room(count):
        while made[0] + count > RING + clock[0] or made[0] + count - HELD > clock[0] - 3 * WAIT:
            turn()

    def opened(count):
        for n in range(made[0], made[0] + count):
            open_sum(n)
        made[0] += count

    def pair_of_halves(dy, base):
        theirs = dy[:, pl.ds(pl.multiple_of(base + (1 - wc) * half, 128), half)]
        ours = dy[:, pl.ds(pl.multiple_of(base + wc * half, 128), half)]
        return jnp.concatenate([theirs, ours], axis=1)

    def weight_grad(x, dy):
        for j in range(dy.shape[1] // width):
            room(1)
            s, h = made[0] % RING, made[0] % HELD

            def tile(q):
                both = t_dot(x[:, lanes_at(q, 4 * depth)], pair_of_halves(dy, j * width)).astype(BF16)
                go_out[s, rows_at(q, 2)] = both[:, :half].reshape(2, 2, depth, half)
                held[h, rows_at(q, 2)] = both[:, half:].reshape(2, 2, depth, half)

            each(LINE // 2, tile)
            opened(1)
            pump(1)

    def tall_weight_grad(x, dy):
        room(4)
        slots = [(n % RING, n % HELD) for n in range(made[0], made[0] + 4)]

        def tile(i):
            both = t_dot(x[:, lanes_at(i, 4 * depth)], pair_of_halves(dy, 0)).astype(BF16)
            for j, (s, h) in enumerate(slots):
                block = both[j * depth : (j + 1) * depth]
                go_out[s, i // 2, i % 2] = block[:, :half]
                held[h, i // 2, i % 2] = block[:, half:]

        each(2 * LINE, tile)
        opened(4)
        pump(1)

    def load(name, src, dst, s):
        loads[name] = pltpu.make_async_copy(src, dst, load_sems.at[s])
        loads[name].start()

    def load_weights(t):
        j = t % 12
        if j < 3:
            dst = w_wide.at[:, :, :, pl.ds(j * width, width)]
        elif j < 4:
            dst = w_tall.at[:, :, 0]
        elif j < 8:
            dst = w_wide.at[:, :, :, pl.ds((j - 4) * width, width)]
        else:
            dst = w_tall.at[:, :, j - 8]
        return pltpu.make_async_copy(i_w.at[t], dst, weight_sems.at[t])

    def chunks_of(name):
        first = {"wq": 0, "wp": 3, "wh": 4, "wo": 8}[name[:2]] + 12 * int(name[2])
        return range(first, first + {"wq": 3, "wp": 1, "wh": 4, "wo": 4}[name[:2]])

    def fetch(name):
        for t in chunks_of(name):
            load_weights(t).start()

    def fetched(name):
        for t in chunks_of(name):
            load_weights(t).wait()

    load("cotangent", cotangent, branch, 1)
    load("act", i_act.at[1], act, 0)
    fetch("wo1")
    load("slope", i_slope.at[1], slope, 2)
    fetch("wh1")
    load("normed", i_normed.at[3], normed, 4)
    load("stream", i_stream.at[3], stream, 5)
    load("context", i_context.at[1], context, 6)
    load("packed", i_packed.at[1], packed, 7)
    load("mix", i_mix, mix, 8)
    load("pad", i_pad.at[2], pad, 9)
    fill_valid(valid, sizes, images, wr, wc)
    clear_borders(grad_pad, images)

    loads["cotangent"].wait()

    def enter(p):
        rows = rows_at(p, PAIR)
        grad[rows, :] = branch[rows, :].astype(F32) * spread(valid[rows, :], width)

    each(pairs, enter)

    def make_branch(row):
        def one(p):
            rows = rows_at(p, PAIR)
            branch[rows, :] = (grad[rows, :] * spread(valid[rows, :], width)).astype(BF16)

        each(pairs, one)

        def store(at, total):
            vecg[row : row + 1, at] = total

        column_sums(branch, images, 256, store)

    def feed_forward(k):
        make_branch(40 + k)
        loads["act"].wait()
        tall_weight_grad(act, branch)
        fetched(f"wo{k}")
        loads["slope"].wait()

        def tile(j):
            at = lanes_at(j, 4 * depth)
            dact = dot_t(branch[...], w_tall[j // 2, j % 2].reshape(4 * depth, width))
            slope[:, at] = (slope[:, at].astype(F32) * dact).astype(BF16)

        each(2 * LINE, tile)
        pump(1)

        def store(at, total):
            hbg[k : k + 1, at] = total

        column_sums(slope, images, 256, store)
        loads["normed"].wait()
        weight_grad(normed, slope)
        fetched(f"wh{k}")

        def tile2(j):
            block = w_wide[rows_at(j, 2)].reshape(4 * depth, hidden)
            dn[:, lanes_at(j, 4 * depth)] = dot_t(slope[...], block)

        each(LINE // 2, tile2)
        pump(1)
        loads["stream"].wait()
        norm_back(stream, images, vec, 1 + 2 * k, dn, grad, vecg)

    def proj(k):
        make_branch(38 + k)
        loads["context"].wait()
        weight_grad(context, branch)
        fetched(f"wp{k}")

        def tile(j):
            block = w_tall[rows_at(j, 2), :, 0].reshape(4 * depth, width)
            context[:, lanes_at(j, 4 * depth)] = dot_t(branch[...], block).astype(BF16)

        each(LINE // 2, tile)

    def qkv(k):
        def store(at, total):
            qbg[k : k + 1, at] = total

        column_sums(packed, images, 256, store)
        loads["normed"].wait()
        weight_grad(normed, packed)
        fetched(f"wq{k}")

        def tile(j):
            block = w_wide[rows_at(j, 2), :, :, 0 : 3 * width].reshape(4 * depth, 3 * width)
            dn[:, lanes_at(j, 4 * depth)] = dot_t(packed[...], block)

        each(LINE // 2, tile)
        loads["stream"].wait()
        norm_back(stream, images, vec, 2 * k, dn, grad, vecg)

    def convolve(k):
        def enter_pad(p):
            to_pad(grad_pad, p, grad[rows_at(p, PAIR), :])

        each(pairs, enter_pad)
        halo(grad_pad, images, wr, wc, row_out.at[k], row_in.at[k], col_out.at[k], col_in.at[k], halo_sems.at[k], vertical, horizontal)
        loads["pad"].wait()
        conv_back(grad_pad, pad, images, vec, k, valid, grad, vecg, left, right)

    feed_forward(1)
    load("act", i_act.at[0], act, 0)
    load("slope", i_slope.at[0], slope, 2)
    fetch("wp1")
    fetch("wq1")
    load("normed", i_normed.at[2], normed, 4)
    load("stream", i_stream.at[2], stream, 5)
    proj(1)
    fetch("wo0")
    loads["packed"].wait()
    pair_grams(packed, 0, context, 0, images, valid, gram)
    sum_windows(gram, gram_in, images, wc, gram_sems, vertical, horizontal)
    loads["mix"].wait()

    def harden(i):
        rows = rows_at(i, 32)
        y, g = mix[rows, :], gram[rows, :]
        gram[rows, :] = y * (g - jnp.sum(y * g, 0, keepdims=True))

    each(images, harden)
    channel_back(packed, images, mix, gram, valid, context)
    load("context", i_context.at[0], context, 6)
    qkv(1)
    fetch("wh0")
    load("packed", i_packed.at[0], packed, 7)
    load("normed", i_normed.at[1], normed, 4)
    load("stream", i_stream.at[1], stream, 5)
    convolve(2)
    pump(1)
    load("pad", i_pad.at[1], pad, 9)
    feed_forward(0)
    fetch("wp0")
    fetch("wq0")
    load("normed", i_normed.at[0], normed, 4)
    load("stream", i_stream.at[0], stream, 5)
    convolve(1)
    pump(1)
    load("pad", i_pad.at[0], pad, 9)
    proj(0)
    loads["packed"].wait()
    window_back(packed, images, sizes, wr, wc, context, pump)
    qkv(0)
    convolve(0)

    def leave(p):
        rows = rows_at(p, PAIR)
        branch[rows, :] = grad[rows, :].astype(BF16)

    each(pairs, leave)
    load("end", branch, patches_grad, 1)
    pack_small(vecg, qbg, hbg, small_out)
    small_in[d] = small_out[d]
    for peer in alike:
        remote(small_out.at[peer[0]], small_in.at[d], small_sems.at[0], peer).start()
    while clock[0] < chunks + len(stages) * WAIT:
        turn()
    for n in (1, 0):
        seven = small_in.at[pl.ds(0, 2 * LINE - 1)]
        pltpu.make_async_copy(seven, seven, small_sems.at[0, n]).wait()
    total = small_in[0]
    for k in range(1, 2 * LINE):
        total = total + small_in[k]
    small_sum[w] = total
    for peer in windows:
        remote(small_sum.at[w], small_sum.at[w], small_sems.at[1], peer).start()
    for n in (1, 0):
        three_of = small_sum.at[pl.ds(0, 3)]
        pltpu.make_async_copy(three_of, three_of, small_sems.at[1, n]).wait()
    tiny[...] = ((small_sum[0] + small_sum[1]) + small_sum[2]) + small_sum[3]
    for n in range(chunks - RING, chunks):
        write_out(n).wait()
    loads["end"].wait()


def run_backward(sizes, cotangent, vec, saved, weights, hidden):
    images = sizes.shape[0]
    depth = weights.shape[3]
    n_rows, width = cotangent.shape
    lines = images * 72
    shapes = (
        ((n_rows, width), BF16),
        ((ROWS_SMALL, 128), F32),
        ((2, depth, 3 * width), F32),
        ((2, depth, width), F32),
        ((2, depth, hidden), F32),
        ((2, 4 * depth, width), F32),
    )
    half = width // 2
    return pl.pallas_call(
        functools.partial(backward_kernel, images, width, hidden),
        out_shape=[jax.ShapeDtypeStruct(*s) for s in shapes],
        in_specs=[SMEM, ANY, VMEM] + [ANY] * 9,
        out_specs=[ANY, VMEM] + [ANY] * 4,
        scratch_shapes=[
            pltpu.VMEM((n_rows, width), F32),
            pltpu.VMEM((lines, width), F32),
            pltpu.VMEM((lines, width), F32),
            pltpu.VMEM((n_rows, width), F32),
            pltpu.VMEM((n_rows, width), BF16),
            pltpu.VMEM((n_rows, 3 * width), BF16),
            pltpu.VMEM((n_rows, width), BF16),
            pltpu.VMEM((n_rows, hidden), BF16),
            pltpu.VMEM((n_rows, hidden), BF16),
            pltpu.VMEM((n_rows, width), F32),
            pltpu.VMEM((n_rows, width), BF16),
            pltpu.VMEM((images * 32, width), F32),
            pltpu.VMEM((images * 32, width), F32),
            pltpu.VMEM((3, images * 16, width), F32),
            pltpu.VMEM((n_rows, 128), F32),
            pltpu.VMEM((LINE, 2, depth, hidden), BF16),
            pltpu.VMEM((LINE, 2, 4, depth, width), BF16),
            pltpu.VMEM((3, images * 8, width), BF16),
            pltpu.VMEM((3, images * 8, width), BF16),
            pltpu.VMEM((3, images * 8, width), BF16),
            pltpu.VMEM((3, images * 8, width), BF16),
            pltpu.VMEM((RING, LINE, 2, depth, half), BF16),
            pltpu.VMEM((RING, LINE, 2, depth, half), BF16),
            pltpu.VMEM((HELD, LINE, 2, depth, half), BF16),
            pltpu.VMEM((RING, LINE, 2, depth // 2, half), BF16),
            pltpu.VMEM((RING, LINE, depth, half), BF16),
            pltpu.VMEM((RING, LINE - 1, depth, half), BF16),
            pltpu.VMEM((RING, depth, half), BF16),
            pltpu.VMEM((RING, depth, half), BF16),
            pltpu.VMEM((RING, depth, half), BF16),
            pltpu.VMEM((RING, depth, half), BF16),
            pltpu.VMEM((RING, depth, width), F32),
            pltpu.SemaphoreType.DMA((3, 2, 2)),
            pltpu.SemaphoreType.DMA((3, 2)),
            pltpu.SemaphoreType.DMA((10,)),
            pltpu.SemaphoreType.DMA((RING,)),
            pltpu.SemaphoreType.DMA((24,)),
            pltpu.SemaphoreType.DMA((24, 6, 2)),
            pltpu.SemaphoreType.REGULAR((8,)),
            pltpu.VMEM((48, width), F32),
            pltpu.VMEM((8, 3 * width), F32),
            pltpu.VMEM((8, hidden), F32),
            pltpu.VMEM((2 * LINE, ROWS_SMALL, 128), F32),
            pltpu.VMEM((2 * LINE, ROWS_SMALL, 128), F32),
            pltpu.VMEM((4, ROWS_SMALL, 128), F32),
            pltpu.SemaphoreType.DMA((2, 2)),
        ],
        compiler_params=pltpu.CompilerParams(
            collective_id=1, has_side_effects=True, vmem_limit_bytes=60 * 2**20
        ),
    )(sizes, cotangent, vec, *saved, weights)


def to_cells(windows):
    images, _, _, width = windows.shape
    grid = windows.reshape(images, 7, 7, width)
    return jnp.pad(grid, ((0, 0), (0, 0), (0, 1), (0, 0))).reshape(images * CELLS, width)


def of_cells(rows, images):
    width = rows.shape[1]
    return rows.reshape(images, 7, 8, width)[:, :, :7].reshape(images, 1, 49, width)


def on_device_fast(
    patches,
    cotangent,
    grid_sizes,
    conv_weight,
    conv_bias,
    norm_gain,
    norm_bias,
    qkv_weight,
    spatial_bias,
    channel_bias,
    proj_weight,
    proj_bias,
    hidden_weight,
    hidden_bias,
    output_weight,
    output_bias,
):
    images = patches.shape[0]
    hidden = hidden_weight.shape[2]
    small = (
        conv_weight, conv_bias, norm_gain, norm_bias, proj_bias, output_bias, spatial_bias, channel_bias, hidden_bias
    )
    rows = jnp.concatenate([a.reshape(-1, SHORT) for a in small], axis=0)
    rows = jnp.pad(rows, ((0, ROWS_SMALL - rows.shape[0]), (0, 128 - SHORT)))
    weights = (qkv_weight, proj_weight, hidden_weight, output_weight)
    forward = run_forward(grid_sizes, to_cells(patches), rows, weights)
    activations, gathered_weights, vec, *saved = forward
    back = run_backward(grid_sizes, to_cells(cotangent), vec, saved, gathered_weights, hidden)
    grads, tiny, g_qkv, g_proj, g_hid, g_out = back
    tiny = tiny[:, :SHORT]
    return (
        of_cells(activations, images),
        of_cells(grads, images),
        tiny[:27].reshape(3, 9, SHORT),
        tiny[27:30],
        tiny[30:34],
        tiny[34:38],
        g_qkv,
        tiny[42:44].reshape(-1),
        tiny[44:47].reshape(-1),
        g_proj,
        tiny[38:40],
        g_hid,
        tiny[47:55].reshape(2, -1),
        g_out,
        tiny[40:42],
    )


def as_sent(array):
    return jax.tree.map(lambda a: a.astype(jnp.bfloat16) if a.dtype == jnp.float32 else a, array)


def image_valid(grid_sizes):
    rows = jnp.arange(7, dtype=jnp.int32)
    windows = jnp.arange(4, dtype=jnp.int32)
    top_rows = (windows // 2)[:, None] * 7 + rows[None, :]
    left_cols = (windows % 2)[:, None] * 7 + rows[None, :]
    sizes = grid_sizes[:, None, None, None]
    inside = (top_rows[None, :, :, None] < sizes) & (left_cols[None, :, None, :] < sizes)
    return inside.astype(jnp.float32).reshape(grid_sizes.shape[0], 4, 49, 1)


def layer_norm(stream, gain_row, shift_row):
    centre = jnp.mean(stream, -1, keepdims=True)
    centered = stream - centre
    variance = jnp.mean(centered * centered, -1, keepdims=True)
    return centered * lax.rsqrt(variance + EPS) * gain_row + shift_row


def gelu_exact(value_in):
    return jax.nn.gelu(value_in, approximate=False)


def matmul(left_rows, right_mat):
    return jnp.dot(left_rows, right_mat, preferred_element_type=jnp.float32)


def contract_rows(left_rows, right_rows):
    return lax.dot_general(
        left_rows, right_rows, (((0,), (0,)), ((), ())), preferred_element_type=jnp.float32
    )


def times_transposed(grad_rows, weight):
    return lax.dot_general(
        grad_rows, weight, (((1,), (1,)), ((), ())), preferred_element_type=jnp.float32
    )


def edge_lines(stream, images):
    channels = stream.shape[-1]
    image_grid = stream.reshape(images, 7, 7, channels)
    return jnp.stack(
        [image_grid[:, 0], image_grid[:, 6], image_grid[:, :, 0], image_grid[:, :, 6]], 1
    )[None]


def padded_tile(image_grid, lines, row_half, col_half):
    zero_line = jnp.zeros_like(lines[0, :, 0])
    upper = jnp.where(
        row_half == 1, jnp.where(col_half == 0, lines[0, :, 1], lines[1, :, 1]), zero_line
    )
    lower = jnp.where(
        row_half == 0, jnp.where(col_half == 0, lines[2, :, 0], lines[3, :, 0]), zero_line
    )
    left_side = jnp.where(
        col_half == 1, jnp.where(row_half == 0, lines[0, :, 3], lines[2, :, 3]), zero_line
    )
    right_side = jnp.where(
        col_half == 0, jnp.where(row_half == 0, lines[1, :, 2], lines[3, :, 2]), zero_line
    )
    zero_cell = zero_line[:, 0]
    top_left = jnp.where((row_half == 1) & (col_half == 1), lines[0, :, 1, 6], zero_cell)
    top_right = jnp.where((row_half == 1) & (col_half == 0), lines[1, :, 1, 0], zero_cell)
    bottom_left = jnp.where((row_half == 0) & (col_half == 1), lines[2, :, 0, 6], zero_cell)
    bottom_right = jnp.where((row_half == 0) & (col_half == 0), lines[3, :, 0, 0], zero_cell)
    middle = jnp.concatenate([left_side[:, :, None], image_grid, right_side[:, :, None]], 2)
    top_row = jnp.concatenate([top_left[:, None], upper, top_right[:, None]], 1)
    bottom_row = jnp.concatenate([bottom_left[:, None], lower, bottom_right[:, None]], 1)
    return jnp.concatenate([top_row[:, None], middle, bottom_row[:, None]], 1)


def position_conv(stream, images, window, weight9, shift_row, valid_rows):
    channels = stream.shape[-1]
    lines = lax.all_gather(as_sent(edge_lines(stream, images)), "win", axis=0, tiled=True)
    padded = padded_tile(stream.reshape(images, 7, 7, channels), lines, window // 2, window % 2)
    summed = jnp.zeros((images, 7, 7, channels), jnp.float32)
    for tap_index in range(9):
        row_shift, col_shift = divmod(tap_index, 3)
        summed = (
            summed
            + weight9[tap_index] * padded[:, row_shift : row_shift + 7, col_shift : col_shift + 7]
        )
    return (stream + valid_rows * (summed + shift_row).reshape(images * 49, channels), padded)


def position_conv_back(grad_stream, padded, images, window, weight9, valid_rows):
    channels = grad_stream.shape[-1]
    masked = valid_rows * grad_stream
    lines = lax.all_gather(as_sent(edge_lines(masked, images)), "win", axis=0, tiled=True)
    image_grid = masked.reshape(images, 7, 7, channels)
    grad_pad = padded_tile(image_grid, lines, window // 2, window % 2)
    summed = jnp.zeros((images, 7, 7, channels), jnp.float32)
    tap_grads = []
    for tap_index in range(9):
        row_shift, col_shift = divmod(tap_index, 3)
        summed = (
            summed
            + weight9[tap_index]
            * grad_pad[:, 2 - row_shift : 9 - row_shift, 2 - col_shift : 9 - col_shift]
        )
        tap_grads.append(
            jnp.sum(
                image_grid * padded[:, row_shift : row_shift + 7, col_shift : col_shift + 7],
                axis=(0, 1, 2),
            )
        )
    return (
        grad_stream + summed.reshape(grad_stream.shape),
        jnp.stack(tap_grads),
        jnp.sum(image_grid, axis=(0, 1, 2)),
    )


def mlp_forward(normed, weight_in, bias_in, weight_out, bias_out):
    activated = gelu_exact(matmul(normed, weight_in) + bias_in).astype(jnp.bfloat16)
    return matmul(activated, weight_out) + bias_out


def mlp_backward(normed, grad_stream, valid_rows, weight_in, bias_in, weight_out):
    hidden_pre = matmul(normed, weight_in) + bias_in
    activated, gelu_pull = jax.vjp(gelu_exact, hidden_pre)
    grad_branch = (valid_rows * grad_stream).astype(jnp.bfloat16)
    grad_weight_out = contract_rows(activated.astype(jnp.bfloat16), grad_branch)
    grad_bias_out = jnp.sum(grad_branch.astype(jnp.float32), 0)
    grad_pre = gelu_pull(times_transposed(grad_branch, weight_out))[0].astype(jnp.bfloat16)
    grad_weight_in = contract_rows(normed, grad_pre)
    grad_bias_in = jnp.sum(grad_pre.astype(jnp.float32), 0)
    return (
        times_transposed(grad_pre, weight_in),
        grad_weight_in,
        grad_bias_in,
        grad_weight_out,
        grad_bias_out,
    )


def norm_backward(stream, gain_row, shift_row, grad_normed):
    unused, norm_pull = jax.vjp(layer_norm, stream, gain_row, shift_row)
    return norm_pull(grad_normed)


def window_probs(packed, images, scaling, valid_rows):
    split = packed.reshape(images, 49, 3, HEADS, HEAD)
    query_rows = split[:, :, 0]
    key_rows = split[:, :, 1]
    value_rows = split[:, :, 2]
    key_ok = valid_rows.reshape(images, 1, 1, 49) > 0.5
    scores = (
        jnp.einsum("iphe,iqhe->ihpq", query_rows, key_rows, preferred_element_type=jnp.float32)
        * scaling
    )
    scores = jnp.where(key_ok, scores, -1000000000.0)
    return (query_rows, key_rows, value_rows, jax.nn.softmax(scores, axis=-1))


def channel_mixing(gram_total, scaling):
    return jax.nn.softmax(gram_total * scaling, axis=-1)


def channel_grads(
    grad_mixing, mixing, grad_context, key_masked, value_masked, valid_cells, scaling
):
    grad_query = jnp.einsum(
        "bgcd,bpgc->bpgd",
        mixing.astype(jnp.bfloat16),
        grad_context,
        preferred_element_type=jnp.float32,
    )
    grad_gram = (mixing * (grad_mixing - jnp.sum(mixing * grad_mixing, -1, keepdims=True))).astype(
        jnp.bfloat16
    )
    grad_keys = (
        jnp.einsum("bgcd,bpgd->bpgc", grad_gram, value_masked, preferred_element_type=jnp.float32)
        * scaling
        * valid_cells
    )
    grad_values = (
        jnp.einsum("bgcd,bpgc->bpgd", grad_gram, key_masked, preferred_element_type=jnp.float32)
        * scaling
        * valid_cells
    )
    return jnp.stack([grad_query, grad_keys, grad_values], 2).astype(jnp.bfloat16)


def on_device(
    patches,
    cotangent,
    grid_sizes,
    conv_weight,
    conv_bias,
    norm_gain,
    norm_bias,
    qkv_weight,
    spatial_bias,
    channel_bias,
    proj_weight,
    proj_bias,
    hidden_weight,
    hidden_bias,
    output_weight,
    output_bias,
):
    (
        conv_w,
        conv_b,
        gains,
        shifts,
        qkv_w,
        sp_bias,
        ch_bias,
        proj_w,
        proj_b,
        hid_w,
        hid_b,
        out_w,
        out_b,
    ) = (
        lax.all_gather(conv_weight, "dp", axis=2, tiled=True),
        lax.all_gather(conv_bias, "dp", axis=1, tiled=True),
        lax.all_gather(norm_gain, "dp", axis=1, tiled=True),
        lax.all_gather(norm_bias, "dp", axis=1, tiled=True),
        lax.all_gather(qkv_weight, "dp", axis=1, tiled=True),
        lax.all_gather(spatial_bias, "dp", axis=0, tiled=True),
        lax.all_gather(channel_bias, "dp", axis=0, tiled=True),
        lax.all_gather(proj_weight, "dp", axis=1, tiled=True),
        lax.all_gather(proj_bias, "dp", axis=1, tiled=True),
        lax.all_gather(hidden_weight, "dp", axis=1, tiled=True),
        lax.all_gather(hidden_bias, "dp", axis=1, tiled=True),
        lax.all_gather(output_weight, "dp", axis=1, tiled=True),
        lax.all_gather(output_bias, "dp", axis=1, tiled=True),
    )
    conv_w = conv_w.astype(jnp.float32)
    conv_b = conv_b.astype(jnp.float32)
    gains = gains.astype(jnp.float32)
    shifts = shifts.astype(jnp.float32)
    sp_bias = sp_bias.astype(jnp.float32)
    ch_bias = ch_bias.astype(jnp.float32)
    proj_b = proj_b.astype(jnp.float32)
    hid_b = hid_b.astype(jnp.float32)
    out_b = out_b.astype(jnp.float32)
    images = patches.shape[0]
    model_width = patches.shape[-1]
    rows_all = images * 49
    group_count = lax.axis_size("win")
    local_heads = HEADS // group_count
    group_width = model_width // group_count
    scaling = HEAD ** (-0.5)
    window = lax.axis_index("win")
    full_valid = image_valid(grid_sizes)
    valid_rows = lax.dynamic_slice_in_dim(full_valid, window, 1, 1).reshape(rows_all, 1)
    stream0 = patches.astype(jnp.float32).reshape(rows_all, model_width) * valid_rows
    stream1, pad_first = position_conv(stream0, images, window, conv_w[0], conv_b[0], valid_rows)
    normed1 = layer_norm(stream1, gains[0], shifts[0]).astype(jnp.bfloat16)
    packed_bias = jnp.concatenate(
        [sp_bias[:model_width], jnp.zeros((model_width,), jnp.float32), sp_bias[model_width:]]
    )
    packed1 = (matmul(normed1, qkv_w[0]) + packed_bias).astype(jnp.bfloat16)
    query1, keys1, values1, probs1 = window_probs(packed1, images, scaling, valid_rows)
    context1 = (
        jnp.einsum(
            "ihpq,iqhe->iphe",
            probs1.astype(jnp.bfloat16),
            values1,
            preferred_element_type=jnp.float32,
        )
        .astype(jnp.bfloat16)
        .reshape(rows_all, model_width)
    )
    stream2 = stream1 + valid_rows * (matmul(context1, proj_w[0]) + proj_b[0])
    stream3, pad_second = position_conv(stream2, images, window, conv_w[1], conv_b[1], valid_rows)
    normed3 = layer_norm(stream3, gains[1], shifts[1]).astype(jnp.bfloat16)
    stream4 = stream3 + valid_rows * mlp_forward(normed3, hid_w[0], hid_b[0], out_w[0], out_b[0])
    stream5, pad_third = position_conv(stream4, images, window, conv_w[2], conv_b[2], valid_rows)
    normed5 = layer_norm(stream5, gains[2], shifts[2]).astype(jnp.bfloat16)
    packed5 = (matmul(normed5, qkv_w[1]) + ch_bias).astype(jnp.bfloat16)
    moved = lax.all_to_all(
        packed5.reshape(images, 1, 49, 3, group_count, group_width),
        "win",
        split_axis=4,
        concat_axis=1,
        tiled=True,
    )
    grouped = moved.reshape(images, 196, 3, local_heads, HEAD)
    valid_cells = full_valid.reshape(images, 196, 1, 1)
    query5 = grouped[:, :, 0]
    key_masked = grouped[:, :, 1] * valid_cells.astype(jnp.bfloat16)
    value_masked = grouped[:, :, 2] * valid_cells.astype(jnp.bfloat16)
    gram_total = jnp.einsum(
        "bpgc,bpgd->bgcd", key_masked, value_masked, preferred_element_type=jnp.float32
    )
    mixing = channel_mixing(gram_total, scaling)
    context_groups = jnp.einsum(
        "bgcd,bpgd->bpgc", mixing.astype(jnp.bfloat16), query5, preferred_element_type=jnp.float32
    ).astype(jnp.bfloat16)
    returned = lax.all_to_all(
        context_groups.reshape(images, 4, 49, 1, group_width),
        "win",
        split_axis=1,
        concat_axis=3,
        tiled=True,
    )
    context5 = returned.reshape(rows_all, model_width)
    stream6 = stream5 + valid_rows * (matmul(context5, proj_w[1]) + proj_b[1])
    normed6 = layer_norm(stream6, gains[3], shifts[3]).astype(jnp.bfloat16)
    stream7 = stream6 + valid_rows * mlp_forward(normed6, hid_w[1], hid_b[1], out_w[1], out_b[1])
    activations = stream7.astype(jnp.bfloat16).reshape(patches.shape)
    grad7 = cotangent.astype(jnp.float32).reshape(rows_all, model_width)
    grad_normed, hid_w_grad1, hid_b_grad1, out_w_grad1, out_b_grad1 = mlp_backward(
        normed6, grad7, valid_rows, hid_w[1], hid_b[1], out_w[1]
    )
    grad_part, gain_grad3, shift_grad3 = norm_backward(stream6, gains[3], shifts[3], grad_normed)
    grad6 = grad7 + grad_part
    branch_grad = (valid_rows * grad6).astype(jnp.bfloat16)
    proj_w_grad1 = contract_rows(context5, branch_grad)
    proj_b_grad1 = jnp.sum(branch_grad.astype(jnp.float32), 0)
    context_grad = times_transposed(branch_grad, proj_w[1]).astype(jnp.bfloat16)
    moved_grad = lax.all_to_all(
        context_grad.reshape(images, 1, 49, group_count, group_width),
        "win",
        split_axis=3,
        concat_axis=1,
        tiled=True,
    )
    group_grad = moved_grad.reshape(images, 196, local_heads, HEAD)
    mixing_grad = jnp.einsum(
        "bpgc,bpgd->bgcd", group_grad, query5, preferred_element_type=jnp.float32
    )
    stacked = channel_grads(
        mixing_grad, mixing, group_grad, key_masked, value_masked, valid_cells, scaling
    )
    sent_back = lax.all_to_all(
        stacked.reshape(images, 4, 49, 3, 1, group_width),
        "win",
        split_axis=1,
        concat_axis=4,
        tiled=True,
    )
    packed_grad5 = sent_back.reshape(rows_all, 3 * model_width)
    qkv_w_grad1 = contract_rows(normed5, packed_grad5)
    ch_bias_grad = jnp.sum(packed_grad5.astype(jnp.float32), 0)
    grad_part, gain_grad2, shift_grad2 = norm_backward(
        stream5, gains[2], shifts[2], times_transposed(packed_grad5, qkv_w[1])
    )
    grad5 = grad6 + grad_part
    grad4, conv_w_grad2, conv_b_grad2 = position_conv_back(
        grad5, pad_third, images, window, conv_w[2], valid_rows
    )
    grad_normed, hid_w_grad0, hid_b_grad0, out_w_grad0, out_b_grad0 = mlp_backward(
        normed3, grad4, valid_rows, hid_w[0], hid_b[0], out_w[0]
    )
    grad_part, gain_grad1, shift_grad1 = norm_backward(stream3, gains[1], shifts[1], grad_normed)
    grad3 = grad4 + grad_part
    grad2, conv_w_grad1, conv_b_grad1 = position_conv_back(
        grad3, pad_second, images, window, conv_w[1], valid_rows
    )
    branch_grad = (valid_rows * grad2).astype(jnp.bfloat16)
    proj_w_grad0 = contract_rows(context1, branch_grad)
    proj_b_grad0 = jnp.sum(branch_grad.astype(jnp.float32), 0)
    context_grad = (
        times_transposed(branch_grad, proj_w[0])
        .astype(jnp.bfloat16)
        .reshape(images, 49, HEADS, HEAD)
    )
    probs_low = probs1.astype(jnp.bfloat16)
    probs_grad = jnp.einsum(
        "iphe,iqhe->ihpq", context_grad, values1, preferred_element_type=jnp.float32
    )
    values_grad = jnp.einsum(
        "ihpq,iphe->iqhe", probs_low, context_grad, preferred_element_type=jnp.float32
    )
    scores_grad = (probs1 * (probs_grad - jnp.sum(probs1 * probs_grad, -1, keepdims=True))).astype(
        jnp.bfloat16
    )
    key_ok = valid_rows.reshape(images, 1, 1, 49) > 0.5
    scores_grad = jnp.where(key_ok, scores_grad, jnp.zeros_like(scores_grad))
    query_grad = (
        jnp.einsum("ihpq,iqhe->iphe", scores_grad, keys1, preferred_element_type=jnp.float32)
        * scaling
    )
    keys_grad = (
        jnp.einsum("ihpq,iphe->iqhe", scores_grad, query1, preferred_element_type=jnp.float32)
        * scaling
    )
    packed_grad1 = (
        jnp.stack([query_grad, keys_grad, values_grad], 2)
        .astype(jnp.bfloat16)
        .reshape(rows_all, 3 * model_width)
    )
    qkv_w_grad0 = contract_rows(normed1, packed_grad1)
    packed_sums = jnp.sum(packed_grad1.astype(jnp.float32), 0)
    sp_bias_grad = jnp.concatenate([packed_sums[:model_width], packed_sums[2 * model_width :]])
    grad_part, gain_grad0, shift_grad0 = norm_backward(
        stream1, gains[0], shifts[0], times_transposed(packed_grad1, qkv_w[0])
    )
    grad1 = grad2 + grad_part
    grad0, conv_w_grad0, conv_b_grad0 = position_conv_back(
        grad1, pad_first, images, window, conv_w[0], valid_rows
    )
    patches_grad = (grad0 * valid_rows).astype(jnp.bfloat16).reshape(patches.shape)
    local_sums = (
        lax.psum_scatter(
            jnp.stack([conv_w_grad0, conv_w_grad1, conv_w_grad2]),
            "dp",
            scatter_dimension=2,
            tiled=True,
        ),
        lax.psum_scatter(
            jnp.stack([conv_b_grad0, conv_b_grad1, conv_b_grad2]),
            "dp",
            scatter_dimension=1,
            tiled=True,
        ),
        lax.psum_scatter(
            jnp.stack([gain_grad0, gain_grad1, gain_grad2, gain_grad3]),
            "dp",
            scatter_dimension=1,
            tiled=True,
        ),
        lax.psum_scatter(
            jnp.stack([shift_grad0, shift_grad1, shift_grad2, shift_grad3]),
            "dp",
            scatter_dimension=1,
            tiled=True,
        ),
        lax.psum_scatter(
            jnp.stack([qkv_w_grad0, qkv_w_grad1]), "dp", scatter_dimension=1, tiled=True
        ),
        lax.psum_scatter(sp_bias_grad, "dp", scatter_dimension=0, tiled=True),
        lax.psum_scatter(ch_bias_grad, "dp", scatter_dimension=0, tiled=True),
        lax.psum_scatter(
            jnp.stack([proj_w_grad0, proj_w_grad1]), "dp", scatter_dimension=1, tiled=True
        ),
        lax.psum_scatter(
            jnp.stack([proj_b_grad0, proj_b_grad1]), "dp", scatter_dimension=1, tiled=True
        ),
        lax.psum_scatter(
            jnp.stack([hid_w_grad0, hid_w_grad1]), "dp", scatter_dimension=1, tiled=True
        ),
        lax.psum_scatter(
            jnp.stack([hid_b_grad0, hid_b_grad1]), "dp", scatter_dimension=1, tiled=True
        ),
        lax.psum_scatter(
            jnp.stack([out_w_grad0, out_w_grad1]), "dp", scatter_dimension=1, tiled=True
        ),
        lax.psum_scatter(
            jnp.stack([out_b_grad0, out_b_grad1]), "dp", scatter_dimension=1, tiled=True
        ),
    )
    summed = (
        lax.psum(local_sums[0].astype(jnp.bfloat16), "win").astype(jnp.float32),
        lax.psum(local_sums[1].astype(jnp.bfloat16), "win").astype(jnp.float32),
        lax.psum(local_sums[2].astype(jnp.bfloat16), "win").astype(jnp.float32),
        lax.psum(local_sums[3].astype(jnp.bfloat16), "win").astype(jnp.float32),
        lax.psum(local_sums[4].astype(jnp.bfloat16), "win").astype(jnp.float32),
        lax.psum(local_sums[5].astype(jnp.bfloat16), "win").astype(jnp.float32),
        lax.psum(local_sums[6].astype(jnp.bfloat16), "win").astype(jnp.float32),
        lax.psum(local_sums[7].astype(jnp.bfloat16), "win").astype(jnp.float32),
        lax.psum(local_sums[8].astype(jnp.bfloat16), "win").astype(jnp.float32),
        lax.psum(local_sums[9].astype(jnp.bfloat16), "win").astype(jnp.float32),
        lax.psum(local_sums[10].astype(jnp.bfloat16), "win").astype(jnp.float32),
        lax.psum(local_sums[11].astype(jnp.bfloat16), "win").astype(jnp.float32),
        lax.psum(local_sums[12].astype(jnp.bfloat16), "win").astype(jnp.float32),
    )
    return (activations, patches_grad) + tuple(summed)


def solution(mesh):
    small = mesh.shape["dp"] == 8 and mesh.shape["win"] == 4
    return jax.shard_map(
        on_device_fast if small else on_device,
        mesh=mesh,
        in_specs=(
            P("dp", "win", None, None),
            P("dp", "win", None, None),
            P("dp"),
            P(None, None, "dp"),
            P(None, "dp"),
            P(None, "dp"),
            P(None, "dp"),
            P(None, "dp", None),
            P("dp"),
            P("dp"),
            P(None, "dp", None),
            P(None, "dp"),
            P(None, "dp", None),
            P(None, "dp"),
            P(None, "dp", None),
            P(None, "dp"),
        ),
        out_specs=(
            P("dp", "win", None, None),
            P("dp", "win", None, None),
            P(None, None, "dp"),
            P(None, "dp"),
            P(None, "dp"),
            P(None, "dp"),
            P(None, "dp", None),
            P("dp"),
            P("dp"),
            P(None, "dp", None),
            P(None, "dp"),
            P(None, "dp", None),
            P(None, "dp"),
            P(None, "dp", None),
            P(None, "dp"),
        ),
        check_vma=False,
    )
```

```python
import functools

import jax
import jax.numpy as jnp
from jax import lax
from jax.experimental import pallas as pl
from jax.experimental.pallas import tpu as pltpu
from jax.sharding import PartitionSpec as P

HEADS = 24
HEAD = 32
EPS = 1e-05
MESH = pl.DeviceIdType.MESH
F32 = jnp.float32
BF16 = jnp.bfloat16
SCALE = HEAD ** (-0.5)
CELLS = 56
PAIR = 112
GROUPS = 3


def dot(left, right):
    return jnp.dot(left, right, preferred_element_type=F32)


def dot_t(left, right):
    return lax.dot_general(left, right, (((1,), (1,)), ((), ())), preferred_element_type=F32)


def t_dot(left, right):
    return lax.dot_general(left, right, (((0,), (0,)), ((), ())), preferred_element_type=F32)


def iota(shape, dim):
    return lax.broadcasted_iota(jnp.int32, shape, dim)


def rows_at(index, count):
    return pl.ds(pl.multiple_of(index * count, count), count)


def lanes_at(index, count, base=0):
    return pl.ds(pl.multiple_of(base + index * count, 128), count)


def each(count, body):
    def step(i, carry):
        body(i)
        return carry

    lax.fori_loop(0, count, step, 0)


def each_few(count, few, load, compute, store):
    def step(n):
        inputs = [load(n * few + u) for u in range(few)]
        results = [compute(*values) for values in inputs]
        for u in range(few):
            store(n * few + u, results[u])

    each(count // few, step)


def gelu_pair(pre):
    t = 1.0 / (1.0 + 0.23164190 * jnp.abs(pre))
    e = jnp.exp(-0.5 * pre * pre)
    poly = (((1.061405429 * t - 1.453152027) * t + 1.421413741) * t - 0.284496736) * t + 0.254829592
    tail = 0.5 * poly * t * e
    cdf = jnp.where(pre >= 0.0, 1.0 - tail, tail)
    return pre * cdf, cdf + pre * (e * 0.3989422804014327)


def place():
    d = lax.axis_index("dp")
    w = lax.axis_index("win")
    return d, w, w // 2, w % 2


def greet(peers):
    barrier = pltpu.get_barrier_semaphore()
    for peer in peers:
        pl.semaphore_signal(barrier, inc=1, device_id=peer, device_id_type=MESH)
    pl.semaphore_wait(barrier, len(peers))


def remote(src, dst, sems, peer):
    return pltpu.make_async_remote_copy(
        src_ref=src, dst_ref=dst, send_sem=sems.at[0], recv_sem=sems.at[1], device_id=peer, device_id_type=MESH
    )


def fill_valid(valid, sizes, images, wr, wc):
    def one(i):
        cell = iota((CELLS, 128), 0)
        r, c = cell >> 3, cell & 7
        inside = (r + 7 * wr < sizes[i]) & (c + 7 * wc < sizes[i]) & (c < 7)
        valid[rows_at(i, CELLS), :] = jnp.where(inside, 1.0, 0.0).astype(F32)

    each(images, one)


def spread(valid_rows, width):
    return jnp.concatenate([valid_rows] * (width // 128), axis=1)


def halo(pad, images, wr, wc, row_out, row_in, col_out, col_in, sems, vertical, horizontal, flights):
    edge = 7 - 6 * wr

    def pack(p):
        one = pad[pl.ds(pl.multiple_of((18 * p + edge) * 8, 8), 8), :]
        two = pad[pl.ds(pl.multiple_of((18 * p + 9 + edge) * 8, 8), 8), :]
        row_out[rows_at(p, 16), :] = jnp.concatenate([one, two], axis=0).astype(BF16)

    each(images // 2, pack)
    copy = remote(row_out, row_in, sems.at[0], vertical)
    copy.start()
    flights[0]()
    copy.wait()
    border = 8 - 8 * wr

    def unpack(p):
        both = row_in[rows_at(p, 16), :].astype(F32)
        pad[pl.ds(pl.multiple_of((18 * p + border) * 8, 8), 8), :] = both[:8]
        pad[pl.ds(pl.multiple_of((18 * p + 9 + border) * 8, 8), 8), :] = both[8:]

    each(images // 2, unpack)
    turn = 2 - 2 * wc
    sub = iota((8, 128), 0)

    def row_of(i, s):
        at_row = border if s == 7 else s + 1
        return pl.ds(pl.multiple_of((9 * i + at_row) * 8, 8), 8)

    def pack_col(p):
        for part in range(pad.shape[1] // 128):
            at = pl.ds(part * 128, 128)
            both = []
            for i in (2 * p, 2 * p + 1):
                line = jnp.zeros((8, 128), F32)
                for s in range(8):
                    line = jnp.where(sub == s, pltpu.roll(pad[row_of(i, s), at], s + turn, 0), line)
                both.append(line)
            col_out[rows_at(p, 16), at] = jnp.concatenate(both, axis=0).astype(BF16)

    each(images // 2, pack_col)
    copy = remote(col_out, col_in, sems.at[1], horizontal)
    copy.start()
    flights[1]()
    copy.wait()

    def unpack_col(p):
        for part in range(pad.shape[1] // 128):
            at = pl.ds(part * 128, 128)
            both = col_in[rows_at(p, 16), at].astype(F32)
            for one in range(2):
                line = both[8 * one : 8 * one + 8]
                for s in range(8):
                    to = row_of(2 * p + one, s)
                    pad[to, at] = jnp.where(sub == 7, pltpu.roll(line, 7 - s, 0), pad[to, at])

    each(images // 2, unpack_col)


def side_masks(wr, wc):
    c = iota((8, 128), 0)
    left = jnp.where((c == 0) & (wc == 0), 0.0, 1.0).astype(F32)
    right = jnp.where((c == 6) & (wc == 1), 0.0, 1.0).astype(F32)
    return left, right


def three(pad, i, at, left, right):
    rows = [pad[pl.ds(pl.multiple_of((9 * i + r) * 8, 8), 8), at] for r in range(9)]
    return [(pltpu.roll(v, 1, 0) * left, v, pltpu.roll(v, 7, 0) * right) for v in rows]


def conv_forward(pad, images, vec, k, valid, out, left, right):
    def one(i):
        for part in range(pad.shape[1] // 128):
            at = pl.ds(part * 128, 128)
            moved = three(pad, i, at, left, right)
            bias = vec[27 + k : 28 + k, at]
            taps = [vec[9 * k + t : 9 * k + t + 1, at] for t in range(9)]
            for r in range(7):
                total = jnp.broadcast_to(bias, (8, 128))
                for t in range(9):
                    total = total + taps[t] * moved[r + t // 3][t % 3]
                to = pl.ds(pl.multiple_of((7 * i + r) * 8, 8), 8)
                out[to, at] = moved[r + 1][1] + valid[to, :] * total

    each(images, one)


def norm_rows(src, images, vec, k, dst):
    gain = vec[30 + k : 31 + k, :]
    shift = vec[34 + k : 35 + k, :]

    def one(p):
        x = src[rows_at(p, PAIR), :]
        centered = x - jnp.mean(x, -1, keepdims=True)
        variance = jnp.mean(centered * centered, -1, keepdims=True)
        dst[rows_at(p, PAIR), :] = (centered * lax.rsqrt(variance + EPS) * gain + shift).astype(BF16)

    each(images // 2, one)


def to_pad(pad, p, rows):
    pad[pl.ds(pl.multiple_of((18 * p + 1) * 8, 8), CELLS), :] = rows[:CELLS]
    pad[pl.ds(pl.multiple_of((18 * p + 10) * 8, 8), CELLS), :] = rows[CELLS:]


def of_pad(pad, p):
    return jnp.concatenate(
        [
            pad[pl.ds(pl.multiple_of((18 * p + 1) * 8, 8), CELLS), :],
            pad[pl.ds(pl.multiple_of((18 * p + 10) * 8, 8), CELLS), :],
        ],
        axis=0,
    )


def clear_borders(pad, images):
    zero = jnp.zeros((8, pad.shape[1]), F32)

    def one(i):
        pad[pl.ds(pl.multiple_of(72 * i, 8), 8), :] = zero
        pad[pl.ds(pl.multiple_of(72 * i + 64, 8), 8), :] = zero

    each(images, one)


def head_masks(kind):
    lane = iota((PAIR, 128), 1) >> 5
    return [jnp.where(lane == h, 1.0, 0.0).astype(F32).astype(kind) for h in range(4)]


def pair_mask(sizes, p, wr, wc):
    row = iota((PAIR, PAIR), 0)
    lane = iota((PAIR, PAIR), 1)
    second = lane >= CELLS
    cell = jnp.where(second, lane - CELLS, lane)
    side = jnp.where(second, sizes[2 * p + 1], sizes[2 * p])
    r, c = cell >> 3, cell & 7
    inside = (r + 7 * wr < side) & (c + 7 * wc < side) & (c < 7)
    return inside & (second == (row >= CELLS))


def stacked(value, masks):
    return jnp.concatenate([value * m for m in masks], axis=0)


def folded(value, masks):
    total = value[:PAIR] * masks[0]
    for h in range(1, 4):
        total = total + value[h * PAIR : (h + 1) * PAIR] * masks[h]
    return total


def pair_probs(query_bd, key, allowed):
    scores = dot_t(query_bd, key) * SCALE
    scores = jnp.where(allowed, scores, -1000000000.0)
    e = jnp.exp(scores - jnp.max(scores, -1, keepdims=True))
    return e * (1.0 / jnp.sum(e, -1, keepdims=True))


def window_attention(packed, images, sizes, wr, wc, context, between):
    width = context.shape[1]

    def pair(p):
        rows = rows_at(p, PAIR)
        allowed = jnp.concatenate([pair_mask(sizes, p, wr, wc).astype(F32)] * 4, axis=0) > 0.5
        low = head_masks(BF16)
        full = head_masks(F32)

        def load(g):
            return tuple(packed[rows, lanes_at(g, 128, n * width)] for n in range(3))

        def compute(query, key, value):
            probs = pair_probs(stacked(query, low), key, allowed).astype(BF16)
            return folded(dot(probs, value), full).astype(BF16)

        def store(g, result):
            context[rows, lanes_at(g, 128)] = result

        each_few(width // 128, GROUPS, load, compute, store)

    for p in range(images // 2):
        pair(p)
        between(1)


def image_halves(kind):
    row = iota((PAIR, 128), 0)
    first = jnp.where(row < CELLS, 1.0, 0.0).astype(F32)
    return first.astype(kind), (1.0 - first).astype(kind)


def fold_heads(square):
    lane = iota((32, 128), 1) >> 5
    total = jnp.zeros((32, 128), F32)
    for h in range(4):
        total = total + jnp.where(lane == h, square[32 * h : 32 * h + 32], 0.0)
    return total


def unfold_heads(block):
    lane = iota((32, 128), 1) >> 5
    return jnp.concatenate([jnp.where(lane == h, block, 0.0) for h in range(4)], axis=0)


def pair_grams(left, left_base, right, right_base, images, valid, out):
    def pair(p):
        rows = rows_at(p, PAIR)
        one, two = image_halves(BF16)
        ok = valid[rows, :].astype(BF16)
        one, two = one * ok, two * ok

        def load(g):
            return left[rows, lanes_at(g, 128, left_base)], right[rows, lanes_at(g, 128, right_base)]

        def compute(a, b):
            both = t_dot(a, jnp.concatenate([b * one, b * two], axis=1))
            return fold_heads(both[:, :128]), fold_heads(both[:, 128:])

        def store(g, result):
            out[pl.ds(pl.multiple_of(64 * p, 32), 32), lanes_at(g, 128)] = result[0]
            out[pl.ds(pl.multiple_of(64 * p + 32, 32), 32), lanes_at(g, 128)] = result[1]

        each_few(out.shape[1] // 128, GROUPS, load, compute, store)

    each(images // 2, pair)


def sum_windows(gram, ins, images, c, sems, vertical, horizontal, flights):
    half = images * 16
    mine = pl.ds(pl.multiple_of(half * c, 32), half)
    other = pl.ds(pl.multiple_of(half * (1 - c), 32), half)

    def add(k):
        def one(i):
            rows = pl.ds(pl.multiple_of(half * c + 32 * i, 32), 32)
            gram[rows, :] = gram[rows, :] + ins[k, rows_at(i, 32), :]

        each(images // 2, one)

    copy = remote(gram.at[other], ins.at[0], sems.at[0], horizontal)
    copy.start()
    flights[0]()
    copy.wait()
    add(0)
    copy = remote(gram.at[mine], ins.at[1], sems.at[1], vertical)
    copy.start()
    flights[1]()
    copy.wait()
    add(1)
    copy = remote(gram.at[mine], ins.at[2], sems.at[2], horizontal)
    copy.start()
    flights[2]()
    copy.wait()

    def take(i):
        gram[pl.ds(pl.multiple_of(half * (1 - c) + 32 * i, 32), 32), :] = ins[2, rows_at(i, 32), :]

    each(images // 2, take)


ROWS_WIDE = 42
ROWS_SMALL = 64
SHORT = 96


def join(pieces):
    tiles = [None] * (SHORT * len(pieces) // 128)
    lane = iota(pieces[0].shape, 1)
    for i, piece in enumerate(pieces):
        t, shift = divmod(SHORT * i, 128)
        moved = pltpu.roll(piece, shift, 1) if shift else piece
        head = jnp.where(lane >= shift, moved, 0.0)
        tiles[t] = head if tiles[t] is None else tiles[t] + head
        if shift > 128 - SHORT:
            tiles[t + 1] = jnp.where(lane < shift - (128 - SHORT), moved, 0.0)
    return tiles


def cut(tiles):
    lane = iota(tiles[0].shape, 1)
    pieces = []
    for i in range(128 * len(tiles) // SHORT):
        t, shift = divmod(SHORT * i, 128)
        piece = pltpu.roll(tiles[t], 128 - shift, 1) if shift else tiles[t]
        if shift > 128 - SHORT:
            piece = jnp.where(lane < 128 - shift, piece, pltpu.roll(tiles[t + 1], 128 - shift, 1))
        pieces.append(piece)
    return pieces


def small_rows():
    return ((42, 2, 0), (44, 3, 1), (47, 4, 2), (51, 4, 3))


def unpack_small(gathered_small, vec, qbias, hbias):
    blocks = [gathered_small[d].astype(F32) for d in range(gathered_small.shape[0])]
    for t, tile in enumerate(join(blocks)):
        vec[:, 128 * t : 128 * t + 128] = tile
    width = vec.shape[1]
    qbias[...] = jnp.zeros(qbias.shape, F32)
    for first, count, row in small_rows():
        lines = [
            jnp.broadcast_to(block[first + r : first + r + 1], (8, 128)) for block in blocks for r in range(count)
        ]
        for t, tile in enumerate(join(lines)):
            line = tile[0:1]
            if row == 0:
                at = 128 * t if 128 * t < width else 128 * t + width
                qbias[0:1, at : at + 128] = line
            elif row == 1:
                qbias[1:2, 128 * t : 128 * t + 128] = line
            else:
                hbias[row - 2 : row - 1, 128 * t : 128 * t + 128] = line


def pack_small(vecg, qbg, hbg, out):
    width = vecg.shape[1]
    for d, piece in enumerate(cut([vecg[:, 128 * t : 128 * t + 128] for t in range(width // 128)])):
        out[d, 0 : vecg.shape[0]] = piece
    for first, count, row in small_rows():
        if row == 0:
            at = [128 * t if 128 * t < width else 128 * t + width for t in range(2 * width // 128)]
            lines = [qbg[0:1, a : a + 128] for a in at]
        elif row == 1:
            lines = [qbg[1:2, 128 * t : 128 * t + 128] for t in range(3 * width // 128)]
        else:
            lines = [hbg[row - 2 : row - 1, 128 * t : 128 * t + 128] for t in range(4 * width // 128)]
        for i, piece in enumerate(cut([jnp.broadcast_to(line, (8, 128)) for line in lines])):
            d, r = divmod(i, count)
            out[d, first + r : first + r + 1] = piece[0:1]


LINE = 4
AHEAD = 2
FIRST = 1
LAGS_FIRST = (0, 1, 2, 3)
LAGS = (0, 2, 4, 5)


def forward_kernel(
    images,
    width,
    hidden,
    sizes,
    patches,
    small,
    qkv_s,
    proj_s,
    hid_s,
    out_s,
    activations,
    o_w,
    vec,
    o_pad,
    o_stream,
    o_normed,
    o_packed,
    o_context,
    o_act,
    o_slope,
    o_mix,
    pad,
    streams,
    normed,
    packed,
    context,
    act,
    slope,
    gram,
    gram_in,
    valid,
    pre,
    wq,
    wp,
    wh,
    wo,
    row_out,
    row_in,
    col_out,
    col_in,
    final,
    halo_sems,
    gram_sems,
    load_sems,
    save_sems,
    z_sems,
    y_sems,
    xa_sems,
    xb_sems,
    c_sems,
    own_sems,
    small_in,
    qbias,
    hbias,
    small_sems,
):
    d, w, wr, wc = place()
    pairs = images // 2
    horizontal = (d, 2 * wr + 1 - wc)
    vertical = (d, 2 * (1 - wr) + wc)
    z, y = d // 2, d % 2
    depth = qkv_s.shape[1]
    others = [lax.rem(z + k, LINE) for k in range(1, LINE)]
    in_line = [(2 * other + y, w) for other in others]
    across = (2 * z + 1 - y, w)
    alike = [(lax.rem(d + k, 2 * LINE), w) for k in range(1, 2 * LINE)]
    greet([horizontal, vertical] + alike)
    for peer in alike:
        remote(small, small_in.at[d], small_sems, peer).start()
    left, right = side_masks(wr, wc)

    columns = pl.ds(pl.multiple_of(wc * (width // 2), 128), width // 2)

    def split(t):
        return t % 4 != 3

    def rows_of(t):
        return pl.ds(pl.multiple_of(wr * (depth // 2), 16), depth // 2) if split(t) else pl.ds(0, depth)

    def shard(t, rows):
        layer, j = t // 12, t % 12
        base = (0, 0, 0, 0, 4, 4, 4, 4, 8, 8, 8, 8)[j]
        if j >= 8:
            start = (j - base) * depth
            return out_s.at[layer, pl.ds(pl.multiple_of(start + rows.start, 16), rows.size), columns]
        source = qkv_s if j < 3 else proj_s if j < 4 else hid_s
        shift = 0 if j == 3 else (j - base) * width
        return source.at[layer, rows, pl.ds(pl.multiple_of(shift + wc * (width // 2), 128), width // 2)]

    def piece(t, z_at, y_at):
        return o_w.at[t, z_at, y_at, rows_of(t), columns]

    def send(src, dst, sems, peer):
        remote(src, dst, sems, peer).start()

    def arrived(ref, sems):
        pltpu.make_async_copy(ref, ref, sems.at[1]).wait()

    def left_here(ref, sems):
        pltpu.make_async_copy(ref, ref, sems.at[0]).wait()

    def all_left(t):
        left_here(o_w.at[t, pl.ds(0, LINE - 1), y, rows_of(t), columns], z_sems.at[t])
        left_here(piece(t, pl.ds(0, LINE), y), y_sems.at[t])
        if split(t):
            left_here(o_w.at[t, pl.ds(0, LINE - 1), y, rows_of(t), columns], xa_sems.at[t])
            left_here(piece(t, pl.ds(0, LINE), 1 - y), xb_sems.at[t])
        left_here(o_w.at[t, pl.ds(0, LINE), pl.ds(0, 2), pl.ds(0, depth), columns], c_sems.at[t])

    def own_copy(t):
        return pltpu.make_async_copy(
            shard(t, pl.ds(0, depth)), o_w.at[t, z, y, pl.ds(0, depth), columns], own_sems.at[t]
        )

    def open_chunk(t):
        own_copy(t).start()
        for peer in in_line:
            send(shard(t, rows_of(t)), piece(t, z, y), z_sems.at[t], peer)
        send(shard(t, rows_of(t)), piece(t, z, y), y_sems.at[t], across)

    def stage_a(t):
        arrived(o_w.at[t, pl.ds(0, LINE - 1), y, rows_of(t), columns], z_sems.at[t])
        for other in others:
            send(piece(t, other, y), piece(t, other, y), y_sems.at[t], across)
        if split(t):
            for other in others:
                send(piece(t, other, y), piece(t, other, y), xa_sems.at[t], vertical)

    def stage_b(t):
        beside = piece(t, pl.ds(0, LINE), 1 - y)
        arrived(beside, y_sems.at[t])
        if split(t):
            send(beside, beside, xb_sems.at[t], vertical)

    def stage_c(t):
        own_copy(t).wait()
        if split(t):
            rows = pl.ds(pl.multiple_of((1 - wr) * (depth // 2), 16), depth // 2)
            arrived(o_w.at[t, pl.ds(0, LINE - 1), y, rows, columns], xa_sems.at[t])
            arrived(o_w.at[t, pl.ds(0, LINE), 1 - y, rows, columns], xb_sems.at[t])
        half = o_w.at[t, pl.ds(0, LINE), pl.ds(0, 2), pl.ds(0, depth), columns]
        send(half, half, c_sems.at[t], horizontal)

    chunks = 24
    kinds = ("q", "q", "q", "p", "h", "h", "h", "h", "o", "o", "o", "o")
    busy = {"q": True, "p": True, "h": True, "o": True}
    landed, waiting = set(), []
    clock, opened = [0], [0]

    def load_of(t):
        j = t % 12
        if j < 3:
            dst = wq.at[:, :, :, pl.ds(j * width, width)]
        elif j < 4:
            dst = wp
        elif j < 8:
            dst = wh.at[:, :, :, pl.ds((j - 4) * width, width)]
        else:
            dst = wo.at[:, :, j - 8]
        return pltpu.make_async_copy(o_w.at[t], dst, load_sems.at[t])

    def stage_d(t):
        other = pl.ds(pl.multiple_of((1 - wc) * (width // 2), 128), width // 2)
        arrived(o_w.at[t, pl.ds(0, LINE), pl.ds(0, 2), pl.ds(0, depth), other], c_sems.at[t])
        if t < 12 or not busy[kinds[t % 12]]:
            load_of(t).start()
            landed.add(t)
        else:
            waiting.append(t)

    order = []
    for t in range(chunks):
        lags = LAGS_FIRST if t < FIRST else LAGS
        for stage, lag in zip((stage_a, stage_b, stage_c, stage_d), lags):
            order.append((t + lag, -lag, t, stage))
    order.sort(key=lambda entry: entry[:2])
    last_step = {t: max(step for step, _, u, _ in order if u == t) for t in range(chunks)}
    final_step = max(last_step.values())

    def advance(count):
        for _ in range(count):
            for step, _, t, stage in order:
                if step == clock[0]:
                    stage(t)
                    if stage is stage_a:
                        for ahead in range(max(opened[0], AHEAD), min(t + 1 + AHEAD, chunks)):
                            open_chunk(ahead)
                            opened[0] = ahead + 1
            clock[0] += 1

    def need(t):
        while clock[0] <= last_step[t]:
            advance(1)
        load_of(t).wait()

    def release(kind):
        busy[kind] = False
        for t in [t for t in waiting if kinds[t % 12] == kind]:
            load_of(t).start()
            landed.add(t)
            waiting.remove(t)

    for t in range(AHEAD):
        open_chunk(t)

    saves = {}

    def save(name, src, dst, s):
        saves[name] = pltpu.make_async_copy(src, dst, save_sems.at[s])
        saves[name].start()

    small_in[d] = small[...]
    fill_valid(valid, sizes, images, wr, wc)
    clear_borders(pad, images)

    def enter(p):
        rows = rows_at(p, PAIR)
        to_pad(pad, p, patches[rows, :].astype(F32) * spread(valid[rows, :], width))

    each(pairs, enter)
    advance(1)
    arrived(small_in.at[pl.ds(0, 2 * LINE - 1)], small_sems)
    unpack_small(small_in, vec, qbias, hbias)
    advance(1)

    def step():
        advance(1)

    def convolve(k, stream):
        halo(pad, images, wr, wc, row_out.at[k], row_in.at[k], col_out.at[k], col_in.at[k], halo_sems.at[k], vertical, horizontal, (step, step))
        conv_forward(pad, images, vec, k, valid, stream, left, right)
        advance(1)

    def columns_of(weights, at):
        block = weights[:, :, :, at]
        return block.reshape(width, block.shape[-1])

    def qkv(k, x):
        for part in range(3):
            need(12 * k + part)

            def tile(j):
                at = lanes_at(j, 256, part * width)
                packed[:, at] = (dot(x[...], columns_of(wq, at)) + qbias[k : k + 1, at]).astype(BF16)

            each(width // 256, tile)
            advance(1)
        release("q")

    def proj(k, stream, store):
        need(12 * k + 3)

        def tile(j):
            at = lanes_at(j, 256)
            pre[...] = dot(context[...], columns_of(wp, at))

            def part(p):
                rows = rows_at(p, PAIR)
                store(p, at, stream[rows, at] + spread(valid[rows, :], 256) * (pre[rows, :] + vec[38 + k : 39 + k, at]))

            each(pairs, part)

        each(width // 256, tile)
        advance(1)
        release("p")

    def feed_forward(k, x, stream, store):
        for block in range(4):
            need(12 * k + 4 + block)

            def tile(j):
                at = lanes_at(j, 256, block * width)
                pre[...] = dot(x[...], columns_of(wh, at))

                def part(p):
                    rows = rows_at(p, PAIR)
                    a, s = gelu_pair(pre[rows, :] + hbias[k : k + 1, at])
                    act[rows, at] = a.astype(BF16)
                    slope[rows, at] = s.astype(BF16)

                each(pairs, part)

            each(width // 256, tile)
            advance(1)
        release("h")
        for block in range(4):
            need(12 * k + 8 + block)

        def tile2(j):
            at = lanes_at(j, 256)
            block = wo[:, :, :, :, at]
            pre[...] = dot(act[...], block.reshape(hidden, 256))

            def part(p):
                rows = rows_at(p, PAIR)
                store(p, at, stream[rows, at] + spread(valid[rows, :], 256) * (pre[rows, :] + vec[40 + k : 41 + k, at]))

            each(pairs, part)

        for j in range(width // 256):
            tile2(j)
            advance(1)
        release("o")

    def into_pad(p, at, value):
        pad[pl.ds(pl.multiple_of((18 * p + 1) * 8, 8), CELLS), at] = value[:CELLS]
        pad[pl.ds(pl.multiple_of((18 * p + 10) * 8, 8), CELLS), at] = value[CELLS:]

    convolve(0, streams.at[0])
    save("pad0", pad, o_pad.at[0], 0)
    save("s1", streams.at[0], o_stream.at[0], 1)
    norm_rows(streams.at[0], images, vec, 0, normed.at[0])
    advance(1)
    save("n1", normed.at[0], o_normed.at[0], 2)
    qkv(0, normed.at[0])
    save("k1", packed, o_packed.at[0], 3)
    window_attention(packed, images, sizes, wr, wc, context, advance)
    save("c1", context, o_context.at[0], 4)
    saves["pad0"].wait()
    proj(0, streams.at[0], into_pad)
    convolve(1, streams.at[1])
    save("pad2", pad, o_pad.at[1], 0)
    save("s3", streams.at[1], o_stream.at[1], 5)
    norm_rows(streams.at[1], images, vec, 1, normed.at[1])
    advance(1)
    save("n3", normed.at[1], o_normed.at[1], 6)
    saves["pad2"].wait()
    feed_forward(0, normed.at[1], streams.at[1], into_pad)
    save("a0", act, o_act.at[0], 7)
    save("g0", slope, o_slope.at[0], 8)
    saves["s1"].wait()
    saves["n1"].wait()
    saves["k1"].wait()
    saves["c1"].wait()
    convolve(2, streams.at[0])
    save("pad4", pad, o_pad.at[2], 0)
    save("s5", streams.at[0], o_stream.at[2], 1)
    norm_rows(streams.at[0], images, vec, 2, normed.at[0])
    advance(1)
    save("n5", normed.at[0], o_normed.at[2], 2)
    qkv(1, normed.at[0])
    save("k5", packed, o_packed.at[1], 3)
    pair_grams(packed, 2 * width, packed, width, images, valid, gram)
    sum_windows(gram, gram_in, images, wc, gram_sems, vertical, horizontal, (step, step, step))

    def soften(i):
        rows = rows_at(i, 32)
        x = gram[rows, :] * SCALE
        e = jnp.exp(x - jnp.max(x, 0, keepdims=True))
        gram[rows, :] = e * (1.0 / jnp.sum(e, 0, keepdims=True))

    each(images, soften)
    save("mix", gram, o_mix, 9)

    def mix_pair(p):
        rows = rows_at(p, PAIR)
        one, two = image_halves(BF16)

        def load(g):
            at = lanes_at(g, 128)
            first = gram[pl.ds(pl.multiple_of(64 * p, 32), 32), at]
            second = gram[pl.ds(pl.multiple_of(64 * p + 32, 32), 32), at]
            return first, second, packed[rows, at]

        def compute(first, second, query):
            mixing = jnp.concatenate([unfold_heads(first), unfold_heads(second)], axis=0).astype(BF16)
            return dot(jnp.concatenate([query * one, query * two], axis=1), mixing).astype(BF16)

        def store(g, result):
            context[rows, lanes_at(g, 128)] = result

        each_few(width // 128, GROUPS, load, compute, store)

    each(pairs, mix_pair)
    save("c5", context, o_context.at[1], 4)
    saves["s3"].wait()
    saves["n3"].wait()

    def into_last(p, at, value):
        streams[1, rows_at(p, PAIR), at] = value

    proj(1, streams.at[0], into_last)
    save("s6", streams.at[1], o_stream.at[3], 5)
    norm_rows(streams.at[1], images, vec, 3, normed.at[1])
    advance(1)
    save("n6", normed.at[1], o_normed.at[3], 6)
    saves["a0"].wait()
    saves["g0"].wait()

    def into_final(p, at, value):
        final[rows_at(p, PAIR), at] = value.astype(BF16)

    feed_forward(1, normed.at[1], streams.at[1], into_final)
    save("a1", act, o_act.at[1], 7)
    save("g1", slope, o_slope.at[1], 8)
    save("end", final, activations, 10)
    advance(final_step + 1 - clock[0])
    for t in range(chunks):
        all_left(t)
    left_here(small_in.at[pl.ds(0, 2 * LINE - 1)], small_sems)
    for name in ("pad4", "s5", "n5", "k5", "mix", "c5", "s6", "n6", "a1", "g1", "end"):
        saves[name].wait()


ANY = pl.BlockSpec(memory_space=pl.ANY)
VMEM = pl.BlockSpec(memory_space=pltpu.VMEM)
SMEM = pl.BlockSpec(memory_space=pltpu.SMEM)


def run_forward(sizes, patches, small, shards):
    images = sizes.shape[0]
    n_rows, width = patches.shape
    hidden = shards[2].shape[2]
    lines = images * 72
    depth = shards[0].shape[1]
    shapes = (
        ((n_rows, width), BF16),
        ((24, LINE, 2, depth, width), BF16),
        ((ROWS_SMALL, width), F32),
        ((3, lines, width), F32),
        ((4, n_rows, width), F32),
        ((4, n_rows, width), BF16),
        ((2, n_rows, 3 * width), BF16),
        ((2, n_rows, width), BF16),
        ((2, n_rows, hidden), BF16),
        ((2, n_rows, hidden), BF16),
        ((images * 32, width), F32),
    )
    return pl.pallas_call(
        functools.partial(forward_kernel, images, width, hidden),
        out_shape=[jax.ShapeDtypeStruct(*s) for s in shapes],
        in_specs=[SMEM, VMEM, VMEM] + [ANY] * 4,
        out_specs=[ANY] * 2 + [VMEM] + [ANY] * 8,
        scratch_shapes=[
            pltpu.VMEM((lines, width), F32),
            pltpu.VMEM((2, n_rows, width), F32),
            pltpu.VMEM((2, n_rows, width), BF16),
            pltpu.VMEM((n_rows, 3 * width), BF16),
            pltpu.VMEM((n_rows, width), BF16),
            pltpu.VMEM((n_rows, hidden), BF16),
            pltpu.VMEM((n_rows, hidden), BF16),
            pltpu.VMEM((images * 32, width), F32),
            pltpu.VMEM((3, images * 16, width), F32),
            pltpu.VMEM((n_rows, 128), F32),
            pltpu.VMEM((n_rows, 256), F32),
            pltpu.VMEM((LINE, 2, depth, 3 * width), BF16),
            pltpu.VMEM((LINE, 2, depth, width), BF16),
            pltpu.VMEM((LINE, 2, depth, hidden), BF16),
            pltpu.VMEM((LINE, 2, 4, depth, width), BF16),
            pltpu.VMEM((3, images * 8, width), BF16),
            pltpu.VMEM((3, images * 8, width), BF16),
            pltpu.VMEM((3, images * 8, width), BF16),
            pltpu.VMEM((3, images * 8, width), BF16),
            pltpu.VMEM((n_rows, width), BF16),
            pltpu.SemaphoreType.DMA((3, 2, 2)),
            pltpu.SemaphoreType.DMA((3, 2)),
            pltpu.SemaphoreType.DMA((24,)),
            pltpu.SemaphoreType.DMA((11,)),
            pltpu.SemaphoreType.DMA((24, 2)),
            pltpu.SemaphoreType.DMA((24, 2)),
            pltpu.SemaphoreType.DMA((24, 2)),
            pltpu.SemaphoreType.DMA((24, 2)),
            pltpu.SemaphoreType.DMA((24, 2)),
            pltpu.SemaphoreType.DMA((24,)),
            pltpu.VMEM((2 * LINE, ROWS_SMALL, 128), BF16),
            pltpu.VMEM((8, 3 * width), F32),
            pltpu.VMEM((8, hidden), F32),
            pltpu.SemaphoreType.DMA((2,)),
        ],
        compiler_params=pltpu.CompilerParams(
            collective_id=0, has_side_effects=True, vmem_limit_bytes=58 * 2**20
        ),
    )(sizes, patches, small, *shards)


def column_sums(src, images, width, store):
    for part in range(src.shape[1] // width):
        at = pl.ds(part * width, width)

        def one(p, total):
            x = src[rows_at(p, PAIR), at].astype(F32)
            return total + jnp.sum(x.reshape(PAIR // 8, 8, width), axis=0)

        total = lax.fori_loop(0, images // 2, one, jnp.zeros((8, width), F32))
        store(at, jnp.sum(total, axis=0, keepdims=True))


def norm_back(stream, images, vec, k, grad_normed, grad, vecg):
    gain = vec[30 + k : 31 + k, :]
    width = stream.shape[1]

    def one(p, carry):
        rows = rows_at(p, PAIR)
        x = stream[rows, :]
        dn = grad_normed[rows, :]
        centered = x - jnp.mean(x, -1, keepdims=True)
        rstd = lax.rsqrt(jnp.mean(centered * centered, -1, keepdims=True) + EPS)
        xhat = centered * rstd
        scaled = dn * gain
        inner = jnp.mean(scaled * xhat, -1, keepdims=True)
        grad[rows, :] = grad[rows, :] + rstd * (scaled - jnp.mean(scaled, -1, keepdims=True) - xhat * inner)
        gains = jnp.sum((dn * xhat).reshape(PAIR // 8, 8, width), axis=0)
        shifts = jnp.sum(dn.reshape(PAIR // 8, 8, width), axis=0)
        return carry[0] + gains, carry[1] + shifts

    zero = jnp.zeros((8, width), F32)
    gains, shifts = lax.fori_loop(0, images // 2, one, (zero, zero))
    vecg[30 + k : 31 + k, :] = jnp.sum(gains, axis=0, keepdims=True)
    vecg[34 + k : 35 + k, :] = jnp.sum(shifts, axis=0, keepdims=True)


def conv_back(grad_pad, pad, images, vec, k, valid, grad, vecg, left, right):
    keep = jnp.where(iota((8, 128), 0) < 7, 1.0, 0.0).astype(F32)
    for part in range(pad.shape[1] // 128):
        at = pl.ds(part * 128, 128)
        taps = [vec[9 * k + t : 9 * k + t + 1, at] for t in range(9)]

        def one(i, sums):
            back = three(grad_pad, i, at, left, right)
            ahead = three(pad, i, at, left, right)
            sums = list(sums)
            for r in range(7):
                own = back[r + 1][1] * keep
                total = own
                for t in range(9):
                    total = total + taps[t] * back[r + 2 - t // 3][2 - t % 3]
                    sums[t] = sums[t] + own * ahead[r + t // 3][t % 3]
                sums[9] = sums[9] + own
                to = pl.ds(pl.multiple_of((7 * i + r) * 8, 8), 8)
                grad[to, at] = valid[to, :] * total
            return tuple(sums)

        sums = lax.fori_loop(0, images, one, tuple(jnp.zeros((8, 128), F32) for _ in range(10)))
        for t in range(9):
            vecg[9 * k + t : 9 * k + t + 1, at] = jnp.sum(sums[t], axis=0, keepdims=True)
        vecg[27 + k : 28 + k, at] = jnp.sum(sums[9], axis=0, keepdims=True)


def window_back(packed, images, sizes, wr, wc, grad_context, between):
    width = grad_context.shape[1]

    def pair(p):
        rows = rows_at(p, PAIR)
        allowed = jnp.concatenate([pair_mask(sizes, p, wr, wc).astype(F32)] * 4, axis=0) > 0.5
        low = head_masks(BF16)
        full = head_masks(F32)

        def load(g):
            return [packed[rows, lanes_at(g, 128, n * width)] for n in range(3)] + [grad_context[rows, lanes_at(g, 128)]]

        def compute(query, key, value, grad):
            query_bd = stacked(query, low)
            grad_bd = stacked(grad, low)
            probs = pair_probs(query_bd, key, allowed)
            grad_probs = dot_t(grad_bd, value)
            grad_value = t_dot(probs.astype(BF16), grad_bd).astype(BF16)
            inner = jnp.sum(probs * grad_probs, -1, keepdims=True)
            grad_scores = jnp.where(allowed, probs * (grad_probs - inner), 0.0).astype(BF16)
            grad_query = (folded(dot(grad_scores, key), full) * SCALE).astype(BF16)
            grad_key = (t_dot(grad_scores, query_bd) * SCALE).astype(BF16)
            return grad_query, grad_key, grad_value

        def store(g, result):
            for n in range(3):
                packed[rows, lanes_at(g, 128, n * width)] = result[n]

        each_few(width // 128, GROUPS, load, compute, store)

    for p in range(images // 2):
        pair(p)
        between(1)


def channel_back(packed, images, mix, grad_gram, valid, grad_context):
    width = grad_context.shape[1]

    def pair(p):
        rows = rows_at(p, PAIR)
        one, two = image_halves(BF16)
        ok = valid[rows, :] * SCALE
        first = pl.ds(pl.multiple_of(64 * p, 32), 32)
        second = pl.ds(pl.multiple_of(64 * p + 32, 32), 32)

        def both(ref, at, axis):
            return jnp.concatenate(
                [unfold_heads(ref[first, at]), unfold_heads(ref[second, at])], axis=axis
            ).astype(BF16)

        def split(value):
            return jnp.concatenate([value * one, value * two], axis=1)

        def load(g):
            at = lanes_at(g, 128)
            values = [packed[rows, lanes_at(g, 128, n * width)] for n in range(1, 3)]
            return values + [grad_context[rows, at], both(mix, at, 1), both(grad_gram, at, 0), both(grad_gram, at, 1)]

        def compute(key, value, grad, mixing, grad_tall, grad_wide):
            grad_query = dot_t(split(grad), mixing).astype(BF16)
            grad_key = (dot(split(value), grad_tall) * ok).astype(BF16)
            grad_value = (dot_t(split(key), grad_wide) * ok).astype(BF16)
            return grad_query, grad_key, grad_value

        def store(g, result):
            for n in range(3):
                packed[rows, lanes_at(g, 128, n * width)] = result[n]

        each_few(width // 128, GROUPS, load, compute, store)

    each(images // 2, pair)


ORDER = (20, 21, 22, 23, 16, 17, 18, 19, 15, 12, 13, 14, 8, 9, 10, 11, 4, 5, 6, 7, 3, 0, 1, 2)
RING = 4
AHEAD_SUMS = 1
HELD = 12
WAIT = 2


def backward_kernel(
    images,
    width,
    hidden,
    sizes,
    cotangent,
    vec,
    i_pad,
    i_stream,
    i_normed,
    i_packed,
    i_context,
    i_act,
    i_slope,
    i_mix,
    i_w,
    patches_grad,
    tiny,
    g_qkv,
    g_proj,
    g_hid,
    g_out,
    grad,
    grad_pad,
    pad,
    stream,
    normed,
    packed,
    context,
    act,
    slope,
    dn,
    branch,
    gram,
    mix,
    gram_in,
    valid,
    w_wide,
    w_tall,
    row_out,
    row_in,
    col_out,
    col_in,
    go_out,
    go_in,
    held,
    x_in,
    y_in,
    z_in,
    part,
    part_in,
    whole,
    whole_in,
    stage,
    halo_sems,
    gram_sems,
    load_sems,
    stage_sems,
    weight_sems,
    sums_sems,
    credits,
    vecg,
    qbg,
    hbg,
    small_out,
    small_in,
    small_sum,
    small_sems,
):
    d, w, wr, wc = place()
    depth = i_w.shape[3]
    pairs = images // 2
    horizontal = (d, 2 * wr + 1 - wc)
    vertical = (d, 2 * (1 - wr) + wc)
    z, y = d // 2, d % 2
    others = [lax.rem(z + k, LINE) for k in range(1, LINE)]
    in_line = [(2 * other + y, w) for other in others]
    across = (2 * z + 1 - y, w)
    alike = [(lax.rem(d + k, 2 * LINE), w) for k in range(1, 2 * LINE)]
    windows = [(d, lax.rem(w + k, 4)) for k in range(1, 4)]
    greet(alike + windows)
    vecg[...] = jnp.zeros(vecg.shape, F32)
    left, right = side_masks(wr, wc)
    loads = {}
    half = width // 2
    rows_mine = pl.ds(pl.multiple_of(wr * (depth // 2), 16), depth // 2)
    rows_other = pl.ds(pl.multiple_of((1 - wr) * (depth // 2), 16), depth // 2)
    cols_mine = pl.ds(pl.multiple_of(wc * half, 128), half)
    cols_other = pl.ds(pl.multiple_of((1 - wc) * half, 128), half)
    chunks = len(ORDER)
    halves = [n for n in range(chunks) if n % 2 == 0]

    def post(n, kind, src, dst, peer):
        copy = remote(src, dst, sums_sems.at[n, kind], peer)
        copy.start()

    def settle(n, kind, ref):
        pltpu.make_async_copy(ref, ref, sums_sems.at[n, kind, 1]).wait()
        pltpu.make_async_copy(ref, ref, sums_sems.at[n, kind, 0]).wait()

    def credit(n, kind, peer):
        if n + RING < chunks:
            pl.semaphore_signal(credits.at[kind], inc=1, device_id=peer, device_id_type=MESH)

    def take_credit(n, kind):
        if n >= RING:
            pl.semaphore_wait(credits.at[kind], 1)

    def open_sum(n):
        take_credit(n, 0)
        post(n, 0, go_out.at[n % RING], go_in.at[n % RING], horizontal)

    def sum_cores(n):
        s, h = n % RING, n % HELD
        settle(n, 0, go_in.at[s])

        def add(i):
            held[h, i // 2, i % 2] = held[h, i // 2, i % 2] + go_in[s, i // 2, i % 2]

        each(2 * LINE, add)
        credit(n, 0, horizontal)
        if n in halves:
            if n >= RING:
                pl.semaphore_wait(credits.at[1], 1)
            post(n, 1, held.at[h, :, :, rows_other], x_in.at[s], vertical)
        else:
            take_credit(n, 8)
            post(n, 2, held.at[h, :, 1 - y], y_in.at[s], across)

    def sum_x(n):
        if n not in halves:
            return
        s, h = n % RING, n % HELD
        settle(n, 1, x_in.at[s])

        def add(i):
            held[h, i // 2, i % 2, rows_mine] = held[h, i // 2, i % 2, rows_mine] + x_in[s, i // 2, i % 2]

        each(2 * LINE, add)
        credit(n, 1, vertical)
        take_credit(n, 2)
        post(n, 2, held.at[h, :, 1 - y, rows_mine], y_in.at[s, :, 0 : depth // 2], across)

    def share(n):
        return (rows_mine, depth // 2) if n in halves else (pl.ds(0, depth), depth)

    def sum_y(n):
        s, h = n % RING, n % HELD
        rows, count = share(n)
        settle(n, 2, y_in.at[s, :, 0:count])

        def add(i):
            held[h, i, y, rows] = held[h, i, y, rows] + y_in[s, i, 0:count]

        each(LINE, add)
        credit(n, 2 if n in halves else 8, across)
        for k in range(LINE - 1):
            take_credit(n, 3 + k)
        for k, (other, peer) in enumerate(zip(others, in_line)):
            post(n, 3, held.at[h, other, y, rows], z_in.at[s, LINE - 2 - k, 0:count], peer)

    def sum_z(n):
        s, h = n % RING, n % HELD
        rows, count = share(n)
        settle(n, 3, z_in.at[s, :, 0:count])
        total = held[h, z, y, rows].astype(F32)
        for k in range(LINE - 1):
            total = total + z_in[s, k, 0:count].astype(F32)
        part[s, rows] = total.astype(BF16)
        for k, peer in enumerate(in_line):
            credit(n, 3 + LINE - 2 - k, peer)
        take_credit(n, 6)
        post(n, 4, part.at[s, rows], part_in.at[s, rows], vertical)

    def sum_windows_x(n):
        s = n % RING
        if n in halves:
            settle(n, 4, part_in.at[s, rows_other])
            whole[s, rows_mine] = part[s, rows_mine]
            whole[s, rows_other] = part_in[s, rows_other]
        else:
            settle(n, 4, part_in.at[s])
            whole[s] = part[s] + part_in[s]
        credit(n, 6, vertical)
        take_credit(n, 7)
        post(n, 5, whole.at[s], whole_in.at[s], horizontal)

    def result_of(n):
        layer, j = ORDER[n] // 12, ORDER[n] % 12
        if j < 3:
            return g_qkv.at[layer, :, pl.ds(j * width, width)]
        if j < 4:
            return g_proj.at[layer]
        if j < 8:
            return g_hid.at[layer, :, pl.ds((j - 4) * width, width)]
        return g_out.at[layer, pl.ds((j - 8) * depth, depth)]

    def write_out(n):
        return pltpu.make_async_copy(stage.at[n % RING], result_of(n), stage_sems.at[n % RING])

    def finish(n):
        s = n % RING
        settle(n, 5, whole_in.at[s])
        if n >= RING:
            write_out(n - RING).wait()
        stage[s, :, cols_mine] = whole[s].astype(F32)
        stage[s, :, cols_other] = whole_in[s].astype(F32)
        credit(n, 7, horizontal)
        write_out(n).start()

    stages = (sum_cores, sum_x, sum_y, sum_z, sum_windows_x, finish)
    made, clock = [0], [0]

    def turn():
        for lag in reversed(range(len(stages))):
            n = clock[0] - lag * WAIT
            if 0 <= n < chunks:
                stages[lag](n)
        clock[0] += 1

    def pump(count):
        for _ in range(count):
            if clock[0] < made[0] - AHEAD_SUMS or (made[0] == chunks and clock[0] < chunks + len(stages) * WAIT):
                turn()

    def room(count):
        while made[0] + count > RING + clock[0] or made[0] + count - HELD > clock[0] - 3 * WAIT:
            turn()

    def opened(count):
        for n in range(made[0], made[0] + count):
            open_sum(n)
        made[0] += count

    def pair_of_halves(dy, base):
        theirs = dy[:, pl.ds(pl.multiple_of(base + (1 - wc) * half, 128), half)]
        ours = dy[:, pl.ds(pl.multiple_of(base + wc * half, 128), half)]
        return jnp.concatenate([theirs, ours], axis=1)

    def weight_grad(x, dy):
        for j in range(dy.shape[1] // width):
            room(1)
            s, h = made[0] % RING, made[0] % HELD

            def tile(q):
                both = t_dot(x[:, lanes_at(q, 4 * depth)], pair_of_halves(dy, j * width)).astype(BF16)
                go_out[s, rows_at(q, 2)] = both[:, :half].reshape(2, 2, depth, half)
                held[h, rows_at(q, 2)] = both[:, half:].reshape(2, 2, depth, half)

            each(LINE // 2, tile)
            opened(1)
            pump(1)

    def tall_weight_grad(x, dy):
        room(4)
        slots = [(n % RING, n % HELD) for n in range(made[0], made[0] + 4)]

        def tile(i):
            both = t_dot(x[:, lanes_at(i, 4 * depth)], pair_of_halves(dy, 0)).astype(BF16)
            for j, (s, h) in enumerate(slots):
                block = both[j * depth : (j + 1) * depth]
                go_out[s, i // 2, i % 2] = block[:, :half]
                held[h, i // 2, i % 2] = block[:, half:]

        each(2 * LINE, tile)
        opened(4)
        pump(1)

    def load(name, src, dst, s):
        loads[name] = pltpu.make_async_copy(src, dst, load_sems.at[s])
        loads[name].start()

    def load_weights(t):
        j = t % 12
        if j < 3:
            dst = w_wide.at[:, :, :, pl.ds(j * width, width)]
        elif j < 4:
            dst = w_tall.at[:, :, 0]
        elif j < 8:
            dst = w_wide.at[:, :, :, pl.ds((j - 4) * width, width)]
        else:
            dst = w_tall.at[:, :, j - 8]
        return pltpu.make_async_copy(i_w.at[t], dst, weight_sems.at[t])

    def chunks_of(name):
        first = {"wq": 0, "wp": 3, "wh": 4, "wo": 8}[name[:2]] + 12 * int(name[2])
        return range(first, first + {"wq": 3, "wp": 1, "wh": 4, "wo": 4}[name[:2]])

    def fetch(name):
        for t in chunks_of(name):
            load_weights(t).start()

    def fetched(name):
        for t in chunks_of(name):
            load_weights(t).wait()

    load("cotangent", cotangent, branch, 1)
    load("act", i_act.at[1], act, 0)
    fetch("wo1")
    load("slope", i_slope.at[1], slope, 2)
    fetch("wh1")
    load("normed", i_normed.at[3], normed, 4)
    load("stream", i_stream.at[3], stream, 5)
    load("context", i_context.at[1], context, 6)
    load("packed", i_packed.at[1], packed, 7)
    load("mix", i_mix, mix, 8)
    load("pad", i_pad.at[2], pad, 9)
    fill_valid(valid, sizes, images, wr, wc)
    clear_borders(grad_pad, images)

    loads["cotangent"].wait()

    def enter(p):
        rows = rows_at(p, PAIR)
        grad[rows, :] = branch[rows, :].astype(F32) * spread(valid[rows, :], width)

    each(pairs, enter)

    def make_branch(row):
        def one(p):
            rows = rows_at(p, PAIR)
            branch[rows, :] = (grad[rows, :] * spread(valid[rows, :], width)).astype(BF16)

        each(pairs, one)

        def store(at, total):
            vecg[row : row + 1, at] = total

        column_sums(branch, images, 256, store)

    def feed_forward(k):
        make_branch(40 + k)
        loads["act"].wait()
        tall_weight_grad(act, branch)
        fetched(f"wo{k}")
        loads["slope"].wait()

        def tile(j):
            at = lanes_at(j, 4 * depth)
            dact = dot_t(branch[...], w_tall[j // 2, j % 2].reshape(4 * depth, width))
            slope[:, at] = (slope[:, at].astype(F32) * dact).astype(BF16)

        each(2 * LINE, tile)
        pump(1)

        def store(at, total):
            hbg[k : k + 1, at] = total

        column_sums(slope, images, 256, store)
        fetched(f"wh{k}")

        def tile2(j):
            block = w_wide[rows_at(j, 2)].reshape(4 * depth, hidden)
            dn[:, lanes_at(j, 4 * depth)] = dot_t(slope[...], block)

        each(LINE // 2, tile2)
        pump(1)
        loads["stream"].wait()
        norm_back(stream, images, vec, 1 + 2 * k, dn, grad, vecg)

    def hidden_grad():
        loads["normed"].wait()
        weight_grad(normed, slope)

    def proj_grad():
        loads["context"].wait()
        weight_grad(context, branch)

    def qkv_grad():
        loads["normed"].wait()
        weight_grad(normed, packed)

    grad_context = act.at[:, pl.ds(0, width)]

    def proj(k):
        make_branch(38 + k)
        fetched(f"wp{k}")

        def tile(j):
            block = w_tall[rows_at(j, 2), :, 0].reshape(4 * depth, width)
            grad_context[:, lanes_at(j, 4 * depth)] = dot_t(branch[...], block).astype(BF16)

        each(LINE // 2, tile)

    def qkv(k):
        def store(at, total):
            qbg[k : k + 1, at] = total

        column_sums(packed, images, 256, store)
        fetched(f"wq{k}")

        def tile(j):
            block = w_wide[rows_at(j, 2), :, :, 0 : 3 * width].reshape(4 * depth, 3 * width)
            dn[:, lanes_at(j, 4 * depth)] = dot_t(packed[...], block)

        each(LINE // 2, tile)
        loads["stream"].wait()
        norm_back(stream, images, vec, 2 * k, dn, grad, vecg)

    def convolve(k, *flights):
        def enter_pad(p):
            to_pad(grad_pad, p, grad[rows_at(p, PAIR), :])

        each(pairs, enter_pad)
        halo(grad_pad, images, wr, wc, row_out.at[k], row_in.at[k], col_out.at[k], col_in.at[k], halo_sems.at[k], vertical, horizontal, flights)
        loads["pad"].wait()
        conv_back(grad_pad, pad, images, vec, k, valid, grad, vecg, left, right)

    def idle():
        pump(1)

    feed_forward(1)
    fetch("wp1")
    fetch("wq1")
    load("stream", i_stream.at[2], stream, 5)
    proj(1)
    fetch("wo0")
    loads["packed"].wait()
    pair_grams(packed, 0, grad_context, 0, images, valid, gram)

    def beside():
        hidden_grad()
        proj_grad()

    sum_windows(gram, gram_in, images, wc, gram_sems, vertical, horizontal, (idle, beside, idle))
    load("slope", i_slope.at[0], slope, 2)
    load("normed", i_normed.at[2], normed, 4)
    load("context", i_context.at[0], context, 6)
    loads["mix"].wait()

    def harden(i):
        rows = rows_at(i, 32)
        y, g = mix[rows, :], gram[rows, :]
        gram[rows, :] = y * (g - jnp.sum(y * g, 0, keepdims=True))

    each(images, harden)
    channel_back(packed, images, mix, gram, valid, grad_context)
    load("act", i_act.at[0], act, 0)
    qkv(1)
    fetch("wh0")
    load("stream", i_stream.at[1], stream, 5)
    convolve(2, qkv_grad, idle)
    load("pad", i_pad.at[1], pad, 9)
    load("packed", i_packed.at[0], packed, 7)
    load("normed", i_normed.at[1], normed, 4)
    feed_forward(0)
    fetch("wp0")
    fetch("wq0")
    load("stream", i_stream.at[0], stream, 5)
    convolve(1, hidden_grad, idle)
    load("pad", i_pad.at[0], pad, 9)
    load("normed", i_normed.at[0], normed, 4)
    proj(0)
    proj_grad()
    loads["packed"].wait()
    window_back(packed, images, sizes, wr, wc, grad_context, pump)
    qkv_grad()
    qkv(0)
    convolve(0, idle, idle)

    def leave(p):
        rows = rows_at(p, PAIR)
        branch[rows, :] = grad[rows, :].astype(BF16)

    each(pairs, leave)
    load("end", branch, patches_grad, 1)
    pack_small(vecg, qbg, hbg, small_out)
    small_in[d] = small_out[d]
    for peer in alike:
        remote(small_out.at[peer[0]], small_in.at[d], small_sems.at[0], peer).start()
    while clock[0] < chunks + len(stages) * WAIT:
        turn()
    for n in (1, 0):
        seven = small_in.at[pl.ds(0, 2 * LINE - 1)]
        pltpu.make_async_copy(seven, seven, small_sems.at[0, n]).wait()
    total = small_in[0]
    for k in range(1, 2 * LINE):
        total = total + small_in[k]
    small_sum[w] = total
    for peer in windows:
        remote(small_sum.at[w], small_sum.at[w], small_sems.at[1], peer).start()
    for n in (1, 0):
        three_of = small_sum.at[pl.ds(0, 3)]
        pltpu.make_async_copy(three_of, three_of, small_sems.at[1, n]).wait()
    tiny[...] = ((small_sum[0] + small_sum[1]) + small_sum[2]) + small_sum[3]
    for n in range(chunks - RING, chunks):
        write_out(n).wait()
    loads["end"].wait()


def run_backward(sizes, cotangent, vec, saved, weights, hidden):
    images = sizes.shape[0]
    depth = weights.shape[3]
    n_rows, width = cotangent.shape
    lines = images * 72
    shapes = (
        ((n_rows, width), BF16),
        ((ROWS_SMALL, 128), F32),
        ((2, depth, 3 * width), F32),
        ((2, depth, width), F32),
        ((2, depth, hidden), F32),
        ((2, 4 * depth, width), F32),
    )
    half = width // 2
    return pl.pallas_call(
        functools.partial(backward_kernel, images, width, hidden),
        out_shape=[jax.ShapeDtypeStruct(*s) for s in shapes],
        in_specs=[SMEM, ANY, VMEM] + [ANY] * 9,
        out_specs=[ANY, VMEM] + [ANY] * 4,
        scratch_shapes=[
            pltpu.VMEM((n_rows, width), F32),
            pltpu.VMEM((lines, width), F32),
            pltpu.VMEM((lines, width), F32),
            pltpu.VMEM((n_rows, width), F32),
            pltpu.VMEM((n_rows, width), BF16),
            pltpu.VMEM((n_rows, 3 * width), BF16),
            pltpu.VMEM((n_rows, width), BF16),
            pltpu.VMEM((n_rows, hidden), BF16),
            pltpu.VMEM((n_rows, hidden), BF16),
            pltpu.VMEM((n_rows, width), F32),
            pltpu.VMEM((n_rows, width), BF16),
            pltpu.VMEM((images * 32, width), F32),
            pltpu.VMEM((images * 32, width), F32),
            pltpu.VMEM((3, images * 16, width), F32),
            pltpu.VMEM((n_rows, 128), F32),
            pltpu.VMEM((LINE, 2, depth, hidden), BF16),
            pltpu.VMEM((LINE, 2, 4, depth, width), BF16),
            pltpu.VMEM((3, images * 8, width), BF16),
            pltpu.VMEM((3, images * 8, width), BF16),
            pltpu.VMEM((3, images * 8, width), BF16),
            pltpu.VMEM((3, images * 8, width), BF16),
            pltpu.VMEM((RING, LINE, 2, depth, half), BF16),
            pltpu.VMEM((RING, LINE, 2, depth, half), BF16),
            pltpu.VMEM((HELD, LINE, 2, depth, half), BF16),
            pltpu.VMEM((RING, LINE, 2, depth // 2, half), BF16),
            pltpu.VMEM((RING, LINE, depth, half), BF16),
            pltpu.VMEM((RING, LINE - 1, depth, half), BF16),
            pltpu.VMEM((RING, depth, half), BF16),
            pltpu.VMEM((RING, depth, half), BF16),
            pltpu.VMEM((RING, depth, half), BF16),
            pltpu.VMEM((RING, depth, half), BF16),
            pltpu.VMEM((RING, depth, width), F32),
            pltpu.SemaphoreType.DMA((3, 2, 2)),
            pltpu.SemaphoreType.DMA((3, 2)),
            pltpu.SemaphoreType.DMA((10,)),
            pltpu.SemaphoreType.DMA((RING,)),
            pltpu.SemaphoreType.DMA((24,)),
            pltpu.SemaphoreType.DMA((24, 6, 2)),
            pltpu.SemaphoreType.REGULAR((9,)),
            pltpu.VMEM((48, width), F32),
            pltpu.VMEM((8, 3 * width), F32),
            pltpu.VMEM((8, hidden), F32),
            pltpu.VMEM((2 * LINE, ROWS_SMALL, 128), F32),
            pltpu.VMEM((2 * LINE, ROWS_SMALL, 128), F32),
            pltpu.VMEM((4, ROWS_SMALL, 128), F32),
            pltpu.SemaphoreType.DMA((2, 2)),
        ],
        compiler_params=pltpu.CompilerParams(
            collective_id=1, has_side_effects=True, vmem_limit_bytes=60 * 2**20
        ),
    )(sizes, cotangent, vec, *saved, weights)


def to_cells(windows):
    images, _, _, width = windows.shape
    grid = windows.reshape(images, 7, 7, width)
    return jnp.pad(grid, ((0, 0), (0, 0), (0, 1), (0, 0))).reshape(images * CELLS, width)


def of_cells(rows, images):
    width = rows.shape[1]
    return rows.reshape(images, 7, 8, width)[:, :, :7].reshape(images, 1, 49, width)


def on_device_fast(
    patches,
    cotangent,
    grid_sizes,
    conv_weight,
    conv_bias,
    norm_gain,
    norm_bias,
    qkv_weight,
    spatial_bias,
    channel_bias,
    proj_weight,
    proj_bias,
    hidden_weight,
    hidden_bias,
    output_weight,
    output_bias,
):
    images = patches.shape[0]
    hidden = hidden_weight.shape[2]
    small = (
        conv_weight, conv_bias, norm_gain, norm_bias, proj_bias, output_bias, spatial_bias, channel_bias, hidden_bias
    )
    rows = jnp.concatenate([a.reshape(-1, SHORT) for a in small], axis=0)
    rows = jnp.pad(rows, ((0, ROWS_SMALL - rows.shape[0]), (0, 128 - SHORT)))
    weights = (qkv_weight, proj_weight, hidden_weight, output_weight)
    forward = run_forward(grid_sizes, to_cells(patches), rows, weights)
    activations, gathered_weights, vec, *saved = forward
    back = run_backward(grid_sizes, to_cells(cotangent), vec, saved, gathered_weights, hidden)
    grads, tiny, g_qkv, g_proj, g_hid, g_out = back
    tiny = tiny[:, :SHORT]
    return (
        of_cells(activations, images),
        of_cells(grads, images),
        tiny[:27].reshape(3, 9, SHORT),
        tiny[27:30],
        tiny[30:34],
        tiny[34:38],
        g_qkv,
        tiny[42:44].reshape(-1),
        tiny[44:47].reshape(-1),
        g_proj,
        tiny[38:40],
        g_hid,
        tiny[47:55].reshape(2, -1),
        g_out,
        tiny[40:42],
    )


def as_sent(array):
    return jax.tree.map(lambda a: a.astype(jnp.bfloat16) if a.dtype == jnp.float32 else a, array)


def image_valid(grid_sizes):
    rows = jnp.arange(7, dtype=jnp.int32)
    windows = jnp.arange(4, dtype=jnp.int32)
    top_rows = (windows // 2)[:, None] * 7 + rows[None, :]
    left_cols = (windows % 2)[:, None] * 7 + rows[None, :]
    sizes = grid_sizes[:, None, None, None]
    inside = (top_rows[None, :, :, None] < sizes) & (left_cols[None, :, None, :] < sizes)
    return inside.astype(jnp.float32).reshape(grid_sizes.shape[0], 4, 49, 1)


def layer_norm(stream, gain_row, shift_row):
    centre = jnp.mean(stream, -1, keepdims=True)
    centered = stream - centre
    variance = jnp.mean(centered * centered, -1, keepdims=True)
    return centered * lax.rsqrt(variance + EPS) * gain_row + shift_row


def gelu_exact(value_in):
    return jax.nn.gelu(value_in, approximate=False)


def matmul(left_rows, right_mat):
    return jnp.dot(left_rows, right_mat, preferred_element_type=jnp.float32)


def contract_rows(left_rows, right_rows):
    return lax.dot_general(
        left_rows, right_rows, (((0,), (0,)), ((), ())), preferred_element_type=jnp.float32
    )


def times_transposed(grad_rows, weight):
    return lax.dot_general(
        grad_rows, weight, (((1,), (1,)), ((), ())), preferred_element_type=jnp.float32
    )


def edge_lines(stream, images):
    channels = stream.shape[-1]
    image_grid = stream.reshape(images, 7, 7, channels)
    return jnp.stack(
        [image_grid[:, 0], image_grid[:, 6], image_grid[:, :, 0], image_grid[:, :, 6]], 1
    )[None]


def padded_tile(image_grid, lines, row_half, col_half):
    zero_line = jnp.zeros_like(lines[0, :, 0])
    upper = jnp.where(
        row_half == 1, jnp.where(col_half == 0, lines[0, :, 1], lines[1, :, 1]), zero_line
    )
    lower = jnp.where(
        row_half == 0, jnp.where(col_half == 0, lines[2, :, 0], lines[3, :, 0]), zero_line
    )
    left_side = jnp.where(
        col_half == 1, jnp.where(row_half == 0, lines[0, :, 3], lines[2, :, 3]), zero_line
    )
    right_side = jnp.where(
        col_half == 0, jnp.where(row_half == 0, lines[1, :, 2], lines[3, :, 2]), zero_line
    )
    zero_cell = zero_line[:, 0]
    top_left = jnp.where((row_half == 1) & (col_half == 1), lines[0, :, 1, 6], zero_cell)
    top_right = jnp.where((row_half == 1) & (col_half == 0), lines[1, :, 1, 0], zero_cell)
    bottom_left = jnp.where((row_half == 0) & (col_half == 1), lines[2, :, 0, 6], zero_cell)
    bottom_right = jnp.where((row_half == 0) & (col_half == 0), lines[3, :, 0, 0], zero_cell)
    middle = jnp.concatenate([left_side[:, :, None], image_grid, right_side[:, :, None]], 2)
    top_row = jnp.concatenate([top_left[:, None], upper, top_right[:, None]], 1)
    bottom_row = jnp.concatenate([bottom_left[:, None], lower, bottom_right[:, None]], 1)
    return jnp.concatenate([top_row[:, None], middle, bottom_row[:, None]], 1)


def position_conv(stream, images, window, weight9, shift_row, valid_rows):
    channels = stream.shape[-1]
    lines = lax.all_gather(as_sent(edge_lines(stream, images)), "win", axis=0, tiled=True)
    padded = padded_tile(stream.reshape(images, 7, 7, channels), lines, window // 2, window % 2)
    summed = jnp.zeros((images, 7, 7, channels), jnp.float32)
    for tap_index in range(9):
        row_shift, col_shift = divmod(tap_index, 3)
        summed = (
            summed
            + weight9[tap_index] * padded[:, row_shift : row_shift + 7, col_shift : col_shift + 7]
        )
    return (stream + valid_rows * (summed + shift_row).reshape(images * 49, channels), padded)


def position_conv_back(grad_stream, padded, images, window, weight9, valid_rows):
    channels = grad_stream.shape[-1]
    masked = valid_rows * grad_stream
    lines = lax.all_gather(as_sent(edge_lines(masked, images)), "win", axis=0, tiled=True)
    image_grid = masked.reshape(images, 7, 7, channels)
    grad_pad = padded_tile(image_grid, lines, window // 2, window % 2)
    summed = jnp.zeros((images, 7, 7, channels), jnp.float32)
    tap_grads = []
    for tap_index in range(9):
        row_shift, col_shift = divmod(tap_index, 3)
        summed = (
            summed
            + weight9[tap_index]
            * grad_pad[:, 2 - row_shift : 9 - row_shift, 2 - col_shift : 9 - col_shift]
        )
        tap_grads.append(
            jnp.sum(
                image_grid * padded[:, row_shift : row_shift + 7, col_shift : col_shift + 7],
                axis=(0, 1, 2),
            )
        )
    return (
        grad_stream + summed.reshape(grad_stream.shape),
        jnp.stack(tap_grads),
        jnp.sum(image_grid, axis=(0, 1, 2)),
    )


def mlp_forward(normed, weight_in, bias_in, weight_out, bias_out):
    activated = gelu_exact(matmul(normed, weight_in) + bias_in).astype(jnp.bfloat16)
    return matmul(activated, weight_out) + bias_out


def mlp_backward(normed, grad_stream, valid_rows, weight_in, bias_in, weight_out):
    hidden_pre = matmul(normed, weight_in) + bias_in
    activated, gelu_pull = jax.vjp(gelu_exact, hidden_pre)
    grad_branch = (valid_rows * grad_stream).astype(jnp.bfloat16)
    grad_weight_out = contract_rows(activated.astype(jnp.bfloat16), grad_branch)
    grad_bias_out = jnp.sum(grad_branch.astype(jnp.float32), 0)
    grad_pre = gelu_pull(times_transposed(grad_branch, weight_out))[0].astype(jnp.bfloat16)
    grad_weight_in = contract_rows(normed, grad_pre)
    grad_bias_in = jnp.sum(grad_pre.astype(jnp.float32), 0)
    return (
        times_transposed(grad_pre, weight_in),
        grad_weight_in,
        grad_bias_in,
        grad_weight_out,
        grad_bias_out,
    )


def norm_backward(stream, gain_row, shift_row, grad_normed):
    unused, norm_pull = jax.vjp(layer_norm, stream, gain_row, shift_row)
    return norm_pull(grad_normed)


def window_probs(packed, images, scaling, valid_rows):
    split = packed.reshape(images, 49, 3, HEADS, HEAD)
    query_rows = split[:, :, 0]
    key_rows = split[:, :, 1]
    value_rows = split[:, :, 2]
    key_ok = valid_rows.reshape(images, 1, 1, 49) > 0.5
    scores = (
        jnp.einsum("iphe,iqhe->ihpq", query_rows, key_rows, preferred_element_type=jnp.float32)
        * scaling
    )
    scores = jnp.where(key_ok, scores, -1000000000.0)
    return (query_rows, key_rows, value_rows, jax.nn.softmax(scores, axis=-1))


def channel_mixing(gram_total, scaling):
    return jax.nn.softmax(gram_total * scaling, axis=-1)


def channel_grads(
    grad_mixing, mixing, grad_context, key_masked, value_masked, valid_cells, scaling
):
    grad_query = jnp.einsum(
        "bgcd,bpgc->bpgd",
        mixing.astype(jnp.bfloat16),
        grad_context,
        preferred_element_type=jnp.float32,
    )
    grad_gram = (mixing * (grad_mixing - jnp.sum(mixing * grad_mixing, -1, keepdims=True))).astype(
        jnp.bfloat16
    )
    grad_keys = (
        jnp.einsum("bgcd,bpgd->bpgc", grad_gram, value_masked, preferred_element_type=jnp.float32)
        * scaling
        * valid_cells
    )
    grad_values = (
        jnp.einsum("bgcd,bpgc->bpgd", grad_gram, key_masked, preferred_element_type=jnp.float32)
        * scaling
        * valid_cells
    )
    return jnp.stack([grad_query, grad_keys, grad_values], 2).astype(jnp.bfloat16)


def on_device(
    patches,
    cotangent,
    grid_sizes,
    conv_weight,
    conv_bias,
    norm_gain,
    norm_bias,
    qkv_weight,
    spatial_bias,
    channel_bias,
    proj_weight,
    proj_bias,
    hidden_weight,
    hidden_bias,
    output_weight,
    output_bias,
):
    (
        conv_w,
        conv_b,
        gains,
        shifts,
        qkv_w,
        sp_bias,
        ch_bias,
        proj_w,
        proj_b,
        hid_w,
        hid_b,
        out_w,
        out_b,
    ) = (
        lax.all_gather(conv_weight, "dp", axis=2, tiled=True),
        lax.all_gather(conv_bias, "dp", axis=1, tiled=True),
        lax.all_gather(norm_gain, "dp", axis=1, tiled=True),
        lax.all_gather(norm_bias, "dp", axis=1, tiled=True),
        lax.all_gather(qkv_weight, "dp", axis=1, tiled=True),
        lax.all_gather(spatial_bias, "dp", axis=0, tiled=True),
        lax.all_gather(channel_bias, "dp", axis=0, tiled=True),
        lax.all_gather(proj_weight, "dp", axis=1, tiled=True),
        lax.all_gather(proj_bias, "dp", axis=1, tiled=True),
        lax.all_gather(hidden_weight, "dp", axis=1, tiled=True),
        lax.all_gather(hidden_bias, "dp", axis=1, tiled=True),
        lax.all_gather(output_weight, "dp", axis=1, tiled=True),
        lax.all_gather(output_bias, "dp", axis=1, tiled=True),
    )
    conv_w = conv_w.astype(jnp.float32)
    conv_b = conv_b.astype(jnp.float32)
    gains = gains.astype(jnp.float32)
    shifts = shifts.astype(jnp.float32)
    sp_bias = sp_bias.astype(jnp.float32)
    ch_bias = ch_bias.astype(jnp.float32)
    proj_b = proj_b.astype(jnp.float32)
    hid_b = hid_b.astype(jnp.float32)
    out_b = out_b.astype(jnp.float32)
    images = patches.shape[0]
    model_width = patches.shape[-1]
    rows_all = images * 49
    group_count = lax.axis_size("win")
    local_heads = HEADS // group_count
    group_width = model_width // group_count
    scaling = HEAD ** (-0.5)
    window = lax.axis_index("win")
    full_valid = image_valid(grid_sizes)
    valid_rows = lax.dynamic_slice_in_dim(full_valid, window, 1, 1).reshape(rows_all, 1)
    stream0 = patches.astype(jnp.float32).reshape(rows_all, model_width) * valid_rows
    stream1, pad_first = position_conv(stream0, images, window, conv_w[0], conv_b[0], valid_rows)
    normed1 = layer_norm(stream1, gains[0], shifts[0]).astype(jnp.bfloat16)
    packed_bias = jnp.concatenate(
        [sp_bias[:model_width], jnp.zeros((model_width,), jnp.float32), sp_bias[model_width:]]
    )
    packed1 = (matmul(normed1, qkv_w[0]) + packed_bias).astype(jnp.bfloat16)
    query1, keys1, values1, probs1 = window_probs(packed1, images, scaling, valid_rows)
    context1 = (
        jnp.einsum(
            "ihpq,iqhe->iphe",
            probs1.astype(jnp.bfloat16),
            values1,
            preferred_element_type=jnp.float32,
        )
        .astype(jnp.bfloat16)
        .reshape(rows_all, model_width)
    )
    stream2 = stream1 + valid_rows * (matmul(context1, proj_w[0]) + proj_b[0])
    stream3, pad_second = position_conv(stream2, images, window, conv_w[1], conv_b[1], valid_rows)
    normed3 = layer_norm(stream3, gains[1], shifts[1]).astype(jnp.bfloat16)
    stream4 = stream3 + valid_rows * mlp_forward(normed3, hid_w[0], hid_b[0], out_w[0], out_b[0])
    stream5, pad_third = position_conv(stream4, images, window, conv_w[2], conv_b[2], valid_rows)
    normed5 = layer_norm(stream5, gains[2], shifts[2]).astype(jnp.bfloat16)
    packed5 = (matmul(normed5, qkv_w[1]) + ch_bias).astype(jnp.bfloat16)
    moved = lax.all_to_all(
        packed5.reshape(images, 1, 49, 3, group_count, group_width),
        "win",
        split_axis=4,
        concat_axis=1,
        tiled=True,
    )
    grouped = moved.reshape(images, 196, 3, local_heads, HEAD)
    valid_cells = full_valid.reshape(images, 196, 1, 1)
    query5 = grouped[:, :, 0]
    key_masked = grouped[:, :, 1] * valid_cells.astype(jnp.bfloat16)
    value_masked = grouped[:, :, 2] * valid_cells.astype(jnp.bfloat16)
    gram_total = jnp.einsum(
        "bpgc,bpgd->bgcd", key_masked, value_masked, preferred_element_type=jnp.float32
    )
    mixing = channel_mixing(gram_total, scaling)
    context_groups = jnp.einsum(
        "bgcd,bpgd->bpgc", mixing.astype(jnp.bfloat16), query5, preferred_element_type=jnp.float32
    ).astype(jnp.bfloat16)
    returned = lax.all_to_all(
        context_groups.reshape(images, 4, 49, 1, group_width),
        "win",
        split_axis=1,
        concat_axis=3,
        tiled=True,
    )
    context5 = returned.reshape(rows_all, model_width)
    stream6 = stream5 + valid_rows * (matmul(context5, proj_w[1]) + proj_b[1])
    normed6 = layer_norm(stream6, gains[3], shifts[3]).astype(jnp.bfloat16)
    stream7 = stream6 + valid_rows * mlp_forward(normed6, hid_w[1], hid_b[1], out_w[1], out_b[1])
    activations = stream7.astype(jnp.bfloat16).reshape(patches.shape)
    grad7 = cotangent.astype(jnp.float32).reshape(rows_all, model_width)
    grad_normed, hid_w_grad1, hid_b_grad1, out_w_grad1, out_b_grad1 = mlp_backward(
        normed6, grad7, valid_rows, hid_w[1], hid_b[1], out_w[1]
    )
    grad_part, gain_grad3, shift_grad3 = norm_backward(stream6, gains[3], shifts[3], grad_normed)
    grad6 = grad7 + grad_part
    branch_grad = (valid_rows * grad6).astype(jnp.bfloat16)
    proj_w_grad1 = contract_rows(context5, branch_grad)
    proj_b_grad1 = jnp.sum(branch_grad.astype(jnp.float32), 0)
    context_grad = times_transposed(branch_grad, proj_w[1]).astype(jnp.bfloat16)
    moved_grad = lax.all_to_all(
        context_grad.reshape(images, 1, 49, group_count, group_width),
        "win",
        split_axis=3,
        concat_axis=1,
        tiled=True,
    )
    group_grad = moved_grad.reshape(images, 196, local_heads, HEAD)
    mixing_grad = jnp.einsum(
        "bpgc,bpgd->bgcd", group_grad, query5, preferred_element_type=jnp.float32
    )
    stacked = channel_grads(
        mixing_grad, mixing, group_grad, key_masked, value_masked, valid_cells, scaling
    )
    sent_back = lax.all_to_all(
        stacked.reshape(images, 4, 49, 3, 1, group_width),
        "win",
        split_axis=1,
        concat_axis=4,
        tiled=True,
    )
    packed_grad5 = sent_back.reshape(rows_all, 3 * model_width)
    qkv_w_grad1 = contract_rows(normed5, packed_grad5)
    ch_bias_grad = jnp.sum(packed_grad5.astype(jnp.float32), 0)
    grad_part, gain_grad2, shift_grad2 = norm_backward(
        stream5, gains[2], shifts[2], times_transposed(packed_grad5, qkv_w[1])
    )
    grad5 = grad6 + grad_part
    grad4, conv_w_grad2, conv_b_grad2 = position_conv_back(
        grad5, pad_third, images, window, conv_w[2], valid_rows
    )
    grad_normed, hid_w_grad0, hid_b_grad0, out_w_grad0, out_b_grad0 = mlp_backward(
        normed3, grad4, valid_rows, hid_w[0], hid_b[0], out_w[0]
    )
    grad_part, gain_grad1, shift_grad1 = norm_backward(stream3, gains[1], shifts[1], grad_normed)
    grad3 = grad4 + grad_part
    grad2, conv_w_grad1, conv_b_grad1 = position_conv_back(
        grad3, pad_second, images, window, conv_w[1], valid_rows
    )
    branch_grad = (valid_rows * grad2).astype(jnp.bfloat16)
    proj_w_grad0 = contract_rows(context1, branch_grad)
    proj_b_grad0 = jnp.sum(branch_grad.astype(jnp.float32), 0)
    context_grad = (
        times_transposed(branch_grad, proj_w[0])
        .astype(jnp.bfloat16)
        .reshape(images, 49, HEADS, HEAD)
    )
    probs_low = probs1.astype(jnp.bfloat16)
    probs_grad = jnp.einsum(
        "iphe,iqhe->ihpq", context_grad, values1, preferred_element_type=jnp.float32
    )
    values_grad = jnp.einsum(
        "ihpq,iphe->iqhe", probs_low, context_grad, preferred_element_type=jnp.float32
    )
    scores_grad = (probs1 * (probs_grad - jnp.sum(probs1 * probs_grad, -1, keepdims=True))).astype(
        jnp.bfloat16
    )
    key_ok = valid_rows.reshape(images, 1, 1, 49) > 0.5
    scores_grad = jnp.where(key_ok, scores_grad, jnp.zeros_like(scores_grad))
    query_grad = (
        jnp.einsum("ihpq,iqhe->iphe", scores_grad, keys1, preferred_element_type=jnp.float32)
        * scaling
    )
    keys_grad = (
        jnp.einsum("ihpq,iphe->iqhe", scores_grad, query1, preferred_element_type=jnp.float32)
        * scaling
    )
    packed_grad1 = (
        jnp.stack([query_grad, keys_grad, values_grad], 2)
        .astype(jnp.bfloat16)
        .reshape(rows_all, 3 * model_width)
    )
    qkv_w_grad0 = contract_rows(normed1, packed_grad1)
    packed_sums = jnp.sum(packed_grad1.astype(jnp.float32), 0)
    sp_bias_grad = jnp.concatenate([packed_sums[:model_width], packed_sums[2 * model_width :]])
    grad_part, gain_grad0, shift_grad0 = norm_backward(
        stream1, gains[0], shifts[0], times_transposed(packed_grad1, qkv_w[0])
    )
    grad1 = grad2 + grad_part
    grad0, conv_w_grad0, conv_b_grad0 = position_conv_back(
        grad1, pad_first, images, window, conv_w[0], valid_rows
    )
    patches_grad = (grad0 * valid_rows).astype(jnp.bfloat16).reshape(patches.shape)
    local_sums = (
        lax.psum_scatter(
            jnp.stack([conv_w_grad0, conv_w_grad1, conv_w_grad2]),
            "dp",
            scatter_dimension=2,
            tiled=True,
        ),
        lax.psum_scatter(
            jnp.stack([conv_b_grad0, conv_b_grad1, conv_b_grad2]),
            "dp",
            scatter_dimension=1,
            tiled=True,
        ),
        lax.psum_scatter(
            jnp.stack([gain_grad0, gain_grad1, gain_grad2, gain_grad3]),
            "dp",
            scatter_dimension=1,
            tiled=True,
        ),
        lax.psum_scatter(
            jnp.stack([shift_grad0, shift_grad1, shift_grad2, shift_grad3]),
            "dp",
            scatter_dimension=1,
            tiled=True,
        ),
        lax.psum_scatter(
            jnp.stack([qkv_w_grad0, qkv_w_grad1]), "dp", scatter_dimension=1, tiled=True
        ),
        lax.psum_scatter(sp_bias_grad, "dp", scatter_dimension=0, tiled=True),
        lax.psum_scatter(ch_bias_grad, "dp", scatter_dimension=0, tiled=True),
        lax.psum_scatter(
            jnp.stack([proj_w_grad0, proj_w_grad1]), "dp", scatter_dimension=1, tiled=True
        ),
        lax.psum_scatter(
            jnp.stack([proj_b_grad0, proj_b_grad1]), "dp", scatter_dimension=1, tiled=True
        ),
        lax.psum_scatter(
            jnp.stack([hid_w_grad0, hid_w_grad1]), "dp", scatter_dimension=1, tiled=True
        ),
        lax.psum_scatter(
            jnp.stack([hid_b_grad0, hid_b_grad1]), "dp", scatter_dimension=1, tiled=True
        ),
        lax.psum_scatter(
            jnp.stack([out_w_grad0, out_w_grad1]), "dp", scatter_dimension=1, tiled=True
        ),
        lax.psum_scatter(
            jnp.stack([out_b_grad0, out_b_grad1]), "dp", scatter_dimension=1, tiled=True
        ),
    )
    summed = (
        lax.psum(local_sums[0].astype(jnp.bfloat16), "win").astype(jnp.float32),
        lax.psum(local_sums[1].astype(jnp.bfloat16), "win").astype(jnp.float32),
        lax.psum(local_sums[2].astype(jnp.bfloat16), "win").astype(jnp.float32),
        lax.psum(local_sums[3].astype(jnp.bfloat16), "win").astype(jnp.float32),
        lax.psum(local_sums[4].astype(jnp.bfloat16), "win").astype(jnp.float32),
        lax.psum(local_sums[5].astype(jnp.bfloat16), "win").astype(jnp.float32),
        lax.psum(local_sums[6].astype(jnp.bfloat16), "win").astype(jnp.float32),
        lax.psum(local_sums[7].astype(jnp.bfloat16), "win").astype(jnp.float32),
        lax.psum(local_sums[8].astype(jnp.bfloat16), "win").astype(jnp.float32),
        lax.psum(local_sums[9].astype(jnp.bfloat16), "win").astype(jnp.float32),
        lax.psum(local_sums[10].astype(jnp.bfloat16), "win").astype(jnp.float32),
        lax.psum(local_sums[11].astype(jnp.bfloat16), "win").astype(jnp.float32),
        lax.psum(local_sums[12].astype(jnp.bfloat16), "win").astype(jnp.float32),
    )
    return (activations, patches_grad) + tuple(summed)


def solution(mesh):
    small = mesh.shape["dp"] == 8 and mesh.shape["win"] == 4
    return jax.shard_map(
        on_device_fast if small else on_device,
        mesh=mesh,
        in_specs=(
            P("dp", "win", None, None),
            P("dp", "win", None, None),
            P("dp"),
            P(None, None, "dp"),
            P(None, "dp"),
            P(None, "dp"),
            P(None, "dp"),
            P(None, "dp", None),
            P("dp"),
            P("dp"),
            P(None, "dp", None),
            P(None, "dp"),
            P(None, "dp", None),
            P(None, "dp"),
            P(None, "dp", None),
            P(None, "dp"),
        ),
        out_specs=(
            P("dp", "win", None, None),
            P("dp", "win", None, None),
            P(None, None, "dp"),
            P(None, "dp"),
            P(None, "dp"),
            P(None, "dp"),
            P(None, "dp", None),
            P("dp"),
            P("dp"),
            P(None, "dp", None),
            P(None, "dp"),
            P(None, "dp", None),
            P(None, "dp"),
            P(None, "dp", None),
            P(None, "dp"),
        ),
        check_vma=False,
    )
```

```python
import functools

import jax
import jax.numpy as jnp
from jax import lax
from jax.experimental import pallas as pl
from jax.experimental.pallas import tpu as pltpu
from jax.sharding import PartitionSpec as P

HEADS = 24
HEAD = 32
EPS = 1e-05
MESH = pl.DeviceIdType.MESH
F32 = jnp.float32
BF16 = jnp.bfloat16
SCALE = HEAD ** (-0.5)
CELLS = 56
PAIR = 112
GROUPS = 3


def dot(left, right):
    return jnp.dot(left, right, preferred_element_type=F32)


def dot_t(left, right):
    return lax.dot_general(left, right, (((1,), (1,)), ((), ())), preferred_element_type=F32)


def t_dot(left, right):
    return lax.dot_general(left, right, (((0,), (0,)), ((), ())), preferred_element_type=F32)


def iota(shape, dim):
    return lax.broadcasted_iota(jnp.int32, shape, dim)


def rows_at(index, count):
    return pl.ds(pl.multiple_of(index * count, count), count)


def lanes_at(index, count, base=0):
    return pl.ds(pl.multiple_of(base + index * count, 128), count)


def each(count, body):
    def step(i, carry):
        body(i)
        return carry

    lax.fori_loop(0, count, step, 0)


def each_few(count, few, load, compute, store):
    def step(n):
        inputs = [load(n * few + u) for u in range(few)]
        results = [compute(*values) for values in inputs]
        for u in range(few):
            store(n * few + u, results[u])

    each(count // few, step)


def gelu_pair(pre):
    t = 1.0 / (1.0 + 0.23164190 * jnp.abs(pre))
    e = jnp.exp(-0.5 * pre * pre)
    poly = (((1.061405429 * t - 1.453152027) * t + 1.421413741) * t - 0.284496736) * t + 0.254829592
    tail = 0.5 * poly * t * e
    cdf = jnp.where(pre >= 0.0, 1.0 - tail, tail)
    return pre * cdf, cdf + pre * (e * 0.3989422804014327)


def place():
    d = lax.axis_index("dp")
    w = lax.axis_index("win")
    return d, w, w // 2, w % 2


def greet(peers):
    barrier = pltpu.get_barrier_semaphore()
    for peer in peers:
        pl.semaphore_signal(barrier, inc=1, device_id=peer, device_id_type=MESH)
    pl.semaphore_wait(barrier, len(peers))


def remote(src, dst, sems, peer):
    return pltpu.make_async_remote_copy(
        src_ref=src, dst_ref=dst, send_sem=sems.at[0], recv_sem=sems.at[1], device_id=peer, device_id_type=MESH
    )


def fill_valid(valid, sizes, images, wr, wc):
    def one(i):
        cell = iota((CELLS, 128), 0)
        r, c = cell >> 3, cell & 7
        inside = (r + 7 * wr < sizes[i]) & (c + 7 * wc < sizes[i]) & (c < 7)
        valid[rows_at(i, CELLS), :] = jnp.where(inside, 1.0, 0.0).astype(F32)

    each(images, one)


def spread(valid_rows, width):
    return jnp.concatenate([valid_rows] * (width // 128), axis=1)


def halo(pad, images, wr, wc, row_out, row_in, col_out, col_in, sems, vertical, horizontal, flights):
    edge = 7 - 6 * wr

    def pack(p):
        one = pad[pl.ds(pl.multiple_of((18 * p + edge) * 8, 8), 8), :]
        two = pad[pl.ds(pl.multiple_of((18 * p + 9 + edge) * 8, 8), 8), :]
        row_out[rows_at(p, 16), :] = jnp.concatenate([one, two], axis=0).astype(BF16)

    each(images // 2, pack)
    copy = remote(row_out, row_in, sems.at[0], vertical)
    copy.start()
    flights[0]()
    copy.wait()
    border = 8 - 8 * wr

    def unpack(p):
        both = row_in[rows_at(p, 16), :].astype(F32)
        pad[pl.ds(pl.multiple_of((18 * p + border) * 8, 8), 8), :] = both[:8]
        pad[pl.ds(pl.multiple_of((18 * p + 9 + border) * 8, 8), 8), :] = both[8:]

    each(images // 2, unpack)
    turn = 2 - 2 * wc
    sub = iota((8, 128), 0)

    def row_of(i, s):
        at_row = border if s == 7 else s + 1
        return pl.ds(pl.multiple_of((9 * i + at_row) * 8, 8), 8)

    def pack_col(p):
        for part in range(pad.shape[1] // 128):
            at = pl.ds(part * 128, 128)
            both = []
            for i in (2 * p, 2 * p + 1):
                line = jnp.zeros((8, 128), F32)
                for s in range(8):
                    line = jnp.where(sub == s, pltpu.roll(pad[row_of(i, s), at], s + turn, 0), line)
                both.append(line)
            col_out[rows_at(p, 16), at] = jnp.concatenate(both, axis=0).astype(BF16)

    each(images // 2, pack_col)
    copy = remote(col_out, col_in, sems.at[1], horizontal)
    copy.start()
    flights[1]()
    copy.wait()

    def unpack_col(p):
        for part in range(pad.shape[1] // 128):
            at = pl.ds(part * 128, 128)
            both = col_in[rows_at(p, 16), at].astype(F32)
            for one in range(2):
                line = both[8 * one : 8 * one + 8]
                for s in range(8):
                    to = row_of(2 * p + one, s)
                    pad[to, at] = jnp.where(sub == 7, pltpu.roll(line, 7 - s, 0), pad[to, at])

    each(images // 2, unpack_col)


def side_masks(wr, wc):
    c = iota((8, 128), 0)
    left = jnp.where((c == 0) & (wc == 0), 0.0, 1.0).astype(F32)
    right = jnp.where((c == 6) & (wc == 1), 0.0, 1.0).astype(F32)
    return left, right


def three(pad, i, at, left, right):
    rows = [pad[pl.ds(pl.multiple_of((9 * i + r) * 8, 8), 8), at] for r in range(9)]
    return [(pltpu.roll(v, 1, 0) * left, v, pltpu.roll(v, 7, 0) * right) for v in rows]


def conv_forward(pad, images, vec, k, valid, out, left, right):
    def one(i):
        for part in range(pad.shape[1] // 128):
            at = pl.ds(part * 128, 128)
            moved = three(pad, i, at, left, right)
            bias = vec[27 + k : 28 + k, at]
            taps = [vec[9 * k + t : 9 * k + t + 1, at] for t in range(9)]
            for r in range(7):
                total = jnp.broadcast_to(bias, (8, 128))
                for t in range(9):
                    total = total + taps[t] * moved[r + t // 3][t % 3]
                to = pl.ds(pl.multiple_of((7 * i + r) * 8, 8), 8)
                out[to, at] = moved[r + 1][1] + valid[to, :] * total

    each(images, one)


def norm_rows(src, images, vec, k, dst):
    gain = vec[30 + k : 31 + k, :]
    shift = vec[34 + k : 35 + k, :]

    def one(p):
        x = src[rows_at(p, PAIR), :]
        centered = x - jnp.mean(x, -1, keepdims=True)
        variance = jnp.mean(centered * centered, -1, keepdims=True)
        dst[rows_at(p, PAIR), :] = (centered * lax.rsqrt(variance + EPS) * gain + shift).astype(BF16)

    each(images // 2, one)


def to_pad(pad, p, rows):
    pad[pl.ds(pl.multiple_of((18 * p + 1) * 8, 8), CELLS), :] = rows[:CELLS]
    pad[pl.ds(pl.multiple_of((18 * p + 10) * 8, 8), CELLS), :] = rows[CELLS:]


def of_pad(pad, p):
    return jnp.concatenate(
        [
            pad[pl.ds(pl.multiple_of((18 * p + 1) * 8, 8), CELLS), :],
            pad[pl.ds(pl.multiple_of((18 * p + 10) * 8, 8), CELLS), :],
        ],
        axis=0,
    )


def clear_borders(pad, images):
    zero = jnp.zeros((8, pad.shape[1]), F32)

    def one(i):
        pad[pl.ds(pl.multiple_of(72 * i, 8), 8), :] = zero
        pad[pl.ds(pl.multiple_of(72 * i + 64, 8), 8), :] = zero

    each(images, one)


def head_masks(kind):
    lane = iota((PAIR, 128), 1) >> 5
    return [jnp.where(lane == h, 1.0, 0.0).astype(F32).astype(kind) for h in range(4)]


def pair_mask(sizes, p, wr, wc):
    row = iota((PAIR, PAIR), 0)
    lane = iota((PAIR, PAIR), 1)
    second = lane >= CELLS
    cell = jnp.where(second, lane - CELLS, lane)
    side = jnp.where(second, sizes[2 * p + 1], sizes[2 * p])
    r, c = cell >> 3, cell & 7
    inside = (r + 7 * wr < side) & (c + 7 * wc < side) & (c < 7)
    return inside & (second == (row >= CELLS))


def stacked(value, masks):
    return jnp.concatenate([value * m for m in masks], axis=0)


def folded(value, masks):
    total = value[:PAIR] * masks[0]
    for h in range(1, 4):
        total = total + value[h * PAIR : (h + 1) * PAIR] * masks[h]
    return total


def pair_probs(query_bd, key, allowed):
    scores = dot_t(query_bd, key) * SCALE
    scores = jnp.where(allowed, scores, -1000000000.0)
    e = jnp.exp(scores - jnp.max(scores, -1, keepdims=True))
    return e * (1.0 / jnp.sum(e, -1, keepdims=True))


def window_attention(packed, images, sizes, wr, wc, context, between):
    width = context.shape[1]

    def pair(p):
        rows = rows_at(p, PAIR)
        allowed = jnp.concatenate([pair_mask(sizes, p, wr, wc).astype(F32)] * 4, axis=0) > 0.5
        low = head_masks(BF16)
        full = head_masks(F32)

        def load(g):
            return tuple(packed[rows, lanes_at(g, 128, n * width)] for n in range(3))

        def compute(query, key, value):
            probs = pair_probs(stacked(query, low), key, allowed).astype(BF16)
            return folded(dot(probs, value), full).astype(BF16)

        def store(g, result):
            context[rows, lanes_at(g, 128)] = result

        each_few(width // 128, GROUPS, load, compute, store)

    for p in range(images // 2):
        pair(p)
        if p % 2 == 1:
            between(1)


def image_halves(kind):
    row = iota((PAIR, 128), 0)
    first = jnp.where(row < CELLS, 1.0, 0.0).astype(F32)
    return first.astype(kind), (1.0 - first).astype(kind)


def fold_heads(square):
    lane = iota((32, 128), 1) >> 5
    total = jnp.zeros((32, 128), F32)
    for h in range(4):
        total = total + jnp.where(lane == h, square[32 * h : 32 * h + 32], 0.0)
    return total


def unfold_heads(block):
    lane = iota((32, 128), 1) >> 5
    return jnp.concatenate([jnp.where(lane == h, block, 0.0) for h in range(4)], axis=0)


def pair_grams(left, left_base, right, right_base, images, valid, out):
    def pair(p):
        rows = rows_at(p, PAIR)
        one, two = image_halves(BF16)
        ok = valid[rows, :].astype(BF16)
        one, two = one * ok, two * ok

        def load(g):
            return left[rows, lanes_at(g, 128, left_base)], right[rows, lanes_at(g, 128, right_base)]

        def compute(a, b):
            both = t_dot(a, jnp.concatenate([b * one, b * two], axis=1))
            return fold_heads(both[:, :128]), fold_heads(both[:, 128:])

        def store(g, result):
            out[pl.ds(pl.multiple_of(64 * p, 32), 32), lanes_at(g, 128)] = result[0]
            out[pl.ds(pl.multiple_of(64 * p + 32, 32), 32), lanes_at(g, 128)] = result[1]

        each_few(out.shape[1] // 128, GROUPS, load, compute, store)

    each(images // 2, pair)


def sum_windows(gram, ins, images, c, sems, vertical, horizontal, flights):
    half = images * 16
    mine = pl.ds(pl.multiple_of(half * c, 32), half)
    other = pl.ds(pl.multiple_of(half * (1 - c), 32), half)

    def add(k):
        def one(i):
            rows = pl.ds(pl.multiple_of(half * c + 32 * i, 32), 32)
            gram[rows, :] = gram[rows, :] + ins[k, rows_at(i, 32), :]

        each(images // 2, one)

    copy = remote(gram.at[other], ins.at[0], sems.at[0], horizontal)
    copy.start()
    flights[0]()
    copy.wait()
    add(0)
    copy = remote(gram.at[mine], ins.at[1], sems.at[1], vertical)
    copy.start()
    flights[1]()
    copy.wait()
    add(1)
    copy = remote(gram.at[mine], ins.at[2], sems.at[2], horizontal)
    copy.start()
    flights[2]()
    copy.wait()

    def take(i):
        gram[pl.ds(pl.multiple_of(half * (1 - c) + 32 * i, 32), 32), :] = ins[2, rows_at(i, 32), :]

    each(images // 2, take)


ROWS_WIDE = 42
ROWS_SMALL = 64
SHORT = 96


def join(pieces):
    tiles = [None] * (SHORT * len(pieces) // 128)
    lane = iota(pieces[0].shape, 1)
    for i, piece in enumerate(pieces):
        t, shift = divmod(SHORT * i, 128)
        moved = pltpu.roll(piece, shift, 1) if shift else piece
        head = jnp.where(lane >= shift, moved, 0.0)
        tiles[t] = head if tiles[t] is None else tiles[t] + head
        if shift > 128 - SHORT:
            tiles[t + 1] = jnp.where(lane < shift - (128 - SHORT), moved, 0.0)
    return tiles


def cut(tiles):
    lane = iota(tiles[0].shape, 1)
    pieces = []
    for i in range(128 * len(tiles) // SHORT):
        t, shift = divmod(SHORT * i, 128)
        piece = pltpu.roll(tiles[t], 128 - shift, 1) if shift else tiles[t]
        if shift > 128 - SHORT:
            piece = jnp.where(lane < 128 - shift, piece, pltpu.roll(tiles[t + 1], 128 - shift, 1))
        pieces.append(piece)
    return pieces


def small_rows():
    return ((42, 2, 0), (44, 3, 1), (47, 4, 2), (51, 4, 3))


def unpack_small(gathered_small, vec, qbias, hbias):
    blocks = [gathered_small[d].astype(F32) for d in range(gathered_small.shape[0])]
    for t, tile in enumerate(join(blocks)):
        vec[:, 128 * t : 128 * t + 128] = tile
    width = vec.shape[1]
    qbias[...] = jnp.zeros(qbias.shape, F32)
    for first, count, row in small_rows():
        lines = [
            jnp.broadcast_to(block[first + r : first + r + 1], (8, 128)) for block in blocks for r in range(count)
        ]
        for t, tile in enumerate(join(lines)):
            line = tile[0:1]
            if row == 0:
                at = 128 * t if 128 * t < width else 128 * t + width
                qbias[0:1, at : at + 128] = line
            elif row == 1:
                qbias[1:2, 128 * t : 128 * t + 128] = line
            else:
                hbias[row - 2 : row - 1, 128 * t : 128 * t + 128] = line


def pack_small(vecg, qbg, hbg, out):
    width = vecg.shape[1]
    for d, piece in enumerate(cut([vecg[:, 128 * t : 128 * t + 128] for t in range(width // 128)])):
        out[d, 0 : vecg.shape[0]] = piece
    for first, count, row in small_rows():
        if row == 0:
            at = [128 * t if 128 * t < width else 128 * t + width for t in range(2 * width // 128)]
            lines = [qbg[0:1, a : a + 128] for a in at]
        elif row == 1:
            lines = [qbg[1:2, 128 * t : 128 * t + 128] for t in range(3 * width // 128)]
        else:
            lines = [hbg[row - 2 : row - 1, 128 * t : 128 * t + 128] for t in range(4 * width // 128)]
        for i, piece in enumerate(cut([jnp.broadcast_to(line, (8, 128)) for line in lines])):
            d, r = divmod(i, count)
            out[d, first + r : first + r + 1] = piece[0:1]


LINE = 4
AHEAD = 2
FIRST = 1
LAGS_FIRST = (0, 1, 2, 3)
LAGS = (0, 2, 4, 5)


def forward_kernel(
    images,
    width,
    hidden,
    sizes,
    patches,
    small,
    qkv_s,
    proj_s,
    hid_s,
    out_s,
    activations,
    o_w,
    vec,
    o_pad,
    o_stream,
    o_normed,
    o_packed,
    o_context,
    o_act,
    o_slope,
    o_mix,
    pad,
    streams,
    normed,
    packed,
    context,
    act,
    slope,
    gram,
    gram_in,
    valid,
    pre,
    wq,
    wp,
    wh,
    wo,
    row_out,
    row_in,
    col_out,
    col_in,
    final,
    halo_sems,
    gram_sems,
    load_sems,
    save_sems,
    z_sems,
    y_sems,
    xa_sems,
    xb_sems,
    c_sems,
    own_sems,
    pre_a,
    pre_b,
    small_in,
    qbias,
    hbias,
    small_sems,
):
    d, w, wr, wc = place()
    pairs = images // 2
    horizontal = (d, 2 * wr + 1 - wc)
    vertical = (d, 2 * (1 - wr) + wc)
    z, y = d // 2, d % 2
    depth = qkv_s.shape[1]
    others = [lax.rem(z + k, LINE) for k in range(1, LINE)]
    in_line = [(2 * other + y, w) for other in others]
    across = (2 * z + 1 - y, w)
    alike = [(lax.rem(d + k, 2 * LINE), w) for k in range(1, 2 * LINE)]
    greet([horizontal, vertical] + alike)
    for peer in alike:
        remote(small, small_in.at[d], small_sems, peer).start()
    left, right = side_masks(wr, wc)

    columns = pl.ds(pl.multiple_of(wc * (width // 2), 128), width // 2)

    def split(t):
        return t % 3 != 2

    def rows_of(t):
        return pl.ds(pl.multiple_of(wr * (depth // 2), 16), depth // 2) if split(t) else pl.ds(0, depth)

    def shard(t, rows):
        layer, j = t // 12, t % 12
        base = (0, 0, 0, 0, 4, 4, 4, 4, 8, 8, 8, 8)[j]
        if j >= 8:
            start = (j - base) * depth
            return out_s.at[layer, pl.ds(pl.multiple_of(start + rows.start, 16), rows.size), columns]
        source = qkv_s if j < 3 else proj_s if j < 4 else hid_s
        shift = 0 if j == 3 else (j - base) * width
        return source.at[layer, rows, pl.ds(pl.multiple_of(shift + wc * (width // 2), 128), width // 2)]

    def piece(t, z_at, y_at):
        return o_w.at[t, z_at, y_at, rows_of(t), columns]

    def send(src, dst, sems, peer):
        remote(src, dst, sems, peer).start()

    def arrived(ref, sems):
        pltpu.make_async_copy(ref, ref, sems.at[1]).wait()

    def left_here(ref, sems):
        pltpu.make_async_copy(ref, ref, sems.at[0]).wait()

    def all_left(t):
        left_here(o_w.at[t, pl.ds(0, LINE - 1), y, rows_of(t), columns], z_sems.at[t])
        left_here(piece(t, pl.ds(0, LINE), y), y_sems.at[t])
        if split(t):
            left_here(o_w.at[t, pl.ds(0, LINE - 1), y, rows_of(t), columns], xa_sems.at[t])
            left_here(piece(t, pl.ds(0, LINE), 1 - y), xb_sems.at[t])
        left_here(o_w.at[t, pl.ds(0, LINE), pl.ds(0, 2), pl.ds(0, depth), columns], c_sems.at[t])

    def own_copy(t):
        return pltpu.make_async_copy(
            shard(t, pl.ds(0, depth)), o_w.at[t, z, y, pl.ds(0, depth), columns], own_sems.at[t]
        )

    def open_chunk(t):
        own_copy(t).start()
        for peer in in_line:
            send(shard(t, rows_of(t)), piece(t, z, y), z_sems.at[t], peer)
        send(shard(t, rows_of(t)), piece(t, z, y), y_sems.at[t], across)

    def stage_a(t):
        arrived(o_w.at[t, pl.ds(0, LINE - 1), y, rows_of(t), columns], z_sems.at[t])
        for other in others:
            send(piece(t, other, y), piece(t, other, y), y_sems.at[t], across)
        if split(t):
            for other in others:
                send(piece(t, other, y), piece(t, other, y), xa_sems.at[t], vertical)

    def stage_b(t):
        beside = piece(t, pl.ds(0, LINE), 1 - y)
        arrived(beside, y_sems.at[t])
        if split(t):
            send(beside, beside, xb_sems.at[t], vertical)

    def stage_c(t):
        own_copy(t).wait()
        if split(t):
            rows = pl.ds(pl.multiple_of((1 - wr) * (depth // 2), 16), depth // 2)
            arrived(o_w.at[t, pl.ds(0, LINE - 1), y, rows, columns], xa_sems.at[t])
            arrived(o_w.at[t, pl.ds(0, LINE), 1 - y, rows, columns], xb_sems.at[t])
        half = o_w.at[t, pl.ds(0, LINE), pl.ds(0, 2), pl.ds(0, depth), columns]
        send(half, half, c_sems.at[t], horizontal)

    chunks = 24
    kinds = ("q", "q", "q", "p", "h", "h", "h", "h", "o", "o", "o", "o")
    busy = {"q": True, "p": True, "h": True, "o": True}
    landed, waiting = set(), []
    clock, opened = [0], [0]

    def load_of(t):
        j = t % 12
        if j < 3:
            dst = wq.at[:, :, :, pl.ds(j * width, width)]
        elif j < 4:
            dst = wp
        elif j < 8:
            dst = wh.at[:, :, :, pl.ds((j - 4) * width, width)]
        else:
            dst = wo.at[:, :, j - 8]
        return pltpu.make_async_copy(o_w.at[t], dst, load_sems.at[t])

    def stage_d(t):
        other = pl.ds(pl.multiple_of((1 - wc) * (width // 2), 128), width // 2)
        arrived(o_w.at[t, pl.ds(0, LINE), pl.ds(0, 2), pl.ds(0, depth), other], c_sems.at[t])
        if t < 12 or not busy[kinds[t % 12]]:
            load_of(t).start()
            landed.add(t)
        else:
            waiting.append(t)

    order = []
    for t in range(chunks):
        lags = LAGS_FIRST if t < FIRST else LAGS
        for stage, lag in zip((stage_a, stage_b, stage_c, stage_d), lags):
            order.append((t + lag, -lag, t, stage))
    order.sort(key=lambda entry: entry[:2])
    last_step = {t: max(step for step, _, u, _ in order if u == t) for t in range(chunks)}
    final_step = max(last_step.values())

    def advance(count):
        for _ in range(count):
            for step, _, t, stage in order:
                if step == clock[0]:
                    stage(t)
                    if stage is stage_a:
                        for ahead in range(max(opened[0], AHEAD), min(t + 1 + AHEAD, chunks)):
                            open_chunk(ahead)
                            opened[0] = ahead + 1
            clock[0] += 1

    def need(t):
        while clock[0] <= last_step[t]:
            advance(1)
        load_of(t).wait()

    def release(kind):
        busy[kind] = False
        for t in [t for t in waiting if kinds[t % 12] == kind]:
            load_of(t).start()
            landed.add(t)
            waiting.remove(t)

    for t in range(AHEAD):
        open_chunk(t)

    saves = {}

    def save(name, src, dst, s):
        saves[name] = pltpu.make_async_copy(src, dst, save_sems.at[s])
        saves[name].start()

    small_in[d] = small[...]
    fill_valid(valid, sizes, images, wr, wc)
    clear_borders(pad, images)

    def enter(p):
        rows = rows_at(p, PAIR)
        to_pad(pad, p, patches[rows, :].astype(F32) * spread(valid[rows, :], width))

    each(pairs, enter)
    advance(1)
    arrived(small_in.at[pl.ds(0, 2 * LINE - 1)], small_sems)
    unpack_small(small_in, vec, qbias, hbias)
    advance(1)

    def step():
        advance(1)

    def convolve(k, stream):
        halo(pad, images, wr, wc, row_out.at[k], row_in.at[k], col_out.at[k], col_in.at[k], halo_sems.at[k], vertical, horizontal, (step, step))
        conv_forward(pad, images, vec, k, valid, stream, left, right)

    def columns_of(weights, at):
        block = weights[:, :, :, at]
        return block.reshape(width, block.shape[-1])

    def qkv(k, x):
        for part in range(3):
            need(12 * k + part)

            def tile(j):
                at = lanes_at(j, 256, part * width)
                packed[:, at] = (dot(x[...], columns_of(wq, at)) + qbias[k : k + 1, at]).astype(BF16)

            each(width // 256, tile)
        release("q")

    def proj(k, stream, store):
        need(12 * k + 3)

        def tile(j):
            at = lanes_at(j, 256)
            pre[...] = dot(context[...], columns_of(wp, at))

            def part(p):
                rows = rows_at(p, PAIR)
                store(p, at, stream[rows, at] + spread(valid[rows, :], 256) * (pre[rows, :] + vec[38 + k : 39 + k, at]))

            each(pairs, part)

        each(width // 256, tile)
        release("p")

    def feed_forward(k, x, stream, store):
        half = width // 2
        tiles = 2 * hidden // width
        pre_b[...] = jnp.zeros(pre_b.shape, F32)

        def multiply(j, to):
            to[...] = dot(x[...], columns_of(wh, lanes_at(j, half)))

        def activate(j, of):
            for r in range(of.shape[0] // 48):
                rows = pl.ds(48 * r, 48)
                for part in range(half // 128):
                    at = pl.ds(pl.multiple_of(j * half + 128 * part, 128), 128)
                    a, s = gelu_pair(of[rows, pl.ds(128 * part, 128)] + hbias[k : k + 1, at])
                    act[rows, at] = a.astype(BF16)
                    slope[rows, at] = s.astype(BF16)

        def two_tiles(b):
            multiply(2 * b, pre_a)
            activate(lax.rem(2 * b + tiles - 1, tiles), pre_b)
            multiply(2 * b + 1, pre_b)
            activate(2 * b, pre_a)

        for block in range(0, 4, 2):
            need(12 * k + 4 + block)
            need(12 * k + 5 + block)
            each(2, lambda b: two_tiles(block + b))
            advance(1)
        activate(tiles - 1, pre_b)
        release("h")
        for block in range(4):
            need(12 * k + 8 + block)

        def tile2(j):
            at = lanes_at(j, 256)
            block = wo[:, :, :, :, at]
            pre[...] = dot(act[...], block.reshape(hidden, 256))

            def part(p):
                rows = rows_at(p, PAIR)
                store(p, at, stream[rows, at] + spread(valid[rows, :], 256) * (pre[rows, :] + vec[40 + k : 41 + k, at]))

            each(pairs, part)

        for j in range(width // 256):
            tile2(j)
        advance(1)
        release("o")

    def into_pad(p, at, value):
        pad[pl.ds(pl.multiple_of((18 * p + 1) * 8, 8), CELLS), at] = value[:CELLS]
        pad[pl.ds(pl.multiple_of((18 * p + 10) * 8, 8), CELLS), at] = value[CELLS:]

    convolve(0, streams.at[0])
    save("pad0", pad, o_pad.at[0], 0)
    save("s1", streams.at[0], o_stream.at[0], 1)
    norm_rows(streams.at[0], images, vec, 0, normed.at[0])
    save("n1", normed.at[0], o_normed.at[0], 2)
    qkv(0, normed.at[0])
    save("k1", packed, o_packed.at[0], 3)
    window_attention(packed, images, sizes, wr, wc, context, advance)
    save("c1", context, o_context.at[0], 4)
    saves["pad0"].wait()
    proj(0, streams.at[0], into_pad)
    convolve(1, streams.at[1])
    save("pad2", pad, o_pad.at[1], 0)
    save("s3", streams.at[1], o_stream.at[1], 5)
    norm_rows(streams.at[1], images, vec, 1, normed.at[1])
    save("n3", normed.at[1], o_normed.at[1], 6)
    saves["pad2"].wait()
    feed_forward(0, normed.at[1], streams.at[1], into_pad)
    save("a0", act, o_act.at[0], 7)
    save("g0", slope, o_slope.at[0], 8)
    saves["s1"].wait()
    saves["n1"].wait()
    saves["k1"].wait()
    saves["c1"].wait()
    convolve(2, streams.at[0])
    save("pad4", pad, o_pad.at[2], 0)
    save("s5", streams.at[0], o_stream.at[2], 1)
    norm_rows(streams.at[0], images, vec, 2, normed.at[0])
    save("n5", normed.at[0], o_normed.at[2], 2)
    qkv(1, normed.at[0])
    save("k5", packed, o_packed.at[1], 3)
    pair_grams(packed, 2 * width, packed, width, images, valid, gram)
    advance(1)
    sum_windows(gram, gram_in, images, wc, gram_sems, vertical, horizontal, (step, step, step))

    def soften(i):
        rows = rows_at(i, 32)
        x = gram[rows, :] * SCALE
        e = jnp.exp(x - jnp.max(x, 0, keepdims=True))
        gram[rows, :] = e * (1.0 / jnp.sum(e, 0, keepdims=True))

    each(images, soften)
    save("mix", gram, o_mix, 9)

    def mix_pair(p):
        rows = rows_at(p, PAIR)
        one, two = image_halves(BF16)

        def load(g):
            at = lanes_at(g, 128)
            first = gram[pl.ds(pl.multiple_of(64 * p, 32), 32), at]
            second = gram[pl.ds(pl.multiple_of(64 * p + 32, 32), 32), at]
            return first, second, packed[rows, at]

        def compute(first, second, query):
            mixing = jnp.concatenate([unfold_heads(first), unfold_heads(second)], axis=0).astype(BF16)
            return dot(jnp.concatenate([query * one, query * two], axis=1), mixing).astype(BF16)

        def store(g, result):
            context[rows, lanes_at(g, 128)] = result

        each_few(width // 128, GROUPS, load, compute, store)

    each(pairs, mix_pair)
    advance(1)
    save("c5", context, o_context.at[1], 4)
    saves["s3"].wait()
    saves["n3"].wait()

    def into_last(p, at, value):
        streams[1, rows_at(p, PAIR), at] = value

    proj(1, streams.at[0], into_last)
    save("s6", streams.at[1], o_stream.at[3], 5)
    norm_rows(streams.at[1], images, vec, 3, normed.at[1])
    save("n6", normed.at[1], o_normed.at[3], 6)
    saves["a0"].wait()
    saves["g0"].wait()

    def into_final(p, at, value):
        final[rows_at(p, PAIR), at] = value.astype(BF16)

    feed_forward(1, normed.at[1], streams.at[1], into_final)
    save("a1", act, o_act.at[1], 7)
    save("g1", slope, o_slope.at[1], 8)
    save("end", final, activations, 10)
    advance(final_step + 1 - clock[0])
    for t in range(chunks):
        all_left(t)
    left_here(small_in.at[pl.ds(0, 2 * LINE - 1)], small_sems)
    for name in ("pad4", "s5", "n5", "k5", "mix", "c5", "s6", "n6", "a1", "g1", "end"):
        saves[name].wait()


ANY = pl.BlockSpec(memory_space=pl.ANY)
VMEM = pl.BlockSpec(memory_space=pltpu.VMEM)
SMEM = pl.BlockSpec(memory_space=pltpu.SMEM)


def run_forward(sizes, patches, small, shards):
    images = sizes.shape[0]
    n_rows, width = patches.shape
    hidden = shards[2].shape[2]
    lines = images * 72
    depth = shards[0].shape[1]
    shapes = (
        ((n_rows, width), BF16),
        ((24, LINE, 2, depth, width), BF16),
        ((ROWS_SMALL, width), F32),
        ((3, lines, width), F32),
        ((4, n_rows, width), F32),
        ((4, n_rows, width), BF16),
        ((2, n_rows, 3 * width), BF16),
        ((2, n_rows, width), BF16),
        ((2, n_rows, hidden), BF16),
        ((2, n_rows, hidden), BF16),
        ((images * 32, width), F32),
    )
    return pl.pallas_call(
        functools.partial(forward_kernel, images, width, hidden),
        out_shape=[jax.ShapeDtypeStruct(*s) for s in shapes],
        in_specs=[SMEM, VMEM, VMEM] + [ANY] * 4,
        out_specs=[ANY] * 2 + [VMEM] + [ANY] * 8,
        scratch_shapes=[
            pltpu.VMEM((lines, width), F32),
            pltpu.VMEM((2, n_rows, width), F32),
            pltpu.VMEM((2, n_rows, width), BF16),
            pltpu.VMEM((n_rows, 3 * width), BF16),
            pltpu.VMEM((n_rows, width), BF16),
            pltpu.VMEM((n_rows, hidden), BF16),
            pltpu.VMEM((n_rows, hidden), BF16),
            pltpu.VMEM((images * 32, width), F32),
            pltpu.VMEM((3, images * 16, width), F32),
            pltpu.VMEM((n_rows, 128), F32),
            pltpu.VMEM((n_rows, 256), F32),
            pltpu.VMEM((LINE, 2, depth, 3 * width), BF16),
            pltpu.VMEM((LINE, 2, depth, width), BF16),
            pltpu.VMEM((LINE, 2, depth, hidden), BF16),
            pltpu.VMEM((LINE, 2, 4, depth, width), BF16),
            pltpu.VMEM((3, images * 8, width), BF16),
            pltpu.VMEM((3, images * 8, width), BF16),
            pltpu.VMEM((3, images * 8, width), BF16),
            pltpu.VMEM((3, images * 8, width), BF16),
            pltpu.VMEM((n_rows, width), BF16),
            pltpu.SemaphoreType.DMA((3, 2, 2)),
            pltpu.SemaphoreType.DMA((3, 2)),
            pltpu.SemaphoreType.DMA((24,)),
            pltpu.SemaphoreType.DMA((11,)),
            pltpu.SemaphoreType.DMA((24, 2)),
            pltpu.SemaphoreType.DMA((24, 2)),
            pltpu.SemaphoreType.DMA((24, 2)),
            pltpu.SemaphoreType.DMA((24, 2)),
            pltpu.SemaphoreType.DMA((24, 2)),
            pltpu.SemaphoreType.DMA((24,)),
            pltpu.VMEM((n_rows, width // 2), F32),
            pltpu.VMEM((n_rows, width // 2), F32),
            pltpu.VMEM((2 * LINE, ROWS_SMALL, 128), BF16),
            pltpu.VMEM((8, 3 * width), F32),
            pltpu.VMEM((8, hidden), F32),
            pltpu.SemaphoreType.DMA((2,)),
        ],
        compiler_params=pltpu.CompilerParams(
            collective_id=0, has_side_effects=True, vmem_limit_bytes=58 * 2**20
        ),
    )(sizes, patches, small, *shards)


def column_sums(src, images, width, store):
    for part in range(src.shape[1] // width):
        at = pl.ds(part * width, width)

        def one(p, total):
            x = src[rows_at(p, PAIR), at].astype(F32)
            return total + jnp.sum(x.reshape(PAIR // 8, 8, width), axis=0)

        total = lax.fori_loop(0, images // 2, one, jnp.zeros((8, width), F32))
        store(at, jnp.sum(total, axis=0, keepdims=True))


def norm_back(stream, images, vec, k, grad_normed, grad, vecg):
    gain = vec[30 + k : 31 + k, :]
    width = stream.shape[1]

    def one(p, carry):
        rows = rows_at(p, PAIR)
        x = stream[rows, :]
        dn = grad_normed[rows, :]
        centered = x - jnp.mean(x, -1, keepdims=True)
        rstd = lax.rsqrt(jnp.mean(centered * centered, -1, keepdims=True) + EPS)
        xhat = centered * rstd
        scaled = dn * gain
        inner = jnp.mean(scaled * xhat, -1, keepdims=True)
        grad[rows, :] = grad[rows, :] + rstd * (scaled - jnp.mean(scaled, -1, keepdims=True) - xhat * inner)
        gains = jnp.sum((dn * xhat).reshape(PAIR // 8, 8, width), axis=0)
        shifts = jnp.sum(dn.reshape(PAIR // 8, 8, width), axis=0)
        return carry[0] + gains, carry[1] + shifts

    zero = jnp.zeros((8, width), F32)
    gains, shifts = lax.fori_loop(0, images // 2, one, (zero, zero))
    vecg[30 + k : 31 + k, :] = jnp.sum(gains, axis=0, keepdims=True)
    vecg[34 + k : 35 + k, :] = jnp.sum(shifts, axis=0, keepdims=True)


def conv_back(grad_pad, pad, images, vec, k, valid, grad, vecg, left, right, between):
    keep = jnp.where(iota((8, 128), 0) < 7, 1.0, 0.0).astype(F32)
    for part in range(pad.shape[1] // 128):
        at = pl.ds(part * 128, 128)
        taps = [vec[9 * k + t : 9 * k + t + 1, at] for t in range(9)]

        def one(i, sums):
            back = three(grad_pad, i, at, left, right)
            ahead = three(pad, i, at, left, right)
            sums = list(sums)
            for r in range(7):
                own = back[r + 1][1] * keep
                total = own
                for t in range(9):
                    total = total + taps[t] * back[r + 2 - t // 3][2 - t % 3]
                    sums[t] = sums[t] + own * ahead[r + t // 3][t % 3]
                sums[9] = sums[9] + own
                to = pl.ds(pl.multiple_of((7 * i + r) * 8, 8), 8)
                grad[to, at] = valid[to, :] * total
            return tuple(sums)

        sums = lax.fori_loop(0, images, one, tuple(jnp.zeros((8, 128), F32) for _ in range(10)))
        for t in range(9):
            vecg[9 * k + t : 9 * k + t + 1, at] = jnp.sum(sums[t], axis=0, keepdims=True)
        vecg[27 + k : 28 + k, at] = jnp.sum(sums[9], axis=0, keepdims=True)
        if part == 2:
            between(1)


def window_back(packed, images, sizes, wr, wc, grad_context, between):
    width = grad_context.shape[1]

    def pair(p):
        rows = rows_at(p, PAIR)
        allowed = jnp.concatenate([pair_mask(sizes, p, wr, wc).astype(F32)] * 4, axis=0) > 0.5
        low = head_masks(BF16)
        full = head_masks(F32)

        def load(g):
            return [packed[rows, lanes_at(g, 128, n * width)] for n in range(3)] + [grad_context[rows, lanes_at(g, 128)]]

        def compute(query, key, value, grad):
            query_bd = stacked(query, low)
            grad_bd = stacked(grad, low)
            probs = pair_probs(query_bd, key, allowed)
            grad_probs = dot_t(grad_bd, value)
            grad_value = t_dot(probs.astype(BF16), grad_bd).astype(BF16)
            inner = jnp.sum(probs * grad_probs, -1, keepdims=True)
            grad_scores = jnp.where(allowed, probs * (grad_probs - inner), 0.0).astype(BF16)
            grad_query = (folded(dot(grad_scores, key), full) * SCALE).astype(BF16)
            grad_key = (t_dot(grad_scores, query_bd) * SCALE).astype(BF16)
            return grad_query, grad_key, grad_value

        def store(g, result):
            for n in range(3):
                packed[rows, lanes_at(g, 128, n * width)] = result[n]

        each_few(width // 128, GROUPS, load, compute, store)

    for p in range(images // 2):
        pair(p)
        between(1)


def channel_back(packed, images, mix, grad_gram, valid, grad_context, between):
    width = grad_context.shape[1]

    def pair(p):
        rows = rows_at(p, PAIR)
        one, two = image_halves(BF16)
        ok = valid[rows, :] * SCALE
        first = pl.ds(pl.multiple_of(64 * p, 32), 32)
        second = pl.ds(pl.multiple_of(64 * p + 32, 32), 32)

        def both(ref, at, axis):
            return jnp.concatenate(
                [unfold_heads(ref[first, at]), unfold_heads(ref[second, at])], axis=axis
            ).astype(BF16)

        def split(value):
            return jnp.concatenate([value * one, value * two], axis=1)

        def load(g):
            at = lanes_at(g, 128)
            values = [packed[rows, lanes_at(g, 128, n * width)] for n in range(1, 3)]
            return values + [grad_context[rows, at], both(mix, at, 1), both(grad_gram, at, 0), both(grad_gram, at, 1)]

        def compute(key, value, grad, mixing, grad_tall, grad_wide):
            grad_query = dot_t(split(grad), mixing).astype(BF16)
            grad_key = (dot(split(value), grad_tall) * ok).astype(BF16)
            grad_value = (dot_t(split(key), grad_wide) * ok).astype(BF16)
            return grad_query, grad_key, grad_value

        def store(g, result):
            for n in range(3):
                packed[rows, lanes_at(g, 128, n * width)] = result[n]

        each_few(width // 128, GROUPS, load, compute, store)

    for p in range(images // 2):
        pair(p)
        if p % 3 == 2:
            between(1)


ORDER = (20, 21, 22, 23, 16, 17, 18, 19, 15, 12, 13, 14, 8, 9, 10, 11, 4, 5, 6, 7, 3, 0, 1, 2)
RING = 4
AHEAD_SUMS = 1
HELD = 12
WAIT = 2


def backward_kernel(
    images,
    width,
    hidden,
    sizes,
    cotangent,
    vec,
    i_pad,
    i_stream,
    i_normed,
    i_packed,
    i_context,
    i_act,
    i_slope,
    i_mix,
    i_w,
    patches_grad,
    tiny,
    g_qkv,
    g_proj,
    g_hid,
    g_out,
    grad,
    grad_pad,
    pad,
    stream,
    normed,
    packed,
    context,
    act,
    slope,
    dn,
    branch,
    gram,
    mix,
    gram_in,
    valid,
    w_wide,
    w_tall,
    row_out,
    row_in,
    col_out,
    col_in,
    go_out,
    go_in,
    held,
    x_in,
    y_in,
    z_in,
    part,
    part_in,
    whole,
    whole_in,
    stage,
    halo_sems,
    gram_sems,
    load_sems,
    stage_sems,
    weight_sems,
    sums_sems,
    credits,
    vecg,
    qbg,
    hbg,
    small_out,
    small_in,
    small_sum,
    small_sems,
):
    d, w, wr, wc = place()
    depth = i_w.shape[3]
    pairs = images // 2
    horizontal = (d, 2 * wr + 1 - wc)
    vertical = (d, 2 * (1 - wr) + wc)
    z, y = d // 2, d % 2
    others = [lax.rem(z + k, LINE) for k in range(1, LINE)]
    in_line = [(2 * other + y, w) for other in others]
    across = (2 * z + 1 - y, w)
    alike = [(lax.rem(d + k, 2 * LINE), w) for k in range(1, 2 * LINE)]
    windows = [(d, lax.rem(w + k, 4)) for k in range(1, 4)]
    greet(alike + windows)
    vecg[...] = jnp.zeros(vecg.shape, F32)
    left, right = side_masks(wr, wc)
    loads = {}
    half = width // 2
    rows_mine = pl.ds(pl.multiple_of(wr * (depth // 2), 16), depth // 2)
    rows_other = pl.ds(pl.multiple_of((1 - wr) * (depth // 2), 16), depth // 2)
    cols_mine = pl.ds(pl.multiple_of(wc * half, 128), half)
    cols_other = pl.ds(pl.multiple_of((1 - wc) * half, 128), half)
    chunks = len(ORDER)
    halves = [n for n in range(chunks) if n % 2 == 1]

    def post(n, kind, src, dst, peer):
        copy = remote(src, dst, sums_sems.at[n, kind], peer)
        copy.start()

    def settle(n, kind, ref):
        pltpu.make_async_copy(ref, ref, sums_sems.at[n, kind, 1]).wait()
        pltpu.make_async_copy(ref, ref, sums_sems.at[n, kind, 0]).wait()

    def credit(n, kind, peer):
        if n + RING < chunks:
            pl.semaphore_signal(credits.at[kind], inc=1, device_id=peer, device_id_type=MESH)

    def take_credit(n, kind):
        if n >= RING:
            pl.semaphore_wait(credits.at[kind], 1)

    def open_sum(n):
        take_credit(n, 0)
        post(n, 0, go_out.at[n % RING], go_in.at[n % RING], horizontal)

    def sum_cores(upto):
        for n in range(cored[0], upto):
            s, h = n % RING, n % HELD
            settle(n, 0, go_in.at[s])

            def add(i):
                held[h, i // 2, i % 2] = held[h, i // 2, i % 2] + go_in[s, i // 2, i % 2]

            each(2 * LINE, add)
            credit(n, 0, horizontal)
        cored[0] = max(cored[0], upto)

    def leave_chip(n):
        sum_cores(n + 1)
        s, h = n % RING, n % HELD
        if n in halves:
            if n >= RING:
                pl.semaphore_wait(credits.at[1], 1)
            post(n, 1, held.at[h, :, :, rows_other], x_in.at[s], vertical)
        else:
            take_credit(n, 8)
            post(n, 2, held.at[h, :, 1 - y], y_in.at[s], across)

    def sum_x(n):
        if n not in halves:
            return
        s, h = n % RING, n % HELD
        settle(n, 1, x_in.at[s])

        def add(i):
            held[h, i // 2, i % 2, rows_mine] = held[h, i // 2, i % 2, rows_mine] + x_in[s, i // 2, i % 2]

        each(2 * LINE, add)
        credit(n, 1, vertical)
        take_credit(n, 2)
        post(n, 2, held.at[h, :, 1 - y, rows_mine], y_in.at[s, :, 0 : depth // 2], across)

    def share(n):
        return (rows_mine, depth // 2) if n in halves else (pl.ds(0, depth), depth)

    def sum_y(n):
        s, h = n % RING, n % HELD
        rows, count = share(n)
        settle(n, 2, y_in.at[s, :, 0:count])

        def add(i):
            held[h, i, y, rows] = held[h, i, y, rows] + y_in[s, i, 0:count]

        each(LINE, add)
        credit(n, 2 if n in halves else 8, across)
        for k in range(LINE - 1):
            take_credit(n, 3 + k)
        for k, (other, peer) in enumerate(zip(others, in_line)):
            post(n, 3, held.at[h, other, y, rows], z_in.at[s, LINE - 2 - k, 0:count], peer)

    def sum_z(n):
        s, h = n % RING, n % HELD
        rows, count = share(n)
        settle(n, 3, z_in.at[s, :, 0:count])
        total = held[h, z, y, rows].astype(F32)
        for k in range(LINE - 1):
            total = total + z_in[s, k, 0:count].astype(F32)
        part[s, rows] = total.astype(BF16)
        for k, peer in enumerate(in_line):
            credit(n, 3 + LINE - 2 - k, peer)
        take_credit(n, 6)
        post(n, 4, part.at[s, rows], part_in.at[s, rows], vertical)

    def sum_windows_x(n):
        s = n % RING
        if n in halves:
            settle(n, 4, part_in.at[s, rows_other])
            whole[s, rows_mine] = part[s, rows_mine]
            whole[s, rows_other] = part_in[s, rows_other]
        else:
            settle(n, 4, part_in.at[s])
            whole[s] = part[s] + part_in[s]
        credit(n, 6, vertical)
        take_credit(n, 7)
        post(n, 5, whole.at[s], whole_in.at[s], horizontal)

    def result_of(n):
        layer, j = ORDER[n] // 12, ORDER[n] % 12
        if j < 3:
            return g_qkv.at[layer, :, pl.ds(j * width, width)]
        if j < 4:
            return g_proj.at[layer]
        if j < 8:
            return g_hid.at[layer, :, pl.ds((j - 4) * width, width)]
        return g_out.at[layer, pl.ds((j - 8) * depth, depth)]

    def write_out(n):
        return pltpu.make_async_copy(stage.at[n % RING], result_of(n), stage_sems.at[n % RING])

    def finish(n):
        s = n % RING
        settle(n, 5, whole_in.at[s])
        if n >= RING:
            write_out(n - RING).wait()
        stage[s, :, cols_mine] = whole[s].astype(F32)
        stage[s, :, cols_other] = whole_in[s].astype(F32)
        credit(n, 7, horizontal)
        write_out(n).start()

    stages = (leave_chip, sum_x, sum_y, sum_z, sum_windows_x, finish)
    made, clock, cored = [0], [0], [0]

    def turn():
        for lag in reversed(range(len(stages))):
            n = clock[0] - lag * WAIT
            if 0 <= n < chunks:
                stages[lag](n)
        clock[0] += 1

    def pump(count):
        for _ in range(2 * count if made[0] == chunks else count):
            if clock[0] < made[0] - AHEAD_SUMS or (made[0] == chunks and clock[0] < chunks + len(stages) * WAIT):
                turn()

    def room(count):
        sum_cores(made[0] + count - RING)
        while made[0] + count - HELD > clock[0] - 3 * WAIT:
            turn()

    def opened(count):
        for n in range(made[0], made[0] + count):
            open_sum(n)
        made[0] += count

    def pair_of_halves(dy, base):
        theirs = dy[:, pl.ds(pl.multiple_of(base + (1 - wc) * half, 128), half)]
        ours = dy[:, pl.ds(pl.multiple_of(base + wc * half, 128), half)]
        return jnp.concatenate([theirs, ours], axis=1)

    def weight_grad(x, dy):
        for j in range(dy.shape[1] // width):
            room(1)
            s, h = made[0] % RING, made[0] % HELD

            def tile(q):
                both = t_dot(x[:, lanes_at(q, 4 * depth)], pair_of_halves(dy, j * width)).astype(BF16)
                go_out[s, rows_at(q, 2)] = both[:, :half].reshape(2, 2, depth, half)
                held[h, rows_at(q, 2)] = both[:, half:].reshape(2, 2, depth, half)

            each(LINE // 2, tile)
            opened(1)
        pump(1)

    def tall_weight_grad(x, dy):
        room(4)
        slots = [(n % RING, n % HELD) for n in range(made[0], made[0] + 4)]

        def tile(i):
            both = t_dot(x[:, lanes_at(i, 4 * depth)], pair_of_halves(dy, 0)).astype(BF16)
            for j, (s, h) in enumerate(slots):
                block = both[j * depth : (j + 1) * depth]
                go_out[s, i // 2, i % 2] = block[:, :half]
                held[h, i // 2, i % 2] = block[:, half:]

        each(2 * LINE, tile)
        opened(4)
        pump(1)

    def load(name, src, dst, s):
        loads[name] = pltpu.make_async_copy(src, dst, load_sems.at[s])
        loads[name].start()

    def load_weights(t):
        j = t % 12
        if j < 3:
            dst = w_wide.at[:, :, :, pl.ds(j * width, width)]
        elif j < 4:
            dst = w_tall.at[:, :, 0]
        elif j < 8:
            dst = w_wide.at[:, :, :, pl.ds((j - 4) * width, width)]
        else:
            dst = w_tall.at[:, :, j - 8]
        return pltpu.make_async_copy(i_w.at[t], dst, weight_sems.at[t])

    def chunks_of(name):
        first = {"wq": 0, "wp": 3, "wh": 4, "wo": 8}[name[:2]] + 12 * int(name[2])
        return range(first, first + {"wq": 3, "wp": 1, "wh": 4, "wo": 4}[name[:2]])

    def fetch(name):
        for t in chunks_of(name):
            load_weights(t).start()

    def fetched(name):
        for t in chunks_of(name):
            load_weights(t).wait()

    load("cotangent", cotangent, branch, 1)
    load("act", i_act.at[1], act, 0)
    fetch("wo1")
    load("slope", i_slope.at[1], slope, 2)
    fetch("wh1")
    load("normed", i_normed.at[3], normed, 4)
    load("stream", i_stream.at[3], stream, 5)
    load("context", i_context.at[1], context, 6)
    load("packed", i_packed.at[1], packed, 7)
    load("mix", i_mix, mix, 8)
    load("pad", i_pad.at[2], pad, 9)
    fill_valid(valid, sizes, images, wr, wc)
    clear_borders(grad_pad, images)

    loads["cotangent"].wait()

    def enter(p):
        rows = rows_at(p, PAIR)
        grad[rows, :] = branch[rows, :].astype(F32) * spread(valid[rows, :], width)

    each(pairs, enter)

    def make_branch(row):
        def one(p):
            rows = rows_at(p, PAIR)
            branch[rows, :] = (grad[rows, :] * spread(valid[rows, :], width)).astype(BF16)

        each(pairs, one)

        def store(at, total):
            vecg[row : row + 1, at] = total

        column_sums(branch, images, 256, store)

    def feed_forward(k):
        make_branch(40 + k)
        loads["act"].wait()
        tall_weight_grad(act, branch)
        fetched(f"wo{k}")
        loads["slope"].wait()

        def tile(j):
            at = lanes_at(j, 4 * depth)
            dact = dot_t(branch[...], w_tall[j // 2, j % 2].reshape(4 * depth, width))
            slope[:, at] = (slope[:, at].astype(F32) * dact).astype(BF16)

        for part in range(2):
            each(LINE, lambda j: tile(LINE * part + j))
            pump(1)

        def store(at, total):
            hbg[k : k + 1, at] = total

        column_sums(slope, images, 256, store)
        fetched(f"wh{k}")

        def tile2(j):
            block = w_wide[rows_at(j, 2)].reshape(4 * depth, hidden)
            dn[:, lanes_at(j, 4 * depth)] = dot_t(slope[...], block)

        each(LINE // 2, tile2)
        pump(1)
        loads["stream"].wait()
        norm_back(stream, images, vec, 1 + 2 * k, dn, grad, vecg)
        pump(1)

    def hidden_grad():
        loads["normed"].wait()
        weight_grad(normed, slope)

    def proj_grad():
        loads["context"].wait()
        weight_grad(context, branch)

    def qkv_grad():
        loads["normed"].wait()
        weight_grad(normed, packed)

    grad_context = act.at[:, pl.ds(0, width)]

    def proj(k):
        make_branch(38 + k)
        pump(1)
        fetched(f"wp{k}")

        def tile(j):
            block = w_tall[rows_at(j, 2), :, 0].reshape(4 * depth, width)
            grad_context[:, lanes_at(j, 4 * depth)] = dot_t(branch[...], block).astype(BF16)

        each(LINE // 2, tile)

    def qkv(k):
        def store(at, total):
            qbg[k : k + 1, at] = total

        column_sums(packed, images, 256, store)
        fetched(f"wq{k}")

        def tile(j):
            block = w_wide[rows_at(j, 2), :, :, 0 : 3 * width].reshape(4 * depth, 3 * width)
            dn[:, lanes_at(j, 4 * depth)] = dot_t(packed[...], block)

        pump(1)
        each(LINE // 2, tile)
        loads["stream"].wait()
        pump(1)
        norm_back(stream, images, vec, 2 * k, dn, grad, vecg)
        pump(1)

    def convolve(k, *flights):
        def enter_pad(p):
            to_pad(grad_pad, p, grad[rows_at(p, PAIR), :])

        each(pairs, enter_pad)
        halo(grad_pad, images, wr, wc, row_out.at[k], row_in.at[k], col_out.at[k], col_in.at[k], halo_sems.at[k], vertical, horizontal, flights)
        loads["pad"].wait()
        conv_back(grad_pad, pad, images, vec, k, valid, grad, vecg, left, right, pump)

    def idle():
        pump(1)

    feed_forward(1)
    fetch("wp1")
    fetch("wq1")
    load("stream", i_stream.at[2], stream, 5)
    proj(1)
    fetch("wo0")
    loads["packed"].wait()
    pump(1)
    pair_grams(packed, 0, grad_context, 0, images, valid, gram)
    pump(1)

    def beside():
        hidden_grad()
        proj_grad()

    sum_windows(gram, gram_in, images, wc, gram_sems, vertical, horizontal, (idle, beside, idle))
    load("slope", i_slope.at[0], slope, 2)
    load("normed", i_normed.at[2], normed, 4)
    load("context", i_context.at[0], context, 6)
    loads["mix"].wait()

    def harden(i):
        rows = rows_at(i, 32)
        y, g = mix[rows, :], gram[rows, :]
        gram[rows, :] = y * (g - jnp.sum(y * g, 0, keepdims=True))

    each(images, harden)
    channel_back(packed, images, mix, gram, valid, grad_context, pump)
    load("act", i_act.at[0], act, 0)
    qkv(1)
    fetch("wh0")
    load("stream", i_stream.at[1], stream, 5)
    convolve(2, qkv_grad, idle)
    load("pad", i_pad.at[1], pad, 9)
    load("packed", i_packed.at[0], packed, 7)
    load("normed", i_normed.at[1], normed, 4)
    feed_forward(0)
    fetch("wp0")
    fetch("wq0")
    load("stream", i_stream.at[0], stream, 5)
    convolve(1, hidden_grad, idle)
    load("pad", i_pad.at[0], pad, 9)
    load("normed", i_normed.at[0], normed, 4)
    proj(0)
    proj_grad()
    loads["packed"].wait()
    window_back(packed, images, sizes, wr, wc, grad_context, pump)
    qkv_grad()
    qkv(0)
    convolve(0, idle, idle)

    def leave(p):
        rows = rows_at(p, PAIR)
        branch[rows, :] = grad[rows, :].astype(BF16)

    each(pairs, leave)
    load("end", branch, patches_grad, 1)
    pack_small(vecg, qbg, hbg, small_out)
    small_in[d] = small_out[d]
    for peer in alike:
        remote(small_out.at[peer[0]], small_in.at[d], small_sems.at[0], peer).start()
    while clock[0] < chunks + (len(stages) - 2) * WAIT:
        turn()
    for n in (1, 0):
        seven = small_in.at[pl.ds(0, 2 * LINE - 1)]
        pltpu.make_async_copy(seven, seven, small_sems.at[0, n]).wait()
    total = small_in[0]
    for k in range(1, 2 * LINE):
        total = total + small_in[k]
    small_sum[w] = total
    for peer in windows:
        remote(small_sum.at[w], small_sum.at[w], small_sems.at[1], peer).start()
    while clock[0] < chunks + len(stages) * WAIT:
        turn()
    for n in (1, 0):
        three_of = small_sum.at[pl.ds(0, 3)]
        pltpu.make_async_copy(three_of, three_of, small_sems.at[1, n]).wait()
    tiny[...] = ((small_sum[0] + small_sum[1]) + small_sum[2]) + small_sum[3]
    for n in range(chunks - RING, chunks):
        write_out(n).wait()
    loads["end"].wait()


def run_backward(sizes, cotangent, vec, saved, weights, hidden):
    images = sizes.shape[0]
    depth = weights.shape[3]
    n_rows, width = cotangent.shape
    lines = images * 72
    shapes = (
        ((n_rows, width), BF16),
        ((ROWS_SMALL, 128), F32),
        ((2, depth, 3 * width), F32),
        ((2, depth, width), F32),
        ((2, depth, hidden), F32),
        ((2, 4 * depth, width), F32),
    )
    half = width // 2
    return pl.pallas_call(
        functools.partial(backward_kernel, images, width, hidden),
        out_shape=[jax.ShapeDtypeStruct(*s) for s in shapes],
        in_specs=[SMEM, ANY, VMEM] + [ANY] * 9,
        out_specs=[ANY, VMEM] + [ANY] * 4,
        scratch_shapes=[
            pltpu.VMEM((n_rows, width), F32),
            pltpu.VMEM((lines, width), F32),
            pltpu.VMEM((lines, width), F32),
            pltpu.VMEM((n_rows, width), F32),
            pltpu.VMEM((n_rows, width), BF16),
            pltpu.VMEM((n_rows, 3 * width), BF16),
            pltpu.VMEM((n_rows, width), BF16),
            pltpu.VMEM((n_rows, hidden), BF16),
            pltpu.VMEM((n_rows, hidden), BF16),
            pltpu.VMEM((n_rows, width), F32),
            pltpu.VMEM((n_rows, width), BF16),
            pltpu.VMEM((images * 32, width), F32),
            pltpu.VMEM((images * 32, width), F32),
            pltpu.VMEM((3, images * 16, width), F32),
            pltpu.VMEM((n_rows, 128), F32),
            pltpu.VMEM((LINE, 2, depth, hidden), BF16),
            pltpu.VMEM((LINE, 2, 4, depth, width), BF16),
            pltpu.VMEM((3, images * 8, width), BF16),
            pltpu.VMEM((3, images * 8, width), BF16),
            pltpu.VMEM((3, images * 8, width), BF16),
            pltpu.VMEM((3, images * 8, width), BF16),
            pltpu.VMEM((RING, LINE, 2, depth, half), BF16),
            pltpu.VMEM((RING, LINE, 2, depth, half), BF16),
            pltpu.VMEM((HELD, LINE, 2, depth, half), BF16),
            pltpu.VMEM((RING, LINE, 2, depth // 2, half), BF16),
            pltpu.VMEM((RING, LINE, depth, half), BF16),
            pltpu.VMEM((RING, LINE - 1, depth, half), BF16),
            pltpu.VMEM((RING, depth, half), BF16),
            pltpu.VMEM((RING, depth, half), BF16),
            pltpu.VMEM((RING, depth, half), BF16),
            pltpu.VMEM((RING, depth, half), BF16),
            pltpu.VMEM((RING, depth, width), F32),
            pltpu.SemaphoreType.DMA((3, 2, 2)),
            pltpu.SemaphoreType.DMA((3, 2)),
            pltpu.SemaphoreType.DMA((10,)),
            pltpu.SemaphoreType.DMA((RING,)),
            pltpu.SemaphoreType.DMA((24,)),
            pltpu.SemaphoreType.DMA((24, 6, 2)),
            pltpu.SemaphoreType.REGULAR((9,)),
            pltpu.VMEM((48, width), F32),
            pltpu.VMEM((8, 3 * width), F32),
            pltpu.VMEM((8, hidden), F32),
            pltpu.VMEM((2 * LINE, ROWS_SMALL, 128), F32),
            pltpu.VMEM((2 * LINE, ROWS_SMALL, 128), F32),
            pltpu.VMEM((4, ROWS_SMALL, 128), F32),
            pltpu.SemaphoreType.DMA((2, 2)),
        ],
        compiler_params=pltpu.CompilerParams(
            collective_id=1, has_side_effects=True, vmem_limit_bytes=60 * 2**20
        ),
    )(sizes, cotangent, vec, *saved, weights)


def to_cells(windows):
    images, _, _, width = windows.shape
    grid = windows.reshape(images, 7, 7, width)
    return jnp.pad(grid, ((0, 0), (0, 0), (0, 1), (0, 0))).reshape(images * CELLS, width)


def of_cells(rows, images):
    width = rows.shape[1]
    return rows.reshape(images, 7, 8, width)[:, :, :7].reshape(images, 1, 49, width)


def on_device_fast(
    patches,
    cotangent,
    grid_sizes,
    conv_weight,
    conv_bias,
    norm_gain,
    norm_bias,
    qkv_weight,
    spatial_bias,
    channel_bias,
    proj_weight,
    proj_bias,
    hidden_weight,
    hidden_bias,
    output_weight,
    output_bias,
):
    images = patches.shape[0]
    hidden = hidden_weight.shape[2]
    small = (
        conv_weight, conv_bias, norm_gain, norm_bias, proj_bias, output_bias, spatial_bias, channel_bias, hidden_bias
    )
    rows = jnp.concatenate([a.reshape(-1, SHORT) for a in small], axis=0)
    rows = jnp.pad(rows, ((0, ROWS_SMALL - rows.shape[0]), (0, 128 - SHORT)))
    weights = (qkv_weight, proj_weight, hidden_weight, output_weight)
    forward = run_forward(grid_sizes, to_cells(patches), rows, weights)
    activations, gathered_weights, vec, *saved = forward
    back = run_backward(grid_sizes, to_cells(cotangent), vec, saved, gathered_weights, hidden)
    grads, tiny, g_qkv, g_proj, g_hid, g_out = back
    tiny = tiny[:, :SHORT]
    return (
        of_cells(activations, images),
        of_cells(grads, images),
        tiny[:27].reshape(3, 9, SHORT),
        tiny[27:30],
        tiny[30:34],
        tiny[34:38],
        g_qkv,
        tiny[42:44].reshape(-1),
        tiny[44:47].reshape(-1),
        g_proj,
        tiny[38:40],
        g_hid,
        tiny[47:55].reshape(2, -1),
        g_out,
        tiny[40:42],
    )


def as_sent(array):
    return jax.tree.map(lambda a: a.astype(jnp.bfloat16) if a.dtype == jnp.float32 else a, array)


def image_valid(grid_sizes):
    rows = jnp.arange(7, dtype=jnp.int32)
    windows = jnp.arange(4, dtype=jnp.int32)
    top_rows = (windows // 2)[:, None] * 7 + rows[None, :]
    left_cols = (windows % 2)[:, None] * 7 + rows[None, :]
    sizes = grid_sizes[:, None, None, None]
    inside = (top_rows[None, :, :, None] < sizes) & (left_cols[None, :, None, :] < sizes)
    return inside.astype(jnp.float32).reshape(grid_sizes.shape[0], 4, 49, 1)


def layer_norm(stream, gain_row, shift_row):
    centre = jnp.mean(stream, -1, keepdims=True)
    centered = stream - centre
    variance = jnp.mean(centered * centered, -1, keepdims=True)
    return centered * lax.rsqrt(variance + EPS) * gain_row + shift_row


def gelu_exact(value_in):
    return jax.nn.gelu(value_in, approximate=False)


def matmul(left_rows, right_mat):
    return jnp.dot(left_rows, right_mat, preferred_element_type=jnp.float32)


def contract_rows(left_rows, right_rows):
    return lax.dot_general(
        left_rows, right_rows, (((0,), (0,)), ((), ())), preferred_element_type=jnp.float32
    )


def times_transposed(grad_rows, weight):
    return lax.dot_general(
        grad_rows, weight, (((1,), (1,)), ((), ())), preferred_element_type=jnp.float32
    )


def edge_lines(stream, images):
    channels = stream.shape[-1]
    image_grid = stream.reshape(images, 7, 7, channels)
    return jnp.stack(
        [image_grid[:, 0], image_grid[:, 6], image_grid[:, :, 0], image_grid[:, :, 6]], 1
    )[None]


def padded_tile(image_grid, lines, row_half, col_half):
    zero_line = jnp.zeros_like(lines[0, :, 0])
    upper = jnp.where(
        row_half == 1, jnp.where(col_half == 0, lines[0, :, 1], lines[1, :, 1]), zero_line
    )
    lower = jnp.where(
        row_half == 0, jnp.where(col_half == 0, lines[2, :, 0], lines[3, :, 0]), zero_line
    )
    left_side = jnp.where(
        col_half == 1, jnp.where(row_half == 0, lines[0, :, 3], lines[2, :, 3]), zero_line
    )
    right_side = jnp.where(
        col_half == 0, jnp.where(row_half == 0, lines[1, :, 2], lines[3, :, 2]), zero_line
    )
    zero_cell = zero_line[:, 0]
    top_left = jnp.where((row_half == 1) & (col_half == 1), lines[0, :, 1, 6], zero_cell)
    top_right = jnp.where((row_half == 1) & (col_half == 0), lines[1, :, 1, 0], zero_cell)
    bottom_left = jnp.where((row_half == 0) & (col_half == 1), lines[2, :, 0, 6], zero_cell)
    bottom_right = jnp.where((row_half == 0) & (col_half == 0), lines[3, :, 0, 0], zero_cell)
    middle = jnp.concatenate([left_side[:, :, None], image_grid, right_side[:, :, None]], 2)
    top_row = jnp.concatenate([top_left[:, None], upper, top_right[:, None]], 1)
    bottom_row = jnp.concatenate([bottom_left[:, None], lower, bottom_right[:, None]], 1)
    return jnp.concatenate([top_row[:, None], middle, bottom_row[:, None]], 1)


def position_conv(stream, images, window, weight9, shift_row, valid_rows):
    channels = stream.shape[-1]
    lines = lax.all_gather(as_sent(edge_lines(stream, images)), "win", axis=0, tiled=True)
    padded = padded_tile(stream.reshape(images, 7, 7, channels), lines, window // 2, window % 2)
    summed = jnp.zeros((images, 7, 7, channels), jnp.float32)
    for tap_index in range(9):
        row_shift, col_shift = divmod(tap_index, 3)
        summed = (
            summed
            + weight9[tap_index] * padded[:, row_shift : row_shift + 7, col_shift : col_shift + 7]
        )
    return (stream + valid_rows * (summed + shift_row).reshape(images * 49, channels), padded)


def position_conv_back(grad_stream, padded, images, window, weight9, valid_rows):
    channels = grad_stream.shape[-1]
    masked = valid_rows * grad_stream
    lines = lax.all_gather(as_sent(edge_lines(masked, images)), "win", axis=0, tiled=True)
    image_grid = masked.reshape(images, 7, 7, channels)
    grad_pad = padded_tile(image_grid, lines, window // 2, window % 2)
    summed = jnp.zeros((images, 7, 7, channels), jnp.float32)
    tap_grads = []
    for tap_index in range(9):
        row_shift, col_shift = divmod(tap_index, 3)
        summed = (
            summed
            + weight9[tap_index]
            * grad_pad[:, 2 - row_shift : 9 - row_shift, 2 - col_shift : 9 - col_shift]
        )
        tap_grads.append(
            jnp.sum(
                image_grid * padded[:, row_shift : row_shift + 7, col_shift : col_shift + 7],
                axis=(0, 1, 2),
            )
        )
    return (
        grad_stream + summed.reshape(grad_stream.shape),
        jnp.stack(tap_grads),
        jnp.sum(image_grid, axis=(0, 1, 2)),
    )


def mlp_forward(normed, weight_in, bias_in, weight_out, bias_out):
    activated = gelu_exact(matmul(normed, weight_in) + bias_in).astype(jnp.bfloat16)
    return matmul(activated, weight_out) + bias_out


def mlp_backward(normed, grad_stream, valid_rows, weight_in, bias_in, weight_out):
    hidden_pre = matmul(normed, weight_in) + bias_in
    activated, gelu_pull = jax.vjp(gelu_exact, hidden_pre)
    grad_branch = (valid_rows * grad_stream).astype(jnp.bfloat16)
    grad_weight_out = contract_rows(activated.astype(jnp.bfloat16), grad_branch)
    grad_bias_out = jnp.sum(grad_branch.astype(jnp.float32), 0)
    grad_pre = gelu_pull(times_transposed(grad_branch, weight_out))[0].astype(jnp.bfloat16)
    grad_weight_in = contract_rows(normed, grad_pre)
    grad_bias_in = jnp.sum(grad_pre.astype(jnp.float32), 0)
    return (
        times_transposed(grad_pre, weight_in),
        grad_weight_in,
        grad_bias_in,
        grad_weight_out,
        grad_bias_out,
    )


def norm_backward(stream, gain_row, shift_row, grad_normed):
    unused, norm_pull = jax.vjp(layer_norm, stream, gain_row, shift_row)
    return norm_pull(grad_normed)


def window_probs(packed, images, scaling, valid_rows):
    split = packed.reshape(images, 49, 3, HEADS, HEAD)
    query_rows = split[:, :, 0]
    key_rows = split[:, :, 1]
    value_rows = split[:, :, 2]
    key_ok = valid_rows.reshape(images, 1, 1, 49) > 0.5
    scores = (
        jnp.einsum("iphe,iqhe->ihpq", query_rows, key_rows, preferred_element_type=jnp.float32)
        * scaling
    )
    scores = jnp.where(key_ok, scores, -1000000000.0)
    return (query_rows, key_rows, value_rows, jax.nn.softmax(scores, axis=-1))


def channel_mixing(gram_total, scaling):
    return jax.nn.softmax(gram_total * scaling, axis=-1)


def channel_grads(
    grad_mixing, mixing, grad_context, key_masked, value_masked, valid_cells, scaling
):
    grad_query = jnp.einsum(
        "bgcd,bpgc->bpgd",
        mixing.astype(jnp.bfloat16),
        grad_context,
        preferred_element_type=jnp.float32,
    )
    grad_gram = (mixing * (grad_mixing - jnp.sum(mixing * grad_mixing, -1, keepdims=True))).astype(
        jnp.bfloat16
    )
    grad_keys = (
        jnp.einsum("bgcd,bpgd->bpgc", grad_gram, value_masked, preferred_element_type=jnp.float32)
        * scaling
        * valid_cells
    )
    grad_values = (
        jnp.einsum("bgcd,bpgc->bpgd", grad_gram, key_masked, preferred_element_type=jnp.float32)
        * scaling
        * valid_cells
    )
    return jnp.stack([grad_query, grad_keys, grad_values], 2).astype(jnp.bfloat16)


def on_device(
    patches,
    cotangent,
    grid_sizes,
    conv_weight,
    conv_bias,
    norm_gain,
    norm_bias,
    qkv_weight,
    spatial_bias,
    channel_bias,
    proj_weight,
    proj_bias,
    hidden_weight,
    hidden_bias,
    output_weight,
    output_bias,
):
    (
        conv_w,
        conv_b,
        gains,
        shifts,
        qkv_w,
        sp_bias,
        ch_bias,
        proj_w,
        proj_b,
        hid_w,
        hid_b,
        out_w,
        out_b,
    ) = (
        lax.all_gather(conv_weight, "dp", axis=2, tiled=True),
        lax.all_gather(conv_bias, "dp", axis=1, tiled=True),
        lax.all_gather(norm_gain, "dp", axis=1, tiled=True),
        lax.all_gather(norm_bias, "dp", axis=1, tiled=True),
        lax.all_gather(qkv_weight, "dp", axis=1, tiled=True),
        lax.all_gather(spatial_bias, "dp", axis=0, tiled=True),
        lax.all_gather(channel_bias, "dp", axis=0, tiled=True),
        lax.all_gather(proj_weight, "dp", axis=1, tiled=True),
        lax.all_gather(proj_bias, "dp", axis=1, tiled=True),
        lax.all_gather(hidden_weight, "dp", axis=1, tiled=True),
        lax.all_gather(hidden_bias, "dp", axis=1, tiled=True),
        lax.all_gather(output_weight, "dp", axis=1, tiled=True),
        lax.all_gather(output_bias, "dp", axis=1, tiled=True),
    )
    conv_w = conv_w.astype(jnp.float32)
    conv_b = conv_b.astype(jnp.float32)
    gains = gains.astype(jnp.float32)
    shifts = shifts.astype(jnp.float32)
    sp_bias = sp_bias.astype(jnp.float32)
    ch_bias = ch_bias.astype(jnp.float32)
    proj_b = proj_b.astype(jnp.float32)
    hid_b = hid_b.astype(jnp.float32)
    out_b = out_b.astype(jnp.float32)
    images = patches.shape[0]
    model_width = patches.shape[-1]
    rows_all = images * 49
    group_count = lax.axis_size("win")
    local_heads = HEADS // group_count
    group_width = model_width // group_count
    scaling = HEAD ** (-0.5)
    window = lax.axis_index("win")
    full_valid = image_valid(grid_sizes)
    valid_rows = lax.dynamic_slice_in_dim(full_valid, window, 1, 1).reshape(rows_all, 1)
    stream0 = patches.astype(jnp.float32).reshape(rows_all, model_width) * valid_rows
    stream1, pad_first = position_conv(stream0, images, window, conv_w[0], conv_b[0], valid_rows)
    normed1 = layer_norm(stream1, gains[0], shifts[0]).astype(jnp.bfloat16)
    packed_bias = jnp.concatenate(
        [sp_bias[:model_width], jnp.zeros((model_width,), jnp.float32), sp_bias[model_width:]]
    )
    packed1 = (matmul(normed1, qkv_w[0]) + packed_bias).astype(jnp.bfloat16)
    query1, keys1, values1, probs1 = window_probs(packed1, images, scaling, valid_rows)
    context1 = (
        jnp.einsum(
            "ihpq,iqhe->iphe",
            probs1.astype(jnp.bfloat16),
            values1,
            preferred_element_type=jnp.float32,
        )
        .astype(jnp.bfloat16)
        .reshape(rows_all, model_width)
    )
    stream2 = stream1 + valid_rows * (matmul(context1, proj_w[0]) + proj_b[0])
    stream3, pad_second = position_conv(stream2, images, window, conv_w[1], conv_b[1], valid_rows)
    normed3 = layer_norm(stream3, gains[1], shifts[1]).astype(jnp.bfloat16)
    stream4 = stream3 + valid_rows * mlp_forward(normed3, hid_w[0], hid_b[0], out_w[0], out_b[0])
    stream5, pad_third = position_conv(stream4, images, window, conv_w[2], conv_b[2], valid_rows)
    normed5 = layer_norm(stream5, gains[2], shifts[2]).astype(jnp.bfloat16)
    packed5 = (matmul(normed5, qkv_w[1]) + ch_bias).astype(jnp.bfloat16)
    moved = lax.all_to_all(
        packed5.reshape(images, 1, 49, 3, group_count, group_width),
        "win",
        split_axis=4,
        concat_axis=1,
        tiled=True,
    )
    grouped = moved.reshape(images, 196, 3, local_heads, HEAD)
    valid_cells = full_valid.reshape(images, 196, 1, 1)
    query5 = grouped[:, :, 0]
    key_masked = grouped[:, :, 1] * valid_cells.astype(jnp.bfloat16)
    value_masked = grouped[:, :, 2] * valid_cells.astype(jnp.bfloat16)
    gram_total = jnp.einsum(
        "bpgc,bpgd->bgcd", key_masked, value_masked, preferred_element_type=jnp.float32
    )
    mixing = channel_mixing(gram_total, scaling)
    context_groups = jnp.einsum(
        "bgcd,bpgd->bpgc", mixing.astype(jnp.bfloat16), query5, preferred_element_type=jnp.float32
    ).astype(jnp.bfloat16)
    returned = lax.all_to_all(
        context_groups.reshape(images, 4, 49, 1, group_width),
        "win",
        split_axis=1,
        concat_axis=3,
        tiled=True,
    )
    context5 = returned.reshape(rows_all, model_width)
    stream6 = stream5 + valid_rows * (matmul(context5, proj_w[1]) + proj_b[1])
    normed6 = layer_norm(stream6, gains[3], shifts[3]).astype(jnp.bfloat16)
    stream7 = stream6 + valid_rows * mlp_forward(normed6, hid_w[1], hid_b[1], out_w[1], out_b[1])
    activations = stream7.astype(jnp.bfloat16).reshape(patches.shape)
    grad7 = cotangent.astype(jnp.float32).reshape(rows_all, model_width)
    grad_normed, hid_w_grad1, hid_b_grad1, out_w_grad1, out_b_grad1 = mlp_backward(
        normed6, grad7, valid_rows, hid_w[1], hid_b[1], out_w[1]
    )
    grad_part, gain_grad3, shift_grad3 = norm_backward(stream6, gains[3], shifts[3], grad_normed)
    grad6 = grad7 + grad_part
    branch_grad = (valid_rows * grad6).astype(jnp.bfloat16)
    proj_w_grad1 = contract_rows(context5, branch_grad)
    proj_b_grad1 = jnp.sum(branch_grad.astype(jnp.float32), 0)
    context_grad = times_transposed(branch_grad, proj_w[1]).astype(jnp.bfloat16)
    moved_grad = lax.all_to_all(
        context_grad.reshape(images, 1, 49, group_count, group_width),
        "win",
        split_axis=3,
        concat_axis=1,
        tiled=True,
    )
    group_grad = moved_grad.reshape(images, 196, local_heads, HEAD)
    mixing_grad = jnp.einsum(
        "bpgc,bpgd->bgcd", group_grad, query5, preferred_element_type=jnp.float32
    )
    stacked = channel_grads(
        mixing_grad, mixing, group_grad, key_masked, value_masked, valid_cells, scaling
    )
    sent_back = lax.all_to_all(
        stacked.reshape(images, 4, 49, 3, 1, group_width),
        "win",
        split_axis=1,
        concat_axis=4,
        tiled=True,
    )
    packed_grad5 = sent_back.reshape(rows_all, 3 * model_width)
    qkv_w_grad1 = contract_rows(normed5, packed_grad5)
    ch_bias_grad = jnp.sum(packed_grad5.astype(jnp.float32), 0)
    grad_part, gain_grad2, shift_grad2 = norm_backward(
        stream5, gains[2], shifts[2], times_transposed(packed_grad5, qkv_w[1])
    )
    grad5 = grad6 + grad_part
    grad4, conv_w_grad2, conv_b_grad2 = position_conv_back(
        grad5, pad_third, images, window, conv_w[2], valid_rows
    )
    grad_normed, hid_w_grad0, hid_b_grad0, out_w_grad0, out_b_grad0 = mlp_backward(
        normed3, grad4, valid_rows, hid_w[0], hid_b[0], out_w[0]
    )
    grad_part, gain_grad1, shift_grad1 = norm_backward(stream3, gains[1], shifts[1], grad_normed)
    grad3 = grad4 + grad_part
    grad2, conv_w_grad1, conv_b_grad1 = position_conv_back(
        grad3, pad_second, images, window, conv_w[1], valid_rows
    )
    branch_grad = (valid_rows * grad2).astype(jnp.bfloat16)
    proj_w_grad0 = contract_rows(context1, branch_grad)
    proj_b_grad0 = jnp.sum(branch_grad.astype(jnp.float32), 0)
    context_grad = (
        times_transposed(branch_grad, proj_w[0])
        .astype(jnp.bfloat16)
        .reshape(images, 49, HEADS, HEAD)
    )
    probs_low = probs1.astype(jnp.bfloat16)
    probs_grad = jnp.einsum(
        "iphe,iqhe->ihpq", context_grad, values1, preferred_element_type=jnp.float32
    )
    values_grad = jnp.einsum(
        "ihpq,iphe->iqhe", probs_low, context_grad, preferred_element_type=jnp.float32
    )
    scores_grad = (probs1 * (probs_grad - jnp.sum(probs1 * probs_grad, -1, keepdims=True))).astype(
        jnp.bfloat16
    )
    key_ok = valid_rows.reshape(images, 1, 1, 49) > 0.5
    scores_grad = jnp.where(key_ok, scores_grad, jnp.zeros_like(scores_grad))
    query_grad = (
        jnp.einsum("ihpq,iqhe->iphe", scores_grad, keys1, preferred_element_type=jnp.float32)
        * scaling
    )
    keys_grad = (
        jnp.einsum("ihpq,iphe->iqhe", scores_grad, query1, preferred_element_type=jnp.float32)
        * scaling
    )
    packed_grad1 = (
        jnp.stack([query_grad, keys_grad, values_grad], 2)
        .astype(jnp.bfloat16)
        .reshape(rows_all, 3 * model_width)
    )
    qkv_w_grad0 = contract_rows(normed1, packed_grad1)
    packed_sums = jnp.sum(packed_grad1.astype(jnp.float32), 0)
    sp_bias_grad = jnp.concatenate([packed_sums[:model_width], packed_sums[2 * model_width :]])
    grad_part, gain_grad0, shift_grad0 = norm_backward(
        stream1, gains[0], shifts[0], times_transposed(packed_grad1, qkv_w[0])
    )
    grad1 = grad2 + grad_part
    grad0, conv_w_grad0, conv_b_grad0 = position_conv_back(
        grad1, pad_first, images, window, conv_w[0], valid_rows
    )
    patches_grad = (grad0 * valid_rows).astype(jnp.bfloat16).reshape(patches.shape)
    local_sums = (
        lax.psum_scatter(
            jnp.stack([conv_w_grad0, conv_w_grad1, conv_w_grad2]),
            "dp",
            scatter_dimension=2,
            tiled=True,
        ),
        lax.psum_scatter(
            jnp.stack([conv_b_grad0, conv_b_grad1, conv_b_grad2]),
            "dp",
            scatter_dimension=1,
            tiled=True,
        ),
        lax.psum_scatter(
            jnp.stack([gain_grad0, gain_grad1, gain_grad2, gain_grad3]),
            "dp",
            scatter_dimension=1,
            tiled=True,
        ),
        lax.psum_scatter(
            jnp.stack([shift_grad0, shift_grad1, shift_grad2, shift_grad3]),
            "dp",
            scatter_dimension=1,
            tiled=True,
        ),
        lax.psum_scatter(
            jnp.stack([qkv_w_grad0, qkv_w_grad1]), "dp", scatter_dimension=1, tiled=True
        ),
        lax.psum_scatter(sp_bias_grad, "dp", scatter_dimension=0, tiled=True),
        lax.psum_scatter(ch_bias_grad, "dp", scatter_dimension=0, tiled=True),
        lax.psum_scatter(
            jnp.stack([proj_w_grad0, proj_w_grad1]), "dp", scatter_dimension=1, tiled=True
        ),
        lax.psum_scatter(
            jnp.stack([proj_b_grad0, proj_b_grad1]), "dp", scatter_dimension=1, tiled=True
        ),
        lax.psum_scatter(
            jnp.stack([hid_w_grad0, hid_w_grad1]), "dp", scatter_dimension=1, tiled=True
        ),
        lax.psum_scatter(
            jnp.stack([hid_b_grad0, hid_b_grad1]), "dp", scatter_dimension=1, tiled=True
        ),
        lax.psum_scatter(
            jnp.stack([out_w_grad0, out_w_grad1]), "dp", scatter_dimension=1, tiled=True
        ),
        lax.psum_scatter(
            jnp.stack([out_b_grad0, out_b_grad1]), "dp", scatter_dimension=1, tiled=True
        ),
    )
    summed = (
        lax.psum(local_sums[0].astype(jnp.bfloat16), "win").astype(jnp.float32),
        lax.psum(local_sums[1].astype(jnp.bfloat16), "win").astype(jnp.float32),
        lax.psum(local_sums[2].astype(jnp.bfloat16), "win").astype(jnp.float32),
        lax.psum(local_sums[3].astype(jnp.bfloat16), "win").astype(jnp.float32),
        lax.psum(local_sums[4].astype(jnp.bfloat16), "win").astype(jnp.float32),
        lax.psum(local_sums[5].astype(jnp.bfloat16), "win").astype(jnp.float32),
        lax.psum(local_sums[6].astype(jnp.bfloat16), "win").astype(jnp.float32),
        lax.psum(local_sums[7].astype(jnp.bfloat16), "win").astype(jnp.float32),
        lax.psum(local_sums[8].astype(jnp.bfloat16), "win").astype(jnp.float32),
        lax.psum(local_sums[9].astype(jnp.bfloat16), "win").astype(jnp.float32),
        lax.psum(local_sums[10].astype(jnp.bfloat16), "win").astype(jnp.float32),
        lax.psum(local_sums[11].astype(jnp.bfloat16), "win").astype(jnp.float32),
        lax.psum(local_sums[12].astype(jnp.bfloat16), "win").astype(jnp.float32),
    )
    return (activations, patches_grad) + tuple(summed)


def solution(mesh):
    small = mesh.shape["dp"] == 8 and mesh.shape["win"] == 4
    return jax.shard_map(
        on_device_fast if small else on_device,
        mesh=mesh,
        in_specs=(
            P("dp", "win", None, None),
            P("dp", "win", None, None),
            P("dp"),
            P(None, None, "dp"),
            P(None, "dp"),
            P(None, "dp"),
            P(None, "dp"),
            P(None, "dp", None),
            P("dp"),
            P("dp"),
            P(None, "dp", None),
            P(None, "dp"),
            P(None, "dp", None),
            P(None, "dp"),
            P(None, "dp", None),
            P(None, "dp"),
        ),
        out_specs=(
            P("dp", "win", None, None),
            P("dp", "win", None, None),
            P(None, None, "dp"),
            P(None, "dp"),
            P(None, "dp"),
            P(None, "dp"),
            P(None, "dp", None),
            P("dp"),
            P("dp"),
            P(None, "dp", None),
            P(None, "dp"),
            P(None, "dp", None),
            P(None, "dp"),
            P(None, "dp", None),
            P(None, "dp"),
        ),
        check_vma=False,
    )
```

```python
import functools

import jax
import jax.numpy as jnp
from jax import lax
from jax.experimental import pallas as pl
from jax.experimental.pallas import tpu as pltpu
from jax.sharding import PartitionSpec as P

HEADS = 24
HEAD = 32
EPS = 1e-05
MESH = pl.DeviceIdType.MESH
F32 = jnp.float32
BF16 = jnp.bfloat16
SCALE = HEAD ** (-0.5)
CELLS = 56
PAIR = 112
GROUPS = 6
BACK_GROUPS = 3


def dot(left, right):
    return jnp.dot(left, right, preferred_element_type=F32)


def dot_t(left, right):
    return lax.dot_general(left, right, (((1,), (1,)), ((), ())), preferred_element_type=F32)


def t_dot(left, right):
    return lax.dot_general(left, right, (((0,), (0,)), ((), ())), preferred_element_type=F32)


def iota(shape, dim):
    return lax.broadcasted_iota(jnp.int32, shape, dim)


def rows_at(index, count):
    return pl.ds(pl.multiple_of(index * count, count), count)


def lanes_at(index, count, base=0):
    return pl.ds(pl.multiple_of(base + index * count, 128), count)


def each(count, body):
    def step(i, carry):
        body(i)
        return carry

    lax.fori_loop(0, count, step, 0)


def each_few(count, few, load, compute, store):
    def step(n):
        inputs = [load(n * few + u) for u in range(few)]
        results = [compute(*values) for values in inputs]
        for u in range(few):
            store(n * few + u, results[u])

    each(count // few, step)


def gelu_pair(pre):
    t = 1.0 / (1.0 + 0.23164190 * jnp.abs(pre))
    e = jnp.exp(-0.5 * pre * pre)
    poly = (((1.061405429 * t - 1.453152027) * t + 1.421413741) * t - 0.284496736) * t + 0.254829592
    tail = 0.5 * poly * t * e
    cdf = jnp.where(pre >= 0.0, 1.0 - tail, tail)
    return pre * cdf, cdf + pre * (e * 0.3989422804014327)


def place():
    d = lax.axis_index("dp")
    w = lax.axis_index("win")
    return d, w, w // 2, w % 2


def greet(peers):
    barrier = pltpu.get_barrier_semaphore()
    for peer in peers:
        pl.semaphore_signal(barrier, inc=1, device_id=peer, device_id_type=MESH)
    pl.semaphore_wait(barrier, len(peers))


def remote(src, dst, sems, peer):
    return pltpu.make_async_remote_copy(
        src_ref=src, dst_ref=dst, send_sem=sems.at[0], recv_sem=sems.at[1], device_id=peer, device_id_type=MESH
    )


def fill_valid(valid, sizes, images, wr, wc):
    def one(i):
        cell = iota((CELLS, 128), 0)
        r, c = cell >> 3, cell & 7
        inside = (r + 7 * wr < sizes[i]) & (c + 7 * wc < sizes[i]) & (c < 7)
        valid[rows_at(i, CELLS), :] = jnp.where(inside, 1.0, 0.0).astype(F32)

    each(images, one)


def spread(valid_rows, width):
    return jnp.concatenate([valid_rows] * (width // 128), axis=1)


def halo(pad, images, wr, wc, row_out, row_in, col_out, col_in, sems, vertical, horizontal, flights):
    edge = 7 - 6 * wr

    def pack(p):
        one = pad[pl.ds(pl.multiple_of((18 * p + edge) * 8, 8), 8), :]
        two = pad[pl.ds(pl.multiple_of((18 * p + 9 + edge) * 8, 8), 8), :]
        row_out[rows_at(p, 16), :] = jnp.concatenate([one, two], axis=0).astype(BF16)

    each(images // 2, pack)
    copy = remote(row_out, row_in, sems.at[0], vertical)
    copy.start()
    flights[0]()
    copy.wait()
    border = 8 - 8 * wr

    def unpack(p):
        both = row_in[rows_at(p, 16), :].astype(F32)
        pad[pl.ds(pl.multiple_of((18 * p + border) * 8, 8), 8), :] = both[:8]
        pad[pl.ds(pl.multiple_of((18 * p + 9 + border) * 8, 8), 8), :] = both[8:]

    each(images // 2, unpack)
    turn = 2 - 2 * wc
    sub = iota((8, 128), 0)

    def row_of(i, s):
        at_row = border if s == 7 else s + 1
        return pl.ds(pl.multiple_of((9 * i + at_row) * 8, 8), 8)

    def pack_col(p):
        for part in range(pad.shape[1] // 128):
            at = pl.ds(part * 128, 128)
            both = []
            for i in (2 * p, 2 * p + 1):
                line = jnp.zeros((8, 128), F32)
                for s in range(8):
                    line = jnp.where(sub == s, pltpu.roll(pad[row_of(i, s), at], s + turn, 0), line)
                both.append(line)
            col_out[rows_at(p, 16), at] = jnp.concatenate(both, axis=0).astype(BF16)

    each(images // 2, pack_col)
    copy = remote(col_out, col_in, sems.at[1], horizontal)
    copy.start()
    flights[1]()
    copy.wait()

    def unpack_col(p):
        for part in range(pad.shape[1] // 128):
            at = pl.ds(part * 128, 128)
            both = col_in[rows_at(p, 16), at].astype(F32)
            for one in range(2):
                line = both[8 * one : 8 * one + 8]
                for s in range(8):
                    to = row_of(2 * p + one, s)
                    pad[to, at] = jnp.where(sub == 7, pltpu.roll(line, 7 - s, 0), pad[to, at])

    each(images // 2, unpack_col)


def side_masks(wr, wc):
    c = iota((8, 128), 0)
    left = jnp.where((c == 0) & (wc == 0), 0.0, 1.0).astype(F32)
    right = jnp.where((c == 6) & (wc == 1), 0.0, 1.0).astype(F32)
    return left, right


def three(pad, i, at, left, right):
    rows = [pad[pl.ds(pl.multiple_of((9 * i + r) * 8, 8), 8), at] for r in range(9)]
    return [(pltpu.roll(v, 1, 0) * left, v, pltpu.roll(v, 7, 0) * right) for v in rows]


def conv_forward(pad, images, vec, k, valid, out, left, right):
    def one(i):
        for part in range(pad.shape[1] // 128):
            at = pl.ds(part * 128, 128)
            moved = three(pad, i, at, left, right)
            bias = vec[27 + k : 28 + k, at]
            taps = [vec[9 * k + t : 9 * k + t + 1, at] for t in range(9)]
            for r in range(7):
                total = jnp.broadcast_to(bias, (8, 128))
                for t in range(9):
                    total = total + taps[t] * moved[r + t // 3][t % 3]
                to = pl.ds(pl.multiple_of((7 * i + r) * 8, 8), 8)
                out[to, at] = moved[r + 1][1] + valid[to, :] * total

    each(images, one)


def norm_rows(src, images, vec, k, dst):
    gain = vec[30 + k : 31 + k, :]
    shift = vec[34 + k : 35 + k, :]

    def one(p):
        x = src[rows_at(p, PAIR), :]
        centered = x - jnp.mean(x, -1, keepdims=True)
        variance = jnp.mean(centered * centered, -1, keepdims=True)
        dst[rows_at(p, PAIR), :] = (centered * lax.rsqrt(variance + EPS) * gain + shift).astype(BF16)

    each(images // 2, one)


def to_pad(pad, p, rows):
    pad[pl.ds(pl.multiple_of((18 * p + 1) * 8, 8), CELLS), :] = rows[:CELLS]
    pad[pl.ds(pl.multiple_of((18 * p + 10) * 8, 8), CELLS), :] = rows[CELLS:]


def of_pad(pad, p):
    return jnp.concatenate(
        [
            pad[pl.ds(pl.multiple_of((18 * p + 1) * 8, 8), CELLS), :],
            pad[pl.ds(pl.multiple_of((18 * p + 10) * 8, 8), CELLS), :],
        ],
        axis=0,
    )


def clear_borders(pad, images):
    zero = jnp.zeros((8, pad.shape[1]), F32)

    def one(i):
        pad[pl.ds(pl.multiple_of(72 * i, 8), 8), :] = zero
        pad[pl.ds(pl.multiple_of(72 * i + 64, 8), 8), :] = zero

    each(images, one)


def head_masks(kind):
    lane = iota((PAIR, 128), 1) >> 5
    return [jnp.where(lane == h, 1.0, 0.0).astype(F32).astype(kind) for h in range(4)]


def pair_mask(sizes, p, wr, wc):
    row = iota((PAIR, PAIR), 0)
    lane = iota((PAIR, PAIR), 1)
    second = lane >= CELLS
    cell = jnp.where(second, lane - CELLS, lane)
    side = jnp.where(second, sizes[2 * p + 1], sizes[2 * p])
    r, c = cell >> 3, cell & 7
    inside = (r + 7 * wr < side) & (c + 7 * wc < side) & (c < 7)
    return inside & (second == (row >= CELLS))


def stacked(value, masks):
    return jnp.concatenate([value * m for m in masks], axis=0)


def folded(value, masks):
    total = value[:PAIR] * masks[0]
    for h in range(1, 4):
        total = total + value[h * PAIR : (h + 1) * PAIR] * masks[h]
    return total


def pair_probs(query_bd, key, allowed):
    scores = dot_t(query_bd, key) * SCALE
    scores = jnp.where(allowed, scores, -1000000000.0)
    e = jnp.exp(scores - jnp.max(scores, -1, keepdims=True))
    return e * (1.0 / jnp.sum(e, -1, keepdims=True))


def window_attention(packed, images, sizes, wr, wc, context, between):
    width = context.shape[1]

    def pair(p):
        rows = rows_at(p, PAIR)
        allowed = jnp.concatenate([pair_mask(sizes, p, wr, wc).astype(F32)] * 4, axis=0) > 0.5
        low = head_masks(BF16)
        full = head_masks(F32)

        def load(g):
            return tuple(packed[rows, lanes_at(g, 128, n * width)] for n in range(3))

        def compute(query, key, value):
            probs = pair_probs(stacked(query, low), key, allowed).astype(BF16)
            return folded(dot(probs, value), full).astype(BF16)

        def store(g, result):
            context[rows, lanes_at(g, 128)] = result

        each_few(width // 128, GROUPS, load, compute, store)

    for p in range(images // 2):
        pair(p)
        if p % 2 == 1:
            between(1)


def image_halves(kind):
    row = iota((PAIR, 128), 0)
    first = jnp.where(row < CELLS, 1.0, 0.0).astype(F32)
    return first.astype(kind), (1.0 - first).astype(kind)


def fold_heads(square):
    lane = iota((32, 128), 1) >> 5
    total = jnp.zeros((32, 128), F32)
    for h in range(4):
        total = total + jnp.where(lane == h, square[32 * h : 32 * h + 32], 0.0)
    return total


def unfold_heads(block):
    lane = iota((32, 128), 1) >> 5
    return jnp.concatenate([jnp.where(lane == h, block, 0.0) for h in range(4)], axis=0)


def pair_grams(left, left_base, right, right_base, images, valid, out):
    def pair(p):
        rows = rows_at(p, PAIR)
        one, two = image_halves(BF16)
        ok = valid[rows, :].astype(BF16)
        one, two = one * ok, two * ok

        def load(g):
            return left[rows, lanes_at(g, 128, left_base)], right[rows, lanes_at(g, 128, right_base)]

        def compute(a, b):
            both = t_dot(a, jnp.concatenate([b * one, b * two], axis=1))
            return fold_heads(both[:, :128]), fold_heads(both[:, 128:])

        def store(g, result):
            out[pl.ds(pl.multiple_of(64 * p, 32), 32), lanes_at(g, 128)] = result[0]
            out[pl.ds(pl.multiple_of(64 * p + 32, 32), 32), lanes_at(g, 128)] = result[1]

        each_few(out.shape[1] // 128, GROUPS, load, compute, store)

    each(images // 2, pair)


def sum_windows(gram, ins, images, c, sems, vertical, horizontal, flights):
    half = images * 16
    mine = pl.ds(pl.multiple_of(half * c, 32), half)
    other = pl.ds(pl.multiple_of(half * (1 - c), 32), half)

    def add(k):
        def one(i):
            rows = pl.ds(pl.multiple_of(half * c + 32 * i, 32), 32)
            gram[rows, :] = gram[rows, :] + ins[k, rows_at(i, 32), :]

        each(images // 2, one)

    copy = remote(gram.at[other], ins.at[0], sems.at[0], horizontal)
    copy.start()
    flights[0]()
    copy.wait()
    add(0)
    copy = remote(gram.at[mine], ins.at[1], sems.at[1], vertical)
    copy.start()
    flights[1]()
    copy.wait()
    add(1)
    copy = remote(gram.at[mine], ins.at[2], sems.at[2], horizontal)
    copy.start()
    flights[2]()
    copy.wait()

    def take(i):
        gram[pl.ds(pl.multiple_of(half * (1 - c) + 32 * i, 32), 32), :] = ins[2, rows_at(i, 32), :]

    each(images // 2, take)


ROWS_WIDE = 42
ROWS_SMALL = 64
SHORT = 96


def join(pieces):
    tiles = [None] * (SHORT * len(pieces) // 128)
    lane = iota(pieces[0].shape, 1)
    for i, piece in enumerate(pieces):
        t, shift = divmod(SHORT * i, 128)
        moved = pltpu.roll(piece, shift, 1) if shift else piece
        head = jnp.where(lane >= shift, moved, 0.0)
        tiles[t] = head if tiles[t] is None else tiles[t] + head
        if shift > 128 - SHORT:
            tiles[t + 1] = jnp.where(lane < shift - (128 - SHORT), moved, 0.0)
    return tiles


def cut(tiles):
    lane = iota(tiles[0].shape, 1)
    pieces = []
    for i in range(128 * len(tiles) // SHORT):
        t, shift = divmod(SHORT * i, 128)
        piece = pltpu.roll(tiles[t], 128 - shift, 1) if shift else tiles[t]
        if shift > 128 - SHORT:
            piece = jnp.where(lane < 128 - shift, piece, pltpu.roll(tiles[t + 1], 128 - shift, 1))
        pieces.append(piece)
    return pieces


def small_rows():
    return ((42, 2, 0), (44, 3, 1), (47, 4, 2), (51, 4, 3))


def unpack_small(gathered_small, vec, qbias, hbias):
    blocks = [gathered_small[d].astype(F32) for d in range(gathered_small.shape[0])]
    for t, tile in enumerate(join(blocks)):
        vec[:, 128 * t : 128 * t + 128] = tile
    width = vec.shape[1]
    qbias[...] = jnp.zeros(qbias.shape, F32)
    for first, count, row in small_rows():
        lines = [
            jnp.broadcast_to(block[first + r : first + r + 1], (8, 128)) for block in blocks for r in range(count)
        ]
        for t, tile in enumerate(join(lines)):
            line = tile[0:1]
            if row == 0:
                at = 128 * t if 128 * t < width else 128 * t + width
                qbias[0:1, at : at + 128] = line
            elif row == 1:
                qbias[1:2, 128 * t : 128 * t + 128] = line
            else:
                hbias[row - 2 : row - 1, 128 * t : 128 * t + 128] = line


def pack_small(vecg, qbg, hbg, out):
    width = vecg.shape[1]
    for d, piece in enumerate(cut([vecg[:, 128 * t : 128 * t + 128] for t in range(width // 128)])):
        out[d, 0 : vecg.shape[0]] = piece
    for first, count, row in small_rows():
        if row == 0:
            at = [128 * t if 128 * t < width else 128 * t + width for t in range(2 * width // 128)]
            lines = [qbg[0:1, a : a + 128] for a in at]
        elif row == 1:
            lines = [qbg[1:2, 128 * t : 128 * t + 128] for t in range(3 * width // 128)]
        else:
            lines = [hbg[row - 2 : row - 1, 128 * t : 128 * t + 128] for t in range(4 * width // 128)]
        for i, piece in enumerate(cut([jnp.broadcast_to(line, (8, 128)) for line in lines])):
            d, r = divmod(i, count)
            out[d, first + r : first + r + 1] = piece[0:1]


LINE = 4
AHEAD = 2
FIRST = 1
LAGS_FIRST = (0, 1, 2, 3)
LAGS = (0, 2, 4, 5)


def forward_kernel(
    images,
    width,
    hidden,
    sizes,
    patches,
    small,
    qkv_s,
    proj_s,
    hid_s,
    out_s,
    activations,
    o_w,
    vec,
    o_pad,
    o_stream,
    o_normed,
    o_packed,
    o_context,
    o_act,
    o_slope,
    o_mix,
    pad,
    streams,
    normed,
    packed,
    context,
    act,
    slope,
    gram,
    gram_in,
    valid,
    pre,
    wq,
    wp,
    wh,
    wo,
    row_out,
    row_in,
    col_out,
    col_in,
    final,
    halo_sems,
    gram_sems,
    load_sems,
    save_sems,
    z_sems,
    y_sems,
    xa_sems,
    xb_sems,
    c_sems,
    own_sems,
    pre_a,
    pre_b,
    small_in,
    qbias,
    hbias,
    small_sems,
):
    d, w, wr, wc = place()
    pairs = images // 2
    horizontal = (d, 2 * wr + 1 - wc)
    vertical = (d, 2 * (1 - wr) + wc)
    z, y = d // 2, d % 2
    depth = qkv_s.shape[1]
    others = [lax.rem(z + k, LINE) for k in range(1, LINE)]
    in_line = [(2 * other + y, w) for other in others]
    across = (2 * z + 1 - y, w)
    alike = [(lax.rem(d + k, 2 * LINE), w) for k in range(1, 2 * LINE)]
    greet([horizontal, vertical] + alike)
    for peer in alike:
        remote(small, small_in.at[d], small_sems, peer).start()
    left, right = side_masks(wr, wc)

    columns = pl.ds(pl.multiple_of(wc * (width // 2), 128), width // 2)

    def split(t):
        return t % 3 != 2

    def rows_of(t):
        return pl.ds(pl.multiple_of(wr * (depth // 2), 16), depth // 2) if split(t) else pl.ds(0, depth)

    def shard(t, rows):
        layer, j = t // 12, t % 12
        base = (0, 0, 0, 0, 4, 4, 4, 4, 8, 8, 8, 8)[j]
        if j >= 8:
            start = (j - base) * depth
            return out_s.at[layer, pl.ds(pl.multiple_of(start + rows.start, 16), rows.size), columns]
        source = qkv_s if j < 3 else proj_s if j < 4 else hid_s
        shift = 0 if j == 3 else (j - base) * width
        return source.at[layer, rows, pl.ds(pl.multiple_of(shift + wc * (width // 2), 128), width // 2)]

    def piece(t, z_at, y_at):
        return o_w.at[t, z_at, y_at, rows_of(t), columns]

    def send(src, dst, sems, peer):
        remote(src, dst, sems, peer).start()

    def arrived(ref, sems):
        pltpu.make_async_copy(ref, ref, sems.at[1]).wait()

    def left_here(ref, sems):
        pltpu.make_async_copy(ref, ref, sems.at[0]).wait()

    def all_left(t):
        left_here(o_w.at[t, pl.ds(0, LINE - 1), y, rows_of(t), columns], z_sems.at[t])
        left_here(piece(t, pl.ds(0, LINE), y), y_sems.at[t])
        if split(t):
            left_here(o_w.at[t, pl.ds(0, LINE - 1), y, rows_of(t), columns], xa_sems.at[t])
            left_here(piece(t, pl.ds(0, LINE), 1 - y), xb_sems.at[t])
        left_here(o_w.at[t, pl.ds(0, LINE), pl.ds(0, 2), pl.ds(0, depth), columns], c_sems.at[t])

    def own_copy(t):
        return pltpu.make_async_copy(
            shard(t, pl.ds(0, depth)), o_w.at[t, z, y, pl.ds(0, depth), columns], own_sems.at[t]
        )

    def open_chunk(t):
        own_copy(t).start()
        for peer in in_line:
            send(shard(t, rows_of(t)), piece(t, z, y), z_sems.at[t], peer)
        send(shard(t, rows_of(t)), piece(t, z, y), y_sems.at[t], across)

    def stage_a(t):
        arrived(o_w.at[t, pl.ds(0, LINE - 1), y, rows_of(t), columns], z_sems.at[t])
        for other in others:
            send(piece(t, other, y), piece(t, other, y), y_sems.at[t], across)
        if split(t):
            for other in others:
                send(piece(t, other, y), piece(t, other, y), xa_sems.at[t], vertical)

    def stage_b(t):
        beside = piece(t, pl.ds(0, LINE), 1 - y)
        arrived(beside, y_sems.at[t])
        if split(t):
            send(beside, beside, xb_sems.at[t], vertical)

    def stage_c(t):
        own_copy(t).wait()
        if split(t):
            rows = pl.ds(pl.multiple_of((1 - wr) * (depth // 2), 16), depth // 2)
            arrived(o_w.at[t, pl.ds(0, LINE - 1), y, rows, columns], xa_sems.at[t])
            arrived(o_w.at[t, pl.ds(0, LINE), 1 - y, rows, columns], xb_sems.at[t])
        half = o_w.at[t, pl.ds(0, LINE), pl.ds(0, 2), pl.ds(0, depth), columns]
        send(half, half, c_sems.at[t], horizontal)

    chunks = 24
    kinds = ("q", "q", "q", "p", "h", "h", "h", "h", "o", "o", "o", "o")
    busy = {"q": True, "p": True, "h": True, "o": True}
    landed, waiting = set(), []
    clock, opened = [0], [0]

    def load_of(t):
        j = t % 12
        if j < 3:
            dst = wq.at[:, :, :, pl.ds(j * width, width)]
        elif j < 4:
            dst = wp
        elif j < 8:
            dst = wh.at[:, :, :, pl.ds((j - 4) * width, width)]
        else:
            dst = wo.at[:, :, j - 8]
        return pltpu.make_async_copy(o_w.at[t], dst, load_sems.at[t])

    def stage_d(t):
        other = pl.ds(pl.multiple_of((1 - wc) * (width // 2), 128), width // 2)
        arrived(o_w.at[t, pl.ds(0, LINE), pl.ds(0, 2), pl.ds(0, depth), other], c_sems.at[t])
        if t < 12 or not busy[kinds[t % 12]]:
            load_of(t).start()
            landed.add(t)
        else:
            waiting.append(t)

    order = []
    for t in range(chunks):
        lags = LAGS_FIRST if t < FIRST else LAGS
        for stage, lag in zip((stage_a, stage_b, stage_c, stage_d), lags):
            order.append((t + lag, -lag, t, stage))
    order.sort(key=lambda entry: entry[:2])
    last_step = {t: max(step for step, _, u, _ in order if u == t) for t in range(chunks)}
    final_step = max(last_step.values())

    def advance(count):
        for _ in range(count):
            for step, _, t, stage in order:
                if step == clock[0]:
                    stage(t)
                    if stage is stage_a:
                        for ahead in range(max(opened[0], AHEAD), min(t + 1 + AHEAD, chunks)):
                            open_chunk(ahead)
                            opened[0] = ahead + 1
            clock[0] += 1

    def need(t):
        while clock[0] <= last_step[t]:
            advance(1)
        load_of(t).wait()

    def release(kind):
        busy[kind] = False
        for t in [t for t in waiting if kinds[t % 12] == kind]:
            load_of(t).start()
            landed.add(t)
            waiting.remove(t)

    for t in range(AHEAD):
        open_chunk(t)

    saves = {}

    def save(name, src, dst, s):
        saves[name] = pltpu.make_async_copy(src, dst, save_sems.at[s])
        saves[name].start()

    small_in[d] = small[...]
    fill_valid(valid, sizes, images, wr, wc)
    clear_borders(pad, images)

    def enter(p):
        rows = rows_at(p, PAIR)
        to_pad(pad, p, patches[rows, :].astype(F32) * spread(valid[rows, :], width))

    each(pairs, enter)
    advance(1)
    arrived(small_in.at[pl.ds(0, 2 * LINE - 1)], small_sems)
    unpack_small(small_in, vec, qbias, hbias)
    advance(1)

    def step():
        advance(1)

    def convolve(k, stream):
        halo(pad, images, wr, wc, row_out.at[k], row_in.at[k], col_out.at[k], col_in.at[k], halo_sems.at[k], vertical, horizontal, (step, step))
        conv_forward(pad, images, vec, k, valid, stream, left, right)

    def columns_of(weights, at):
        block = weights[:, :, :, at]
        return block.reshape(width, block.shape[-1])

    def qkv(k, x):
        for part in range(3):
            need(12 * k + part)

            def tile(j):
                at = lanes_at(j, 256, part * width)
                packed[:, at] = (dot(x[...], columns_of(wq, at)) + qbias[k : k + 1, at]).astype(BF16)

            each(width // 256, tile)
        release("q")

    def proj(k, stream, store):
        need(12 * k + 3)

        def tile(j):
            at = lanes_at(j, 256)
            pre[...] = dot(context[...], columns_of(wp, at))

            def part(p):
                rows = rows_at(p, PAIR)
                store(p, at, stream[rows, at] + spread(valid[rows, :], 256) * (pre[rows, :] + vec[38 + k : 39 + k, at]))

            each(pairs, part)

        each(width // 256, tile)
        release("p")

    def feed_forward(k, x, stream, store):
        half = width // 2
        tiles = 2 * hidden // width
        pre_b[...] = jnp.zeros(pre_b.shape, F32)

        def multiply(j, to):
            to[...] = dot(x[...], columns_of(wh, lanes_at(j, half)))

        def activate(j, of):
            for r in range(of.shape[0] // 48):
                rows = pl.ds(48 * r, 48)
                for part in range(half // 128):
                    at = pl.ds(pl.multiple_of(j * half + 128 * part, 128), 128)
                    a, s = gelu_pair(of[rows, pl.ds(128 * part, 128)] + hbias[k : k + 1, at])
                    act[rows, at] = a.astype(BF16)
                    slope[rows, at] = s.astype(BF16)

        def two_tiles(b):
            multiply(2 * b, pre_a)
            activate(lax.rem(2 * b + tiles - 1, tiles), pre_b)
            multiply(2 * b + 1, pre_b)
            activate(2 * b, pre_a)

        for block in range(0, 4, 2):
            need(12 * k + 4 + block)
            need(12 * k + 5 + block)
            each(2, lambda b: two_tiles(block + b))
            advance(1)
        activate(tiles - 1, pre_b)
        save(f"a{k}", act, o_act.at[k], 7)
        save(f"g{k}", slope, o_slope.at[k], 8)
        release("h")
        for block in range(4):
            need(12 * k + 8 + block)

        def tile2(j):
            at = lanes_at(j, 256)
            block = wo[:, :, :, :, at]
            pre[...] = dot(act[...], block.reshape(hidden, 256))

            def part(p):
                rows = rows_at(p, PAIR)
                store(p, at, stream[rows, at] + spread(valid[rows, :], 256) * (pre[rows, :] + vec[40 + k : 41 + k, at]))

            each(pairs, part)

        for j in range(width // 256):
            tile2(j)
        advance(1)
        release("o")

    def into_pad(p, at, value):
        pad[pl.ds(pl.multiple_of((18 * p + 1) * 8, 8), CELLS), at] = value[:CELLS]
        pad[pl.ds(pl.multiple_of((18 * p + 10) * 8, 8), CELLS), at] = value[CELLS:]

    convolve(0, streams.at[0])
    save("pad0", pad, o_pad.at[0], 0)
    save("s1", streams.at[0], o_stream.at[0], 1)
    norm_rows(streams.at[0], images, vec, 0, normed.at[0])
    save("n1", normed.at[0], o_normed.at[0], 2)
    qkv(0, normed.at[0])
    save("k1", packed, o_packed.at[0], 3)
    window_attention(packed, images, sizes, wr, wc, context, advance)
    save("c1", context, o_context.at[0], 4)
    saves["pad0"].wait()
    proj(0, streams.at[0], into_pad)
    convolve(1, streams.at[1])
    save("pad2", pad, o_pad.at[1], 0)
    save("s3", streams.at[1], o_stream.at[1], 5)
    norm_rows(streams.at[1], images, vec, 1, normed.at[1])
    save("n3", normed.at[1], o_normed.at[1], 6)
    saves["pad2"].wait()
    feed_forward(0, normed.at[1], streams.at[1], into_pad)
    saves["s1"].wait()
    saves["n1"].wait()
    saves["k1"].wait()
    saves["c1"].wait()
    convolve(2, streams.at[0])
    save("pad4", pad, o_pad.at[2], 0)
    save("s5", streams.at[0], o_stream.at[2], 1)
    norm_rows(streams.at[0], images, vec, 2, normed.at[0])
    save("n5", normed.at[0], o_normed.at[2], 2)
    qkv(1, normed.at[0])
    save("k5", packed, o_packed.at[1], 3)
    pair_grams(packed, 2 * width, packed, width, images, valid, gram)
    advance(1)
    sum_windows(gram, gram_in, images, wc, gram_sems, vertical, horizontal, (step, step, step))

    def soften(i):
        rows = rows_at(i, 32)
        x = gram[rows, :] * SCALE
        e = jnp.exp(x - jnp.max(x, 0, keepdims=True))
        gram[rows, :] = e * (1.0 / jnp.sum(e, 0, keepdims=True))

    each(images, soften)
    save("mix", gram, o_mix, 9)

    def mix_pair(p):
        rows = rows_at(p, PAIR)
        one, two = image_halves(BF16)

        def load(g):
            at = lanes_at(g, 128)
            first = gram[pl.ds(pl.multiple_of(64 * p, 32), 32), at]
            second = gram[pl.ds(pl.multiple_of(64 * p + 32, 32), 32), at]
            return first, second, packed[rows, at]

        def compute(first, second, query):
            mixing = jnp.concatenate([unfold_heads(first), unfold_heads(second)], axis=0).astype(BF16)
            return dot(jnp.concatenate([query * one, query * two], axis=1), mixing).astype(BF16)

        def store(g, result):
            context[rows, lanes_at(g, 128)] = result

        each_few(width // 128, GROUPS, load, compute, store)

    each(pairs, mix_pair)
    advance(1)
    save("c5", context, o_context.at[1], 4)
    saves["s3"].wait()
    saves["n3"].wait()

    def into_last(p, at, value):
        streams[1, rows_at(p, PAIR), at] = value

    proj(1, streams.at[0], into_last)
    save("s6", streams.at[1], o_stream.at[3], 5)
    norm_rows(streams.at[1], images, vec, 3, normed.at[1])
    save("n6", normed.at[1], o_normed.at[3], 6)
    saves["a0"].wait()
    saves["g0"].wait()

    def into_final(p, at, value):
        final[rows_at(p, PAIR), at] = value.astype(BF16)

    feed_forward(1, normed.at[1], streams.at[1], into_final)
    save("end", final, activations, 10)
    advance(final_step + 1 - clock[0])
    for t in range(chunks):
        all_left(t)
    left_here(small_in.at[pl.ds(0, 2 * LINE - 1)], small_sems)
    for name in ("pad4", "s5", "n5", "k5", "mix", "c5", "s6", "n6", "a1", "g1", "end"):
        saves[name].wait()


ANY = pl.BlockSpec(memory_space=pl.ANY)
VMEM = pl.BlockSpec(memory_space=pltpu.VMEM)
SMEM = pl.BlockSpec(memory_space=pltpu.SMEM)


def run_forward(sizes, patches, small, shards):
    images = sizes.shape[0]
    n_rows, width = patches.shape
    hidden = shards[2].shape[2]
    lines = images * 72
    depth = shards[0].shape[1]
    shapes = (
        ((n_rows, width), BF16),
        ((24, LINE, 2, depth, width), BF16),
        ((ROWS_SMALL, width), F32),
        ((3, lines, width), F32),
        ((4, n_rows, width), F32),
        ((4, n_rows, width), BF16),
        ((2, n_rows, 3 * width), BF16),
        ((2, n_rows, width), BF16),
        ((2, n_rows, hidden), BF16),
        ((2, n_rows, hidden), BF16),
        ((images * 32, width), F32),
    )
    return pl.pallas_call(
        functools.partial(forward_kernel, images, width, hidden),
        out_shape=[jax.ShapeDtypeStruct(*s) for s in shapes],
        in_specs=[SMEM, VMEM, VMEM] + [ANY] * 4,
        out_specs=[ANY] * 2 + [VMEM] + [ANY] * 8,
        scratch_shapes=[
            pltpu.VMEM((lines, width), F32),
            pltpu.VMEM((2, n_rows, width), F32),
            pltpu.VMEM((2, n_rows, width), BF16),
            pltpu.VMEM((n_rows, 3 * width), BF16),
            pltpu.VMEM((n_rows, width), BF16),
            pltpu.VMEM((n_rows, hidden), BF16),
            pltpu.VMEM((n_rows, hidden), BF16),
            pltpu.VMEM((images * 32, width), F32),
            pltpu.VMEM((3, images * 16, width), F32),
            pltpu.VMEM((n_rows, 128), F32),
            pltpu.VMEM((n_rows, 256), F32),
            pltpu.VMEM((LINE, 2, depth, 3 * width), BF16),
            pltpu.VMEM((LINE, 2, depth, width), BF16),
            pltpu.VMEM((LINE, 2, depth, hidden), BF16),
            pltpu.VMEM((LINE, 2, 4, depth, width), BF16),
            pltpu.VMEM((3, images * 8, width), BF16),
            pltpu.VMEM((3, images * 8, width), BF16),
            pltpu.VMEM((3, images * 8, width), BF16),
            pltpu.VMEM((3, images * 8, width), BF16),
            pltpu.VMEM((n_rows, width), BF16),
            pltpu.SemaphoreType.DMA((3, 2, 2)),
            pltpu.SemaphoreType.DMA((3, 2)),
            pltpu.SemaphoreType.DMA((24,)),
            pltpu.SemaphoreType.DMA((11,)),
            pltpu.SemaphoreType.DMA((24, 2)),
            pltpu.SemaphoreType.DMA((24, 2)),
            pltpu.SemaphoreType.DMA((24, 2)),
            pltpu.SemaphoreType.DMA((24, 2)),
            pltpu.SemaphoreType.DMA((24, 2)),
            pltpu.SemaphoreType.DMA((24,)),
            pltpu.VMEM((n_rows, width // 2), F32),
            pltpu.VMEM((n_rows, width // 2), F32),
            pltpu.VMEM((2 * LINE, ROWS_SMALL, 128), BF16),
            pltpu.VMEM((8, 3 * width), F32),
            pltpu.VMEM((8, hidden), F32),
            pltpu.SemaphoreType.DMA((2,)),
        ],
        compiler_params=pltpu.CompilerParams(
            collective_id=0, has_side_effects=True, vmem_limit_bytes=58 * 2**20
        ),
    )(sizes, patches, small, *shards)


def column_sums(src, images, width, store):
    for part in range(src.shape[1] // width):
        at = pl.ds(part * width, width)

        def one(p, total):
            x = src[rows_at(p, PAIR), at].astype(F32)
            return total + jnp.sum(x.reshape(PAIR // 8, 8, width), axis=0)

        total = lax.fori_loop(0, images // 2, one, jnp.zeros((8, width), F32))
        store(at, jnp.sum(total, axis=0, keepdims=True))


def norm_back(stream, images, vec, k, grad_normed, grad, vecg):
    gain = vec[30 + k : 31 + k, :]
    width = stream.shape[1]

    def one(p, carry):
        rows = rows_at(p, PAIR)
        x = stream[rows, :]
        dn = grad_normed[rows, :]
        centered = x - jnp.mean(x, -1, keepdims=True)
        rstd = lax.rsqrt(jnp.mean(centered * centered, -1, keepdims=True) + EPS)
        xhat = centered * rstd
        scaled = dn * gain
        inner = jnp.mean(scaled * xhat, -1, keepdims=True)
        grad[rows, :] = grad[rows, :] + rstd * (scaled - jnp.mean(scaled, -1, keepdims=True) - xhat * inner)
        gains = jnp.sum((dn * xhat).reshape(PAIR // 8, 8, width), axis=0)
        shifts = jnp.sum(dn.reshape(PAIR // 8, 8, width), axis=0)
        return carry[0] + gains, carry[1] + shifts

    zero = jnp.zeros((8, width), F32)
    gains, shifts = lax.fori_loop(0, images // 2, one, (zero, zero))
    vecg[30 + k : 31 + k, :] = jnp.sum(gains, axis=0, keepdims=True)
    vecg[34 + k : 35 + k, :] = jnp.sum(shifts, axis=0, keepdims=True)


def conv_back(grad_pad, pad, images, vec, k, valid, grad, vecg, left, right, between):
    keep = jnp.where(iota((8, 128), 0) < 7, 1.0, 0.0).astype(F32)
    for part in range(pad.shape[1] // 128):
        at = pl.ds(part * 128, 128)
        taps = [vec[9 * k + t : 9 * k + t + 1, at] for t in range(9)]

        def one(i, sums):
            back = three(grad_pad, i, at, left, right)
            ahead = three(pad, i, at, left, right)
            sums = list(sums)
            for r in range(7):
                own = back[r + 1][1] * keep
                total = own
                for t in range(9):
                    total = total + taps[t] * back[r + 2 - t // 3][2 - t % 3]
                    sums[t] = sums[t] + own * ahead[r + t // 3][t % 3]
                sums[9] = sums[9] + own
                to = pl.ds(pl.multiple_of((7 * i + r) * 8, 8), 8)
                grad[to, at] = valid[to, :] * total
            return tuple(sums)

        sums = lax.fori_loop(0, images, one, tuple(jnp.zeros((8, 128), F32) for _ in range(10)))
        for t in range(9):
            vecg[9 * k + t : 9 * k + t + 1, at] = jnp.sum(sums[t], axis=0, keepdims=True)
        vecg[27 + k : 28 + k, at] = jnp.sum(sums[9], axis=0, keepdims=True)
        if part == 2:
            between(1)


def window_back(packed, images, sizes, wr, wc, grad_context, between):
    width = grad_context.shape[1]

    def pair(p):
        rows = rows_at(p, PAIR)
        allowed = jnp.concatenate([pair_mask(sizes, p, wr, wc).astype(F32)] * 4, axis=0) > 0.5
        low = head_masks(BF16)
        full = head_masks(F32)

        def load(g):
            return [packed[rows, lanes_at(g, 128, n * width)] for n in range(3)] + [grad_context[rows, lanes_at(g, 128)]]

        def compute(query, key, value, grad):
            query_bd = stacked(query, low)
            grad_bd = stacked(grad, low)
            probs = pair_probs(query_bd, key, allowed)
            grad_probs = dot_t(grad_bd, value)
            grad_value = t_dot(probs.astype(BF16), grad_bd).astype(BF16)
            inner = jnp.sum(probs * grad_probs, -1, keepdims=True)
            grad_scores = jnp.where(allowed, probs * (grad_probs - inner), 0.0).astype(BF16)
            grad_query = (folded(dot(grad_scores, key), full) * SCALE).astype(BF16)
            grad_key = (t_dot(grad_scores, query_bd) * SCALE).astype(BF16)
            return grad_query, grad_key, grad_value

        def store(g, result):
            for n in range(3):
                packed[rows, lanes_at(g, 128, n * width)] = result[n]

        each_few(width // 128, BACK_GROUPS, load, compute, store)

    for p in range(images // 2):
        pair(p)
        between(1)


def channel_back(packed, images, mix, grad_gram, valid, grad_context, between):
    width = grad_context.shape[1]

    def pair(p):
        rows = rows_at(p, PAIR)
        one, two = image_halves(BF16)
        ok = valid[rows, :] * SCALE
        first = pl.ds(pl.multiple_of(64 * p, 32), 32)
        second = pl.ds(pl.multiple_of(64 * p + 32, 32), 32)

        def both(ref, at, axis):
            return jnp.concatenate(
                [unfold_heads(ref[first, at]), unfold_heads(ref[second, at])], axis=axis
            ).astype(BF16)

        def split(value):
            return jnp.concatenate([value * one, value * two], axis=1)

        def load(g):
            at = lanes_at(g, 128)
            values = [packed[rows, lanes_at(g, 128, n * width)] for n in range(1, 3)]
            return values + [grad_context[rows, at], both(mix, at, 1), both(grad_gram, at, 0), both(grad_gram, at, 1)]

        def compute(key, value, grad, mixing, grad_tall, grad_wide):
            grad_query = dot_t(split(grad), mixing).astype(BF16)
            grad_key = (dot(split(value), grad_tall) * ok).astype(BF16)
            grad_value = (dot_t(split(key), grad_wide) * ok).astype(BF16)
            return grad_query, grad_key, grad_value

        def store(g, result):
            for n in range(3):
                packed[rows, lanes_at(g, 128, n * width)] = result[n]

        each_few(width // 128, BACK_GROUPS, load, compute, store)

    for p in range(images // 2):
        pair(p)
        if p % 3 == 2:
            between(1)


ORDER = (20, 21, 22, 23, 16, 17, 18, 19, 15, 12, 13, 14, 8, 9, 10, 11, 4, 5, 6, 7, 3, 0, 1, 2)
RING = 4
AHEAD_SUMS = 1
HELD = 12
WAIT = 2


def backward_kernel(
    images,
    width,
    hidden,
    sizes,
    cotangent,
    vec,
    i_pad,
    i_stream,
    i_normed,
    i_packed,
    i_context,
    i_act,
    i_slope,
    i_mix,
    i_w,
    patches_grad,
    tiny,
    g_qkv,
    g_proj,
    g_hid,
    g_out,
    grad,
    grad_pad,
    pad,
    stream,
    normed,
    packed,
    context,
    act,
    slope,
    dn,
    branch,
    gram,
    mix,
    gram_in,
    valid,
    w_wide,
    w_tall,
    row_out,
    row_in,
    col_out,
    col_in,
    go_out,
    go_in,
    held,
    x_in,
    y_in,
    z_in,
    part,
    part_in,
    whole,
    whole_in,
    stage,
    halo_sems,
    gram_sems,
    load_sems,
    stage_sems,
    weight_sems,
    sums_sems,
    credits,
    vecg,
    qbg,
    hbg,
    small_out,
    small_in,
    small_sum,
    small_sems,
):
    d, w, wr, wc = place()
    depth = i_w.shape[3]
    pairs = images // 2
    horizontal = (d, 2 * wr + 1 - wc)
    vertical = (d, 2 * (1 - wr) + wc)
    z, y = d // 2, d % 2
    others = [lax.rem(z + k, LINE) for k in range(1, LINE)]
    in_line = [(2 * other + y, w) for other in others]
    across = (2 * z + 1 - y, w)
    alike = [(lax.rem(d + k, 2 * LINE), w) for k in range(1, 2 * LINE)]
    windows = [(d, lax.rem(w + k, 4)) for k in range(1, 4)]
    greet(alike + windows)
    vecg[...] = jnp.zeros(vecg.shape, F32)
    left, right = side_masks(wr, wc)
    loads = {}
    half = width // 2
    rows_mine = pl.ds(pl.multiple_of(wr * (depth // 2), 16), depth // 2)
    rows_other = pl.ds(pl.multiple_of((1 - wr) * (depth // 2), 16), depth // 2)
    cols_mine = pl.ds(pl.multiple_of(wc * half, 128), half)
    cols_other = pl.ds(pl.multiple_of((1 - wc) * half, 128), half)
    chunks = len(ORDER)
    halves = [n for n in range(chunks) if n % 2 == 1]

    def post(n, kind, src, dst, peer):
        copy = remote(src, dst, sums_sems.at[n, kind], peer)
        copy.start()

    def settle(n, kind, ref):
        pltpu.make_async_copy(ref, ref, sums_sems.at[n, kind, 1]).wait()
        pltpu.make_async_copy(ref, ref, sums_sems.at[n, kind, 0]).wait()

    def credit(n, kind, peer):
        if n + RING < chunks:
            pl.semaphore_signal(credits.at[kind], inc=1, device_id=peer, device_id_type=MESH)

    def take_credit(n, kind):
        if n >= RING:
            pl.semaphore_wait(credits.at[kind], 1)

    def open_sum(n):
        take_credit(n, 0)
        post(n, 0, go_out.at[n % RING], go_in.at[n % RING], horizontal)

    def sum_cores(upto):
        for n in range(cored[0], upto):
            s, h = n % RING, n % HELD
            settle(n, 0, go_in.at[s])

            def add(i):
                held[h, i // 2, i % 2] = held[h, i // 2, i % 2] + go_in[s, i // 2, i % 2]

            each(2 * LINE, add)
            credit(n, 0, horizontal)
        cored[0] = max(cored[0], upto)

    def leave_chip(n):
        sum_cores(n + 1)
        s, h = n % RING, n % HELD
        if n in halves:
            if n >= RING:
                pl.semaphore_wait(credits.at[1], 1)
            post(n, 1, held.at[h, :, :, rows_other], x_in.at[s], vertical)
        else:
            take_credit(n, 8)
            post(n, 2, held.at[h, :, 1 - y], y_in.at[s], across)

    def sum_x(n):
        if n not in halves:
            return
        s, h = n % RING, n % HELD
        settle(n, 1, x_in.at[s])

        def add(i):
            held[h, i // 2, i % 2, rows_mine] = held[h, i // 2, i % 2, rows_mine] + x_in[s, i // 2, i % 2]

        each(2 * LINE, add)
        credit(n, 1, vertical)
        take_credit(n, 2)
        post(n, 2, held.at[h, :, 1 - y, rows_mine], y_in.at[s, :, 0 : depth // 2], across)

    def share(n):
        return (rows_mine, depth // 2) if n in halves else (pl.ds(0, depth), depth)

    def sum_y(n):
        s, h = n % RING, n % HELD
        rows, count = share(n)
        settle(n, 2, y_in.at[s, :, 0:count])

        def add(i):
            held[h, i, y, rows] = held[h, i, y, rows] + y_in[s, i, 0:count]

        each(LINE, add)
        credit(n, 2 if n in halves else 8, across)
        for k in range(LINE - 1):
            take_credit(n, 3 + k)
        for k, (other, peer) in enumerate(zip(others, in_line)):
            post(n, 3, held.at[h, other, y, rows], z_in.at[s, LINE - 2 - k, 0:count], peer)

    def sum_z(n):
        s, h = n % RING, n % HELD
        rows, count = share(n)
        settle(n, 3, z_in.at[s, :, 0:count])
        total = held[h, z, y, rows].astype(F32)
        for k in range(LINE - 1):
            total = total + z_in[s, k, 0:count].astype(F32)
        part[s, rows] = total.astype(BF16)
        for k, peer in enumerate(in_line):
            credit(n, 3 + LINE - 2 - k, peer)
        take_credit(n, 6)
        post(n, 4, part.at[s, rows], part_in.at[s, rows], vertical)

    def sum_windows_x(n):
        s = n % RING
        if n in halves:
            settle(n, 4, part_in.at[s, rows_other])
            whole[s, rows_mine] = part[s, rows_mine]
            whole[s, rows_other] = part_in[s, rows_other]
        else:
            settle(n, 4, part_in.at[s])
            whole[s] = part[s] + part_in[s]
        credit(n, 6, vertical)
        take_credit(n, 7)
        post(n, 5, whole.at[s], whole_in.at[s], horizontal)

    def result_of(n):
        layer, j = ORDER[n] // 12, ORDER[n] % 12
        if j < 3:
            return g_qkv.at[layer, :, pl.ds(j * width, width)]
        if j < 4:
            return g_proj.at[layer]
        if j < 8:
            return g_hid.at[layer, :, pl.ds((j - 4) * width, width)]
        return g_out.at[layer, pl.ds((j - 8) * depth, depth)]

    def write_out(n):
        return pltpu.make_async_copy(stage.at[n % RING], result_of(n), stage_sems.at[n % RING])

    def finish(n):
        s = n % RING
        settle(n, 5, whole_in.at[s])
        if n >= RING:
            write_out(n - RING).wait()
        stage[s, :, cols_mine] = whole[s].astype(F32)
        stage[s, :, cols_other] = whole_in[s].astype(F32)
        credit(n, 7, horizontal)
        write_out(n).start()

    stages = (leave_chip, sum_x, sum_y, sum_z, sum_windows_x, finish)
    made, clock, cored = [0], [0], [0]

    def turn():
        for lag in reversed(range(len(stages))):
            n = clock[0] - lag * WAIT
            if 0 <= n < chunks:
                stages[lag](n)
        clock[0] += 1

    def pump(count):
        for _ in range(2 * count if made[0] == chunks else count):
            if clock[0] < made[0] - AHEAD_SUMS or (made[0] == chunks and clock[0] < chunks + len(stages) * WAIT):
                turn()

    def room(count):
        sum_cores(made[0] + count - RING)
        while made[0] + count - HELD > clock[0] - 3 * WAIT:
            turn()

    def opened(count):
        for n in range(made[0], made[0] + count):
            open_sum(n)
        made[0] += count

    def pair_of_halves(dy, base):
        theirs = dy[:, pl.ds(pl.multiple_of(base + (1 - wc) * half, 128), half)]
        ours = dy[:, pl.ds(pl.multiple_of(base + wc * half, 128), half)]
        return jnp.concatenate([theirs, ours], axis=1)

    def weight_grad(x, dy):
        for j in range(dy.shape[1] // width):
            room(1)
            s, h = made[0] % RING, made[0] % HELD

            def tile(q):
                both = t_dot(x[:, lanes_at(q, 4 * depth)], pair_of_halves(dy, j * width)).astype(BF16)
                go_out[s, rows_at(q, 2)] = both[:, :half].reshape(2, 2, depth, half)
                held[h, rows_at(q, 2)] = both[:, half:].reshape(2, 2, depth, half)

            each(LINE // 2, tile)
            opened(1)
        pump(1)

    def tall_weight_grad(x, dy):
        room(4)
        slots = [(n % RING, n % HELD) for n in range(made[0], made[0] + 4)]

        def tile(i):
            both = t_dot(x[:, lanes_at(i, 4 * depth)], pair_of_halves(dy, 0)).astype(BF16)
            for j, (s, h) in enumerate(slots):
                block = both[j * depth : (j + 1) * depth]
                go_out[s, i // 2, i % 2] = block[:, :half]
                held[h, i // 2, i % 2] = block[:, half:]

        each(2 * LINE, tile)
        opened(4)
        pump(1)

    def load(name, src, dst, s):
        loads[name] = pltpu.make_async_copy(src, dst, load_sems.at[s])
        loads[name].start()

    def load_weights(t):
        j = t % 12
        if j < 3:
            dst = w_wide.at[:, :, :, pl.ds(j * width, width)]
        elif j < 4:
            dst = w_tall.at[:, :, 0]
        elif j < 8:
            dst = w_wide.at[:, :, :, pl.ds((j - 4) * width, width)]
        else:
            dst = w_tall.at[:, :, j - 8]
        return pltpu.make_async_copy(i_w.at[t], dst, weight_sems.at[t])

    def chunks_of(name):
        first = {"wq": 0, "wp": 3, "wh": 4, "wo": 8}[name[:2]] + 12 * int(name[2])
        return range(first, first + {"wq": 3, "wp": 1, "wh": 4, "wo": 4}[name[:2]])

    def fetch(name):
        for t in chunks_of(name):
            load_weights(t).start()

    def fetched(name):
        for t in chunks_of(name):
            load_weights(t).wait()

    load("cotangent", cotangent, branch, 1)
    load("act", i_act.at[1], act, 0)
    fetch("wo1")
    load("slope", i_slope.at[1], slope, 2)
    fetch("wh1")
    load("normed", i_normed.at[3], normed, 4)
    load("stream", i_stream.at[3], stream, 5)
    load("context", i_context.at[1], context, 6)
    load("packed", i_packed.at[1], packed, 7)
    load("mix", i_mix, mix, 8)
    load("pad", i_pad.at[2], pad, 9)
    fill_valid(valid, sizes, images, wr, wc)
    clear_borders(grad_pad, images)

    loads["cotangent"].wait()

    def enter(p):
        rows = rows_at(p, PAIR)
        grad[rows, :] = branch[rows, :].astype(F32) * spread(valid[rows, :], width)

    each(pairs, enter)

    def make_branch(row):
        def one(p):
            rows = rows_at(p, PAIR)
            branch[rows, :] = (grad[rows, :] * spread(valid[rows, :], width)).astype(BF16)

        each(pairs, one)

        def store(at, total):
            vecg[row : row + 1, at] = total

        column_sums(branch, images, 256, store)

    def feed_forward(k):
        make_branch(40 + k)
        loads["act"].wait()
        tall_weight_grad(act, branch)
        fetched(f"wo{k}")
        loads["slope"].wait()

        def tile(j):
            at = lanes_at(j, 4 * depth)
            dact = dot_t(branch[...], w_tall[j // 2, j % 2].reshape(4 * depth, width))
            slope[:, at] = (slope[:, at].astype(F32) * dact).astype(BF16)

        for part in range(2):
            each(LINE, lambda j: tile(LINE * part + j))
            pump(1)

        def store(at, total):
            hbg[k : k + 1, at] = total

        column_sums(slope, images, 256, store)
        fetched(f"wh{k}")

        def tile2(j):
            block = w_wide[rows_at(j, 2)].reshape(4 * depth, hidden)
            dn[:, lanes_at(j, 4 * depth)] = dot_t(slope[...], block)

        each(LINE // 2, tile2)
        pump(1)
        loads["stream"].wait()
        norm_back(stream, images, vec, 1 + 2 * k, dn, grad, vecg)
        pump(1)

    def hidden_grad():
        loads["normed"].wait()
        weight_grad(normed, slope)

    def proj_grad():
        loads["context"].wait()
        weight_grad(context, branch)

    def qkv_grad():
        loads["normed"].wait()
        weight_grad(normed, packed)

    grad_context = act.at[:, pl.ds(0, width)]

    def proj(k):
        make_branch(38 + k)
        pump(1)
        fetched(f"wp{k}")

        def tile(j):
            block = w_tall[rows_at(j, 2), :, 0].reshape(4 * depth, width)
            grad_context[:, lanes_at(j, 4 * depth)] = dot_t(branch[...], block).astype(BF16)

        each(LINE // 2, tile)

    def qkv(k):
        def store(at, total):
            qbg[k : k + 1, at] = total

        column_sums(packed, images, 256, store)
        fetched(f"wq{k}")

        def tile(j):
            block = w_wide[rows_at(j, 2), :, :, 0 : 3 * width].reshape(4 * depth, 3 * width)
            dn[:, lanes_at(j, 4 * depth)] = dot_t(packed[...], block)

        pump(1)
        each(LINE // 2, tile)
        loads["stream"].wait()
        pump(1)
        norm_back(stream, images, vec, 2 * k, dn, grad, vecg)
        pump(1)

    def convolve(k, *flights):
        def enter_pad(p):
            to_pad(grad_pad, p, grad[rows_at(p, PAIR), :])

        each(pairs, enter_pad)
        halo(grad_pad, images, wr, wc, row_out.at[k], row_in.at[k], col_out.at[k], col_in.at[k], halo_sems.at[k], vertical, horizontal, flights)
        loads["pad"].wait()
        conv_back(grad_pad, pad, images, vec, k, valid, grad, vecg, left, right, pump)

    def idle():
        pump(1)

    feed_forward(1)
    fetch("wp1")
    fetch("wq1")
    load("stream", i_stream.at[2], stream, 5)
    proj(1)
    fetch("wo0")
    loads["packed"].wait()
    pump(1)
    pair_grams(packed, 0, grad_context, 0, images, valid, gram)
    pump(1)

    def beside():
        hidden_grad()
        proj_grad()

    sum_windows(gram, gram_in, images, wc, gram_sems, vertical, horizontal, (idle, beside, idle))
    load("slope", i_slope.at[0], slope, 2)
    load("normed", i_normed.at[2], normed, 4)
    load("context", i_context.at[0], context, 6)
    loads["mix"].wait()

    def harden(i):
        rows = rows_at(i, 32)
        y, g = mix[rows, :], gram[rows, :]
        gram[rows, :] = y * (g - jnp.sum(y * g, 0, keepdims=True))

    each(images, harden)
    channel_back(packed, images, mix, gram, valid, grad_context, pump)
    load("act", i_act.at[0], act, 0)
    qkv(1)
    fetch("wh0")
    load("stream", i_stream.at[1], stream, 5)
    convolve(2, qkv_grad, idle)
    load("pad", i_pad.at[1], pad, 9)
    load("packed", i_packed.at[0], packed, 7)
    load("normed", i_normed.at[1], normed, 4)
    feed_forward(0)
    fetch("wp0")
    fetch("wq0")
    load("stream", i_stream.at[0], stream, 5)
    convolve(1, hidden_grad, idle)
    load("pad", i_pad.at[0], pad, 9)
    load("normed", i_normed.at[0], normed, 4)
    proj(0)
    proj_grad()
    loads["packed"].wait()
    window_back(packed, images, sizes, wr, wc, grad_context, pump)
    qkv_grad()
    qkv(0)
    convolve(0, idle, idle)

    def leave(p):
        rows = rows_at(p, PAIR)
        branch[rows, :] = grad[rows, :].astype(BF16)

    each(pairs, leave)
    load("end", branch, patches_grad, 1)
    pack_small(vecg, qbg, hbg, small_out)
    small_in[d] = small_out[d]
    for peer in alike:
        remote(small_out.at[peer[0]], small_in.at[d], small_sems.at[0], peer).start()
    while clock[0] < chunks + (len(stages) - 2) * WAIT:
        turn()
    for n in (1, 0):
        seven = small_in.at[pl.ds(0, 2 * LINE - 1)]
        pltpu.make_async_copy(seven, seven, small_sems.at[0, n]).wait()
    total = small_in[0]
    for k in range(1, 2 * LINE):
        total = total + small_in[k]
    small_sum[w] = total
    for peer in windows:
        remote(small_sum.at[w], small_sum.at[w], small_sems.at[1], peer).start()
    while clock[0] < chunks + len(stages) * WAIT:
        turn()
    for n in (1, 0):
        three_of = small_sum.at[pl.ds(0, 3)]
        pltpu.make_async_copy(three_of, three_of, small_sems.at[1, n]).wait()
    tiny[...] = ((small_sum[0] + small_sum[1]) + small_sum[2]) + small_sum[3]
    for n in range(chunks - RING, chunks):
        write_out(n).wait()
    loads["end"].wait()


def run_backward(sizes, cotangent, vec, saved, weights, hidden):
    images = sizes.shape[0]
    depth = weights.shape[3]
    n_rows, width = cotangent.shape
    lines = images * 72
    shapes = (
        ((n_rows, width), BF16),
        ((ROWS_SMALL, 128), F32),
        ((2, depth, 3 * width), F32),
        ((2, depth, width), F32),
        ((2, depth, hidden), F32),
        ((2, 4 * depth, width), F32),
    )
    half = width // 2
    return pl.pallas_call(
        functools.partial(backward_kernel, images, width, hidden),
        out_shape=[jax.ShapeDtypeStruct(*s) for s in shapes],
        in_specs=[SMEM, ANY, VMEM] + [ANY] * 9,
        out_specs=[ANY, VMEM] + [ANY] * 4,
        scratch_shapes=[
            pltpu.VMEM((n_rows, width), F32),
            pltpu.VMEM((lines, width), F32),
            pltpu.VMEM((lines, width), F32),
            pltpu.VMEM((n_rows, width), F32),
            pltpu.VMEM((n_rows, width), BF16),
            pltpu.VMEM((n_rows, 3 * width), BF16),
            pltpu.VMEM((n_rows, width), BF16),
            pltpu.VMEM((n_rows, hidden), BF16),
            pltpu.VMEM((n_rows, hidden), BF16),
            pltpu.VMEM((n_rows, width), F32),
            pltpu.VMEM((n_rows, width), BF16),
            pltpu.VMEM((images * 32, width), F32),
            pltpu.VMEM((images * 32, width), F32),
            pltpu.VMEM((3, images * 16, width), F32),
            pltpu.VMEM((n_rows, 128), F32),
            pltpu.VMEM((LINE, 2, depth, hidden), BF16),
            pltpu.VMEM((LINE, 2, 4, depth, width), BF16),
            pltpu.VMEM((3, images * 8, width), BF16),
            pltpu.VMEM((3, images * 8, width), BF16),
            pltpu.VMEM((3, images * 8, width), BF16),
            pltpu.VMEM((3, images * 8, width), BF16),
            pltpu.VMEM((RING, LINE, 2, depth, half), BF16),
            pltpu.VMEM((RING, LINE, 2, depth, half), BF16),
            pltpu.VMEM((HELD, LINE, 2, depth, half), BF16),
            pltpu.VMEM((RING, LINE, 2, depth // 2, half), BF16),
            pltpu.VMEM((RING, LINE, depth, half), BF16),
            pltpu.VMEM((RING, LINE - 1, depth, half), BF16),
            pltpu.VMEM((RING, depth, half), BF16),
            pltpu.VMEM((RING, depth, half), BF16),
            pltpu.VMEM((RING, depth, half), BF16),
            pltpu.VMEM((RING, depth, half), BF16),
            pltpu.VMEM((RING, depth, width), F32),
            pltpu.SemaphoreType.DMA((3, 2, 2)),
            pltpu.SemaphoreType.DMA((3, 2)),
            pltpu.SemaphoreType.DMA((10,)),
            pltpu.SemaphoreType.DMA((RING,)),
            pltpu.SemaphoreType.DMA((24,)),
            pltpu.SemaphoreType.DMA((24, 6, 2)),
            pltpu.SemaphoreType.REGULAR((9,)),
            pltpu.VMEM((48, width), F32),
            pltpu.VMEM((8, 3 * width), F32),
            pltpu.VMEM((8, hidden), F32),
            pltpu.VMEM((2 * LINE, ROWS_SMALL, 128), F32),
            pltpu.VMEM((2 * LINE, ROWS_SMALL, 128), F32),
            pltpu.VMEM((4, ROWS_SMALL, 128), F32),
            pltpu.SemaphoreType.DMA((2, 2)),
        ],
        compiler_params=pltpu.CompilerParams(
            collective_id=1, has_side_effects=True, vmem_limit_bytes=60 * 2**20
        ),
    )(sizes, cotangent, vec, *saved, weights)


def to_cells(windows):
    images, _, _, width = windows.shape
    grid = windows.reshape(images, 7, 7, width)
    return jnp.pad(grid, ((0, 0), (0, 0), (0, 1), (0, 0))).reshape(images * CELLS, width)


def of_cells(rows, images):
    width = rows.shape[1]
    return rows.reshape(images, 7, 8, width)[:, :, :7].reshape(images, 1, 49, width)


def on_device_fast(
    patches,
    cotangent,
    grid_sizes,
    conv_weight,
    conv_bias,
    norm_gain,
    norm_bias,
    qkv_weight,
    spatial_bias,
    channel_bias,
    proj_weight,
    proj_bias,
    hidden_weight,
    hidden_bias,
    output_weight,
    output_bias,
):
    images = patches.shape[0]
    hidden = hidden_weight.shape[2]
    small = (
        conv_weight, conv_bias, norm_gain, norm_bias, proj_bias, output_bias, spatial_bias, channel_bias, hidden_bias
    )
    rows = jnp.concatenate([a.reshape(-1, SHORT) for a in small], axis=0)
    rows = jnp.pad(rows, ((0, ROWS_SMALL - rows.shape[0]), (0, 128 - SHORT)))
    weights = (qkv_weight, proj_weight, hidden_weight, output_weight)
    forward = run_forward(grid_sizes, to_cells(patches), rows, weights)
    activations, gathered_weights, vec, *saved = forward
    back = run_backward(grid_sizes, to_cells(cotangent), vec, saved, gathered_weights, hidden)
    grads, tiny, g_qkv, g_proj, g_hid, g_out = back
    tiny = tiny[:, :SHORT]
    return (
        of_cells(activations, images),
        of_cells(grads, images),
        tiny[:27].reshape(3, 9, SHORT),
        tiny[27:30],
        tiny[30:34],
        tiny[34:38],
        g_qkv,
        tiny[42:44].reshape(-1),
        tiny[44:47].reshape(-1),
        g_proj,
        tiny[38:40],
        g_hid,
        tiny[47:55].reshape(2, -1),
        g_out,
        tiny[40:42],
    )


def as_sent(array):
    return jax.tree.map(lambda a: a.astype(jnp.bfloat16) if a.dtype == jnp.float32 else a, array)


def image_valid(grid_sizes):
    rows = jnp.arange(7, dtype=jnp.int32)
    windows = jnp.arange(4, dtype=jnp.int32)
    top_rows = (windows // 2)[:, None] * 7 + rows[None, :]
    left_cols = (windows % 2)[:, None] * 7 + rows[None, :]
    sizes = grid_sizes[:, None, None, None]
    inside = (top_rows[None, :, :, None] < sizes) & (left_cols[None, :, None, :] < sizes)
    return inside.astype(jnp.float32).reshape(grid_sizes.shape[0], 4, 49, 1)


def layer_norm(stream, gain_row, shift_row):
    centre = jnp.mean(stream, -1, keepdims=True)
    centered = stream - centre
    variance = jnp.mean(centered * centered, -1, keepdims=True)
    return centered * lax.rsqrt(variance + EPS) * gain_row + shift_row


def gelu_exact(value_in):
    return jax.nn.gelu(value_in, approximate=False)


def matmul(left_rows, right_mat):
    return jnp.dot(left_rows, right_mat, preferred_element_type=jnp.float32)


def contract_rows(left_rows, right_rows):
    return lax.dot_general(
        left_rows, right_rows, (((0,), (0,)), ((), ())), preferred_element_type=jnp.float32
    )


def times_transposed(grad_rows, weight):
    return lax.dot_general(
        grad_rows, weight, (((1,), (1,)), ((), ())), preferred_element_type=jnp.float32
    )


def edge_lines(stream, images):
    channels = stream.shape[-1]
    image_grid = stream.reshape(images, 7, 7, channels)
    return jnp.stack(
        [image_grid[:, 0], image_grid[:, 6], image_grid[:, :, 0], image_grid[:, :, 6]], 1
    )[None]


def padded_tile(image_grid, lines, row_half, col_half):
    zero_line = jnp.zeros_like(lines[0, :, 0])
    upper = jnp.where(
        row_half == 1, jnp.where(col_half == 0, lines[0, :, 1], lines[1, :, 1]), zero_line
    )
    lower = jnp.where(
        row_half == 0, jnp.where(col_half == 0, lines[2, :, 0], lines[3, :, 0]), zero_line
    )
    left_side = jnp.where(
        col_half == 1, jnp.where(row_half == 0, lines[0, :, 3], lines[2, :, 3]), zero_line
    )
    right_side = jnp.where(
        col_half == 0, jnp.where(row_half == 0, lines[1, :, 2], lines[3, :, 2]), zero_line
    )
    zero_cell = zero_line[:, 0]
    top_left = jnp.where((row_half == 1) & (col_half == 1), lines[0, :, 1, 6], zero_cell)
    top_right = jnp.where((row_half == 1) & (col_half == 0), lines[1, :, 1, 0], zero_cell)
    bottom_left = jnp.where((row_half == 0) & (col_half == 1), lines[2, :, 0, 6], zero_cell)
    bottom_right = jnp.where((row_half == 0) & (col_half == 0), lines[3, :, 0, 0], zero_cell)
    middle = jnp.concatenate([left_side[:, :, None], image_grid, right_side[:, :, None]], 2)
    top_row = jnp.concatenate([top_left[:, None], upper, top_right[:, None]], 1)
    bottom_row = jnp.concatenate([bottom_left[:, None], lower, bottom_right[:, None]], 1)
    return jnp.concatenate([top_row[:, None], middle, bottom_row[:, None]], 1)


def position_conv(stream, images, window, weight9, shift_row, valid_rows):
    channels = stream.shape[-1]
    lines = lax.all_gather(as_sent(edge_lines(stream, images)), "win", axis=0, tiled=True)
    padded = padded_tile(stream.reshape(images, 7, 7, channels), lines, window // 2, window % 2)
    summed = jnp.zeros((images, 7, 7, channels), jnp.float32)
    for tap_index in range(9):
        row_shift, col_shift = divmod(tap_index, 3)
        summed = (
            summed
            + weight9[tap_index] * padded[:, row_shift : row_shift + 7, col_shift : col_shift + 7]
        )
    return (stream + valid_rows * (summed + shift_row).reshape(images * 49, channels), padded)


def position_conv_back(grad_stream, padded, images, window, weight9, valid_rows):
    channels = grad_stream.shape[-1]
    masked = valid_rows * grad_stream
    lines = lax.all_gather(as_sent(edge_lines(masked, images)), "win", axis=0, tiled=True)
    image_grid = masked.reshape(images, 7, 7, channels)
    grad_pad = padded_tile(image_grid, lines, window // 2, window % 2)
    summed = jnp.zeros((images, 7, 7, channels), jnp.float32)
    tap_grads = []
    for tap_index in range(9):
        row_shift, col_shift = divmod(tap_index, 3)
        summed = (
            summed
            + weight9[tap_index]
            * grad_pad[:, 2 - row_shift : 9 - row_shift, 2 - col_shift : 9 - col_shift]
        )
        tap_grads.append(
            jnp.sum(
                image_grid * padded[:, row_shift : row_shift + 7, col_shift : col_shift + 7],
                axis=(0, 1, 2),
            )
        )
    return (
        grad_stream + summed.reshape(grad_stream.shape),
        jnp.stack(tap_grads),
        jnp.sum(image_grid, axis=(0, 1, 2)),
    )


def mlp_forward(normed, weight_in, bias_in, weight_out, bias_out):
    activated = gelu_exact(matmul(normed, weight_in) + bias_in).astype(jnp.bfloat16)
    return matmul(activated, weight_out) + bias_out


def mlp_backward(normed, grad_stream, valid_rows, weight_in, bias_in, weight_out):
    hidden_pre = matmul(normed, weight_in) + bias_in
    activated, gelu_pull = jax.vjp(gelu_exact, hidden_pre)
    grad_branch = (valid_rows * grad_stream).astype(jnp.bfloat16)
    grad_weight_out = contract_rows(activated.astype(jnp.bfloat16), grad_branch)
    grad_bias_out = jnp.sum(grad_branch.astype(jnp.float32), 0)
    grad_pre = gelu_pull(times_transposed(grad_branch, weight_out))[0].astype(jnp.bfloat16)
    grad_weight_in = contract_rows(normed, grad_pre)
    grad_bias_in = jnp.sum(grad_pre.astype(jnp.float32), 0)
    return (
        times_transposed(grad_pre, weight_in),
        grad_weight_in,
        grad_bias_in,
        grad_weight_out,
        grad_bias_out,
    )


def norm_backward(stream, gain_row, shift_row, grad_normed):
    unused, norm_pull = jax.vjp(layer_norm, stream, gain_row, shift_row)
    return norm_pull(grad_normed)


def window_probs(packed, images, scaling, valid_rows):
    split = packed.reshape(images, 49, 3, HEADS, HEAD)
    query_rows = split[:, :, 0]
    key_rows = split[:, :, 1]
    value_rows = split[:, :, 2]
    key_ok = valid_rows.reshape(images, 1, 1, 49) > 0.5
    scores = (
        jnp.einsum("iphe,iqhe->ihpq", query_rows, key_rows, preferred_element_type=jnp.float32)
        * scaling
    )
    scores = jnp.where(key_ok, scores, -1000000000.0)
    return (query_rows, key_rows, value_rows, jax.nn.softmax(scores, axis=-1))


def channel_mixing(gram_total, scaling):
    return jax.nn.softmax(gram_total * scaling, axis=-1)


def channel_grads(
    grad_mixing, mixing, grad_context, key_masked, value_masked, valid_cells, scaling
):
    grad_query = jnp.einsum(
        "bgcd,bpgc->bpgd",
        mixing.astype(jnp.bfloat16),
        grad_context,
        preferred_element_type=jnp.float32,
    )
    grad_gram = (mixing * (grad_mixing - jnp.sum(mixing * grad_mixing, -1, keepdims=True))).astype(
        jnp.bfloat16
    )
    grad_keys = (
        jnp.einsum("bgcd,bpgd->bpgc", grad_gram, value_masked, preferred_element_type=jnp.float32)
        * scaling
        * valid_cells
    )
    grad_values = (
        jnp.einsum("bgcd,bpgc->bpgd", grad_gram, key_masked, preferred_element_type=jnp.float32)
        * scaling
        * valid_cells
    )
    return jnp.stack([grad_query, grad_keys, grad_values], 2).astype(jnp.bfloat16)


def on_device(
    patches,
    cotangent,
    grid_sizes,
    conv_weight,
    conv_bias,
    norm_gain,
    norm_bias,
    qkv_weight,
    spatial_bias,
    channel_bias,
    proj_weight,
    proj_bias,
    hidden_weight,
    hidden_bias,
    output_weight,
    output_bias,
):
    (
        conv_w,
        conv_b,
        gains,
        shifts,
        qkv_w,
        sp_bias,
        ch_bias,
        proj_w,
        proj_b,
        hid_w,
        hid_b,
        out_w,
        out_b,
    ) = (
        lax.all_gather(conv_weight, "dp", axis=2, tiled=True),
        lax.all_gather(conv_bias, "dp", axis=1, tiled=True),
        lax.all_gather(norm_gain, "dp", axis=1, tiled=True),
        lax.all_gather(norm_bias, "dp", axis=1, tiled=True),
        lax.all_gather(qkv_weight, "dp", axis=1, tiled=True),
        lax.all_gather(spatial_bias, "dp", axis=0, tiled=True),
        lax.all_gather(channel_bias, "dp", axis=0, tiled=True),
        lax.all_gather(proj_weight, "dp", axis=1, tiled=True),
        lax.all_gather(proj_bias, "dp", axis=1, tiled=True),
        lax.all_gather(hidden_weight, "dp", axis=1, tiled=True),
        lax.all_gather(hidden_bias, "dp", axis=1, tiled=True),
        lax.all_gather(output_weight, "dp", axis=1, tiled=True),
        lax.all_gather(output_bias, "dp", axis=1, tiled=True),
    )
    conv_w = conv_w.astype(jnp.float32)
    conv_b = conv_b.astype(jnp.float32)
    gains = gains.astype(jnp.float32)
    shifts = shifts.astype(jnp.float32)
    sp_bias = sp_bias.astype(jnp.float32)
    ch_bias = ch_bias.astype(jnp.float32)
    proj_b = proj_b.astype(jnp.float32)
    hid_b = hid_b.astype(jnp.float32)
    out_b = out_b.astype(jnp.float32)
    images = patches.shape[0]
    model_width = patches.shape[-1]
    rows_all = images * 49
    group_count = lax.axis_size("win")
    local_heads = HEADS // group_count
    group_width = model_width // group_count
    scaling = HEAD ** (-0.5)
    window = lax.axis_index("win")
    full_valid = image_valid(grid_sizes)
    valid_rows = lax.dynamic_slice_in_dim(full_valid, window, 1, 1).reshape(rows_all, 1)
    stream0 = patches.astype(jnp.float32).reshape(rows_all, model_width) * valid_rows
    stream1, pad_first = position_conv(stream0, images, window, conv_w[0], conv_b[0], valid_rows)
    normed1 = layer_norm(stream1, gains[0], shifts[0]).astype(jnp.bfloat16)
    packed_bias = jnp.concatenate(
        [sp_bias[:model_width], jnp.zeros((model_width,), jnp.float32), sp_bias[model_width:]]
    )
    packed1 = (matmul(normed1, qkv_w[0]) + packed_bias).astype(jnp.bfloat16)
    query1, keys1, values1, probs1 = window_probs(packed1, images, scaling, valid_rows)
    context1 = (
        jnp.einsum(
            "ihpq,iqhe->iphe",
            probs1.astype(jnp.bfloat16),
            values1,
            preferred_element_type=jnp.float32,
        )
        .astype(jnp.bfloat16)
        .reshape(rows_all, model_width)
    )
    stream2 = stream1 + valid_rows * (matmul(context1, proj_w[0]) + proj_b[0])
    stream3, pad_second = position_conv(stream2, images, window, conv_w[1], conv_b[1], valid_rows)
    normed3 = layer_norm(stream3, gains[1], shifts[1]).astype(jnp.bfloat16)
    stream4 = stream3 + valid_rows * mlp_forward(normed3, hid_w[0], hid_b[0], out_w[0], out_b[0])
    stream5, pad_third = position_conv(stream4, images, window, conv_w[2], conv_b[2], valid_rows)
    normed5 = layer_norm(stream5, gains[2], shifts[2]).astype(jnp.bfloat16)
    packed5 = (matmul(normed5, qkv_w[1]) + ch_bias).astype(jnp.bfloat16)
    moved = lax.all_to_all(
        packed5.reshape(images, 1, 49, 3, group_count, group_width),
        "win",
        split_axis=4,
        concat_axis=1,
        tiled=True,
    )
    grouped = moved.reshape(images, 196, 3, local_heads, HEAD)
    valid_cells = full_valid.reshape(images, 196, 1, 1)
    query5 = grouped[:, :, 0]
    key_masked = grouped[:, :, 1] * valid_cells.astype(jnp.bfloat16)
    value_masked = grouped[:, :, 2] * valid_cells.astype(jnp.bfloat16)
    gram_total = jnp.einsum(
        "bpgc,bpgd->bgcd", key_masked, value_masked, preferred_element_type=jnp.float32
    )
    mixing = channel_mixing(gram_total, scaling)
    context_groups = jnp.einsum(
        "bgcd,bpgd->bpgc", mixing.astype(jnp.bfloat16), query5, preferred_element_type=jnp.float32
    ).astype(jnp.bfloat16)
    returned = lax.all_to_all(
        context_groups.reshape(images, 4, 49, 1, group_width),
        "win",
        split_axis=1,
        concat_axis=3,
        tiled=True,
    )
    context5 = returned.reshape(rows_all, model_width)
    stream6 = stream5 + valid_rows * (matmul(context5, proj_w[1]) + proj_b[1])
    normed6 = layer_norm(stream6, gains[3], shifts[3]).astype(jnp.bfloat16)
    stream7 = stream6 + valid_rows * mlp_forward(normed6, hid_w[1], hid_b[1], out_w[1], out_b[1])
    activations = stream7.astype(jnp.bfloat16).reshape(patches.shape)
    grad7 = cotangent.astype(jnp.float32).reshape(rows_all, model_width)
    grad_normed, hid_w_grad1, hid_b_grad1, out_w_grad1, out_b_grad1 = mlp_backward(
        normed6, grad7, valid_rows, hid_w[1], hid_b[1], out_w[1]
    )
    grad_part, gain_grad3, shift_grad3 = norm_backward(stream6, gains[3], shifts[3], grad_normed)
    grad6 = grad7 + grad_part
    branch_grad = (valid_rows * grad6).astype(jnp.bfloat16)
    proj_w_grad1 = contract_rows(context5, branch_grad)
    proj_b_grad1 = jnp.sum(branch_grad.astype(jnp.float32), 0)
    context_grad = times_transposed(branch_grad, proj_w[1]).astype(jnp.bfloat16)
    moved_grad = lax.all_to_all(
        context_grad.reshape(images, 1, 49, group_count, group_width),
        "win",
        split_axis=3,
        concat_axis=1,
        tiled=True,
    )
    group_grad = moved_grad.reshape(images, 196, local_heads, HEAD)
    mixing_grad = jnp.einsum(
        "bpgc,bpgd->bgcd", group_grad, query5, preferred_element_type=jnp.float32
    )
    stacked = channel_grads(
        mixing_grad, mixing, group_grad, key_masked, value_masked, valid_cells, scaling
    )
    sent_back = lax.all_to_all(
        stacked.reshape(images, 4, 49, 3, 1, group_width),
        "win",
        split_axis=1,
        concat_axis=4,
        tiled=True,
    )
    packed_grad5 = sent_back.reshape(rows_all, 3 * model_width)
    qkv_w_grad1 = contract_rows(normed5, packed_grad5)
    ch_bias_grad = jnp.sum(packed_grad5.astype(jnp.float32), 0)
    grad_part, gain_grad2, shift_grad2 = norm_backward(
        stream5, gains[2], shifts[2], times_transposed(packed_grad5, qkv_w[1])
    )
    grad5 = grad6 + grad_part
    grad4, conv_w_grad2, conv_b_grad2 = position_conv_back(
        grad5, pad_third, images, window, conv_w[2], valid_rows
    )
    grad_normed, hid_w_grad0, hid_b_grad0, out_w_grad0, out_b_grad0 = mlp_backward(
        normed3, grad4, valid_rows, hid_w[0], hid_b[0], out_w[0]
    )
    grad_part, gain_grad1, shift_grad1 = norm_backward(stream3, gains[1], shifts[1], grad_normed)
    grad3 = grad4 + grad_part
    grad2, conv_w_grad1, conv_b_grad1 = position_conv_back(
        grad3, pad_second, images, window, conv_w[1], valid_rows
    )
    branch_grad = (valid_rows * grad2).astype(jnp.bfloat16)
    proj_w_grad0 = contract_rows(context1, branch_grad)
    proj_b_grad0 = jnp.sum(branch_grad.astype(jnp.float32), 0)
    context_grad = (
        times_transposed(branch_grad, proj_w[0])
        .astype(jnp.bfloat16)
        .reshape(images, 49, HEADS, HEAD)
    )
    probs_low = probs1.astype(jnp.bfloat16)
    probs_grad = jnp.einsum(
        "iphe,iqhe->ihpq", context_grad, values1, preferred_element_type=jnp.float32
    )
    values_grad = jnp.einsum(
        "ihpq,iphe->iqhe", probs_low, context_grad, preferred_element_type=jnp.float32
    )
    scores_grad = (probs1 * (probs_grad - jnp.sum(probs1 * probs_grad, -1, keepdims=True))).astype(
        jnp.bfloat16
    )
    key_ok = valid_rows.reshape(images, 1, 1, 49) > 0.5
    scores_grad = jnp.where(key_ok, scores_grad, jnp.zeros_like(scores_grad))
    query_grad = (
        jnp.einsum("ihpq,iqhe->iphe", scores_grad, keys1, preferred_element_type=jnp.float32)
        * scaling
    )
    keys_grad = (
        jnp.einsum("ihpq,iphe->iqhe", scores_grad, query1, preferred_element_type=jnp.float32)
        * scaling
    )
    packed_grad1 = (
        jnp.stack([query_grad, keys_grad, values_grad], 2)
        .astype(jnp.bfloat16)
        .reshape(rows_all, 3 * model_width)
    )
    qkv_w_grad0 = contract_rows(normed1, packed_grad1)
    packed_sums = jnp.sum(packed_grad1.astype(jnp.float32), 0)
    sp_bias_grad = jnp.concatenate([packed_sums[:model_width], packed_sums[2 * model_width :]])
    grad_part, gain_grad0, shift_grad0 = norm_backward(
        stream1, gains[0], shifts[0], times_transposed(packed_grad1, qkv_w[0])
    )
    grad1 = grad2 + grad_part
    grad0, conv_w_grad0, conv_b_grad0 = position_conv_back(
        grad1, pad_first, images, window, conv_w[0], valid_rows
    )
    patches_grad = (grad0 * valid_rows).astype(jnp.bfloat16).reshape(patches.shape)
    local_sums = (
        lax.psum_scatter(
            jnp.stack([conv_w_grad0, conv_w_grad1, conv_w_grad2]),
            "dp",
            scatter_dimension=2,
            tiled=True,
        ),
        lax.psum_scatter(
            jnp.stack([conv_b_grad0, conv_b_grad1, conv_b_grad2]),
            "dp",
            scatter_dimension=1,
            tiled=True,
        ),
        lax.psum_scatter(
            jnp.stack([gain_grad0, gain_grad1, gain_grad2, gain_grad3]),
            "dp",
            scatter_dimension=1,
            tiled=True,
        ),
        lax.psum_scatter(
            jnp.stack([shift_grad0, shift_grad1, shift_grad2, shift_grad3]),
            "dp",
            scatter_dimension=1,
            tiled=True,
        ),
        lax.psum_scatter(
            jnp.stack([qkv_w_grad0, qkv_w_grad1]), "dp", scatter_dimension=1, tiled=True
        ),
        lax.psum_scatter(sp_bias_grad, "dp", scatter_dimension=0, tiled=True),
        lax.psum_scatter(ch_bias_grad, "dp", scatter_dimension=0, tiled=True),
        lax.psum_scatter(
            jnp.stack([proj_w_grad0, proj_w_grad1]), "dp", scatter_dimension=1, tiled=True
        ),
        lax.psum_scatter(
            jnp.stack([proj_b_grad0, proj_b_grad1]), "dp", scatter_dimension=1, tiled=True
        ),
        lax.psum_scatter(
            jnp.stack([hid_w_grad0, hid_w_grad1]), "dp", scatter_dimension=1, tiled=True
        ),
        lax.psum_scatter(
            jnp.stack([hid_b_grad0, hid_b_grad1]), "dp", scatter_dimension=1, tiled=True
        ),
        lax.psum_scatter(
            jnp.stack([out_w_grad0, out_w_grad1]), "dp", scatter_dimension=1, tiled=True
        ),
        lax.psum_scatter(
            jnp.stack([out_b_grad0, out_b_grad1]), "dp", scatter_dimension=1, tiled=True
        ),
    )
    summed = (
        lax.psum(local_sums[0].astype(jnp.bfloat16), "win").astype(jnp.float32),
        lax.psum(local_sums[1].astype(jnp.bfloat16), "win").astype(jnp.float32),
        lax.psum(local_sums[2].astype(jnp.bfloat16), "win").astype(jnp.float32),
        lax.psum(local_sums[3].astype(jnp.bfloat16), "win").astype(jnp.float32),
        lax.psum(local_sums[4].astype(jnp.bfloat16), "win").astype(jnp.float32),
        lax.psum(local_sums[5].astype(jnp.bfloat16), "win").astype(jnp.float32),
        lax.psum(local_sums[6].astype(jnp.bfloat16), "win").astype(jnp.float32),
        lax.psum(local_sums[7].astype(jnp.bfloat16), "win").astype(jnp.float32),
        lax.psum(local_sums[8].astype(jnp.bfloat16), "win").astype(jnp.float32),
        lax.psum(local_sums[9].astype(jnp.bfloat16), "win").astype(jnp.float32),
        lax.psum(local_sums[10].astype(jnp.bfloat16), "win").astype(jnp.float32),
        lax.psum(local_sums[11].astype(jnp.bfloat16), "win").astype(jnp.float32),
        lax.psum(local_sums[12].astype(jnp.bfloat16), "win").astype(jnp.float32),
    )
    return (activations, patches_grad) + tuple(summed)


def solution(mesh):
    small = mesh.shape["dp"] == 8 and mesh.shape["win"] == 4
    return jax.shard_map(
        on_device_fast if small else on_device,
        mesh=mesh,
        in_specs=(
            P("dp", "win", None, None),
            P("dp", "win", None, None),
            P("dp"),
            P(None, None, "dp"),
            P(None, "dp"),
            P(None, "dp"),
            P(None, "dp"),
            P(None, "dp", None),
            P("dp"),
            P("dp"),
            P(None, "dp", None),
            P(None, "dp"),
            P(None, "dp", None),
            P(None, "dp"),
            P(None, "dp", None),
            P(None, "dp"),
        ),
        out_specs=(
            P("dp", "win", None, None),
            P("dp", "win", None, None),
            P(None, None, "dp"),
            P(None, "dp"),
            P(None, "dp"),
            P(None, "dp"),
            P(None, "dp", None),
            P("dp"),
            P("dp"),
            P(None, "dp", None),
            P(None, "dp"),
            P(None, "dp", None),
            P(None, "dp"),
            P(None, "dp", None),
            P(None, "dp"),
        ),
        check_vma=False,
    )
```
